128 devices in a mesh: row: 16 (over y_lo, z, core), col: 8 (over y_hi, x).
Axes of the slice: x: 4, y: 4 (y_hi: 2, y_lo: 2; y = y_hi * 2 + y_lo), z: 4, core: 2. Of those that a mesh axis runs over, the one named last changes fastest.
Arguments:
- hidden_in: bfloat16 [2, 4096, 2048], P(None, 'row', 'col'), may hold values from -6 to 6
- gain_first: float32 [2048], replicated, may hold values from 0.25 to 1.75
- query_down: bfloat16 [2048, 1536], P('row', 'col'), may hold values from -0.125 to 0.125
- query_gain: float32 [1536], replicated, may hold values from 0.25 to 1.75
- query_up: bfloat16 [1536, 3072], P('row', 'col'), may hold values from -0.15625 to 0.15625
- latent_down: bfloat16 [2048, 576], P('row', 'col'), may hold values from -0.125 to 0.125
- latent_gain: float32 [512], replicated, may hold values from 0.25 to 1.75
- latent_up: bfloat16 [512, 4096], P('row', 'col'), may hold values from -0.25 to 0.25
- attention_out: bfloat16 [2048, 2048], P('col', 'row'), may hold values from -2 to 2
- gain_second: float32 [2048], replicated, may hold values from 0.25 to 1.75
- router: bfloat16 [2048, 16], P('row'), may hold values from -0.0625 to 0.0625
- expert_gate: bfloat16 [16, 2048, 1408], P('col', 'row'), may hold values from -0.125 to 0.125
- expert_up: bfloat16 [16, 2048, 1408], P('col', 'row'), may hold values from -0.125 to 0.125
- expert_down: bfloat16 [16, 1408, 2048], P('col', 'row'), may hold values from -0.15625 to 0.15625
- shared_gate: bfloat16 [2048, 2816], P('row', 'col'), may hold values from -0.125 to 0.125
- shared_up: bfloat16 [2048, 2816], P('row', 'col'), may hold values from -0.125 to 0.125
- shared_down: bfloat16 [2816, 2048], P('col', 'row'), may hold values from -0.109375 to 0.109375
- seq_lens: int32 [2], replicated, may hold values from 1024 to 4096, as said below
- routes: int32 [2, 4096, 6], P(None, 'row'), may hold values from 0 to 15, all different within a row; in each aligned block of 256 rows (0 to 255, 256 to 511, ..., all dimensions but the last counted through in order) at most 120 rows name the same one
- out_grad: bfloat16 [2, 4096, 2048], P(None, 'row', 'col'), may hold values from -6 to 6
Outputs:
- block_out: bfloat16 [2, 4096, 2048], P(None, 'row', 'col')
- hidden_grad: float32 [2, 4096, 2048], P(None, 'row', 'col')
- gain_first_grad: float32 [2048], replicated
- query_down_grad: float32 [2048, 1536], P('row', 'col')
- query_gain_grad: float32 [1536], replicated
- query_up_grad: float32 [1536, 3072], P('row', 'col')
- latent_down_grad: float32 [2048, 576], P('row', 'col')
- latent_gain_grad: float32 [512], replicated
- latent_up_grad: float32 [512, 4096], P('row', 'col')
- attention_out_grad: float32 [2048, 2048], P('col', 'row')
- gain_second_grad: float32 [2048], replicated
- router_grad: float32 [2048, 16], P('row')
- expert_gate_grad: float32 [16, 2048, 1408], P('col', 'row')
- expert_up_grad: float32 [16, 2048, 1408], P('col', 'row')
- expert_down_grad: float32 [16, 1408, 2048], P('col', 'row')
- shared_gate_grad: float32 [2048, 2816], P('row', 'col')
- shared_up_grad: float32 [2048, 2816], P('row', 'col')
- shared_down_grad: float32 [2816, 2048], P('col', 'row')
The draws below stay inside these ranges and needn't reach their ends.
Inputs may be any that keep to these rules, and one draw needn't show every extreme that they name: `seq_lens`: every live length lies between 1024 and 4096; one sequence of the batch is 4096 long. `routes`: each position names 6 different experts; in each aligned block of 256 positions of a sequence no expert is named by more than 120 positions, and in some block one expert is named by exactly 120.
All inputs are finite; a program needn't handle non-finite values.
Results may differ from the reference program's by a relative error of at most 0.028.
Values may be sent and summed in bfloat16 or wider, within the bound.
A program may use at most 256 MiB of HBM per device.

```python
import math
import jax
import jax.numpy as jnp
import numpy as np
from jax import lax

D = 2048
H = 16
DN = 128
DR = 64
DV = 128
QL = 1536
KL = 512
FF = 1408
SF = 2816
EXPERTS = 16
TOPK = 6
SEQS = 2
TS = 256
LEN = 4096
MOST = 120


def draw_seq_lens(key, part):
    key = jax.random.fold_in(key, 11)
    first_key, second_key = jax.random.split(key)
    others = jax.random.randint(first_key, (SEQS,), LEN // 4, LEN + 1)
    longest = jax.random.randint(second_key, (), 0, SEQS)
    return jnp.where(jnp.arange(SEQS) == longest, LEN, others).astype(jnp.int32)


def block_scale(stream_key, dims, shards, low, largest):
    level, own = 1.0, jax.random.fold_in(stream_key, 6)
    for dim, blocks in shards:
        draws = jnp.exp(jax.random.uniform(jax.random.fold_in(own, dim), (blocks,), jnp.float32, low / len(shards), largest / len(shards)))
        level = level * jnp.repeat(draws, dims[dim] // blocks).reshape([-1 if axis == dim else 1 for axis in range(len(dims))])
    return level


def deal_out(key, own, number, rows, count, top, bound, lean):
    ranking = jax.random.permutation(key, count)
    crowded, common = portions_of(count, rows * top, bound, lean, True), portions_of(count, rows * top, bound, lean, False)
    places = jnp.arange(count)

    def named(sizes, rotation):
        used = int((sizes > 0).sum())
        fixed = max(1, used // 4)
        moved = fixed + (places - fixed + rotation * (used - fixed)) % max(1, count - fixed)
        return jnp.zeros((count,), jnp.int32).at[ranking[jnp.where(places < fixed, places, moved)]].set(jnp.asarray(sizes, jnp.int32))

    sizes = jnp.where(number % 4 == 0, named(crowded, number // 4), named(common, number - number // 4 - 1))
    mixed = jax.random.permutation(jax.random.fold_in(own, 3), count)
    giver, sink = mixed[0:count // 2 * 2:2], mixed[1:count // 2 * 2:2]
    slack = jnp.minimum(sizes[giver] - 1, bound - sizes[sink]) // 2
    slack = jnp.where((giver == ranking[0]) | (sink == ranking[0]) | (sizes[sink] == 0), 0, jnp.maximum(slack, 0))
    moved = jax.random.randint(jax.random.fold_in(own, 4), (count // 2,), 0, 1 << 20) % (slack + 1)
    sizes = sizes.at[giver].add(-moved).at[sink].add(moved)
    items = jnp.searchsorted(jnp.cumsum(sizes), jnp.arange(rows * top), side="right").astype(jnp.int32)
    listing = items.reshape(top, rows).T
    listing = listing[jax.random.permutation(jax.random.fold_in(own, 1), rows)]
    rotation = jax.random.randint(jax.random.fold_in(own, 2), (rows, 1), 0, top)
    return jnp.take_along_axis(listing, (jnp.arange(top)[None, :] + rotation) % top, axis=1)


def portions_of(number_of, total, reach, lean, full):
    portions = [(1 << 20) // math.isqrt(rank ** lean) + 1 for rank in range(1, number_of + 1)]
    largest = reach if full else min(reach, max(-(-total // number_of), total * portions[0] // sum(portions)))
    least = 1 if total - largest >= number_of - 1 else 0
    given, spare = [largest] + [least] * (number_of - 1), total - largest - least * (number_of - 1)
    while spare > 0:
        movable = [i for i in range(1, number_of) if given[i] < largest] or [i for i in range(1, number_of) if given[i] < reach]
        mass, budget = sum([portions[i] for i in movable]), spare
        for i in movable:
            addition = min(reach - given[i], max(1, budget * portions[i] // mass), spare)
            given[i] = given[i] + addition
            spare = spare - addition
    return np.array(given)


def normal_values(stream_key, shape, deviation, reach, cuts=(), kind=jnp.bfloat16):
    drawn = jax.random.normal(stream_key, shape, jnp.float32) * deviation
    if len(cuts) > 0:
        drawn = block_scale(stream_key, shape, cuts, -0.22, 0.18) * drawn
    return jnp.clip(drawn, min=-reach, max=reach).astype(kind)


def setup_inputs(seed: int = 0) -> dict:
    seeds = jax.random.split(jax.random.key(seed), 21)
    hidden_in = normal_values(seeds[0], (SEQS, LEN, D), 1.0, 6.0, ((1, 16), (2, 8)))
    gain_first = jnp.clip(1.0 + 0.15 * jax.random.normal(seeds[1], (D,), jnp.float32), 0.25, 1.75)
    query_down = normal_values(seeds[2], (D, QL), D ** -0.5, 0.125, ((0, 16), (1, 8)))
    query_gain = jnp.clip(1.0 + 0.15 * jax.random.normal(seeds[3], (QL,), jnp.float32), 0.25, 1.75)
    query_up = normal_values(seeds[4], (QL, H * (DN + DR)), QL ** -0.5, 0.15625, ((0, 16), (1, 8)))
    latent_down = normal_values(seeds[5], (D, KL + DR), D ** -0.5, 0.125, ((0, 16), (1, 8)))
    latent_gain = jnp.clip(1.0 + 0.15 * jax.random.normal(seeds[6], (KL,), jnp.float32), 0.25, 1.75)
    latent_up = normal_values(seeds[7], (KL, H * (DN + DV)), KL ** -0.5, 0.25, ((0, 16), (1, 8)))
    attention_out = normal_values(seeds[8], (H * DV, D), (max(H * DV * 16 // LEN, 1)) ** -0.5, 2.0, ((0, 8), (1, 16)))
    gain_second = jnp.clip(1.0 + 0.15 * jax.random.normal(seeds[9], (D,), jnp.float32), 0.25, 1.75)
    router = normal_values(seeds[10], (D, EXPERTS), (4 * D) ** -0.5, 0.0625, ((0, 16),))
    expert_gate = normal_values(seeds[11], (EXPERTS, D, FF), D ** -0.5, 0.125, ((0, 8), (1, 16)))
    expert_up = normal_values(seeds[12], (EXPERTS, D, FF), D ** -0.5, 0.125, ((0, 8), (1, 16)))
    expert_down = normal_values(seeds[13], (EXPERTS, FF, D), FF ** -0.5, 0.15625, ((0, 8), (1, 16)))
    shared_gate = normal_values(seeds[14], (D, SF), D ** -0.5, 0.125, ((0, 16), (1, 8)))
    shared_up = normal_values(seeds[15], (D, SF), D ** -0.5, 0.125, ((0, 16), (1, 8)))
    shared_down = normal_values(seeds[16], (SF, D), SF ** -0.5, 0.109375, ((0, 8), (1, 16)))
    seq_lens = draw_seq_lens(jax.random.fold_in(seeds[20], 71), 0)
    routes_keys = jax.random.split(jax.random.fold_in(seeds[18], 1), SEQS * LEN // TS)
    routes_turns = jax.random.permutation(jax.random.fold_in(seeds[18], 3), SEQS * LEN // TS)
    routes = jax.vmap(lambda own, number: deal_out(jax.random.fold_in(seeds[18], 2), own, number, TS, EXPERTS, TOPK, MOST, 1))(routes_keys, routes_turns).reshape((SEQS, LEN, TOPK))
    out_grad = normal_values(seeds[19], (SEQS, LEN, D), 1.0, 6.0, ((1, 16), (2, 8)))
    return dict(hidden_in=hidden_in, gain_first=gain_first, query_down=query_down, query_gain=query_gain, query_up=query_up, latent_down=latent_down, latent_gain=latent_gain, latent_up=latent_up, attention_out=attention_out, gain_second=gain_second, router=router, expert_gate=expert_gate, expert_up=expert_up, expert_down=expert_down, shared_gate=shared_gate, shared_up=shared_up, shared_down=shared_down, seq_lens=seq_lens, routes=routes, out_grad=out_grad)


eps = 1e-06
route_scale = 2.446
rope_base = 50000.0

@jax.custom_vjp
def low(v):
    return lax.optimization_barrier(v.astype(jnp.bfloat16)).astype(jnp.float32)

@jax.custom_vjp
def low_back(v):
    return v

def low_keep(v):
    return (low(v), None)

def low_pass(kept, grad):
    return (grad,)

def back_keep(v):
    return (v, None)

def back_low(kept, grad):
    return (low(grad),)
low.defvjp(low_keep, low_pass)
low_back.defvjp(back_keep, back_low)

def rope_tables(positions, width):
    half_width = width // 2
    frequency = jnp.exp(-jnp.log(rope_base) * (2.0 * jnp.arange(half_width, dtype=jnp.float32) / width))
    angles = positions.astype(jnp.float32)[:, None] * frequency[None, :]
    return (jnp.cos(angles), jnp.sin(angles))

def rotate(values, rope_cos, rope_sin):
    half_width = values.shape[-1] // 2
    first_half = values[..., :half_width]
    second_half = values[..., half_width:]
    return jnp.concatenate([first_half * rope_cos - second_half * rope_sin, second_half * rope_cos + first_half * rope_sin], axis=-1)

def matmul(left, right):
    return jnp.matmul(left, right, precision=lax.Precision.HIGHEST)

def normalize(values, gain):
    return values * lax.rsqrt(lax.optimization_barrier(jnp.mean(values * values, axis=-1, keepdims=True)) + eps) * gain

def attend_block(query_block, start, key_all, value_all, seq_lens):
    score_scale = 1.0 / math.sqrt(DN + DR)
    scores = jnp.einsum('sqhd,skhd->shqk', query_block, key_all, precision=lax.Precision.HIGHEST) * score_scale
    scores = low_back(scores)
    query_pos = start + jnp.arange(query_block.shape[1], dtype=jnp.int32)
    key_pos = jnp.arange(key_all.shape[1], dtype=jnp.int32)
    key_valid = (key_pos[None, None, :] <= query_pos[None, :, None]) & (key_pos[None, None, :] < seq_lens[:, None, None])
    scores = jnp.where(key_valid[:, None], scores, -1e+30)
    row_max = lax.optimization_barrier(jnp.max(scores, axis=-1, keepdims=True))
    weights = jnp.exp(scores - row_max)
    probability = low(weights / lax.optimization_barrier(jnp.sum(weights, axis=-1, keepdims=True)))
    return jnp.einsum('shqk,skhd->sqhd', probability, value_all, precision=lax.Precision.HIGHEST)

def forward(hidden, gain_first, query_down, query_gain, query_up, latent_down, latent_gain, latent_up, attention_out, gain_second, router, expert_gate, expert_up, expert_down, shared_gate, shared_up, shared_down, seq_lens, routes):
    row_total = SEQS * LEN
    flat_hidden = hidden.reshape(row_total, D)
    normed_first = low(normalize(flat_hidden, gain_first))
    query_latent = low(low_back(matmul(normed_first, query_down)))
    kv_latent = low(low_back(matmul(normed_first, latent_down)))
    query_input = low(normalize(query_latent, query_gain))
    latent_input = low(normalize(kv_latent[:, :KL], latent_gain))
    positions = jnp.arange(LEN, dtype=jnp.int32)
    rope_cos, rope_sin = rope_tables(positions, DR)
    query_proj = low_back(matmul(query_input, query_up)).reshape(SEQS, LEN, H, DN + DR)
    query_rot = rotate(query_proj[..., DN:], rope_cos[None, :, None, :], rope_sin[None, :, None, :])
    query_all = low(jnp.concatenate([query_proj[..., :DN], query_rot], axis=-1))
    key_value = low_back(matmul(latent_input, latent_up)).reshape(SEQS, LEN, H, DN + DV)
    key_rope = rotate(kv_latent[:, KL:].reshape(SEQS, LEN, DR), rope_cos[None], rope_sin[None])
    key_all = low(jnp.concatenate([key_value[..., :DN], jnp.broadcast_to(key_rope[:, :, None, :], (SEQS, LEN, H, DR))], axis=-1))
    value_all = low(key_value[..., DN:])
    block_rows = math.gcd(LEN, 512)
    block_count = LEN // block_rows
    query_blocks = jnp.transpose(query_all.reshape(SEQS, block_count, block_rows, H, DN + DR), (1, 0, 2, 3, 4))
    starts = jnp.arange(block_count, dtype=jnp.int32) * block_rows

    def attend_one(block_pair):
        return attend_block(block_pair[0], block_pair[1], key_all, value_all, seq_lens)
    attended = lax.map(jax.checkpoint(attend_one), (query_blocks, starts))
    attended = jnp.transpose(attended, (1, 0, 2, 3, 4)).reshape(row_total, H * DV)
    attended = low(low_back(attended))
    attention_sum = low_back(matmul(attended, attention_out))
    residual_one = flat_hidden + attention_sum
    normed_second = low(normalize(residual_one, gain_second))
    logits = low_back(matmul(normed_second, router))
    sigmoid_all = jax.nn.sigmoid(logits)
    chosen = lax.optimization_barrier(jnp.sum((routes.reshape(row_total, TOPK)[:, :, None] == jnp.arange(EXPERTS, dtype=jnp.int32)[None, None, :]).astype(jnp.float32), axis=1))
    gate_weights = route_scale * sigmoid_all * chosen / lax.optimization_barrier(jnp.sum(sigmoid_all * chosen, axis=-1, keepdims=True))

    def expert_step(carried, stacked):
        gate_weight, up_weight, down_weight, gate_column = stacked
        gate_value = low_back(matmul(normed_second, gate_weight))
        up_value = low_back(matmul(normed_second, up_weight))
        hidden_act = low(jax.nn.silu(gate_value) * up_value)
        expert_value = low_back(matmul(hidden_act, down_weight))
        return (carried + gate_column[:, None] * expert_value, None)
    routed, unused = lax.scan(jax.checkpoint(expert_step), jnp.zeros((row_total, D), jnp.float32), (expert_gate, expert_up, expert_down, gate_weights.T))
    shared_gate_val = low_back(matmul(normed_second, shared_gate))
    shared_up_val = low_back(matmul(normed_second, shared_up))
    shared_act = low(jax.nn.silu(shared_gate_val) * shared_up_val)
    shared_result = matmul(shared_act, shared_down)
    return (residual_one + routed + shared_result).reshape(SEQS, LEN, D)

def reference(hidden_in, gain_first, query_down, query_gain, query_up, latent_down, latent_gain, latent_up, attention_out, gain_second, router, expert_gate, expert_up, expert_down, shared_gate, shared_up, shared_down, seq_lens, routes, out_grad):
    inputs = (hidden_in, gain_first, query_down, query_gain, query_up, latent_down, latent_gain, latent_up, attention_out, gain_second, router, expert_gate, expert_up, expert_down, shared_gate, shared_up, shared_down)
    floats = tuple((array_in.astype(jnp.float32) for array_in in inputs))

    def closed(*arrays):
        return forward(*arrays, seq_lens, routes)
    result, pullback = jax.vjp(closed, *floats)
    gradients = pullback(out_grad.astype(jnp.float32))
    return (result.astype(jnp.bfloat16), gradients[0], gradients[1], gradients[2], gradients[3], gradients[4], gradients[5], gradients[6], gradients[7], gradients[8], gradients[9], gradients[10], gradients[11], gradients[12], gradients[13], gradients[14], gradients[15], gradients[16])
```

```python
import functools
import math

import jax
import jax.numpy as jnp
from jax import lax
from jax.experimental import pallas as pl
from jax.experimental.pallas import tpu as pltpu
from jax.sharding import PartitionSpec as P

D = 2048
H = 16
DN = 128
DR = 64
DV = 128
QL = 1536
KL = 512
EXP_DEV = 2
TOPK = 6
ROWS = 16
COLS = 8
TS = 256
CUT = 208

eps = 1e-06
route_scale = 2.446
rope_base = 50000.0
score_scale = 1.0 / math.sqrt(DN + DR)
score_bits = score_scale * math.log2(math.e)

bf16 = jnp.bfloat16
f32 = jnp.float32
ANY = pl.ANY
VM = pltpu.VMEM


def shape_of(shape, dtype):
    return jax.ShapeDtypeStruct(shape, dtype)

MESH = pl.DeviceIdType.MESH
RING = 4
VMEM_BYTES = 56 * 2**20


class Place:
    def __init__(self, axis):
        self.axis = axis
        self.index = lax.axis_index(axis)
        self.cores = 2 if axis == "row" else 1
        self.core = lax.rem(self.index, self.cores)
        self.ring = lax.rem(lax.div(self.index, self.cores), RING)
        self.pair = lax.div(self.index, self.cores * RING)

    def at(self, pair, ring, core=None):
        core = self.core if core is None else core
        return (pair * RING + ring) * self.cores + core

    def turn(self, step):
        return lax.rem(self.ring + step + RING, RING)

    def peers(self):
        found = [self.at(self.pair, self.turn(step)) for step in (1, 2, 3)]
        found.append(self.at(1 - self.pair, self.ring))
        if self.cores == 2:
            found.append(self.at(self.pair, self.ring, 1 - self.core))
        return found


class Net:
    def __init__(self, send_sems, recv_sems):
        self.send_sems, self.recv_sems = send_sems, recv_sems
        self.count = 0
        self.sent = []
        self.own = []

    def send(self, source, target, axis, index):
        number = self.count
        self.count += 1
        copy = pltpu.make_async_remote_copy(
            source,
            target,
            self.send_sems.at[number],
            self.recv_sems.at[number],
            device_id={axis: index},
            device_id_type=MESH,
        )
        copy.start()
        self.sent.append(copy)
        return number

    def receive(self, number, target, axis, index):
        pltpu.make_async_remote_copy(
            target,
            target,
            self.send_sems.at[number],
            self.recv_sems.at[number],
            device_id={axis: index},
            device_id_type=MESH,
        ).wait_recv()

    def local(self, source, target):
        number = self.count
        self.count += 1
        copy = pltpu.make_async_copy(source, target, self.send_sems.at[number])
        copy.start()
        self.own.append(copy)

    def settle(self):
        for copy in self.own:
            copy.wait()
        self.own = []

    def finish(self):
        for copy in self.sent:
            copy.wait_send()
        self.settle()


def greet(*places):
    barrier = pltpu.get_barrier_semaphore()
    count = 0
    for place in places:
        for peer in place.peers():
            pl.semaphore_signal(
                barrier, inc=1, device_id={place.axis: peer}, device_id_type=MESH
            )
            count += 1
    pl.semaphore_wait(barrier, count)


class Gather:
    def __init__(self, net, place, source, slot, rows, cut):
        self.net, self.place, self.source, self.slot = net, place, source, slot
        self.rows, self.cut = rows, cut
        self.first, self.second = (0, cut), (cut, rows - cut)
        self.crossed = []

    def _send(self, owner, part, peer, own=False):
        piece = self.slot(owner, *part)
        start = self.source.at[pl.ds(*part)] if own else piece
        return self.net.send(start, piece, self.place.axis, peer)

    def _receive(self, number, pair, ring, part, peer, cross=True):
        place = self.place
        self.net.receive(number, self.slot(place.at(pair, ring), *part), place.axis, peer)
        if cross and place.cores == 2:
            self._cross(pair, ring, part)

    def _cross(self, pair, ring, part, own=False):
        place = self.place
        partner = place.at(place.pair, place.ring, 1 - place.core)
        number = self._send(place.at(pair, ring), part, partner, own)
        self.crossed.append((number, pair, ring, part))

    def start_first(self):
        place = self.place
        me, other = place.index, place.at(1 - place.pair, place.ring)
        if self.cut:
            self.across = self._send(me, self.first, other, True)
            self.near = [
                self._send(me, self.first, place.at(place.pair, place.turn(step)), True)
                for step in (1, 2, 3)
            ]

    def start_second(self):
        place = self.place
        me, other = place.index, place.at(1 - place.pair, place.ring)
        if self.second[1]:
            self.round = [
                self._send(me, self.second, place.at(place.pair, place.turn(step)), True)
                for step in (1, 2, 3)
            ]
            self.over = [self._send(me, self.second, other, True)]
        if place.cores == 2:
            self._cross(place.pair, place.ring, (0, self.rows), True)
        self.net.local(self.source, self.slot(me, 0, self.rows))

    def start(self):
        self.start_first()
        self.start_second()

    def forward_first(self):
        place = self.place
        other = place.at(1 - place.pair, place.ring)
        if self.cut:
            self._receive(self.across, 1 - place.pair, place.ring, self.first, other)
            self.far = [
                self._send(other, self.first, place.at(place.pair, place.turn(step)))
                for step in (1, 2, 3)
            ]

    def forward_second(self):
        place = self.place
        other = place.at(1 - place.pair, place.ring)
        if self.second[1]:
            for step in (1, 3, 2):
                ring = place.turn(-step)
                owner = place.at(place.pair, ring)
                self._receive(self.round[step - 1], place.pair, ring, self.second, owner, False)
                self.over.append(self._send(owner, self.second, other))
                if place.cores == 2:
                    self._cross(place.pair, ring, self.second)

    def land(self):
        place = self.place
        other = place.at(1 - place.pair, place.ring)
        if self.cut:
            for step in (1, 3, 2):
                ring = place.turn(-step)
                owner = place.at(place.pair, ring)
                self._receive(self.near[step - 1], place.pair, ring, self.first, owner)
            for step in (1, 3, 2):
                ring = place.turn(-step)
                owner = place.at(place.pair, ring)
                self._receive(self.far[step - 1], 1 - place.pair, ring, self.first, owner)
        if self.second[1]:
            for number, step in zip(self.over, (0, 1, 3, 2)):
                ring = place.turn(-step)
                self._receive(number, 1 - place.pair, ring, self.second, other)

    def end(self):
        place = self.place
        partner = place.at(place.pair, place.ring, 1 - place.core)
        for number, pair, ring, part in self.crossed:
            piece = self.slot(place.at(pair, ring, 1 - place.core), *part)
            self.net.receive(number, piece, place.axis, partner)


def run_gathers(*gathers):
    for gather in gathers:
        gather.start()
    for gather in gathers:
        gather.forward_first()
    for gather in gathers:
        gather.forward_second()
    for gather in gathers:
        gather.land()
    for gather in gathers:
        gather.end()


def row_slots(ref, rows):
    return lambda owner, low, count: ref.at[
        pl.ds(pl.multiple_of(owner * rows + low, 16), count)
    ]


def lead_slots(ref):
    return lambda owner, low, count: ref.at[owner, pl.ds(low, count)]


def lane_slots(ref, width):
    return lambda owner, low, count: ref.at[
        pl.ds(low, count), pl.ds(pl.multiple_of(owner * width, 128), width)
    ]


class Scatter:
    def __init__(self, net, place, block, rows, cut, scratch, keep):
        self.net, self.place, self.block, self.rows, self.cut = net, place, block, rows, cut
        self.scratch, self.keep = scratch, keep
        self.first, self.second = (0, cut), (cut, rows - cut)

    @staticmethod
    def scratch_of(rows, cut, width, dtype=jnp.bfloat16):
        shapes = []
        if cut:
            shapes += [(3, 2, cut, width), (2, cut, width)]
        if rows - cut:
            shapes += [(4, rows - cut, width), (4, rows - cut, width), (3, rows - cut, width)]
        return [pltpu.VMEM(shape, dtype) for shape in shapes]

    def _refs(self):
        refs = list(self.scratch)
        first = refs[:2] if self.cut else None
        second = refs[-3:] if self.second[1] else None
        return first, second

    def _owner(self, pair, ring):
        return self.place.at(pair, ring)

    def start(self):
        place, net = self.place, self.net
        first, second = self._refs()
        if first:
            self.round = [
                [
                    net.send(
                        self.block(self._owner(pair, place.turn(step)), *self.first),
                        first[0].at[step - 1, pair],
                        place.axis,
                        place.at(place.pair, place.turn(step)),
                    )
                    for pair in (0, 1)
                ]
                for step in (1, 2, 3)
            ]
        if second:
            self.across = [
                net.send(
                    self.block(self._owner(1 - place.pair, ring), *self.second),
                    second[0].at[ring],
                    place.axis,
                    place.at(1 - place.pair, place.ring),
                )
                for ring in range(RING)
            ]

    def forward_second(self):
        place, net = self.place, self.net
        first, second = self._refs()
        if not second:
            return
        other = place.at(1 - place.pair, place.ring)
        for ring in range(RING):
            net.receive(self.across[ring], second[0].at[ring], place.axis, other)
        for ring in range(RING):
            total = (
                self.block(self._owner(place.pair, ring), *self.second)[...].astype(jnp.float32)
                + second[0][ring].astype(jnp.float32)
            )
            second[1][ring] = total.astype(second[1].dtype)
        self.last = [
            net.send(
                second[1].at[place.turn(step)],
                second[2].at[step - 1],
                place.axis,
                place.at(place.pair, place.turn(step)),
            )
            for step in (1, 2, 3)
        ]

    def forward_first(self):
        place, net = self.place, self.net
        first, second = self._refs()
        if not first:
            return
        for step in (1, 3, 2):
            owner = place.at(place.pair, place.turn(-step))
            for pair in (0, 1):
                net.receive(self.round[step - 1][pair], first[0].at[step - 1, pair], place.axis, owner)
        other = 1 - place.pair
        total = self.block(self._owner(other, place.ring), *self.first)[...].astype(jnp.float32)
        for step in range(3):
            total = total + first[0][step, other].astype(jnp.float32)
        first[1][0] = total.astype(first[1].dtype)
        self.over = net.send(
            first[1].at[0], first[1].at[1], place.axis, place.at(other, place.ring)
        )

    def end_first(self):
        place, net = self.place, self.net
        first, second = self._refs()
        if not first:
            return
        total = self.block(self._owner(place.pair, place.ring), *self.first)[...].astype(jnp.float32)
        for step in range(3):
            total = total + first[0][step, place.pair].astype(jnp.float32)
        other = place.at(1 - place.pair, place.ring)
        net.receive(self.over, first[1].at[1], place.axis, other)
        self.keep(self.first, total + first[1][1].astype(jnp.float32))

    def end_second(self):
        place, net = self.place, self.net
        first, second = self._refs()
        if not second:
            return
        total = (
            self.block(self._owner(place.pair, place.ring), *self.second)[...].astype(jnp.float32)
            + second[0][place.ring].astype(jnp.float32)
        )
        for step in (1, 3, 2):
            owner = place.at(place.pair, place.turn(-step))
            net.receive(self.last[step - 1], second[2].at[step - 1], place.axis, owner)
            total = total + second[2][step - 1].astype(jnp.float32)
        self.keep(self.second, total)


def comm_call(body, name, collective_id, out_shapes, in_spaces, out_spaces, copies, scratch=(), args=()):
    return pl.pallas_call(
        body,
        name=name,
        out_shape=out_shapes,
        in_specs=[pl.BlockSpec(memory_space=space) for space in in_spaces],
        out_specs=tuple(pl.BlockSpec(memory_space=space) for space in out_spaces),
        scratch_shapes=[
            pltpu.SemaphoreType.DMA((copies,)),
            pltpu.SemaphoreType.DMA((copies,)),
            *scratch,
        ],
        compiler_params=pltpu.CompilerParams(
            collective_id=collective_id, has_side_effects=True, vmem_limit_bytes=VMEM_BYTES
        ),
    )(*args)


def front_body(hidden, w1, qu, lu, ao, hidden_all, w1_all, qu_all, lu_all, ao_all, ss, rs):
    row, col = Place("row"), Place("col")
    greet(row, col)
    net = Net(ss, rs)
    run_gathers(
        Gather(net, col, hidden, lane_slots(hidden_all, D // COLS), 2 * TS, CUT),
        Gather(net, row, w1, row_slots(w1_all, w1.shape[0]), w1.shape[0], 0),
        Gather(net, row, qu, row_slots(qu_all, qu.shape[0]), qu.shape[0], qu.shape[0]),
        Gather(net, row, lu, row_slots(lu_all, lu.shape[0]), lu.shape[0], lu.shape[0]),
        Gather(net, row, ao, lane_slots(ao_all, ao.shape[1]), ao.shape[0], 0),
    )
    net.finish()


def front(hidden, w1, qu, lu, ao):
    return comm_call(
        front_body,
        "gather_front",
        1,
        (
            shape_of((2 * TS, D), bf16),
            shape_of((ROWS * w1.shape[0], w1.shape[1]), bf16),
            shape_of((ROWS * qu.shape[0], qu.shape[1]), bf16),
            shape_of((ROWS * lu.shape[0], lu.shape[1]), bf16),
            shape_of((ao.shape[0], ROWS * ao.shape[1]), bf16),
        ),
        [ANY] * 5,
        [ANY] * 5,
        96,
        args=(hidden, w1, qu, lu, ao),
    )


def latent_body(latent, sgu, sd, latent_all, sgu_all, sd_all, ss, rs):
    row, col = Place("row"), Place("col")
    greet(row, col)
    net = Net(ss, rs)
    run_gathers(
        Gather(net, col, latent, lead_slots(latent_all), 2 * TS, CUT),
        Gather(net, row, sgu, row_slots(sgu_all, sgu.shape[0]), sgu.shape[0], 0),
        Gather(net, row, sd, lane_slots(sd_all, sd.shape[1]), sd.shape[0], sd.shape[0]),
    )
    net.finish()


def latents(latent, sgu, sd):
    return comm_call(
        latent_body,
        "gather_latents",
        2,
        (
            shape_of((COLS, *latent.shape), bf16),
            shape_of((ROWS * sgu.shape[0], sgu.shape[1]), bf16),
            shape_of((sd.shape[0], ROWS * sd.shape[1]), bf16),
        ),
        [ANY] * 3,
        [ANY] * 3,
        64,
        args=(latent, sgu, sd),
    )


def keys_body(kvr, grad, kvr_all, grad_all, ss, rs):
    row, col = Place("row"), Place("col")
    greet(row, col)
    net = Net(ss, rs)
    run_gathers(
        Gather(net, row, kvr, lead_slots(kvr_all), 2 * TS, CUT),
        Gather(net, col, grad, lane_slots(grad_all, D // COLS), 2 * TS, CUT),
    )
    net.finish()


def keys(kvr, grad):
    return comm_call(
        keys_body,
        "gather_keys",
        3,
        (shape_of((ROWS, *kvr.shape), bf16), shape_of((2 * TS, D), bf16)),
        [ANY] * 2,
        [ANY] * 2,
        64,
        args=(kvr, grad),
    )


def sum_body(with_rows, term, extra, total_all, extra_all, ss, rs, *scratch):
    row, col = Place("row"), Place("col")
    greet(*((row, col) if with_rows else (col,)))
    net = Net(ss, rs)
    width = D // COLS
    mine = scratch[-1]

    def keep(part, value):
        mine[pl.ds(*part)] = value.astype(mine.dtype)

    scatter = Scatter(net, col, lane_slots(term, width), 2 * TS, CUT, scratch[:-1], keep)
    gather = Gather(net, col, mine, lane_slots(total_all, width), 2 * TS, CUT)
    if with_rows:
        beside = Gather(net, row, extra, lead_slots(extra_all), extra.shape[0], CUT)
    else:
        beside = Gather(net, col, extra, lead_slots(extra_all), extra.shape[0], extra.shape[0])
    scatter.start()
    beside.start()
    scatter.forward_second()
    scatter.forward_first()
    beside.forward_first()
    beside.forward_second()
    scatter.end_first()
    gather.start_first()
    scatter.end_second()
    gather.start_second()
    gather.forward_first()
    gather.forward_second()
    beside.land()
    gather.land()
    beside.end()
    gather.end()
    net.finish()


def sum_over_col(name, collective_id, term, extra, with_rows):
    return comm_call(
        functools.partial(sum_body, with_rows),
        name,
        collective_id,
        (
            shape_of((2 * TS, D), bf16),
            shape_of((ROWS if with_rows else COLS, *extra.shape), extra.dtype),
        ),
        [VM, ANY],
        [ANY, ANY],
        96,
        [*Scatter.scratch_of(2 * TS, CUT, D // COLS), pltpu.VMEM((2 * TS, D // COLS), bf16)],
        (term, extra),
    )


def back_body(grad, stats, branch, grad_all, stats_all, branch_sum, ss, rs, *scratch):
    row, col = Place("row"), Place("col")
    greet(row, col)
    net = Net(ss, rs)

    def keep(part, value):
        branch_sum[pl.ds(*part)] = value

    scatter = Scatter(net, col, lane_slots(branch, D // COLS), 2 * TS, CUT, scratch, keep)
    gathers = (
        Gather(net, row, grad, lead_slots(grad_all), 2 * TS, CUT),
        Gather(net, row, stats, lead_slots(stats_all), stats.shape[0], stats.shape[0]),
    )
    for gather in gathers:
        gather.start()
    scatter.start()
    for gather in gathers:
        gather.forward_first()
    for gather in gathers:
        gather.forward_second()
    scatter.forward_second()
    scatter.forward_first()
    for gather in gathers:
        gather.land()
    scatter.end_first()
    scatter.end_second()
    for gather in gathers:
        gather.end()
    net.finish()


def back(grad, stats, branch):
    return comm_call(
        back_body,
        "gather_back",
        6,
        (
            shape_of((ROWS, *grad.shape), bf16),
            shape_of((ROWS, *stats.shape), f32),
            shape_of((2 * TS, D // COLS), f32),
        ),
        [ANY, ANY, VM],
        [ANY, ANY, VM],
        96,
        Scatter.scratch_of(2 * TS, CUT, D // COLS),
        (grad, stats, branch),
    )


class RowScatter:
    def __init__(self, net, place, term, cut, scratch, keep):
        self.net, self.place, self.term = net, place, term
        self.arrived, self.summed = scratch[:2]
        rows = term.shape[3]

        def block(owner, low, count):
            return self.summed.at[lax.div(owner, 2), pl.ds(low, count)]

        self.inner = Scatter(net, place, block, rows, cut, scratch[2:], keep)

    @staticmethod
    def scratch_of(rows, cut, width):
        return [
            pltpu.VMEM((2, RING, rows, width), bf16),
            pltpu.VMEM((2 * RING, rows, width), bf16),
            *Scatter.scratch_of(rows, cut, width),
        ]

    def start(self):
        place = self.place
        self.partner = place.at(place.pair, place.ring, 1 - place.core)
        self.number = self.net.send(
            self.term.at[:, :, 1 - place.core], self.arrived, place.axis, self.partner
        )

    def middle(self):
        place = self.place
        self.net.receive(self.number, self.arrived, place.axis, self.partner)
        for pair in range(2):
            for ring in range(RING):
                self.summed[pair * RING + ring] = (
                    self.term[pair, ring, place.core].astype(f32)
                    + self.arrived[pair, ring].astype(f32)
                ).astype(bf16)
        self.inner.start()


def run_scatters(scatters):
    for scatter in scatters:
        scatter.forward_second()
    for scatter in scatters:
        scatter.forward_first()
    for scatter in scatters:
        scatter.end_first()
    for scatter in scatters:
        scatter.end_second()


def keep_in(ref):
    def keep(part, value):
        ref[pl.ds(*part)] = value

    return keep


def block_slots(ref):
    return lambda owner, low, count: ref.at[owner, pl.ds(low, count)]


def latent_sum_body(term, extra, total, extra_all, ss, rs, *scratch):
    col = Place("col")
    greet(col)
    net = Net(ss, rs)
    scatter = Scatter(net, col, block_slots(term), 2 * TS, CUT, scratch, keep_in(total))
    beside = Gather(net, col, extra, lead_slots(extra_all), extra.shape[0], extra.shape[0])
    scatter.start()
    beside.start()
    beside.forward_first()
    scatter.forward_second()
    scatter.forward_first()
    scatter.end_first()
    scatter.end_second()
    beside.land()
    net.finish()


def latent_sum(term, extra):
    width = term.shape[2]
    return comm_call(
        latent_sum_body,
        "sum_latents",
        7,
        (shape_of((2 * TS, width), f32), shape_of((COLS, *extra.shape), f32)),
        [VM, ANY],
        [VM, ANY],
        64,
        Scatter.scratch_of(2 * TS, CUT, width),
        (term, extra),
    )


def first_sum_body(term, extra, sgu, sd, total, extra_all, sgu_sum, sd_sum, ss, rs, *scratch):
    row, col = Place("row"), Place("col")
    greet(row, col)
    net = Net(ss, rs)
    scatter = Scatter(
        net, col, lane_slots(term, D // COLS), 2 * TS, CUT, scratch[:5], keep_in(total)
    )
    beside = Gather(net, col, extra, lead_slots(extra_all), extra.shape[0], extra.shape[0])
    rows_sgu = RowScatter(net, row, sgu, 0, scratch[5:10], keep_in(sgu_sum))
    rows_sd = RowScatter(net, row, sd, sd.shape[3], scratch[10:14], keep_in(sd_sum))
    rows_sgu.start()
    rows_sd.start()
    scatter.start()
    beside.start()
    rows_sgu.middle()
    rows_sd.middle()
    beside.forward_first()
    run_scatters((scatter, rows_sgu.inner, rows_sd.inner))
    beside.land()
    net.finish()


def first_sum(term, extra, sgu, sd):
    return comm_call(
        first_sum_body,
        "sum_first",
        8,
        (
            shape_of((2 * TS, D // COLS), f32),
            shape_of((COLS, *extra.shape), f32),
            shape_of(sgu.shape[3:], f32),
            shape_of(sd.shape[3:], f32),
        ),
        [VM, ANY, VM, VM],
        [VM, ANY, VM, VM],
        96,
        [
            *Scatter.scratch_of(2 * TS, CUT, D // COLS),
            *RowScatter.scratch_of(sgu.shape[3], 0, sgu.shape[4]),
            *RowScatter.scratch_of(sd.shape[3], sd.shape[3], sd.shape[4]),
        ],
        (term, extra, sgu, sd),
    )


def last_body(g1, qu, lu, ao, gains, g1_sum, qu_sum, lu_sum, ao_sum, gains_all, ss, rs, *scratch):
    row, col = Place("row"), Place("col")
    greet(row, col)
    net = Net(ss, rs)
    gains_rows, gains_mine = scratch[-2:]
    beside = Gather(net, row, gains, lead_slots(gains_rows), 8, 8)
    parts = (
        RowScatter(net, row, g1, 0, scratch[0:5], keep_in(g1_sum)),
        RowScatter(net, row, qu, qu.shape[3], scratch[5:9], keep_in(qu_sum)),
        RowScatter(net, row, lu, lu.shape[3], scratch[9:13], keep_in(lu_sum)),
        RowScatter(net, row, ao, 0, scratch[13:18], keep_in(ao_sum)),
    )
    beside.start()
    for part in parts:
        part.start()
    beside.forward_first()
    for part in parts:
        part.middle()
    beside.land()
    beside.end()
    net.settle()
    total = gains_rows[0]
    for index in range(1, ROWS):
        total = total + gains_rows[index]
    gains_mine[...] = total
    spread = Gather(net, col, gains_mine, lead_slots(gains_all), 8, 8)
    spread.start()
    spread.forward_first()
    run_scatters([part.inner for part in parts])
    spread.land()
    net.finish()


def last(g1, qu, lu, ao, gains):
    scratch = []
    for term, cut in ((g1, 0), (qu, 1), (lu, 1), (ao, 0)):
        rows, width = term.shape[3:]
        scratch += RowScatter.scratch_of(rows, rows * cut, width)
    return comm_call(
        last_body,
        "sum_last",
        9,
        (
            *(shape_of(term.shape[3:], f32) for term in (g1, qu, lu, ao)),
            shape_of((COLS, 8, 128), f32),
        ),
        [VM, VM, VM, VM, VM],
        [VM, VM, VM, VM, VM],
        128,
        [*scratch, pltpu.VMEM((ROWS, 8, 128), f32), pltpu.VMEM((8, 128), f32)],
        (g1, qu, lu, ao, gains),
    )


def contract(left, right):
    return lax.dot_general(left, right, (((1,), (1,)), ((), ())), preferred_element_type=f32)


def attend_body(lens, query, kvr, out, lse, scores):
    seq = pl.program_id(0)
    mine = lax.axis_index("row")
    live = lens[seq]
    steps = lax.div(jnp.minimum(mine + 1, lax.div(live + TS - 1, TS)) + 1, 2)
    width = 2 * TS
    places = mine * TS + lax.broadcasted_iota(jnp.int32, (TS, 1), 0)
    limit = jnp.minimum(places + 1, live)
    offsets = lax.broadcasted_iota(jnp.int32, (TS, width), 1)
    queries = [query[0, head] for head in range(2)]

    def first(step, tops):
        valid = offsets < limit - step * width
        block = kvr[pl.ds(2 * step, 2)].reshape(width, kvr.shape[2])
        found = []
        for head in range(2):
            value = contract(queries[head], block[:, head * 128 : head * 128 + 256])
            value = jnp.where(valid, value, -1e30)
            scores[head, step] = value
            top = tops[head]
            for low in range(0, width, 128):
                top = jnp.maximum(top, value[:, low : low + 128])
            found.append(top)
        return tuple(found)

    tops = lax.fori_loop(0, steps, first, (jnp.full((TS, 128), -1e30, f32),) * 2)
    tops = [jnp.max(top, axis=1, keepdims=True) * score_bits for top in tops]

    def second(step, carried):
        block = kvr[pl.ds(2 * step, 2)].reshape(width, kvr.shape[2])
        found = []
        for head in range(2):
            sums, total = carried[head]
            weight = jnp.exp2(scores[head, step] * score_bits - tops[head])
            for low in range(0, width, 128):
                sums = sums + weight[:, low : low + 128]
            value = block[:, 384 + head * 128 : 512 + head * 128]
            total = total + jnp.dot(weight.astype(bf16), value, preferred_element_type=f32)
            found.append((sums, total))
        return tuple(found)

    zero = jnp.zeros((TS, 128), f32)
    carried = lax.fori_loop(0, steps, second, ((zero, zero),) * 2)
    for head in range(2):
        sums, total = carried[head]
        whole = jnp.sum(sums, axis=1, keepdims=True)
        lanes = pl.ds(head * 128, 128)
        out[:, lanes] = total / whole
        lse[:, lanes] = jnp.broadcast_to(tops[head] + jnp.log2(whole), (TS, 128))


def attend(lens, query, kvr):
    return pl.pallas_call(
        attend_body,
        name="attend",
        grid=(2,),
        out_shape=(shape_of((2 * TS, 256), f32), shape_of((2 * TS, 256), f32)),
        in_specs=[
            pl.BlockSpec(memory_space=pltpu.SMEM),
            pl.BlockSpec((1, 2, TS, 256), lambda s: (s, 0, 0, 0)),
            pl.BlockSpec((ROWS, TS, kvr.shape[2]), lambda s: (0, s, 0)),
        ],
        out_specs=(
            pl.BlockSpec((TS, 256), lambda s: (s, 0)),
            pl.BlockSpec((TS, 256), lambda s: (s, 0)),
        ),
        scratch_shapes=[pltpu.VMEM((2, ROWS // 2, TS, 2 * TS), f32)],
        compiler_params=pltpu.CompilerParams(vmem_limit_bytes=VMEM_BYTES),
        cost_estimate=pl.CostEstimate(
            flops=6 * 10**9, bytes_accessed=12 * 10**6, transcendentals=4 * 10**6
        ),
    )(lens, query, kvr)


def attend_back_body(lens, query, kvr, grad, lse, delta, near, query_all, grad_all, stats, dq, dk, dv):
    seq = pl.program_id(0)
    mine = lax.axis_index("row")
    live = lens[seq]
    width = 2 * TS
    steps = lax.div(jnp.minimum(mine + 1, lax.div(live + TS - 1, TS)) + 1, 2)
    places = mine * TS + lax.broadcasted_iota(jnp.int32, (TS, 1), 0)
    limit = jnp.minimum(places + 1, live)
    offsets = lax.broadcasted_iota(jnp.int32, (TS, width), 1)

    def queries_step(step, carried):
        valid = offsets < limit - step * width
        block = kvr[pl.ds(2 * step, 2)].reshape(width, kvr.shape[2])
        found = []
        for head in range(2):
            key = block[:, head * 128 : head * 128 + 256]
            value = block[:, 384 + head * 128 : 512 + head * 128]
            lanes = pl.ds(head * 128, 128)
            score = contract(query[0, head], key) * score_bits - lse[:, lanes][:, :1]
            weight = jnp.exp2(jnp.where(valid, score, -1e30))
            slope = contract(grad[:, lanes], value) - delta[:, lanes][:, :1]
            low = (weight * slope).astype(bf16)
            found.append(carried[head] + jnp.dot(low, key, preferred_element_type=f32))
        return tuple(found)

    totals = lax.fori_loop(0, steps, queries_step, (jnp.zeros((TS, 256), f32),) * 2)
    for head in range(2):
        dq[0, head] = totals[head]

    bar = jnp.where(places < live, places, 2 * ROWS * TS)

    def keys_step(step, carried):
        valid = offsets >= bar - step * width
        queries = query_all[pl.ds(2 * step, 2)].reshape(width, query_all.shape[2])
        grads = grad_all[pl.ds(2 * step, 2)].reshape(width, 256)
        numbers = stats[pl.ds(2 * step, 2)]
        numbers = jnp.concatenate([numbers[0], numbers[1]], axis=1)
        found = []
        for head in range(2):
            key_total, value_total = carried[head]
            asked = queries[:, head * 128 : head * 128 + 256]
            given = grads[:, head * 128 : head * 128 + 128]
            score = contract(near[0, head], asked) * score_bits - numbers[head : head + 1]
            weight = jnp.exp2(jnp.where(valid, score, -1e30))
            value_total = value_total + jnp.dot(
                weight.astype(bf16), given, preferred_element_type=f32
            )
            value = kvr[mine, :, 384 + head * 128 : 512 + head * 128]
            slope = contract(value, given) - numbers[2 + head : 3 + head]
            low = (weight * slope).astype(bf16)
            key_total = key_total + jnp.dot(low, asked, preferred_element_type=f32)
            found.append((key_total, value_total))
        return tuple(found)

    zero = (jnp.zeros((TS, 256), f32), jnp.zeros((TS, 128), f32))
    last_step = jnp.where(mine * TS < live, ROWS // 2, 0)
    totals = lax.fori_loop(lax.div(mine, 2), last_step, keys_step, (zero, zero))
    for head in range(2):
        dk[0, head] = totals[head][0]
        dv[0, head] = totals[head][1]


def attend_back(lens, query, kvr, grad, lse, delta, near, query_all, grad_all, stats):
    lanes = pl.BlockSpec((TS, 256), lambda s: (s, 0))
    heads = pl.BlockSpec((1, 2, TS, 256), lambda s: (s, 0, 0, 0))
    return pl.pallas_call(
        attend_back_body,
        name="attend_back",
        grid=(2,),
        out_shape=(
            shape_of((2, 2, TS, 256), f32),
            shape_of((2, 2, TS, 256), f32),
            shape_of((2, 2, TS, 128), f32),
        ),
        in_specs=[
            pl.BlockSpec(memory_space=pltpu.SMEM),
            heads,
            pl.BlockSpec((ROWS, TS, kvr.shape[2]), lambda s: (0, s, 0)),
            lanes,
            lanes,
            lanes,
            heads,
            pl.BlockSpec((ROWS, TS, query_all.shape[2]), lambda s: (0, s, 0)),
            pl.BlockSpec((ROWS, TS, 256), lambda s: (0, s, 0)),
            pl.BlockSpec((ROWS, 8, TS), lambda s: (0, 0, s)),
        ],
        out_specs=(heads, heads, pl.BlockSpec((1, 2, TS, 128), lambda s: (s, 0, 0, 0))),
        compiler_params=pltpu.CompilerParams(vmem_limit_bytes=VMEM_BYTES),
        cost_estimate=pl.CostEstimate(
            flops=12 * 10**9, bytes_accessed=24 * 10**6, transcendentals=8 * 10**6
        ),
    )(lens, query, kvr, grad, lse, delta, near, query_all, grad_all, stats)


def rope_tables(positions, width):
    half_width = width // 2
    frequency = jnp.exp(
        -jnp.log(rope_base) * (2.0 * jnp.arange(half_width, dtype=jnp.float32) / width)
    )
    angles = positions.astype(jnp.float32)[:, None] * frequency[None, :]
    return (jnp.cos(angles), jnp.sin(angles))


def rotate(values, rope_cos, rope_sin):
    half_width = values.shape[-1] // 2
    first_half = values[..., :half_width]
    second_half = values[..., half_width:]
    return jnp.concatenate(
        [
            first_half * rope_cos - second_half * rope_sin,
            second_half * rope_cos + first_half * rope_sin,
        ],
        axis=-1,
    )


def unrotate(grads_in, rope_cos, rope_sin):
    return rotate(grads_in, rope_cos, -rope_sin)


def rms_scale(values):
    return lax.rsqrt(jnp.mean(values * values, axis=-1, keepdims=True) + eps)


def silu_parts(gate_value):
    sigmoid_value = jax.nn.sigmoid(gate_value)
    return (gate_value * sigmoid_value, sigmoid_value * (1.0 + gate_value * (1.0 - sigmoid_value)))


def product(left, right):
    return jnp.dot(left, right, preferred_element_type=jnp.float32)


def left_product(left, right):
    return lax.dot_general(
        left, right, (((0,), (0,)), ((), ())), preferred_element_type=jnp.float32
    )


def right_product(left, right):
    return lax.dot_general(
        left, right, (((1,), (1,)), ((), ())), preferred_element_type=jnp.float32
    )


def einsum(text, *terms):
    return jnp.einsum(text, *terms, preferred_element_type=f32)


def to_blocks(term):
    return term.reshape(2, RING, 2, term.shape[0] // ROWS, term.shape[1])


def local(
    hidden_in,
    gain_first,
    query_down,
    query_gain,
    query_up,
    latent_down,
    latent_gain,
    latent_up,
    attention_out,
    gain_second,
    router,
    expert_gate,
    expert_up,
    expert_down,
    shared_gate,
    shared_up,
    shared_down,
    seq_lens,
    routes,
    out_grad,
):
    row_index = lax.axis_index("row")
    col_index = lax.axis_index("col")
    seq_count, local_len, col_width = hidden_in.shape
    row_total = seq_count * local_len
    experts_all = EXP_DEV * COLS
    most_rows = (5 * local_len * TOPK + 4 * experts_all - 1) // (4 * experts_all)
    capacity = seq_count * most_rows
    query_cols = QL // COLS
    kv_cols = (KL + DR) // COLS

    def here(values, axis=-1):
        width = values.shape[axis] // COLS
        return lax.dynamic_slice_in_dim(values, col_index * width, width, axis)

    expert_in = lax.all_gather(
        jnp.concatenate([expert_gate, expert_up], axis=0), "row", axis=1, tiled=True
    )
    expert_down_all = lax.all_gather(expert_down, "row", axis=1, tiled=True)
    expert_gate_all, expert_up_all = expert_in[:EXP_DEV], expert_in[EXP_DEV:]

    hidden_low, down_all, query_up_all, latent_up_all, attention_out_all = front(
        hidden_in.reshape(row_total, col_width),
        jnp.concatenate([query_down, latent_down, router], axis=1),
        query_up,
        latent_up,
        attention_out,
    )
    hidden = hidden_low.astype(f32)
    scale_first = rms_scale(hidden)
    normed_first = (hidden * scale_first * gain_first).astype(bf16)
    latent_width = query_cols + kv_cols
    latent_weights = down_all[:, :latent_width]
    router_all = down_all[:, latent_width:]
    latent_here = product(normed_first, latent_weights).astype(bf16)
    latent_all, shared_in_all, shared_down_all = latents(
        latent_here, jnp.concatenate([shared_gate, shared_up], axis=1), shared_down
    )
    shared_width = shared_gate.shape[1]
    query_latent = (
        latent_all[:, :, :query_cols].transpose(1, 0, 2).reshape(row_total, QL)
    )
    kv_latent = latent_all[:, :, query_cols:].transpose(1, 0, 2).reshape(row_total, KL + DR)
    query_float = query_latent.astype(f32)
    query_scale = rms_scale(query_float)
    query_input = (query_float * query_scale * query_gain).astype(bf16)
    latent_float = kv_latent[:, :KL].astype(f32)
    latent_scale = rms_scale(latent_float)
    latent_input = (latent_float * latent_scale * latent_gain).astype(bf16)
    positions = row_index * local_len + jnp.arange(local_len, dtype=jnp.int32)
    rope_cos, rope_sin = rope_tables(positions, DR)
    rope_cos = jnp.concatenate([rope_cos] * seq_count, axis=0)
    rope_sin = jnp.concatenate([rope_sin] * seq_count, axis=0)
    query_proj = product(query_input, query_up_all)
    split = DN + DR
    nope = [query_proj[:, split * head : split * head + DN].astype(bf16) for head in range(2)]
    rope = [
        rotate(
            query_proj[:, split * head + DN : split * (head + 1)], rope_cos, rope_sin
        ).astype(bf16)
        for head in range(2)
    ]
    blank = jnp.zeros((row_total, DR), bf16)
    query_cat = jnp.stack(
        [
            jnp.concatenate([nope[0], rope[0], blank], axis=1),
            jnp.concatenate([rope[1], blank, nope[1]], axis=1),
        ],
        axis=0,
    )
    query_cat = query_cat.reshape(2, seq_count, local_len, 256).transpose(1, 0, 2, 3)
    query_pack = jnp.concatenate([nope[0], rope[0], rope[1], nope[1]], axis=1)
    key_value = product(latent_input, latent_up_all).astype(bf16)
    key_rope = rotate(kv_latent[:, KL:].astype(f32), rope_cos, rope_sin).astype(bf16)
    key_zero, value_zero = key_value[:, :DN], key_value[:, DN : 2 * DN]
    key_one, value_one = key_value[:, 2 * DN : 3 * DN], key_value[:, 3 * DN :]
    kvr = jnp.concatenate([key_zero, key_rope, blank, key_one, value_zero, value_one], axis=1)
    near = jnp.stack(
        [
            jnp.concatenate([key_zero, key_rope, blank], axis=1),
            jnp.concatenate([blank, key_rope, key_one], axis=1),
        ],
        axis=0,
    )
    near = near.reshape(2, seq_count, local_len, 256).transpose(1, 0, 2, 3)
    kvr_all, grad_full = keys(kvr, out_grad.reshape(row_total, col_width))

    attended_float, lse = attend(seq_lens, query_cat, kvr_all)
    attended = attended_float.astype(bf16)
    attention_part = product(attended, attention_out_all).astype(bf16)
    attention_sum, query_all = sum_over_col("sum_attention", 4, attention_part, query_pack, True)

    residual_one = hidden + attention_sum.astype(f32)
    scale_second = rms_scale(residual_one)
    normed_second = (residual_one * scale_second * gain_second).astype(bf16)
    logits = product(normed_second, router_all)
    sigmoid_all = jax.nn.sigmoid(logits)
    chosen = jnp.sum(
        (
            routes.reshape(row_total, TOPK)[:, :, None]
            == jnp.arange(experts_all, dtype=jnp.int32)[None, None, :]
        ).astype(f32),
        axis=1,
    )
    weighted_sig = sigmoid_all * chosen
    denominator = jnp.sum(weighted_sig, axis=-1, keepdims=True)
    gate_weights = route_scale * weighted_sig / denominator
    gate_here = here(gate_weights)
    chosen_here = here(chosen)
    member = chosen_here.astype(jnp.int32).reshape(seq_count, local_len, EXP_DEV)
    slot_rank = jnp.cumsum(member, axis=1) - 1
    seq_base = (jnp.arange(seq_count, dtype=jnp.int32) * most_rows)[:, None, None]
    slot_index = jnp.where(member > 0, seq_base + slot_rank, capacity).reshape(row_total, EXP_DEV)
    dispatch = (
        slot_index.T[:, None, :] == jnp.arange(capacity, dtype=jnp.int32)[None, :, None]
    ).astype(f32)
    dispatch_low = dispatch.astype(bf16)
    normed_slots = einsum("ecr,rd->ecd", dispatch_low, normed_second).astype(bf16)
    gate_slot = jnp.sum(dispatch * gate_here.T[:, None, :], axis=-1)
    gate_hidden = einsum("ecd,edf->ecf", normed_slots, expert_gate_all)
    up_hidden = einsum("ecd,edf->ecf", normed_slots, expert_up_all)
    silu_value, silu_slope = silu_parts(gate_hidden)
    expert_act = (silu_value * up_hidden).astype(bf16)
    expert_result = einsum("ecf,efd->ecd", expert_act, expert_down_all)
    routed_sum = einsum(
        "ecr,ecd->rd", dispatch_low, (gate_slot[:, :, None] * expert_result).astype(bf16)
    )
    shared_gate_all = shared_in_all[:, :shared_width]
    shared_up_all = shared_in_all[:, shared_width:]
    shared_gate_val = product(normed_second, shared_gate_all)
    shared_up_val = product(normed_second, shared_up_all)
    shared_value, shared_slope = silu_parts(shared_gate_val)
    shared_act = (shared_value * shared_up_val).astype(bf16)
    branch_part = (routed_sum + product(shared_act, shared_down_all)).astype(bf16)

    grad_float = grad_full.astype(f32)
    grad_slots = einsum("ecr,rd->ecd", dispatch_low, grad_full)
    routed_grad = (gate_slot[:, :, None] * grad_slots).astype(bf16)
    gate_grad_slot = jnp.sum(grad_slots * expert_result, axis=-1)
    gate_grad_here = jnp.sum(dispatch * gate_grad_slot[:, :, None], axis=1).T
    act_grad = einsum("ecd,efd->ecf", routed_grad, expert_down_all)
    gate_hidden_grad = (act_grad * up_hidden * silu_slope).astype(bf16)
    up_hidden_grad = (act_grad * silu_value).astype(bf16)
    slot_normed_grad = einsum("ecf,edf->ecd", gate_hidden_grad, expert_gate_all)
    slot_normed_grad = slot_normed_grad + einsum("ecf,edf->ecd", up_hidden_grad, expert_up_all)
    normed_grad = einsum("ecr,ecd->rd", dispatch_low, slot_normed_grad.astype(bf16))
    shared_act_grad = right_product(grad_full, shared_down_all)
    shared_down_grad = left_product(shared_act, grad_full)
    shared_gate_hgrad = (shared_act_grad * shared_up_val * shared_slope).astype(bf16)
    shared_up_hgrad = (shared_act_grad * shared_value).astype(bf16)
    shared_in_hgrad = jnp.concatenate([shared_gate_hgrad, shared_up_hgrad], axis=1)
    shared_in_grad = left_product(normed_second, shared_in_hgrad)
    normed_grad = normed_grad + right_product(shared_in_hgrad, shared_in_all)
    gate_grad_all = lax.dynamic_update_slice_in_dim(
        jnp.zeros((row_total, experts_all), f32), gate_grad_here, col_index * EXP_DEV, 1
    )
    inner_sum = jnp.sum(gate_grad_all * gate_weights, axis=-1, keepdims=True)
    logit_part = (
        sigmoid_all
        * (1.0 - sigmoid_all)
        * chosen
        / denominator
        * (route_scale * gate_grad_all - inner_sum)
    )
    gate_full_grad = einsum("ecd,ecf->edf", normed_slots, gate_hidden_grad)
    up_full_grad = einsum("ecd,ecf->edf", normed_slots, up_hidden_grad)
    down_full_grad = einsum("ecf,ecd->efd", expert_act, routed_grad)
    expert_in_grad = lax.psum_scatter(
        jnp.concatenate([gate_full_grad.astype(bf16), up_full_grad.astype(bf16)], axis=0),
        "row",
        scatter_dimension=1,
        tiled=True,
    ).astype(f32)
    expert_down_grad = lax.psum_scatter(
        down_full_grad.astype(bf16), "row", scatter_dimension=1, tiled=True
    ).astype(f32)

    normed_sum, logit_all = sum_over_col(
        "sum_normed", 5, normed_grad.astype(bf16), logit_part.T, False
    )
    logit_low = jnp.sum(logit_all, axis=0).T.astype(bf16)
    normed_grad = normed_sum.astype(f32) + right_product(logit_low, router_all)
    router_grad = left_product(normed_second, logit_low)
    weighted = normed_grad * gain_second
    residual_grad = (
        grad_float
        + scale_second * weighted
        - residual_one
        * (scale_second * scale_second * scale_second)
        * jnp.mean(weighted * residual_one, axis=-1, keepdims=True)
    )
    gain_second_part = jnp.sum(here(normed_grad) * here(residual_one) * scale_second, axis=0)

    attention_grad = residual_grad.astype(bf16)
    attention_out_grad = einsum(
        "rk,rbn->bkn", attended, attention_grad.reshape(row_total, ROWS, D // ROWS)
    ).astype(bf16)
    attended_grad = right_product(attention_grad, attention_out_all).astype(bf16)
    delta = jnp.sum(
        (attended_grad.astype(f32) * attended_float).reshape(row_total, 2, DV), axis=-1
    )
    delta_lanes = jnp.repeat(delta, DV, axis=1)
    lse_two = lse.reshape(row_total, 2, DV)[:, :, 0]
    stats = jnp.concatenate([lse_two.T, delta.T, jnp.zeros((4, row_total), f32)], axis=0)
    attended_grad_all, stats_all, branch_here = back(attended_grad, stats, branch_part)
    block_out = (
        (here(residual_one) + branch_here).astype(bf16).reshape(seq_count, local_len, col_width)
    )
    dq, dk, dv = attend_back(
        seq_lens,
        query_cat,
        kvr_all,
        attended_grad,
        lse,
        delta_lanes,
        near,
        query_all,
        attended_grad_all,
        stats_all,
    )
    dq = dq.transpose(1, 0, 2, 3).reshape(2, row_total, 256) * score_scale
    dk = dk.transpose(1, 0, 2, 3).reshape(2, row_total, 256) * score_scale
    dv = dv.transpose(1, 0, 2, 3).reshape(2, row_total, DV)
    query_grad = jnp.concatenate(
        [
            dq[0, :, :DN],
            unrotate(dq[0, :, DN:split], rope_cos, rope_sin),
            dq[1, :, DN:],
            unrotate(dq[1, :, :DR], rope_cos, rope_sin),
        ],
        axis=1,
    ).astype(bf16)
    kv_grad = jnp.concatenate([dk[0, :, :DN], dv[0], dk[1, :, DN:], dv[1]], axis=1).astype(bf16)
    rope_grad = unrotate(dk[0, :, DN:split] + dk[1, :, DR:DN], rope_cos, rope_sin)
    latent_up_grad = left_product(latent_input, kv_grad).astype(bf16)
    latent_in_grad = right_product(kv_grad, latent_up_all)
    query_up_grad = left_product(query_input, query_grad).astype(bf16)
    query_in_grad = right_product(query_grad, query_up_all)
    query_number = jnp.sum(query_in_grad * query_gain * query_float, axis=-1)
    latent_number = jnp.sum(latent_in_grad * latent_gain * latent_float, axis=-1)
    numbers = jnp.concatenate(
        [query_number[None], latent_number[None], jnp.zeros((6, row_total), f32)], axis=0
    )
    kv_part = jnp.concatenate([latent_in_grad, rope_grad], axis=1)
    latent_part = jnp.concatenate(
        [
            query_in_grad.reshape(row_total, COLS, query_cols),
            kv_part.reshape(row_total, COLS, kv_cols),
        ],
        axis=2,
    )
    latent_part = latent_part.transpose(1, 0, 2).astype(bf16)
    latent_total, numbers_all = latent_sum(latent_part, numbers)
    numbers_sum = jnp.sum(numbers_all, axis=0)
    query_mean = (numbers_sum[0] / QL)[:, None]
    latent_mean = (numbers_sum[1] / KL)[:, None]
    query_in_here = latent_total[:, :query_cols]
    kv_in_here = latent_total[:, query_cols:]
    query_float_here = here(query_float)
    query_latent_here = (
        query_scale * query_in_here * here(query_gain)
        - query_float_here * (query_scale * query_scale * query_scale) * query_mean
    ).astype(bf16)
    kv_float_here = here(kv_latent).astype(f32)
    is_latent = (col_index * kv_cols + jnp.arange(kv_cols)) < KL
    latent_gain_here = here(jnp.concatenate([latent_gain, jnp.ones((DR,), f32)]))
    kv_latent_here = jnp.where(
        is_latent,
        latent_scale * kv_in_here * latent_gain_here
        - kv_float_here * (latent_scale * latent_scale * latent_scale) * latent_mean,
        kv_in_here,
    ).astype(bf16)
    query_gain_part = jnp.sum(query_in_here * query_float_here * query_scale, axis=0)
    latent_gain_part = jnp.sum(kv_in_here * kv_float_here * latent_scale, axis=0)
    latent_here_grad = jnp.concatenate([query_latent_here, kv_latent_here], axis=1)
    latent_down_grads = left_product(normed_first, latent_here_grad)
    first_part = right_product(latent_here_grad, latent_weights)
    first_number = jnp.sum(first_part * gain_first * hidden, axis=-1)
    first_numbers = jnp.concatenate([first_number[None], jnp.zeros((7, row_total), f32)], axis=0)
    shared_in_blocks = to_blocks(shared_in_grad.astype(bf16))
    shared_down_blocks = (
        shared_down_grad.astype(bf16)
        .reshape(shared_width, ROWS, D // ROWS)
        .transpose(1, 0, 2)
        .reshape(2, RING, 2, shared_width, D // ROWS)
    )
    first_here, first_numbers_all, shared_in_sum, shared_down_sum = first_sum(
        first_part.astype(bf16), first_numbers, shared_in_blocks, shared_down_blocks
    )
    first_mean = (jnp.sum(first_numbers_all[:, 0], axis=0) / D)[:, None]
    hidden_here = here(hidden)
    hidden_grad = (
        here(residual_grad)
        + scale_first * first_here * here(gain_first)
        - hidden_here * (scale_first * scale_first * scale_first) * first_mean
    ).reshape(seq_count, local_len, col_width)
    gain_first_part = jnp.sum(first_here * hidden_here * scale_first, axis=0)
    gains = jnp.concatenate(
        [
            gain_first_part,
            gain_second_part,
            query_gain_part,
            jnp.zeros((64,), f32),
            latent_gain_part,
            jnp.zeros((1024 - 768 - kv_cols,), f32),
        ]
    ).reshape(8, 128)
    down_sum, query_up_sum, latent_up_sum, attention_out_sum, gains_all = last(
        to_blocks(
            jnp.concatenate([latent_down_grads.astype(bf16), router_grad.astype(bf16)], axis=1)
        ),
        to_blocks(query_up_grad),
        to_blocks(latent_up_grad),
        attention_out_grad.reshape(2, RING, 2, col_width, D // ROWS),
        gains,
    )
    gains_all = gains_all.reshape(COLS, 1024)
    return (
        block_out,
        hidden_grad,
        gains_all[:, :col_width].reshape(D),
        down_sum[:, :query_cols],
        gains_all[:, 512 : 512 + query_cols].reshape(QL),
        query_up_sum,
        down_sum[:, query_cols:latent_width],
        gains_all[:, 768 : 768 + kv_cols].reshape(KL + DR)[:KL],
        latent_up_sum,
        attention_out_sum,
        gains_all[:, col_width : 2 * col_width].reshape(D),
        down_sum[:, latent_width:],
        expert_in_grad[:EXP_DEV],
        expert_in_grad[EXP_DEV:],
        expert_down_grad,
        shared_in_sum[:, :shared_width],
        shared_in_sum[:, shared_width:],
        shared_down_sum,
    )


def solution(mesh):
    in_specs = (
        P(None, "row", "col"),
        P(),
        P("row", "col"),
        P(),
        P("row", "col"),
        P("row", "col"),
        P(),
        P("row", "col"),
        P("col", "row"),
        P(),
        P("row", None),
        P("col", "row", None),
        P("col", "row", None),
        P("col", "row", None),
        P("row", "col"),
        P("row", "col"),
        P("col", "row"),
        P(),
        P(None, "row", None),
        P(None, "row", "col"),
    )
    out_specs = (
        P(None, "row", "col"),
        P(None, "row", "col"),
        P(),
        P("row", "col"),
        P(),
        P("row", "col"),
        P("row", "col"),
        P(),
        P("row", "col"),
        P("col", "row"),
        P(),
        P("row", None),
        P("col", "row", None),
        P("col", "row", None),
        P("col", "row", None),
        P("row", "col"),
        P("row", "col"),
        P("col", "row"),
    )
    return jax.shard_map(local, mesh=mesh, in_specs=in_specs, out_specs=out_specs, check_vma=False)
```

```python
import functools
import math

import jax
import jax.numpy as jnp
from jax import lax
from jax.experimental import pallas as pl
from jax.experimental.pallas import tpu as pltpu
from jax.sharding import PartitionSpec as P

D = 2048
H = 16
DN = 128
DR = 64
DV = 128
QL = 1536
KL = 512
EXP_DEV = 2
TOPK = 6
ROWS = 16
COLS = 8
TS = 256
CUT = 208

eps = 1e-06
route_scale = 2.446
rope_base = 50000.0
score_scale = 1.0 / math.sqrt(DN + DR)
score_bits = score_scale * math.log2(math.e)

bf16 = jnp.bfloat16
f32 = jnp.float32
ANY = pl.ANY
VM = pltpu.VMEM


def shape_of(shape, dtype):
    return jax.ShapeDtypeStruct(shape, dtype)

MESH = pl.DeviceIdType.MESH
RING = 4
VMEM_BYTES = 56 * 2**20


class Place:
    def __init__(self, axis):
        self.axis = axis
        self.index = lax.axis_index(axis)
        self.cores = 2 if axis == "row" else 1
        self.core = lax.rem(self.index, self.cores)
        self.ring = lax.rem(lax.div(self.index, self.cores), RING)
        self.pair = lax.div(self.index, self.cores * RING)

    def at(self, pair, ring, core=None):
        core = self.core if core is None else core
        return (pair * RING + ring) * self.cores + core

    def turn(self, step):
        return lax.rem(self.ring + step + RING, RING)

    def peers(self):
        found = [self.at(self.pair, self.turn(step)) for step in (1, 2, 3)]
        found.append(self.at(1 - self.pair, self.ring))
        if self.cores == 2:
            found.append(self.at(self.pair, self.ring, 1 - self.core))
        return found


class Net:
    def __init__(self, send_sems, recv_sems):
        self.send_sems, self.recv_sems = send_sems, recv_sems
        self.count = 0
        self.sent = []
        self.own = []

    def send(self, source, target, axis, index):
        number = self.count
        self.count += 1
        copy = pltpu.make_async_remote_copy(
            source,
            target,
            self.send_sems.at[number],
            self.recv_sems.at[number],
            device_id={axis: index},
            device_id_type=MESH,
        )
        copy.start()
        self.sent.append(copy)
        return number

    def receive(self, number, target, axis, index):
        pltpu.make_async_remote_copy(
            target,
            target,
            self.send_sems.at[number],
            self.recv_sems.at[number],
            device_id={axis: index},
            device_id_type=MESH,
        ).wait_recv()

    def local(self, source, target):
        number = self.count
        self.count += 1
        copy = pltpu.make_async_copy(source, target, self.send_sems.at[number])
        copy.start()
        self.own.append(copy)

    def settle(self):
        for copy in self.own:
            copy.wait()
        self.own = []

    def finish(self):
        for copy in self.sent:
            copy.wait_send()
        self.settle()


def greet(*places):
    barrier = pltpu.get_barrier_semaphore()
    count = 0
    for place in places:
        for peer in place.peers():
            pl.semaphore_signal(
                barrier, inc=1, device_id={place.axis: peer}, device_id_type=MESH
            )
            count += 1
    pl.semaphore_wait(barrier, count)


class Gather:
    def __init__(self, net, place, source, slot, rows, cut):
        self.net, self.place, self.source, self.slot = net, place, source, slot
        self.rows, self.cut = rows, cut
        self.first, self.second = (0, cut), (cut, rows - cut)
        self.crossed = []

    def _send(self, owner, part, peer, own=False):
        piece = self.slot(owner, *part)
        start = self.source.at[pl.ds(*part)] if own else piece
        return self.net.send(start, piece, self.place.axis, peer)

    def _receive(self, number, pair, ring, part, peer, cross=True):
        place = self.place
        self.net.receive(number, self.slot(place.at(pair, ring), *part), place.axis, peer)
        if cross and place.cores == 2:
            self._cross(pair, ring, part)

    def _cross(self, pair, ring, part, own=False):
        place = self.place
        partner = place.at(place.pair, place.ring, 1 - place.core)
        number = self._send(place.at(pair, ring), part, partner, own)
        self.crossed.append((number, pair, ring, part))

    def start_first(self):
        place = self.place
        me, other = place.index, place.at(1 - place.pair, place.ring)
        if self.cut:
            self.across = self._send(me, self.first, other, True)
            self.near = [
                self._send(me, self.first, place.at(place.pair, place.turn(step)), True)
                for step in (1, 2, 3)
            ]

    def start_second(self):
        place = self.place
        me, other = place.index, place.at(1 - place.pair, place.ring)
        if self.second[1]:
            self.round = [
                self._send(me, self.second, place.at(place.pair, place.turn(step)), True)
                for step in (1, 2, 3)
            ]
            self.over = [self._send(me, self.second, other, True)]
        if place.cores == 2:
            self._cross(place.pair, place.ring, (0, self.rows), True)
        self.net.local(self.source, self.slot(me, 0, self.rows))

    def start(self):
        self.start_first()
        self.start_second()

    def forward_first(self):
        place = self.place
        other = place.at(1 - place.pair, place.ring)
        if self.cut:
            self._receive(self.across, 1 - place.pair, place.ring, self.first, other)
            self.far = [
                self._send(other, self.first, place.at(place.pair, place.turn(step)))
                for step in (1, 2, 3)
            ]

    def forward_second(self):
        place = self.place
        other = place.at(1 - place.pair, place.ring)
        if self.second[1]:
            for step in (1, 3, 2):
                ring = place.turn(-step)
                owner = place.at(place.pair, ring)
                self._receive(self.round[step - 1], place.pair, ring, self.second, owner, False)
                self.over.append(self._send(owner, self.second, other))
                if place.cores == 2:
                    self._cross(place.pair, ring, self.second)

    def land(self):
        place = self.place
        other = place.at(1 - place.pair, place.ring)
        if self.cut:
            for step in (1, 3, 2):
                ring = place.turn(-step)
                owner = place.at(place.pair, ring)
                self._receive(self.near[step - 1], place.pair, ring, self.first, owner)
            for step in (1, 3, 2):
                ring = place.turn(-step)
                owner = place.at(place.pair, ring)
                self._receive(self.far[step - 1], 1 - place.pair, ring, self.first, owner)
        if self.second[1]:
            for number, step in zip(self.over, (0, 1, 3, 2)):
                ring = place.turn(-step)
                self._receive(number, 1 - place.pair, ring, self.second, other)

    def end(self):
        place = self.place
        partner = place.at(place.pair, place.ring, 1 - place.core)
        for number, pair, ring, part in self.crossed:
            piece = self.slot(place.at(pair, ring, 1 - place.core), *part)
            self.net.receive(number, piece, place.axis, partner)


def run_gathers(*gathers):
    for gather in gathers:
        gather.start()
    for gather in gathers:
        gather.forward_first()
    for gather in gathers:
        gather.forward_second()
    for gather in gathers:
        gather.land()
    for gather in gathers:
        gather.end()


def row_slots(ref, rows):
    return lambda owner, low, count: ref.at[
        pl.ds(pl.multiple_of(owner * rows + low, 16), count)
    ]


def lead_slots(ref):
    return lambda owner, low, count: ref.at[owner, pl.ds(low, count)]


def lane_slots(ref, width):
    return lambda owner, low, count: ref.at[
        pl.ds(low, count), pl.ds(pl.multiple_of(owner * width, 128), width)
    ]


class Scatter:
    def __init__(self, net, place, block, rows, cut, scratch, keep):
        self.net, self.place, self.block, self.rows, self.cut = net, place, block, rows, cut
        self.scratch, self.keep = scratch, keep
        self.first, self.second = (0, cut), (cut, rows - cut)

    @staticmethod
    def scratch_of(rows, cut, width, dtype=jnp.bfloat16):
        shapes = []
        if cut:
            shapes += [(3, 2, cut, width), (2, cut, width)]
        if rows - cut:
            shapes += [(4, rows - cut, width), (4, rows - cut, width), (3, rows - cut, width)]
        return [pltpu.VMEM(shape, dtype) for shape in shapes]

    def _refs(self):
        refs = list(self.scratch)
        first = refs[:2] if self.cut else None
        second = refs[-3:] if self.second[1] else None
        return first, second

    def _owner(self, pair, ring):
        return self.place.at(pair, ring)

    def start(self):
        place, net = self.place, self.net
        first, second = self._refs()
        if first:
            self.round = [
                [
                    net.send(
                        self.block(self._owner(pair, place.turn(step)), *self.first),
                        first[0].at[step - 1, pair],
                        place.axis,
                        place.at(place.pair, place.turn(step)),
                    )
                    for pair in (0, 1)
                ]
                for step in (1, 2, 3)
            ]
        if second:
            self.across = [
                net.send(
                    self.block(self._owner(1 - place.pair, ring), *self.second),
                    second[0].at[ring],
                    place.axis,
                    place.at(1 - place.pair, place.ring),
                )
                for ring in range(RING)
            ]

    def forward_second(self):
        place, net = self.place, self.net
        first, second = self._refs()
        if not second:
            return
        other = place.at(1 - place.pair, place.ring)
        for ring in range(RING):
            net.receive(self.across[ring], second[0].at[ring], place.axis, other)
        for ring in range(RING):
            total = (
                self.block(self._owner(place.pair, ring), *self.second)[...].astype(jnp.float32)
                + second[0][ring].astype(jnp.float32)
            )
            second[1][ring] = total.astype(second[1].dtype)
        self.last = [
            net.send(
                second[1].at[place.turn(step)],
                second[2].at[step - 1],
                place.axis,
                place.at(place.pair, place.turn(step)),
            )
            for step in (1, 2, 3)
        ]

    def forward_first(self):
        place, net = self.place, self.net
        first, second = self._refs()
        if not first:
            return
        for step in (1, 3, 2):
            owner = place.at(place.pair, place.turn(-step))
            for pair in (0, 1):
                net.receive(self.round[step - 1][pair], first[0].at[step - 1, pair], place.axis, owner)
        other = 1 - place.pair
        total = self.block(self._owner(other, place.ring), *self.first)[...].astype(jnp.float32)
        for step in range(3):
            total = total + first[0][step, other].astype(jnp.float32)
        first[1][0] = total.astype(first[1].dtype)
        self.over = net.send(
            first[1].at[0], first[1].at[1], place.axis, place.at(other, place.ring)
        )

    def end_first(self):
        place, net = self.place, self.net
        first, second = self._refs()
        if not first:
            return
        total = self.block(self._owner(place.pair, place.ring), *self.first)[...].astype(jnp.float32)
        for step in range(3):
            total = total + first[0][step, place.pair].astype(jnp.float32)
        other = place.at(1 - place.pair, place.ring)
        net.receive(self.over, first[1].at[1], place.axis, other)
        self.keep(self.first, total + first[1][1].astype(jnp.float32))

    def end_second(self):
        place, net = self.place, self.net
        first, second = self._refs()
        if not second:
            return
        total = (
            self.block(self._owner(place.pair, place.ring), *self.second)[...].astype(jnp.float32)
            + second[0][place.ring].astype(jnp.float32)
        )
        for step in (1, 3, 2):
            owner = place.at(place.pair, place.turn(-step))
            net.receive(self.last[step - 1], second[2].at[step - 1], place.axis, owner)
            total = total + second[2][step - 1].astype(jnp.float32)
        self.keep(self.second, total)


def comm_call(body, name, collective_id, out_shapes, in_spaces, out_spaces, copies, scratch=(), args=()):
    return pl.pallas_call(
        body,
        name=name,
        out_shape=out_shapes,
        in_specs=[pl.BlockSpec(memory_space=space) for space in in_spaces],
        out_specs=tuple(pl.BlockSpec(memory_space=space) for space in out_spaces),
        scratch_shapes=[
            pltpu.SemaphoreType.DMA((copies,)),
            pltpu.SemaphoreType.DMA((copies,)),
            *scratch,
        ],
        compiler_params=pltpu.CompilerParams(
            collective_id=collective_id, has_side_effects=True, vmem_limit_bytes=VMEM_BYTES
        ),
    )(*args)


def front_body(hidden, w1, qu, lu, ao, sg, su, sd, *rest):
    hidden_all, w1_all, qu_all, lu_all, ao_all, sg_all, su_all, sd_all, ss, rs = rest
    row, col = Place("row"), Place("col")
    greet(row, col)
    net = Net(ss, rs)
    run_gathers(
        Gather(net, col, hidden, lane_slots(hidden_all, D // COLS), 2 * TS, CUT),
        Gather(net, row, w1, row_slots(w1_all, w1.shape[0]), w1.shape[0], 0),
        Gather(net, row, qu, row_slots(qu_all, qu.shape[0]), qu.shape[0], qu.shape[0]),
        Gather(net, row, lu, row_slots(lu_all, lu.shape[0]), lu.shape[0], lu.shape[0]),
        Gather(net, row, ao, lane_slots(ao_all, ao.shape[1]), ao.shape[0], 0),
        Gather(net, row, sg, row_slots(sg_all, sg.shape[0]), sg.shape[0], sg.shape[0]),
        Gather(net, row, su, row_slots(su_all, su.shape[0]), su.shape[0], 0),
        Gather(net, row, sd, lane_slots(sd_all, sd.shape[1]), sd.shape[0], 0),
    )
    net.finish()


def stacked(term):
    return shape_of((ROWS * term.shape[0], term.shape[1]), term.dtype)


def side_by_side(term):
    return shape_of((term.shape[0], ROWS * term.shape[1]), term.dtype)


def front(hidden, w1, qu, lu, ao, sg, su, sd):
    return comm_call(
        front_body,
        "gather_front",
        1,
        (
            shape_of((2 * TS, D), bf16),
            stacked(w1),
            stacked(qu),
            stacked(lu),
            side_by_side(ao),
            stacked(sg),
            stacked(su),
            side_by_side(sd),
        ),
        [ANY] * 8,
        [ANY] * 8,
        160,
        args=(hidden, w1, qu, lu, ao, sg, su, sd),
    )


def latent_body(query, latent, query_all, latent_all, ss, rs):
    col = Place("col")
    greet(col)
    net = Net(ss, rs)
    run_gathers(
        Gather(net, col, query, row_slots(query_all, query.shape[0]), query.shape[0], 96),
        Gather(net, col, latent, lead_slots(latent_all), latent.shape[0], 0),
    )
    net.finish()


def latents(query, latent):
    return comm_call(
        latent_body,
        "gather_latents",
        2,
        (
            shape_of((COLS * query.shape[0], query.shape[1]), bf16),
            shape_of((COLS, *latent.shape), bf16),
        ),
        [ANY] * 2,
        [ANY] * 2,
        64,
        args=(query, latent),
    )


def keys_body(kvr, grad, kvr_all, grad_all, ss, rs):
    row, col = Place("row"), Place("col")
    greet(row, col)
    net = Net(ss, rs)
    run_gathers(
        Gather(net, row, kvr, lead_slots(kvr_all), 2 * TS, CUT),
        Gather(net, col, grad, lane_slots(grad_all, D // COLS), 2 * TS, 2 * TS),
    )
    net.finish()


def keys(kvr, grad):
    return comm_call(
        keys_body,
        "gather_keys",
        3,
        (shape_of((ROWS, *kvr.shape), bf16), shape_of((2 * TS, D), bf16)),
        [ANY] * 2,
        [ANY] * 2,
        64,
        args=(kvr, grad),
    )


def sum_body(kinds, term, *rest):
    count = len(kinds)
    extras, total_all, extras_all = rest[:count], rest[count], rest[count + 1 : 2 * count + 1]
    ss, rs, *scratch = rest[2 * count + 1 :]
    places = {"row": Place("row"), "col": Place("col")}
    greet(*(places[axis] for axis in sorted({"col", *(axis for axis, cut in kinds)})))
    net = Net(ss, rs)
    width = D // COLS
    mine = scratch[-1]

    def keep(part, value):
        mine[pl.ds(*part)] = value.astype(mine.dtype)

    col = places["col"]
    scatter = Scatter(net, col, lane_slots(term, width), 2 * TS, CUT, scratch[:-1], keep)
    gather = Gather(net, col, mine, lane_slots(total_all, width), 2 * TS, CUT)
    beside = [
        Gather(net, places[axis], extra, lead_slots(extra_all), extra.shape[0], cut)
        for (axis, cut), extra, extra_all in zip(kinds, extras, extras_all)
    ]
    scatter.start()
    for extra in beside:
        extra.start()
    for extra in beside:
        extra.forward_first()
    scatter.forward_second()
    scatter.forward_first()
    for extra in beside:
        extra.forward_second()
    scatter.end_first()
    gather.start_first()
    scatter.end_second()
    gather.start_second()
    gather.forward_first()
    gather.forward_second()
    for extra in beside:
        extra.land()
    gather.land()
    for extra in beside:
        extra.end()
    gather.end()
    net.finish()


def sum_over_col(name, collective_id, term, kinds, *extras):
    counts = {"row": ROWS, "col": COLS}
    return comm_call(
        functools.partial(sum_body, kinds),
        name,
        collective_id,
        (
            shape_of((2 * TS, D), bf16),
            *(
                shape_of((counts[axis], *extra.shape), extra.dtype)
                for (axis, cut), extra in zip(kinds, extras)
            ),
        ),
        [VM] + [ANY] * len(extras),
        [ANY] * (1 + len(extras)),
        128,
        [*Scatter.scratch_of(2 * TS, CUT, D // COLS), pltpu.VMEM((2 * TS, D // COLS), bf16)],
        (term, *extras),
    )


def back_body(grad, stats, branch, grad_all, stats_all, branch_sum, ss, rs, *scratch):
    row, col = Place("row"), Place("col")
    greet(row, col)
    net = Net(ss, rs)

    def keep(part, value):
        branch_sum[pl.ds(*part)] = value

    scatter = Scatter(net, col, lane_slots(branch, D // COLS), 2 * TS, CUT, scratch, keep)
    gathers = (
        Gather(net, row, grad, lead_slots(grad_all), 2 * TS, CUT),
        Gather(net, row, stats, lead_slots(stats_all), stats.shape[0], stats.shape[0]),
    )
    for gather in gathers:
        gather.start()
    scatter.start()
    for gather in gathers:
        gather.forward_first()
    for gather in gathers:
        gather.forward_second()
    scatter.forward_second()
    scatter.forward_first()
    for gather in gathers:
        gather.land()
    scatter.end_first()
    scatter.end_second()
    for gather in gathers:
        gather.end()
    net.finish()


def back(grad, stats, branch):
    return comm_call(
        back_body,
        "gather_back",
        6,
        (
            shape_of((ROWS, *grad.shape), bf16),
            shape_of((ROWS, *stats.shape), f32),
            shape_of((2 * TS, D // COLS), f32),
        ),
        [ANY, ANY, VM],
        [ANY, ANY, VM],
        96,
        Scatter.scratch_of(2 * TS, CUT, D // COLS),
        (grad, stats, branch),
    )


class RowScatter:
    def __init__(self, net, place, term, cut, scratch, keep):
        self.net, self.place, self.term = net, place, term
        self.arrived, self.summed = scratch[:2]
        rows = term.shape[3]

        def block(owner, low, count):
            return self.summed.at[lax.div(owner, 2), pl.ds(low, count)]

        self.inner = Scatter(net, place, block, rows, cut, scratch[2:], keep)

    @staticmethod
    def scratch_of(rows, cut, width):
        return [
            pltpu.VMEM((2, RING, rows, width), bf16),
            pltpu.VMEM((2 * RING, rows, width), bf16),
            *Scatter.scratch_of(rows, cut, width),
        ]

    def start(self):
        place = self.place
        self.partner = place.at(place.pair, place.ring, 1 - place.core)
        self.number = self.net.send(
            self.term.at[:, :, 1 - place.core], self.arrived, place.axis, self.partner
        )

    def middle(self):
        place = self.place
        self.net.receive(self.number, self.arrived, place.axis, self.partner)
        for pair in range(2):
            for ring in range(RING):
                self.summed[pair * RING + ring] = (
                    self.term[pair, ring, place.core].astype(f32)
                    + self.arrived[pair, ring].astype(f32)
                ).astype(bf16)
        self.inner.start()


def run_scatters(scatters):
    for scatter in scatters:
        scatter.forward_second()
    for scatter in scatters:
        scatter.forward_first()
    for scatter in scatters:
        scatter.end_first()
    for scatter in scatters:
        scatter.end_second()


def keep_in(ref):
    def keep(part, value):
        ref[pl.ds(*part)] = value

    return keep


def block_slots(ref):
    return lambda owner, low, count: ref.at[owner, pl.ds(low, count)]


def rows_sum(net, place, terms, cuts, totals, scratch):
    parts = []
    for term, cut, total in zip(terms, cuts, totals):
        count = len(RowScatter.scratch_of(term.shape[3], cut, term.shape[4]))
        parts.append(RowScatter(net, place, term, cut, scratch[:count], keep_in(total)))
        scratch = scratch[count:]
    return parts


def rows_scratch(terms, cuts):
    found = []
    for term, cut in zip(terms, cuts):
        found += RowScatter.scratch_of(term.shape[3], cut, term.shape[4])
    return found


def col_and_row_body(col_cuts, row_cuts, slots, *rest):
    cols, rows = len(col_cuts), len(row_cuts)
    col_terms, rest = rest[:cols], rest[cols:]
    extra, rest = rest[0], rest[1:]
    row_terms, rest = rest[:rows], rest[rows:]
    col_totals, rest = rest[:cols], rest[cols:]
    extra_all, rest = rest[0], rest[1:]
    row_totals, rest = rest[:rows], rest[rows:]
    ss, rs, *scratch = rest
    row, col = Place("row"), Place("col")
    greet(row, col)
    net = Net(ss, rs)
    scatters = []
    for term, cut, total in zip(col_terms, col_cuts, col_totals):
        height, width = total.shape
        block = lane_slots(term, width) if slots == "lane" else block_slots(term)
        count = len(Scatter.scratch_of(height, cut, width))
        scatters.append(Scatter(net, col, block, height, cut, scratch[:count], keep_in(total)))
        scratch = scratch[count:]
    beside = Gather(net, col, extra, lead_slots(extra_all), extra.shape[0], extra.shape[0])
    parts = rows_sum(net, row, row_terms, row_cuts, row_totals, scratch)
    for part in parts:
        part.start()
    for scatter in scatters:
        scatter.start()
    beside.start()
    for part in parts:
        part.middle()
    beside.forward_first()
    run_scatters(scatters + [part.inner for part in parts])
    beside.land()
    net.finish()


def col_and_row(name, collective_id, slots, col_terms, col_shapes, col_cuts, extra, row_terms, row_cuts):
    scratch = []
    for shape, cut in zip(col_shapes, col_cuts):
        scratch += Scatter.scratch_of(shape[0], cut, shape[1])
    found = comm_call(
        functools.partial(col_and_row_body, tuple(col_cuts), tuple(row_cuts), slots),
        name,
        collective_id,
        (
            *(shape_of(shape, f32) for shape in col_shapes),
            shape_of((COLS, *extra.shape), f32),
            *(shape_of(term.shape[3:], f32) for term in row_terms),
        ),
        [*([VM] * len(col_terms)), ANY, *([VM] * len(row_terms))],
        [*([VM] * len(col_terms)), ANY, *([VM] * len(row_terms))],
        128,
        [*scratch, *rows_scratch(row_terms, row_cuts)],
        (*col_terms, extra, *row_terms),
    )
    count = len(col_terms)
    return found[:count], found[count], found[count + 1 :]


def last_body(gains, gains_all, ss, rs, gains_rows, gains_mine):
    row, col = Place("row"), Place("col")
    greet(row, col)
    net = Net(ss, rs)
    beside = Gather(net, row, gains, lead_slots(gains_rows), 8, 8)
    beside.start()
    beside.forward_first()
    beside.land()
    beside.end()
    net.settle()
    total = gains_rows[0]
    for index in range(1, ROWS):
        total = total + gains_rows[index]
    gains_mine[...] = total
    run_gathers(Gather(net, col, gains_mine, lead_slots(gains_all), 8, 8))
    net.finish()


def last(gains):
    return comm_call(
        last_body,
        "sum_last",
        9,
        (shape_of((COLS, 8, 128), f32),),
        [VM],
        [VM],
        64,
        [pltpu.VMEM((ROWS, 8, 128), f32), pltpu.VMEM((8, 128), f32)],
        (gains,),
    )[0]


def contract(left, right):
    return lax.dot_general(left, right, (((1,), (1,)), ((), ())), preferred_element_type=f32)


def attend_body(lens, query, kvr, out, lse, scores):
    seq = pl.program_id(0)
    mine = lax.axis_index("row")
    live = lens[seq]
    steps = lax.div(jnp.minimum(mine + 1, lax.div(live + TS - 1, TS)) + 1, 2)
    width = 2 * TS
    places = mine * TS + lax.broadcasted_iota(jnp.int32, (TS, 1), 0)
    limit = jnp.minimum(places + 1, live)
    offsets = lax.broadcasted_iota(jnp.int32, (TS, width), 1)
    queries = [query[0, head] for head in range(2)]

    def first(step, tops):
        valid = offsets < limit - step * width
        block = kvr[pl.ds(2 * step, 2)].reshape(width, kvr.shape[2])
        found = []
        for head in range(2):
            value = contract(queries[head], block[:, head * 128 : head * 128 + 256])
            value = jnp.where(valid, value, -1e30)
            scores[head, step] = value
            top = tops[head]
            for low in range(0, width, 128):
                top = jnp.maximum(top, value[:, low : low + 128])
            found.append(top)
        return tuple(found)

    tops = lax.fori_loop(0, steps, first, (jnp.full((TS, 128), -1e30, f32),) * 2)
    tops = [jnp.max(top, axis=1, keepdims=True) * score_bits for top in tops]

    def second(step, carried):
        block = kvr[pl.ds(2 * step, 2)].reshape(width, kvr.shape[2])
        found = []
        for head in range(2):
            sums, total = carried[head]
            weight = jnp.exp2(scores[head, step] * score_bits - tops[head])
            for low in range(0, width, 128):
                sums = sums + weight[:, low : low + 128]
            value = block[:, 384 + head * 128 : 512 + head * 128]
            total = total + jnp.dot(weight.astype(bf16), value, preferred_element_type=f32)
            found.append((sums, total))
        return tuple(found)

    zero = jnp.zeros((TS, 128), f32)
    carried = lax.fori_loop(0, steps, second, ((zero, zero),) * 2)
    for head in range(2):
        sums, total = carried[head]
        whole = jnp.sum(sums, axis=1, keepdims=True)
        lanes = pl.ds(head * 128, 128)
        out[:, lanes] = total / whole
        lse[:, lanes] = jnp.broadcast_to(tops[head] + jnp.log2(whole), (TS, 128))


def attend(lens, query, kvr):
    return pl.pallas_call(
        attend_body,
        name="attend",
        grid=(2,),
        out_shape=(shape_of((2 * TS, 256), f32), shape_of((2 * TS, 256), f32)),
        in_specs=[
            pl.BlockSpec(memory_space=pltpu.SMEM),
            pl.BlockSpec((1, 2, TS, 256), lambda s: (s, 0, 0, 0)),
            pl.BlockSpec((ROWS, TS, kvr.shape[2]), lambda s: (0, s, 0)),
        ],
        out_specs=(
            pl.BlockSpec((TS, 256), lambda s: (s, 0)),
            pl.BlockSpec((TS, 256), lambda s: (s, 0)),
        ),
        scratch_shapes=[pltpu.VMEM((2, ROWS // 2, TS, 2 * TS), f32)],
        compiler_params=pltpu.CompilerParams(vmem_limit_bytes=VMEM_BYTES),
        cost_estimate=pl.CostEstimate(
            flops=6 * 10**9, bytes_accessed=12 * 10**6, transcendentals=4 * 10**6
        ),
    )(lens, query, kvr)


def attend_back_body(lens, query, kvr, grad, lse, delta, near, query_all, grad_all, stats, dq, dk, dv):
    seq = pl.program_id(0)
    mine = lax.axis_index("row")
    live = lens[seq]
    width = 2 * TS
    steps = lax.div(jnp.minimum(mine + 1, lax.div(live + TS - 1, TS)) + 1, 2)
    places = mine * TS + lax.broadcasted_iota(jnp.int32, (TS, 1), 0)
    limit = jnp.minimum(places + 1, live)
    offsets = lax.broadcasted_iota(jnp.int32, (TS, width), 1)

    def queries_step(step, carried):
        valid = offsets < limit - step * width
        block = kvr[pl.ds(2 * step, 2)].reshape(width, kvr.shape[2])
        found = []
        for head in range(2):
            key = block[:, head * 128 : head * 128 + 256]
            value = block[:, 384 + head * 128 : 512 + head * 128]
            lanes = pl.ds(head * 128, 128)
            score = contract(query[0, head], key) * score_bits - lse[:, lanes][:, :1]
            weight = jnp.exp2(jnp.where(valid, score, -1e30))
            slope = contract(grad[:, lanes], value) - delta[:, lanes][:, :1]
            low = (weight * slope).astype(bf16)
            found.append(carried[head] + jnp.dot(low, key, preferred_element_type=f32))
        return tuple(found)

    totals = lax.fori_loop(0, steps, queries_step, (jnp.zeros((TS, 256), f32),) * 2)
    for head in range(2):
        dq[0, head] = totals[head]

    bar = jnp.where(places < live, places, 2 * ROWS * TS)

    def keys_step(step, carried):
        valid = offsets >= bar - step * width
        queries = query_all[pl.ds(2 * step, 2)].reshape(width, query_all.shape[2])
        grads = grad_all[pl.ds(2 * step, 2)].reshape(width, 256)
        numbers = stats[pl.ds(2 * step, 2)]
        numbers = jnp.concatenate([numbers[0], numbers[1]], axis=1)
        found = []
        for head in range(2):
            key_total, value_total = carried[head]
            asked = queries[:, head * 128 : head * 128 + 256]
            given = grads[:, head * 128 : head * 128 + 128]
            score = contract(near[0, head], asked) * score_bits - numbers[head : head + 1]
            weight = jnp.exp2(jnp.where(valid, score, -1e30))
            value_total = value_total + jnp.dot(
                weight.astype(bf16), given, preferred_element_type=f32
            )
            value = kvr[mine, :, 384 + head * 128 : 512 + head * 128]
            slope = contract(value, given) - numbers[2 + head : 3 + head]
            low = (weight * slope).astype(bf16)
            key_total = key_total + jnp.dot(low, asked, preferred_element_type=f32)
            found.append((key_total, value_total))
        return tuple(found)

    zero = (jnp.zeros((TS, 256), f32), jnp.zeros((TS, 128), f32))
    last_step = jnp.where(mine * TS < live, ROWS // 2, 0)
    totals = lax.fori_loop(lax.div(mine, 2), last_step, keys_step, (zero, zero))
    for head in range(2):
        dk[0, head] = totals[head][0]
        dv[0, head] = totals[head][1]


def attend_back(lens, query, kvr, grad, lse, delta, near, query_all, grad_all, stats):
    lanes = pl.BlockSpec((TS, 256), lambda s: (s, 0))
    heads = pl.BlockSpec((1, 2, TS, 256), lambda s: (s, 0, 0, 0))
    return pl.pallas_call(
        attend_back_body,
        name="attend_back",
        grid=(2,),
        out_shape=(
            shape_of((2, 2, TS, 256), f32),
            shape_of((2, 2, TS, 256), f32),
            shape_of((2, 2, TS, 128), f32),
        ),
        in_specs=[
            pl.BlockSpec(memory_space=pltpu.SMEM),
            heads,
            pl.BlockSpec((ROWS, TS, kvr.shape[2]), lambda s: (0, s, 0)),
            lanes,
            lanes,
            lanes,
            heads,
            pl.BlockSpec((ROWS, TS, query_all.shape[2]), lambda s: (0, s, 0)),
            pl.BlockSpec((ROWS, TS, 256), lambda s: (0, s, 0)),
            pl.BlockSpec((ROWS, 8, TS), lambda s: (0, 0, s)),
        ],
        out_specs=(heads, heads, pl.BlockSpec((1, 2, TS, 128), lambda s: (s, 0, 0, 0))),
        compiler_params=pltpu.CompilerParams(vmem_limit_bytes=VMEM_BYTES),
        cost_estimate=pl.CostEstimate(
            flops=12 * 10**9, bytes_accessed=24 * 10**6, transcendentals=8 * 10**6
        ),
    )(lens, query, kvr, grad, lse, delta, near, query_all, grad_all, stats)


def silu_parts(gate_value):
    sigmoid_value = 1.0 / (1.0 + jnp.exp(-gate_value))
    return (gate_value * sigmoid_value, sigmoid_value * (1.0 + gate_value * (1.0 - sigmoid_value)))


def transposed(left, right):
    return lax.dot_general(left, right, (((0,), (0,)), ((), ())), preferred_element_type=f32)


def shared_body(normed, grad, gate, up, down, branch, back_grad, gate_grad, up_grad, down_grad):
    normed_value, grad_value = normed[...], grad[...]
    gate_value = jnp.dot(normed_value, gate[...], preferred_element_type=f32)
    up_value = jnp.dot(normed_value, up[...], preferred_element_type=f32)
    silu_value, slope = silu_parts(gate_value)
    act = (silu_value * up_value).astype(bf16)
    act_grad = contract(grad_value, down[...])
    gate_low = (act_grad * up_value * slope).astype(bf16)
    up_low = (act_grad * silu_value).astype(bf16)
    branch[...] = jnp.dot(act, down[...], preferred_element_type=f32)
    back_grad[...] = contract(gate_low, gate[...]) + contract(up_low, up[...])
    gate_grad[...] = transposed(normed_value, gate_low).astype(bf16)
    up_grad[...] = transposed(normed_value, up_low).astype(bf16)
    width = down_grad.shape[2]
    for index in range(ROWS):
        part = grad_value[:, index * width : (index + 1) * width]
        down_grad[index] = transposed(act, part).astype(bf16)


def shared_experts(normed, grad, gate, up, down):
    units = gate.shape[1]
    return pl.pallas_call(
        shared_body,
        name="shared_experts",
        out_shape=(
            shape_of((2 * TS, D), f32),
            shape_of((2 * TS, D), f32),
            shape_of((D, units), bf16),
            shape_of((D, units), bf16),
            shape_of((ROWS, units, D // ROWS), bf16),
        ),
        in_specs=[pl.BlockSpec(memory_space=VM)] * 5,
        out_specs=(pl.BlockSpec(memory_space=VM),) * 5,
        compiler_params=pltpu.CompilerParams(vmem_limit_bytes=VMEM_BYTES),
        cost_estimate=pl.CostEstimate(
            flops=8 * 10**9, bytes_accessed=24 * 10**6, transcendentals=10**6
        ),
    )(normed, grad, gate, up, down)


def experts_body(
    slots, gates, normed, grad, branch_in, back_in, w_in, w_down,
    branch, back_grad, gate_grad, w_in_grad, w_down_grad,
    dispatch, taken, taken_turned, given, routed, result, back_sum, branch_sum, back_total,
):
    expert, step = pl.program_id(0), pl.program_id(1)
    steps = pl.num_programs(1)
    capacity = dispatch.shape[0]
    units = w_down.shape[1]

    @pl.when(step == 0)
    def _():
        places = lax.broadcasted_iota(jnp.int32, dispatch.shape, 0)
        chosen = places == slots[pl.ds(expert, 1)]
        dispatch[...] = chosen.astype(bf16)
        weight = jnp.sum(jnp.where(chosen, gates[pl.ds(expert, 1)], 0.0), axis=1, keepdims=True)
        rows = jnp.dot(dispatch[...], normed[...], preferred_element_type=f32).astype(bf16)
        taken[...] = rows
        taken_turned[...] = rows.T
        grads = jnp.dot(dispatch[...], grad[...], preferred_element_type=f32)
        given[...] = grads.astype(bf16)
        routed[...] = (weight * grads).astype(bf16)
        result[...] = jnp.zeros_like(result)
        back_sum[...] = jnp.zeros_like(back_sum)

    hidden = jnp.dot(taken[...], w_in[0], preferred_element_type=f32)
    gate_value, up_value = hidden[:, :units], hidden[:, units:]
    silu_value, slope = silu_parts(gate_value)
    act = (silu_value * up_value).astype(bf16)
    act_grad = contract(routed[...], w_down[0])
    low = jnp.concatenate(
        [
            (act_grad * up_value * slope).astype(bf16),
            (act_grad * silu_value).astype(bf16),
        ],
        axis=1,
    )
    result[...] += jnp.dot(act, w_down[0], preferred_element_type=f32)
    back_sum[...] += contract(low, w_in[0])
    w_in_grad[0] = jnp.dot(taken_turned[...], low, preferred_element_type=f32).astype(bf16)
    w_down_grad[0] = transposed(act, routed[...]).astype(bf16)

    @pl.when(step == steps - 1)
    def _():
        places = lax.broadcasted_iota(jnp.int32, dispatch.shape, 0)
        chosen = places == slots[pl.ds(expert, 1)]
        weight = jnp.sum(jnp.where(chosen, gates[pl.ds(expert, 1)], 0.0), axis=1, keepdims=True)
        number = jnp.sum(result[...] * given[...].astype(f32), axis=1, keepdims=True)
        gate_grad[pl.ds(expert, 1)] = jnp.sum(
            jnp.where(chosen, number, 0.0), axis=0, keepdims=True
        )
        outward = transposed(dispatch[...], (weight * result[...]).astype(bf16))
        inward = transposed(dispatch[...], back_sum[...].astype(bf16))

        @pl.when(expert == 0)
        def _():
            branch_sum[...] = branch_in[...] + outward
            back_total[...] = back_in[...] + inward

        @pl.when(expert == EXP_DEV - 1)
        def _():
            branch[...] = (branch_sum[...] + outward).astype(bf16)
            back_grad[...] = (back_total[...] + inward).astype(bf16)


def experts(capacity, slots, gates, normed, grad, branch_in, back_in, w_in, w_down):
    units = 128
    steps = w_down.shape[1] // units
    whole = pl.BlockSpec(memory_space=VM)
    in_block = pl.BlockSpec((1, D, 2 * units), lambda e, k: (e, 0, k))
    down_block = pl.BlockSpec((1, units, D), lambda e, k: (e, k, 0))
    return pl.pallas_call(
        experts_body,
        name="experts",
        grid=(EXP_DEV, steps),
        out_shape=(
            shape_of((2 * TS, D), bf16),
            shape_of((2 * TS, D), bf16),
            shape_of((8, 2 * TS), f32),
            shape_of(w_in.shape, bf16),
            shape_of(w_down.shape, bf16),
        ),
        in_specs=[whole] * 6 + [in_block, down_block],
        out_specs=(whole, whole, whole, in_block, down_block),
        scratch_shapes=[
            pltpu.VMEM((capacity, 2 * TS), bf16),
            pltpu.VMEM((capacity, D), bf16),
            pltpu.VMEM((D, capacity), bf16),
            pltpu.VMEM((capacity, D), bf16),
            pltpu.VMEM((capacity, D), bf16),
            pltpu.VMEM((capacity, D), f32),
            pltpu.VMEM((capacity, D), f32),
            pltpu.VMEM((2 * TS, D), f32),
            pltpu.VMEM((2 * TS, D), f32),
        ],
        compiler_params=pltpu.CompilerParams(vmem_limit_bytes=VMEM_BYTES),
        cost_estimate=pl.CostEstimate(
            flops=40 * 10**9, bytes_accessed=80 * 10**6, transcendentals=10**6
        ),
    )(slots, gates, normed, grad, branch_in, back_in, w_in, w_down)


def rope_tables(positions, width):
    half_width = width // 2
    frequency = jnp.exp(
        -jnp.log(rope_base) * (2.0 * jnp.arange(half_width, dtype=jnp.float32) / width)
    )
    angles = positions.astype(jnp.float32)[:, None] * frequency[None, :]
    return (jnp.cos(angles), jnp.sin(angles))


def rotate(values, rope_cos, rope_sin):
    half_width = values.shape[-1] // 2
    first_half = values[..., :half_width]
    second_half = values[..., half_width:]
    return jnp.concatenate(
        [
            first_half * rope_cos - second_half * rope_sin,
            second_half * rope_cos + first_half * rope_sin,
        ],
        axis=-1,
    )


def unrotate(grads_in, rope_cos, rope_sin):
    return rotate(grads_in, rope_cos, -rope_sin)


def rms_scale(values):
    return lax.rsqrt(jnp.mean(values * values, axis=-1, keepdims=True) + eps)


def product(left, right):
    return jnp.dot(left, right, preferred_element_type=jnp.float32)


def left_product(left, right):
    return lax.dot_general(
        left, right, (((0,), (0,)), ((), ())), preferred_element_type=jnp.float32
    )


def right_product(left, right):
    return lax.dot_general(
        left, right, (((1,), (1,)), ((), ())), preferred_element_type=jnp.float32
    )


def turned_product(left, right):
    return lax.dot_general(
        left, right, (((0,), (1,)), ((), ())), preferred_element_type=jnp.float32
    )


def einsum(text, *terms):
    return jnp.einsum(text, *terms, preferred_element_type=f32)


def to_blocks(term):
    return term.reshape(2, RING, 2, term.shape[0] // ROWS, term.shape[1])


def local(
    hidden_in,
    gain_first,
    query_down,
    query_gain,
    query_up,
    latent_down,
    latent_gain,
    latent_up,
    attention_out,
    gain_second,
    router,
    expert_gate,
    expert_up,
    expert_down,
    shared_gate,
    shared_up,
    shared_down,
    seq_lens,
    routes,
    out_grad,
):
    row_index = lax.axis_index("row")
    col_index = lax.axis_index("col")
    seq_count, local_len, col_width = hidden_in.shape
    row_total = seq_count * local_len
    experts_all = EXP_DEV * COLS
    most_rows = (5 * local_len * TOPK + 4 * experts_all - 1) // (4 * experts_all)
    capacity = seq_count * most_rows
    query_cols = QL // COLS
    kv_cols = (KL + DR) // COLS

    def here(values, axis=-1):
        width = values.shape[axis] // COLS
        return lax.dynamic_slice_in_dim(values, col_index * width, width, axis)

    (
        hidden_low,
        down_all,
        query_up_all,
        latent_up_all,
        attention_out_all,
        shared_gate_all,
        shared_up_all,
        shared_down_all,
    ) = front(
        hidden_in.reshape(row_total, col_width),
        jnp.concatenate([query_down, latent_down, router], axis=1),
        query_up,
        latent_up,
        attention_out,
        shared_gate,
        shared_up,
        shared_down,
    )
    expert_units = expert_gate.shape[2]
    expert_in = jnp.stack(
        [
            weight.reshape(EXP_DEV, -1, expert_units // 128, 128)
            for weight in (expert_gate, expert_up)
        ],
        axis=3,
    ).reshape(EXP_DEV, -1, 2 * expert_units)
    expert_in, expert_down_late, hidden_low = lax.optimization_barrier(
        (expert_in, expert_down, hidden_low)
    )
    expert_in_all = lax.all_gather(expert_in, "row", axis=1, tiled=True)
    expert_down_all = lax.all_gather(expert_down_late, "row", axis=1, tiled=True)

    hidden = hidden_low.astype(f32)
    scale_first = rms_scale(hidden)
    normed_first = (hidden * scale_first * gain_first).astype(bf16)
    latent_width = query_cols + kv_cols
    latent_weights = down_all[:, :latent_width]
    router_all = down_all[:, latent_width:]
    latent_here = turned_product(latent_weights, normed_first).astype(bf16)
    kv_pad = (-kv_cols) % 16
    query_latent, kv_latent = latents(
        latent_here[:query_cols], jnp.pad(latent_here[query_cols:], ((0, kv_pad), (0, 0)))
    )
    kv_latent = kv_latent[:, :kv_cols].reshape(KL + DR, row_total)
    query_float = query_latent.astype(f32)
    query_scale = lax.rsqrt(jnp.mean(query_float * query_float, axis=0, keepdims=True) + eps)
    query_input = (query_float * query_scale * query_gain[:, None]).astype(bf16)
    latent_float = kv_latent[:KL].astype(f32)
    latent_scale = lax.rsqrt(jnp.mean(latent_float * latent_float, axis=0, keepdims=True) + eps)
    latent_input = (latent_float * latent_scale * latent_gain[:, None]).astype(bf16)
    positions = row_index * local_len + jnp.arange(local_len, dtype=jnp.int32)
    rope_cos, rope_sin = rope_tables(positions, DR)
    rope_cos = jnp.concatenate([rope_cos] * seq_count, axis=0)
    rope_sin = jnp.concatenate([rope_sin] * seq_count, axis=0)
    query_proj = left_product(query_input, query_up_all)
    split = DN + DR
    nope = [query_proj[:, split * head : split * head + DN].astype(bf16) for head in range(2)]
    rope = [
        rotate(
            query_proj[:, split * head + DN : split * (head + 1)], rope_cos, rope_sin
        ).astype(bf16)
        for head in range(2)
    ]
    blank = jnp.zeros((row_total, DR), bf16)
    query_cat = jnp.stack(
        [
            jnp.concatenate([nope[0], rope[0], blank], axis=1),
            jnp.concatenate([rope[1], blank, nope[1]], axis=1),
        ],
        axis=0,
    )
    query_cat = query_cat.reshape(2, seq_count, local_len, 256).transpose(1, 0, 2, 3)
    query_pack = jnp.concatenate([nope[0], rope[0], rope[1], nope[1]], axis=1)
    key_value = left_product(latent_input, latent_up_all).astype(bf16)
    key_rope = rotate(kv_latent[KL:].T.astype(f32), rope_cos, rope_sin).astype(bf16)
    key_zero, value_zero = key_value[:, :DN], key_value[:, DN : 2 * DN]
    key_one, value_one = key_value[:, 2 * DN : 3 * DN], key_value[:, 3 * DN :]
    kvr = jnp.concatenate([key_zero, key_rope, blank, key_one, value_zero, value_one], axis=1)
    near = jnp.stack(
        [
            jnp.concatenate([key_zero, key_rope, blank], axis=1),
            jnp.concatenate([blank, key_rope, key_one], axis=1),
        ],
        axis=0,
    )
    near = near.reshape(2, seq_count, local_len, 256).transpose(1, 0, 2, 3)
    kvr_all, grad_full = keys(kvr, out_grad.reshape(row_total, col_width))

    attended_float, lse = attend(seq_lens, query_cat, kvr_all)
    attended = attended_float.astype(bf16)
    attention_part = product(attended, attention_out_all).astype(bf16)
    (attention_sum,) = sum_over_col("sum_attention", 4, attention_part, ())

    residual_one = hidden + attention_sum.astype(f32)
    scale_second = rms_scale(residual_one)
    normed_second = (residual_one * scale_second * gain_second).astype(bf16)
    logits = turned_product(router_all, normed_second)
    sigmoid_all = jax.nn.sigmoid(logits)
    routes_turned = routes.reshape(row_total, TOPK).T
    chosen = jnp.sum(
        (
            routes_turned[:, None, :] == jnp.arange(experts_all, dtype=jnp.int32)[None, :, None]
        ).astype(f32),
        axis=0,
    )
    weighted_sig = sigmoid_all * chosen
    denominator = jnp.sum(weighted_sig, axis=0, keepdims=True)
    gate_weights = route_scale * weighted_sig / denominator
    gate_here = here(gate_weights, 0)
    member = here(chosen, 0).reshape(EXP_DEV * seq_count, local_len)
    before = jnp.triu(jnp.ones((local_len, local_len), bf16), 1)
    rank = product(member.astype(bf16), before).reshape(EXP_DEV, seq_count, local_len)
    rank = rank + (jnp.arange(seq_count, dtype=f32) * most_rows)[None, :, None]
    slots = jnp.where(member.reshape(rank.shape) > 0, rank, float(capacity))
    slots = slots.astype(jnp.int32).reshape(EXP_DEV, row_total)
    shared_branch, shared_back, shared_gate_grad, shared_up_grad, shared_down_grad = shared_experts(
        normed_second, grad_full, shared_gate_all, shared_up_all, shared_down_all
    )
    branch_part, normed_part, gate_grad_here, expert_in_part, expert_down_part = experts(
        capacity,
        slots,
        gate_here,
        normed_second,
        grad_full,
        shared_branch,
        shared_back,
        expert_in_all,
        expert_down_all,
    )
    expert_in_sum = lax.psum_scatter(expert_in_part, "row", scatter_dimension=1, tiled=True)
    expert_down_sum = lax.psum_scatter(
        expert_down_part.reshape(EXP_DEV, ROWS, expert_units // ROWS, D),
        "row",
        scatter_dimension=1,
        tiled=False,
    )
    gate_grad_all = lax.dynamic_update_slice_in_dim(
        jnp.zeros((experts_all, row_total), f32), gate_grad_here[:EXP_DEV], col_index * EXP_DEV, 0
    )
    inner_sum = jnp.sum(gate_grad_all * gate_weights, axis=0, keepdims=True)
    logit_part = (
        sigmoid_all
        * (1.0 - sigmoid_all)
        * chosen
        / denominator
        * (route_scale * gate_grad_all - inner_sum)
    )
    normed_sum, logit_all, query_all = sum_over_col(
        "sum_normed",
        5,
        normed_part,
        (("col", experts_all), ("row", CUT)),
        logit_part,
        query_pack,
    )
    logit_low = jnp.sum(logit_all, axis=0).astype(bf16)
    normed_grad = normed_sum.astype(f32) + turned_product(logit_low, router_all)
    router_grad = turned_product(normed_second, logit_low)
    weighted = normed_grad * gain_second
    residual_grad = (
        grad_full.astype(f32)
        + scale_second * weighted
        - residual_one
        * (scale_second * scale_second * scale_second)
        * jnp.mean(weighted * residual_one, axis=-1, keepdims=True)
    )
    gain_second_part = jnp.sum(here(normed_grad) * here(residual_one) * scale_second, axis=0)

    attention_grad = residual_grad.astype(bf16)
    attention_out_grad = einsum(
        "rk,rbn->bkn", attended, attention_grad.reshape(row_total, ROWS, D // ROWS)
    ).astype(bf16)
    attended_grad = right_product(attention_grad, attention_out_all).astype(bf16)
    delta = jnp.sum(
        (attended_grad.astype(f32) * attended_float).reshape(row_total, 2, DV), axis=-1
    )
    delta_lanes = jnp.repeat(delta, DV, axis=1)
    lse_two = lse.reshape(row_total, 2, DV)[:, :, 0]
    stats = jnp.concatenate([lse_two.T, delta.T, jnp.zeros((4, row_total), f32)], axis=0)
    attended_grad_all, stats_all, branch_here = back(attended_grad, stats, branch_part)
    block_out = (
        (here(residual_one) + branch_here).astype(bf16).reshape(seq_count, local_len, col_width)
    )
    dq, dk, dv = attend_back(
        seq_lens,
        query_cat,
        kvr_all,
        attended_grad,
        lse,
        delta_lanes,
        near,
        query_all,
        attended_grad_all,
        stats_all,
    )
    dq = dq.transpose(1, 0, 2, 3).reshape(2, row_total, 256) * score_scale
    dk = dk.transpose(1, 0, 2, 3).reshape(2, row_total, 256) * score_scale
    dv = dv.transpose(1, 0, 2, 3).reshape(2, row_total, DV)
    query_grad = jnp.concatenate(
        [
            dq[0, :, :DN],
            unrotate(dq[0, :, DN:split], rope_cos, rope_sin),
            dq[1, :, DN:],
            unrotate(dq[1, :, :DR], rope_cos, rope_sin),
        ],
        axis=1,
    ).astype(bf16)
    kv_grad = jnp.concatenate([dk[0, :, :DN], dv[0], dk[1, :, DN:], dv[1]], axis=1).astype(bf16)
    rope_grad = unrotate(dk[0, :, DN:split] + dk[1, :, DR:DN], rope_cos, rope_sin)
    latent_up_grad = product(latent_input, kv_grad).astype(bf16)
    latent_in_grad = right_product(latent_up_all, kv_grad)
    query_up_grad = product(query_input, query_grad).astype(bf16)
    query_in_grad = right_product(query_up_all, query_grad)
    query_number = jnp.sum(query_in_grad * query_gain[:, None] * query_float, axis=0)
    latent_number = jnp.sum(latent_in_grad * latent_gain[:, None] * latent_float, axis=0)
    numbers = jnp.concatenate(
        [query_number[None], latent_number[None], jnp.zeros((6, row_total), f32)], axis=0
    )
    kv_part = jnp.concatenate([latent_in_grad, rope_grad.T], axis=0).astype(bf16)
    kv_part = jnp.pad(kv_part.reshape(COLS, kv_cols, row_total), ((0, 0), (0, kv_pad), (0, 0)))
    shared_width = shared_gate.shape[1]
    (query_in_here, kv_in_here), numbers_all, summed = col_and_row(
        "sum_latents",
        7,
        "lead",
        (query_in_grad.astype(bf16).reshape(COLS, query_cols, row_total), kv_part),
        ((query_cols, row_total), (kv_cols + kv_pad, row_total)),
        (96, 0),
        numbers,
        (
            attention_out_grad.reshape(2, RING, 2, col_width, D // ROWS),
            to_blocks(shared_gate_grad),
            to_blocks(shared_up_grad),
            shared_down_grad.reshape(2, RING, 2, shared_width, D // ROWS),
        ),
        (col_width, D // ROWS, 0, 0),
    )
    attention_out_sum, shared_gate_sum, shared_up_sum, shared_down_sum = summed
    kv_in_here = kv_in_here[:kv_cols]
    numbers_sum = jnp.sum(numbers_all, axis=0)
    query_mean = numbers_sum[:1] / QL
    latent_mean = numbers_sum[1:2] / KL
    query_float_here = here(query_float, 0)
    query_latent_here = (
        query_scale * query_in_here * here(query_gain)[:, None]
        - query_float_here * (query_scale * query_scale * query_scale) * query_mean
    )
    kv_float_here = here(kv_latent, 0).astype(f32)
    is_latent = (col_index * kv_cols + jnp.arange(kv_cols)) < KL
    latent_gain_here = here(jnp.concatenate([latent_gain, jnp.ones((DR,), f32)]))
    kv_latent_here = jnp.where(
        is_latent[:, None],
        latent_scale * kv_in_here * latent_gain_here[:, None]
        - kv_float_here * (latent_scale * latent_scale * latent_scale) * latent_mean,
        kv_in_here,
    )
    query_gain_part = jnp.sum(query_in_here * query_float_here * query_scale, axis=1)
    latent_gain_part = jnp.sum(kv_in_here * kv_float_here * latent_scale, axis=1)
    latent_here_grad = jnp.concatenate([query_latent_here, kv_latent_here], axis=0).astype(bf16)
    latent_down_grads = turned_product(normed_first, latent_here_grad)
    first_part = turned_product(latent_here_grad, latent_weights)
    first_number = jnp.sum(first_part * gain_first * hidden, axis=-1)
    first_numbers = jnp.concatenate([first_number[None], jnp.zeros((7, row_total), f32)], axis=0)
    (first_here,), first_numbers_all, summed = col_and_row(
        "sum_first",
        8,
        "lane",
        (first_part.astype(bf16),),
        ((row_total, col_width),),
        (CUT,),
        first_numbers,
        (
            to_blocks(
                jnp.concatenate([latent_down_grads.astype(bf16), router_grad.astype(bf16)], axis=1)
            ),
            to_blocks(query_up_grad),
            to_blocks(latent_up_grad),
        ),
        (0, QL // ROWS, KL // ROWS),
    )
    down_sum, query_up_sum, latent_up_sum = summed
    first_mean = (jnp.sum(first_numbers_all[:, 0], axis=0) / D)[:, None]
    hidden_here = here(hidden)
    hidden_grad = (
        here(residual_grad)
        + scale_first * first_here * here(gain_first)
        - hidden_here * (scale_first * scale_first * scale_first) * first_mean
    ).reshape(seq_count, local_len, col_width)
    gain_first_part = jnp.sum(first_here * hidden_here * scale_first, axis=0)
    gains = jnp.concatenate(
        [
            gain_first_part,
            gain_second_part,
            query_gain_part,
            jnp.zeros((64,), f32),
            latent_gain_part,
            jnp.zeros((1024 - 768 - kv_cols,), f32),
        ]
    ).reshape(8, 128)
    gains_all = last(gains).reshape(COLS, 1024)
    expert_in_grad = expert_in_sum.reshape(EXP_DEV, -1, expert_units // 128, 2, 128).astype(f32)
    expert_gate_grad, expert_up_grad = (
        expert_in_grad[:, :, :, half].reshape(EXP_DEV, -1, expert_units) for half in range(2)
    )
    return (
        block_out,
        hidden_grad,
        gains_all[:, :col_width].reshape(D),
        down_sum[:, :query_cols],
        gains_all[:, 512 : 512 + query_cols].reshape(QL),
        query_up_sum,
        down_sum[:, query_cols:latent_width],
        gains_all[:, 768 : 768 + kv_cols].reshape(KL + DR)[:KL],
        latent_up_sum,
        attention_out_sum,
        gains_all[:, col_width : 2 * col_width].reshape(D),
        down_sum[:, latent_width:],
        expert_gate_grad,
        expert_up_grad,
        expert_down_sum.astype(f32),
        shared_gate_sum,
        shared_up_sum,
        shared_down_sum,
    )


def solution(mesh):
    in_specs = (
        P(None, "row", "col"),
        P(),
        P("row", "col"),
        P(),
        P("row", "col"),
        P("row", "col"),
        P(),
        P("row", "col"),
        P("col", "row"),
        P(),
        P("row", None),
        P("col", "row", None),
        P("col", "row", None),
        P("col", "row", None),
        P("row", "col"),
        P("row", "col"),
        P("col", "row"),
        P(),
        P(None, "row", None),
        P(None, "row", "col"),
    )
    out_specs = (
        P(None, "row", "col"),
        P(None, "row", "col"),
        P(),
        P("row", "col"),
        P(),
        P("row", "col"),
        P("row", "col"),
        P(),
        P("row", "col"),
        P("col", "row"),
        P(),
        P("row", None),
        P("col", "row", None),
        P("col", "row", None),
        P("col", "row", None),
        P("row", "col"),
        P("row", "col"),
        P("col", "row"),
    )
    return jax.shard_map(local, mesh=mesh, in_specs=in_specs, out_specs=out_specs, check_vma=False)
```

```python
import functools
import math

import jax
import jax.numpy as jnp
from jax import lax
from jax.experimental import pallas as pl
from jax.experimental.pallas import tpu as pltpu
from jax.sharding import PartitionSpec as P

D = 2048
H = 16
DN = 128
DR = 64
DV = 128
QL = 1536
KL = 512
EXP_DEV = 2
TOPK = 6
ROWS = 16
COLS = 8
TS = 256
CUT = 208
COL_CUT = 400
LATENT_CUT = 5

eps = 1e-06
route_scale = 2.446
rope_base = 50000.0
score_scale = 1.0 / math.sqrt(DN + DR)
score_bits = score_scale * math.log2(math.e)

bf16 = jnp.bfloat16
f32 = jnp.float32
ANY = pl.ANY
VM = pltpu.VMEM


def shape_of(shape, dtype):
    return jax.ShapeDtypeStruct(shape, dtype)

MESH = pl.DeviceIdType.MESH
RING = 4
VMEM_BYTES = 56 * 2**20


class Place:
    def __init__(self, axis):
        self.axis = axis
        self.index = lax.axis_index(axis)
        self.cores = 2 if axis == "row" else 1
        self.core = lax.rem(self.index, self.cores)
        self.ring = lax.rem(lax.div(self.index, self.cores), RING)
        self.pair = lax.div(self.index, self.cores * RING)

    def at(self, pair, ring, core=None):
        core = self.core if core is None else core
        return (pair * RING + ring) * self.cores + core

    def turn(self, step):
        return lax.rem(self.ring + step + RING, RING)

    def peers(self):
        found = [self.at(self.pair, self.turn(step)) for step in (1, 2, 3)]
        found.append(self.at(1 - self.pair, self.ring))
        if self.cores == 2:
            found.append(self.at(self.pair, self.ring, 1 - self.core))
        return found


class Net:
    def __init__(self, send_sems, recv_sems):
        self.send_sems, self.recv_sems = send_sems, recv_sems
        self.count = 0
        self.sent = []
        self.own = []

    def send(self, source, target, axis, index):
        number = self.count
        self.count += 1
        copy = pltpu.make_async_remote_copy(
            source,
            target,
            self.send_sems.at[number],
            self.recv_sems.at[number],
            device_id={axis: index},
            device_id_type=MESH,
        )
        copy.start()
        self.sent.append(copy)
        return number

    def receive(self, number, target, axis, index):
        pltpu.make_async_remote_copy(
            target,
            target,
            self.send_sems.at[number],
            self.recv_sems.at[number],
            device_id={axis: index},
            device_id_type=MESH,
        ).wait_recv()

    def local(self, source, target):
        number = self.count
        self.count += 1
        copy = pltpu.make_async_copy(source, target, self.send_sems.at[number])
        copy.start()
        self.own.append(copy)

    def settle(self):
        for copy in self.own:
            copy.wait()
        self.own = []

    def finish(self):
        for copy in self.sent:
            copy.wait_send()
        self.settle()


def greet(*places, everyone=False):
    barrier = pltpu.get_barrier_semaphore()
    count = 0
    for place in places:
        members = lax.axis_size(place.axis)
        all_peers = [lax.rem(place.index + step, members) for step in range(1, members)]
        for peer in all_peers if everyone else place.peers():
            pl.semaphore_signal(
                barrier, inc=1, device_id={place.axis: peer}, device_id_type=MESH
            )
            count += 1
    pl.semaphore_wait(barrier, count)


class Gather:
    def __init__(self, net, place, source, slot, rows, cut, relay=False, cross=None):
        self.net, self.place, self.source, self.slot = net, place, source, slot
        self.rows, self.cut, self.relay = rows, cut, relay
        self.first, self.second = (0, cut), (cut, rows - cut)
        self.crossed = []
        if place.cores == 2:
            partner = place.at(place.pair, place.ring, 1 - place.core)

            def other(pair, ring, low, count):
                return slot(place.at(pair, ring, 1 - place.core), low, count)

            cross = (place.axis, partner, other)
        self.cross = cross

    def _send(self, owner, part, peer, own=False):
        piece = self.slot(owner, *part)
        start = self.source.at[pl.ds(*part)] if own else piece
        return self.net.send(start, piece, self.place.axis, peer)

    def _receive(self, number, pair, ring, part, peer):
        place = self.place
        self.net.receive(number, self.slot(place.at(pair, ring), *part), place.axis, peer)

    def _cross(self, pair, ring, part, own=False):
        if self.cross is None:
            return
        piece = self.slot(self.place.at(pair, ring), *part)
        start = self.source.at[pl.ds(*part)] if own else piece
        number = self.net.send(start, piece, self.cross[0], self.cross[1])
        self.crossed.append((number, pair, ring, part))

    def _halves(self, part):
        low, count = part
        unit = 16 if count % 16 == 0 else 1
        half = max(count // 2 // unit, 1) * unit
        return (low, half), (low + half, count - half)

    def _relays(self, part):
        return self.relay and part[1] >= (32 if part[1] % 16 == 0 else 2)

    def _round(self, pair, part, own=False):
        place = self.place
        owner = place.at(pair, place.ring)
        steps = (1, 3) if self._relays(part) else (1, 3, 2)
        return {
            step: self._send(owner, part, place.at(place.pair, place.turn(step)), own)
            for step in steps
        }

    def _arrive(self, numbers, pair, part, then):
        place = self.place
        passed = {}
        for step in (1, 3):
            ring = place.turn(-step)
            self._receive(numbers[step], pair, ring, part, place.at(place.pair, ring))
            if self._relays(part):
                half = self._halves(part)[step // 2]
                passed[step] = self._send(
                    place.at(pair, ring), half, place.at(place.pair, place.turn(step))
                )
            then(pair, ring, part)
        far = place.turn(2)
        if self._relays(part):
            for step in (1, 3):
                half = self._halves(part)[step // 2]
                self._receive(
                    passed[step], pair, far, half, place.at(place.pair, place.turn(-step))
                )
        else:
            self._receive(numbers[2], pair, far, part, place.at(place.pair, far))
        then(pair, far, part)

    def start_first(self):
        place = self.place
        if self.cut:
            other = place.at(1 - place.pair, place.ring)
            self.across = self._send(place.index, self.first, other, True)
            self.near = self._round(place.pair, self.first, True)

    def start_second(self):
        place = self.place
        if self.second[1]:
            self.round = self._round(place.pair, self.second, True)
            other = place.at(1 - place.pair, place.ring)
            self.over = [(place.ring, self._send(place.index, self.second, other, True))]
        self._cross(place.pair, place.ring, (0, self.rows), True)
        self.net.local(self.source, self.slot(place.index, 0, self.rows))

    def start(self):
        self.start_first()
        self.start_second()

    def forward_first(self):
        place = self.place
        if self.cut:
            other = place.at(1 - place.pair, place.ring)
            self._receive(self.across, 1 - place.pair, place.ring, self.first, other)
            self.far = self._round(1 - place.pair, self.first)
            self._cross(1 - place.pair, place.ring, self.first)

    def forward_second(self):
        place = self.place
        other = place.at(1 - place.pair, place.ring)

        def then(pair, ring, part):
            self.over.append((ring, self._send(place.at(pair, ring), part, other)))
            self._cross(pair, ring, part)

        if self.second[1]:
            self._arrive(self.round, place.pair, self.second, then)

    def land(self):
        place = self.place
        if self.cut:
            self._arrive(self.near, place.pair, self.first, self._cross)
            self._arrive(self.far, 1 - place.pair, self.first, self._cross)
        if self.second[1]:
            other = place.at(1 - place.pair, place.ring)
            for ring, number in self.over:
                self._receive(number, 1 - place.pair, ring, self.second, other)
                self._cross(1 - place.pair, ring, self.second)

    def end(self):
        for number, pair, ring, part in self.crossed:
            axis, partner, other = self.cross
            self.net.receive(number, other(pair, ring, *part), axis, partner)


class Direct:
    def __init__(self, net, place, source, ref, count):
        self.net, self.place, self.source, self.ref, self.count = net, place, source, ref, count

    def start(self):
        place = self.place
        self.numbers = [
            self.net.send(
                self.source,
                self.ref.at[place.index],
                place.axis,
                lax.rem(place.index + step, self.count),
            )
            for step in range(1, self.count)
        ]
        self.net.local(self.source, self.ref.at[place.index])

    def land(self):
        place = self.place
        for step, number in zip(range(1, self.count), self.numbers):
            owner = lax.rem(place.index + self.count - step, self.count)
            self.net.receive(number, self.ref.at[owner], place.axis, owner)


def run_gathers(*gathers):
    for gather in gathers:
        gather.start()
    for gather in gathers:
        gather.forward_first()
    for gather in gathers:
        gather.forward_second()
    for gather in gathers:
        gather.land()
    for gather in gathers:
        gather.end()


def row_slots(ref, rows):
    return lambda owner, low, count: ref.at[
        pl.ds(pl.multiple_of(owner * rows + low, 16), count)
    ]


def lead_slots(ref):
    return lambda owner, low, count: ref.at[owner, pl.ds(low, count)]


def lane_slots(ref, width):
    return lambda owner, low, count: ref.at[
        pl.ds(low, count), pl.ds(pl.multiple_of(owner * width, 128), width)
    ]


class Scatter:
    def __init__(self, net, place, block, rows, cut, scratch, keep):
        self.net, self.place, self.block, self.rows, self.cut = net, place, block, rows, cut
        self.scratch, self.keep = scratch, keep
        self.first, self.second = (0, cut), (cut, rows - cut)

    @staticmethod
    def scratch_of(rows, cut, width, dtype=jnp.bfloat16):
        shapes = []
        if cut:
            shapes += [(3, 2, cut, width), (2, cut, width)]
        if rows - cut:
            shapes += [(4, rows - cut, width), (4, rows - cut, width), (3, rows - cut, width)]
        return [pltpu.VMEM(shape, dtype) for shape in shapes]

    def _refs(self):
        refs = list(self.scratch)
        first = refs[:2] if self.cut else None
        second = refs[-3:] if self.second[1] else None
        return first, second

    def _owner(self, pair, ring):
        return self.place.at(pair, ring)

    def start(self):
        place, net = self.place, self.net
        first, second = self._refs()
        if first:
            self.round = [
                [
                    net.send(
                        self.block(self._owner(pair, place.turn(step)), *self.first),
                        first[0].at[step - 1, pair],
                        place.axis,
                        place.at(place.pair, place.turn(step)),
                    )
                    for pair in (0, 1)
                ]
                for step in (1, 2, 3)
            ]
        if second:
            self.across = [
                net.send(
                    self.block(self._owner(1 - place.pair, ring), *self.second),
                    second[0].at[ring],
                    place.axis,
                    place.at(1 - place.pair, place.ring),
                )
                for ring in range(RING)
            ]

    def forward_second(self):
        place, net = self.place, self.net
        first, second = self._refs()
        if not second:
            return
        other = place.at(1 - place.pair, place.ring)
        for ring in range(RING):
            net.receive(self.across[ring], second[0].at[ring], place.axis, other)
        for ring in range(RING):
            total = (
                self.block(self._owner(place.pair, ring), *self.second)[...].astype(jnp.float32)
                + second[0][ring].astype(jnp.float32)
            )
            second[1][ring] = total.astype(second[1].dtype)
        self.last = [
            net.send(
                second[1].at[place.turn(step)],
                second[2].at[step - 1],
                place.axis,
                place.at(place.pair, place.turn(step)),
            )
            for step in (1, 2, 3)
        ]

    def forward_first(self):
        place, net = self.place, self.net
        first, second = self._refs()
        if not first:
            return
        for step in (1, 3, 2):
            owner = place.at(place.pair, place.turn(-step))
            for pair in (0, 1):
                net.receive(self.round[step - 1][pair], first[0].at[step - 1, pair], place.axis, owner)
        other = 1 - place.pair
        total = self.block(self._owner(other, place.ring), *self.first)[...].astype(jnp.float32)
        for step in range(3):
            total = total + first[0][step, other].astype(jnp.float32)
        first[1][0] = total.astype(first[1].dtype)
        self.over = net.send(
            first[1].at[0], first[1].at[1], place.axis, place.at(other, place.ring)
        )

    def end_first(self):
        place, net = self.place, self.net
        first, second = self._refs()
        if not first:
            return
        total = self.block(self._owner(place.pair, place.ring), *self.first)[...].astype(jnp.float32)
        for step in range(3):
            total = total + first[0][step, place.pair].astype(jnp.float32)
        other = place.at(1 - place.pair, place.ring)
        net.receive(self.over, first[1].at[1], place.axis, other)
        self.keep(self.first, total + first[1][1].astype(jnp.float32))

    def end_second(self):
        place, net = self.place, self.net
        first, second = self._refs()
        if not second:
            return
        total = (
            self.block(self._owner(place.pair, place.ring), *self.second)[...].astype(jnp.float32)
            + second[0][place.ring].astype(jnp.float32)
        )
        for step in (1, 3, 2):
            owner = place.at(place.pair, place.turn(-step))
            net.receive(self.last[step - 1], second[2].at[step - 1], place.axis, owner)
            total = total + second[2][step - 1].astype(jnp.float32)
        self.keep(self.second, total)


def comm_call(body, name, collective_id, out_shapes, in_spaces, out_spaces, copies, scratch=(), args=()):
    return pl.pallas_call(
        body,
        name=name,
        out_shape=out_shapes,
        in_specs=[pl.BlockSpec(memory_space=space) for space in in_spaces],
        out_specs=tuple(pl.BlockSpec(memory_space=space) for space in out_spaces),
        scratch_shapes=[
            pltpu.SemaphoreType.DMA((copies,)),
            pltpu.SemaphoreType.DMA((copies,)),
            *scratch,
        ],
        compiler_params=pltpu.CompilerParams(
            collective_id=collective_id, has_side_effects=True, vmem_limit_bytes=VMEM_BYTES
        ),
    )(*args)


def front_body(hidden, grad, w1, qu, lu, ao, sg, su, sd, *rest):
    hidden_all, grad_all, w1_all, qu_all, lu_all, ao_all, sg_all, su_all, sd_all, ss, rs = rest
    row, col = Place("row"), Place("col")
    greet(row, col)
    net = Net(ss, rs)
    run_gathers(
        Gather(net, col, hidden, lane_slots(hidden_all, D // COLS), 2 * TS, 2 * TS, True),
        Gather(net, row, w1, row_slots(w1_all, w1.shape[0]), w1.shape[0], w1.shape[0]),
        Gather(net, row, qu, row_slots(qu_all, qu.shape[0]), qu.shape[0], qu.shape[0]),
        Gather(net, row, lu, row_slots(lu_all, lu.shape[0]), lu.shape[0], 0),
        Gather(net, row, ao, lane_slots(ao_all, ao.shape[1]), ao.shape[0], 0),
        Gather(net, row, sg, row_slots(sg_all, sg.shape[0]), sg.shape[0], sg.shape[0]),
        Gather(net, row, su, row_slots(su_all, su.shape[0]), su.shape[0], 0),
        Gather(net, row, sd, lane_slots(sd_all, sd.shape[1]), sd.shape[0], 0),
        Gather(net, col, grad, lane_slots(grad_all, D // COLS), 2 * TS, 2 * TS, True),
    )
    net.finish()


def stacked(term):
    return shape_of((ROWS * term.shape[0], term.shape[1]), term.dtype)


def side_by_side(term):
    return shape_of((term.shape[0], ROWS * term.shape[1]), term.dtype)


def front(hidden, grad, w1, qu, lu, ao, sg, su, sd):
    return comm_call(
        front_body,
        "gather_front",
        1,
        (
            shape_of((2 * TS, D), bf16),
            shape_of((2 * TS, D), bf16),
            stacked(w1),
            stacked(qu),
            stacked(lu),
            side_by_side(ao),
            stacked(sg),
            stacked(su),
            side_by_side(sd),
        ),
        [ANY] * 9,
        [ANY] * 9,
        192,
        args=(hidden, grad, w1, qu, lu, ao, sg, su, sd),
    )


def latent_body(query, latent, query_all, rows_all, latent_all, ss, rs):
    row, col = Place("row"), Place("col")
    greet(row, col)
    net = Net(ss, rs)
    queries = Gather(net, col, query, row_slots(query_all, query.shape[0]), query.shape[0], 96)
    rows = Gather(net, row, latent, lead_slots(rows_all), latent.shape[0], 48)
    half = ROWS // 2
    base = row.core * half
    partner = row.at(row.pair, row.ring, 1 - row.core)

    def slot(owner, low, count):
        return latent_all.at[owner, pl.ds(base + low, count)]

    def other(pair, ring, low, count):
        return latent_all.at[col.at(pair, ring), pl.ds(half - base + low, count)]

    every = Gather(
        net, col, rows_all.at[pl.ds(base, half)], slot, half, LATENT_CUT, True, ("row", partner, other)
    )
    rows.start()
    queries.start()
    rows.forward_first()
    rows.forward_second()
    queries.forward_first()
    rows.land()
    rows.end()
    net.settle()
    every.start()
    queries.forward_second()
    every.forward_first()
    every.forward_second()
    queries.land()
    every.land()
    every.end()
    net.finish()


def latents(query, latent):
    return comm_call(
        latent_body,
        "gather_latents",
        2,
        (
            shape_of((COLS * query.shape[0], query.shape[1]), bf16),
            shape_of((ROWS, *latent.shape), bf16),
            shape_of((COLS, ROWS, *latent.shape), bf16),
        ),
        [ANY] * 2,
        [ANY] * 3,
        128,
        args=(query, latent),
    )


def expand_body(latent, weight, gain, cos, sin, out):
    @pl.when(pl.program_id(0) <= lax.axis_index("row") + 1)
    def _():
        features = latent.shape[0] * latent.shape[2]
        values = latent[:, 0].reshape(features, latent.shape[3]).astype(f32)
        live = features - latent.shape[2] + 8
        square = jnp.sum(values[:live] * values[:live], axis=0, keepdims=True)
        scaled = (values * lax.rsqrt(square / KL + eps) * gain[...]).astype(bf16)
        found = jnp.dot(weight[...], scaled, preferred_element_type=f32).astype(bf16)
        turn_cos = jnp.concatenate([cos[...], cos[...]], axis=1)
        turn_sin = jnp.concatenate([sin[...], sin[...]], axis=1)
        first, second = values[live : live + 32], values[live + 32 : live + 64]
        rope = jnp.concatenate(
            [first * turn_cos - second * turn_sin, second * turn_cos + first * turn_sin], axis=0
        ).astype(bf16)
        out[0, 0:128] = found[0:128]
        out[0, 128:192] = rope
        out[0, 192:256] = rope
        out[0, 256:384] = found[256:384]
        out[0, 384:512] = found[128:256]
        out[0, 512:640] = found[384:512]


def expand(latent, weight, gain, cos, sin):
    cols, rows, height, width = latent.shape
    return pl.pallas_call(
        expand_body,
        name="expand_keys",
        grid=(rows,),
        out_shape=shape_of((rows, 640, width), bf16),
        in_specs=[
            pl.BlockSpec((cols, 1, height, width), lambda r: (0, r, 0, 0)),
            pl.BlockSpec(weight.shape, lambda r: (0, 0)),
            pl.BlockSpec(gain.shape, lambda r: (0, 0)),
            pl.BlockSpec((32, TS), lambda r: (0, r)),
            pl.BlockSpec((32, TS), lambda r: (0, r)),
        ],
        out_specs=pl.BlockSpec((1, 640, width), lambda r: (r, 0, 0)),
        compiler_params=pltpu.CompilerParams(vmem_limit_bytes=VMEM_BYTES),
        cost_estimate=pl.CostEstimate(
            flops=6 * 10**9, bytes_accessed=22 * 10**6, transcendentals=8192
        ),
    )(latent, weight, gain, cos, sin)


def sum_body(cut, kinds, term, *rest):
    count = len(kinds)
    extras, total_all, extras_all = rest[:count], rest[count], rest[count + 1 : 2 * count + 1]
    ss, rs, *scratch = rest[2 * count + 1 :]
    places = {"row": Place("row"), "col": Place("col")}
    greet(*(places[axis] for axis in sorted({"col", *(axis for axis, _ in kinds)})))
    net = Net(ss, rs)
    width = D // COLS
    mine = scratch[-1]

    def keep(part, value):
        mine[pl.ds(*part)] = value.astype(mine.dtype)

    col = places["col"]
    scatter = Scatter(net, col, lane_slots(term, width), 2 * TS, cut, scratch[:-1], keep)
    gather = Gather(net, col, mine, lane_slots(total_all, width), 2 * TS, cut, True)
    beside = [
        Gather(net, places[axis], extra, lead_slots(extra_all), extra.shape[0], extra_cut, True)
        for (axis, extra_cut), extra, extra_all in zip(kinds, extras, extras_all)
    ]
    scatter.start()
    for extra in beside:
        extra.start()
    for extra in beside:
        extra.forward_first()
    scatter.forward_second()
    scatter.forward_first()
    for extra in beside:
        extra.forward_second()
    scatter.end_first()
    gather.start_first()
    scatter.end_second()
    gather.start_second()
    gather.forward_first()
    gather.forward_second()
    for extra in beside:
        extra.land()
    gather.land()
    for extra in beside:
        extra.end()
    gather.end()
    net.finish()


def sum_over_col(name, collective_id, term, cut, kinds, *extras):
    counts = {"row": ROWS, "col": COLS}
    return comm_call(
        functools.partial(sum_body, cut, kinds),
        name,
        collective_id,
        (
            shape_of((2 * TS, D), bf16),
            *(
                shape_of((counts[axis], *extra.shape), extra.dtype)
                for (axis, _), extra in zip(kinds, extras)
            ),
        ),
        [VM] + [ANY] * len(extras),
        [ANY] * (1 + len(extras)),
        128,
        [*Scatter.scratch_of(2 * TS, cut, D // COLS), pltpu.VMEM((2 * TS, D // COLS), bf16)],
        (term, *extras),
    )


def back_body(grad, stats, branch, grad_all, stats_all, branch_sum, ss, rs, *scratch):
    row, col = Place("row"), Place("col")
    greet(row, col)
    net = Net(ss, rs)

    def keep(part, value):
        branch_sum[pl.ds(*part)] = value

    scatter = Scatter(net, col, lane_slots(branch, D // COLS), 2 * TS, COL_CUT, scratch, keep)
    gathers = (
        Gather(net, row, grad, lead_slots(grad_all), 2 * TS, CUT, True),
        Gather(net, row, stats, lead_slots(stats_all), stats.shape[0], stats.shape[0]),
    )
    for gather in gathers:
        gather.start()
    scatter.start()
    for gather in gathers:
        gather.forward_first()
    for gather in gathers:
        gather.forward_second()
    scatter.forward_second()
    scatter.forward_first()
    for gather in gathers:
        gather.land()
    scatter.end_first()
    scatter.end_second()
    for gather in gathers:
        gather.end()
    net.finish()


def back(grad, stats, branch):
    return comm_call(
        back_body,
        "gather_back",
        6,
        (
            shape_of((ROWS, *grad.shape), bf16),
            shape_of((ROWS, *stats.shape), f32),
            shape_of((2 * TS, D // COLS), f32),
        ),
        [ANY, ANY, VM],
        [ANY, ANY, VM],
        96,
        Scatter.scratch_of(2 * TS, COL_CUT, D // COLS),
        (grad, stats, branch),
    )


class RowScatter:
    def __init__(self, net, place, term, cut, scratch, keep):
        self.net, self.place, self.term = net, place, term
        self.arrived, self.summed = scratch[:2]
        rows = term.shape[3]

        def block(owner, low, count):
            return self.summed.at[lax.div(owner, 2), pl.ds(low, count)]

        self.inner = Scatter(net, place, block, rows, cut, scratch[2:], keep)

    @staticmethod
    def scratch_of(rows, cut, width):
        return [
            pltpu.VMEM((2, RING, rows, width), bf16),
            pltpu.VMEM((2 * RING, rows, width), bf16),
            *Scatter.scratch_of(rows, cut, width),
        ]

    def start(self):
        place = self.place
        self.partner = place.at(place.pair, place.ring, 1 - place.core)
        self.number = self.net.send(
            self.term.at[:, :, 1 - place.core], self.arrived, place.axis, self.partner
        )

    def middle(self):
        place = self.place
        self.net.receive(self.number, self.arrived, place.axis, self.partner)
        for pair in range(2):
            for ring in range(RING):
                self.summed[pair * RING + ring] = (
                    self.term[pair, ring, place.core].astype(f32)
                    + self.arrived[pair, ring].astype(f32)
                ).astype(bf16)
        self.inner.start()


def run_scatters(scatters):
    for scatter in scatters:
        scatter.forward_second()
    for scatter in scatters:
        scatter.forward_first()
    for scatter in scatters:
        scatter.end_first()
    for scatter in scatters:
        scatter.end_second()


def keep_in(ref):
    def keep(part, value):
        ref[pl.ds(*part)] = value

    return keep


def block_slots(ref):
    return lambda owner, low, count: ref.at[owner, pl.ds(low, count)]


def rows_sum(net, place, terms, cuts, totals, scratch):
    parts = []
    for term, cut, total in zip(terms, cuts, totals):
        count = len(RowScatter.scratch_of(term.shape[3], cut, term.shape[4]))
        parts.append(RowScatter(net, place, term, cut, scratch[:count], keep_in(total)))
        scratch = scratch[count:]
    return parts


def rows_scratch(terms, cuts):
    found = []
    for term, cut in zip(terms, cuts):
        found += RowScatter.scratch_of(term.shape[3], cut, term.shape[4])
    return found


def col_and_row_body(col_cuts, row_cuts, slots, *rest):
    cols, rows = len(col_cuts), len(row_cuts)
    col_terms, rest = rest[:cols], rest[cols:]
    extra, rest = rest[0], rest[1:]
    row_terms, rest = rest[:rows], rest[rows:]
    col_totals, rest = rest[:cols], rest[cols:]
    extra_all, rest = rest[0], rest[1:]
    row_totals, rest = rest[:rows], rest[rows:]
    ss, rs, *scratch = rest
    row, col = Place("row"), Place("col")
    greet(row, col)
    net = Net(ss, rs)
    scatters = []
    for term, cut, total in zip(col_terms, col_cuts, col_totals):
        height, width = total.shape
        block = lane_slots(term, width) if slots == "lane" else block_slots(term)
        count = len(Scatter.scratch_of(height, cut, width))
        scatters.append(Scatter(net, col, block, height, cut, scratch[:count], keep_in(total)))
        scratch = scratch[count:]
    beside = Gather(net, col, extra, lead_slots(extra_all), extra.shape[0], extra.shape[0])
    parts = rows_sum(net, row, row_terms, row_cuts, row_totals, scratch)
    for part in parts:
        part.start()
    for scatter in scatters:
        scatter.start()
    beside.start()
    for part in parts:
        part.middle()
    beside.forward_first()
    run_scatters(scatters + [part.inner for part in parts])
    beside.land()
    net.finish()


def col_and_row(name, collective_id, slots, col_terms, col_shapes, col_cuts, extra, row_terms, row_cuts):
    scratch = []
    for shape, cut in zip(col_shapes, col_cuts):
        scratch += Scatter.scratch_of(shape[0], cut, shape[1])
    found = comm_call(
        functools.partial(col_and_row_body, tuple(col_cuts), tuple(row_cuts), slots),
        name,
        collective_id,
        (
            *(shape_of(shape, f32) for shape in col_shapes),
            shape_of((COLS, *extra.shape), f32),
            *(shape_of(term.shape[3:], f32) for term in row_terms),
        ),
        [*([VM] * len(col_terms)), ANY, *([VM] * len(row_terms))],
        [*([VM] * len(col_terms)), ANY, *([VM] * len(row_terms))],
        128,
        [*scratch, *rows_scratch(row_terms, row_cuts)],
        (*col_terms, extra, *row_terms),
    )
    count = len(col_terms)
    return found[:count], found[count], found[count + 1 :]


def last_body(gains, gains_all, ss, rs, gains_rows, gains_mine):
    row, col = Place("row"), Place("col")
    greet(row, col, everyone=True)
    net = Net(ss, rs)
    beside = Direct(net, row, gains, gains_rows, ROWS)
    beside.start()
    beside.land()
    net.settle()
    total = gains_rows[0]
    for index in range(1, ROWS):
        total = total + gains_rows[index]
    gains_mine[...] = total
    spread = Direct(net, col, gains_mine, gains_all, COLS)
    spread.start()
    spread.land()
    net.finish()


def last(gains):
    return comm_call(
        last_body,
        "sum_last",
        9,
        (shape_of((COLS, 8, 128), f32),),
        [VM],
        [VM],
        64,
        [pltpu.VMEM((ROWS, 8, 128), f32), pltpu.VMEM((8, 128), f32)],
        (gains,),
    )[0]


def contract(left, right):
    return lax.dot_general(left, right, (((1,), (1,)), ((), ())), preferred_element_type=f32)


def masked_queries(pack):
    lanes = lax.broadcasted_iota(jnp.int32, (pack.shape[0], 256), 1)
    zero = jnp.zeros((), pack.dtype)
    return (
        jnp.where(lanes < 192, pack[:, :256], zero),
        jnp.where(lanes >= 64, pack[:, 128:], zero),
    )


def attend_body(lens, query, kvt, out, lse, lse_rows, scores):
    seq = pl.program_id(0)
    mine = lax.axis_index("row")
    live = lens[seq]
    steps = lax.div(jnp.minimum(mine + 1, lax.div(live + TS - 1, TS)) + 1, 2)
    places = mine * TS + lax.broadcasted_iota(jnp.int32, (TS, 1), 0)
    limit = jnp.minimum(places + 1, live)
    offsets = lax.broadcasted_iota(jnp.int32, (TS, TS), 1)
    queries = masked_queries(query[...])

    def first(step, tops):
        tops = list(tops)
        for half in range(2):
            index = 2 * step + half
            valid = offsets < limit - index * TS
            for head in range(2):
                key = kvt[index, head * 128 : head * 128 + 256]
                value = jnp.dot(queries[head], key, preferred_element_type=f32)
                value = jnp.where(valid, value, -1e30)
                scores[head, index] = value
                tops[head] = jnp.maximum(
                    tops[head], jnp.maximum(value[:, :128], value[:, 128:])
                )
        return tuple(tops)

    tops = lax.fori_loop(0, steps, first, (jnp.full((TS, 128), -1e30, f32),) * 2)
    tops = [jnp.max(top, axis=1, keepdims=True) * score_bits for top in tops]

    def second(step, carried):
        found = []
        for head in range(2):
            sums, total = carried[head]
            for half in range(2):
                index = 2 * step + half
                weight = jnp.exp2(scores[head, index] * score_bits - tops[head])
                sums = sums + (weight[:, :128] + weight[:, 128:])
                value = kvt[index, 384 + head * 128 : 512 + head * 128]
                total = total + contract(weight.astype(bf16), value)
            found.append((sums, total))
        return tuple(found)

    zero = jnp.zeros((TS, 128), f32)
    carried = lax.fori_loop(0, steps, second, ((zero, zero),) * 2)
    for head in range(2):
        sums, total = carried[head]
        whole = jnp.sum(sums, axis=1, keepdims=True)
        lanes = pl.ds(head * 128, 128)
        out[:, lanes] = total / whole
        value = jnp.broadcast_to(tops[head] + jnp.log2(whole), (TS, 128))
        lse[:, lanes] = value
        lse_rows[head : head + 1] = value.T[:1]


def attend(lens, query, kvt):
    return pl.pallas_call(
        attend_body,
        name="attend",
        grid=(2,),
        out_shape=(
            shape_of((2 * TS, 256), f32),
            shape_of((2 * TS, 256), f32),
            shape_of((8, 2 * TS), f32),
        ),
        in_specs=[
            pl.BlockSpec(memory_space=pltpu.SMEM),
            pl.BlockSpec((TS, 384), lambda s: (s, 0)),
            pl.BlockSpec((ROWS, 640, TS), lambda s: (0, 0, s)),
        ],
        out_specs=(
            pl.BlockSpec((TS, 256), lambda s: (s, 0)),
            pl.BlockSpec((TS, 256), lambda s: (s, 0)),
            pl.BlockSpec((8, TS), lambda s: (0, s)),
        ),
        scratch_shapes=[pltpu.VMEM((2, ROWS, TS, TS), f32)],
        compiler_params=pltpu.CompilerParams(vmem_limit_bytes=VMEM_BYTES),
        cost_estimate=pl.CostEstimate(
            flops=6 * 10**9, bytes_accessed=12 * 10**6, transcendentals=4 * 10**6
        ),
    )(lens, query, kvt)


def attend_back_body(lens, query, kvt, grad, lse, delta, near, query_all, grad_all, stats, dq, dk, dv):
    seq = pl.program_id(0)
    mine = lax.axis_index("row")
    live = lens[seq]
    width = 2 * TS
    steps = lax.div(jnp.minimum(mine + 1, lax.div(live + TS - 1, TS)) + 1, 2)
    places = mine * TS + lax.broadcasted_iota(jnp.int32, (TS, 1), 0)
    limit = jnp.minimum(places + 1, live)
    narrow = lax.broadcasted_iota(jnp.int32, (TS, TS), 1)
    wide = lax.broadcasted_iota(jnp.int32, (TS, width), 1)
    queries = masked_queries(query[...])

    def queries_step(step, carried):
        totals = list(carried)
        for half in range(2):
            index = 2 * step + half
            valid = narrow < limit - index * TS
            for head in range(2):
                key = kvt[index, head * 128 : head * 128 + 256]
                value = kvt[index, 384 + head * 128 : 512 + head * 128]
                lanes = pl.ds(head * 128, 128)
                score = jnp.dot(queries[head], key, preferred_element_type=f32)
                score = score * score_bits - lse[:, lanes][:, :1]
                weight = jnp.exp2(jnp.where(valid, score, -1e30))
                slope = jnp.dot(grad[:, lanes], value, preferred_element_type=f32)
                low = (weight * (slope - delta[:, lanes][:, :1])).astype(bf16)
                totals[head] = totals[head] + contract(low, key)
        return tuple(totals)

    totals = lax.fori_loop(0, steps, queries_step, (jnp.zeros((TS, 256), f32),) * 2)
    edge = lax.broadcasted_iota(jnp.int32, (TS, 128), 1) < DR
    dq[:, 0:128] = totals[0][:, :128] * score_scale
    dq[:, 128:256] = jnp.where(edge, totals[0][:, 128:], totals[1][:, :128]) * score_scale
    dq[:, 256:384] = totals[1][:, 128:] * score_scale

    bar = jnp.where(places < live, places, 2 * ROWS * TS)
    keys = masked_queries(near[:, :384])

    def keys_step(step, carried):
        valid = wide >= bar - step * width
        queries = query_all[pl.ds(2 * step, 2)].reshape(width, query_all.shape[2])
        grads = grad_all[pl.ds(2 * step, 2)].reshape(width, 256)
        numbers = stats[pl.ds(2 * step, 2)]
        numbers = jnp.concatenate([numbers[0], numbers[1]], axis=1)
        found = []
        for head in range(2):
            key_total, value_total = carried[head]
            asked = queries[:, head * 128 : head * 128 + 256]
            given = grads[:, head * 128 : head * 128 + 128]
            score = contract(keys[head], asked) * score_bits - numbers[head : head + 1]
            weight = jnp.exp2(jnp.where(valid, score, -1e30))
            value_total = value_total + jnp.dot(
                weight.astype(bf16), given, preferred_element_type=f32
            )
            value = near[:, 384 + head * 128 : 512 + head * 128]
            slope = contract(value, given) - numbers[2 + head : 3 + head]
            low = (weight * slope).astype(bf16)
            key_total = key_total + jnp.dot(low, asked, preferred_element_type=f32)
            found.append((key_total, value_total))
        return tuple(found)

    zero = (jnp.zeros((TS, 256), f32), jnp.zeros((TS, 128), f32))
    last_step = jnp.where(mine * TS < live, ROWS // 2, 0)
    totals = lax.fori_loop(lax.div(mine, 2), last_step, keys_step, (zero, zero))
    dk[:, 0:128] = totals[0][0][:, :128] * score_scale
    dk[:, 128:256] = jnp.where(edge, totals[0][0][:, 128:], totals[1][0][:, :128]) * score_scale
    dk[:, 256:384] = totals[1][0][:, 128:] * score_scale
    dv[:, 0:128] = totals[0][1]
    dv[:, 128:256] = totals[1][1]


def attend_back(lens, query, kvt, grad, lse, delta, near, query_all, grad_all, stats):
    def lanes(width):
        return pl.BlockSpec((TS, width), lambda s: (s, 0))

    return pl.pallas_call(
        attend_back_body,
        name="attend_back",
        grid=(2,),
        out_shape=(
            shape_of((2 * TS, 384), f32),
            shape_of((2 * TS, 384), f32),
            shape_of((2 * TS, 256), f32),
        ),
        in_specs=[
            pl.BlockSpec(memory_space=pltpu.SMEM),
            lanes(384),
            pl.BlockSpec((ROWS, 640, TS), lambda s: (0, 0, s)),
            lanes(256),
            lanes(256),
            lanes(256),
            lanes(640),
            pl.BlockSpec((ROWS, TS, query_all.shape[2]), lambda s: (0, s, 0)),
            pl.BlockSpec((ROWS, TS, 256), lambda s: (0, s, 0)),
            pl.BlockSpec((ROWS, 8, TS), lambda s: (0, 0, s)),
        ],
        out_specs=(lanes(384), lanes(384), lanes(256)),
        compiler_params=pltpu.CompilerParams(vmem_limit_bytes=VMEM_BYTES),
        cost_estimate=pl.CostEstimate(
            flops=12 * 10**9, bytes_accessed=24 * 10**6, transcendentals=8 * 10**6
        ),
    )(lens, query, kvt, grad, lse, delta, near, query_all, grad_all, stats)


def project_back_body(
    dq, dk, dv, cos, sin, query_up, latent_up, query_in, latent_in, query_raw, latent_raw,
    query_gain, latent_gain, query_up_grad, latent_up_grad, query_grad, latent_grad, numbers,
):
    lane = lax.broadcasted_iota(jnp.int32, (2 * TS, 128), 1)
    lower = lax.rem(lane, DR) < DR // 2

    def turn_back(tile):
        swapped = jnp.where(
            lower, pltpu.roll(tile, 128 - DR // 2, 1), pltpu.roll(tile, DR // 2, 1)
        )
        return tile * cos[...] - swapped * sin[...]

    queries = jnp.concatenate(
        [dq[:, :128], turn_back(dq[:, 128:256]), dq[:, 256:]], axis=1
    ).astype(bf16)
    middle = dk[:, 128:256]
    middle = middle + pltpu.roll(middle, DR, 1)
    rope = turn_back(middle)
    pairs = jnp.concatenate(
        [dk[:, :128], dv[:, :128], dk[:, 256:], dv[:, 128:]], axis=1
    ).astype(bf16)
    query_up_grad[...] = jnp.dot(query_in[...], queries, preferred_element_type=f32).astype(bf16)
    latent_up_grad[...] = jnp.dot(latent_in[...], pairs, preferred_element_type=f32).astype(bf16)
    back = contract(query_up[...], queries)
    query_grad[...] = back.astype(bf16)
    numbers[...] = jnp.zeros_like(numbers)
    numbers[0:1] = jnp.sum(back * query_gain[...] * query_raw[...].astype(f32), axis=0, keepdims=True)
    back = contract(latent_up[...], pairs)
    numbers[1:2] = jnp.sum(
        back * latent_gain[...] * latent_raw[...].astype(f32), axis=0, keepdims=True
    )
    latent_grad[:KL] = back.astype(bf16)
    latent_grad[KL:] = rope.T[:DR].astype(bf16)


def project_back(*terms):
    query_up, latent_up, query_in, latent_in = terms[5:9]
    return pl.pallas_call(
        project_back_body,
        name="project_back",
        out_shape=(
            shape_of(query_up.shape, bf16),
            shape_of(latent_up.shape, bf16),
            shape_of(query_in.shape, bf16),
            shape_of((KL + DR, 2 * TS), bf16),
            shape_of((8, 2 * TS), f32),
        ),
        in_specs=[pl.BlockSpec(memory_space=VM)] * len(terms),
        out_specs=(pl.BlockSpec(memory_space=VM),) * 5,
        compiler_params=pltpu.CompilerParams(vmem_limit_bytes=VMEM_BYTES),
        cost_estimate=pl.CostEstimate(
            flops=2 * 10**9, bytes_accessed=16 * 10**6, transcendentals=0
        ),
    )(*terms)


def silu_parts(gate_value):
    sigmoid_value = 1.0 / (1.0 + jnp.exp(-gate_value))
    return (gate_value * sigmoid_value, sigmoid_value * (1.0 + gate_value * (1.0 - sigmoid_value)))


def transposed(left, right):
    return lax.dot_general(left, right, (((0,), (0,)), ((), ())), preferred_element_type=f32)


def shared_body(normed, grad, gate, up, down, branch, back_grad, gate_grad, up_grad, down_grad):
    normed_value, grad_value = normed[...], grad[...]
    gate_value = jnp.dot(normed_value, gate[...], preferred_element_type=f32)
    up_value = jnp.dot(normed_value, up[...], preferred_element_type=f32)
    silu_value, slope = silu_parts(gate_value)
    act = (silu_value * up_value).astype(bf16)
    act_grad = contract(grad_value, down[...])
    gate_low = (act_grad * up_value * slope).astype(bf16)
    up_low = (act_grad * silu_value).astype(bf16)
    branch[...] = jnp.dot(act, down[...], preferred_element_type=f32)
    back_grad[...] = contract(gate_low, gate[...]) + contract(up_low, up[...])
    gate_grad[...] = transposed(normed_value, gate_low).astype(bf16)
    up_grad[...] = transposed(normed_value, up_low).astype(bf16)
    width = down_grad.shape[2]
    for index in range(ROWS):
        part = grad_value[:, index * width : (index + 1) * width]
        down_grad[index] = transposed(act, part).astype(bf16)


def shared_experts(normed, grad, gate, up, down):
    units = gate.shape[1]
    return pl.pallas_call(
        shared_body,
        name="shared_experts",
        out_shape=(
            shape_of((2 * TS, D), f32),
            shape_of((2 * TS, D), f32),
            shape_of((D, units), bf16),
            shape_of((D, units), bf16),
            shape_of((ROWS, units, D // ROWS), bf16),
        ),
        in_specs=[pl.BlockSpec(memory_space=VM)] * 5,
        out_specs=(pl.BlockSpec(memory_space=VM),) * 5,
        compiler_params=pltpu.CompilerParams(vmem_limit_bytes=VMEM_BYTES),
        cost_estimate=pl.CostEstimate(
            flops=8 * 10**9, bytes_accessed=24 * 10**6, transcendentals=10**6
        ),
    )(normed, grad, gate, up, down)


def experts_body(
    slots, gates, normed, grad, branch_in, back_in, w_in, w_down,
    branch, back_grad, gate_grad, w_in_grad, w_down_grad,
    dispatch, taken, taken_turned, given, routed, result, back_sum, branch_sum, back_total,
):
    expert, step = pl.program_id(0), pl.program_id(1)
    steps = pl.num_programs(1)
    capacity = dispatch.shape[0]
    units = w_down.shape[1]

    @pl.when(step == 0)
    def _():
        places = lax.broadcasted_iota(jnp.int32, dispatch.shape, 0)
        chosen = places == slots[pl.ds(expert, 1)]
        dispatch[...] = chosen.astype(bf16)
        weight = jnp.sum(jnp.where(chosen, gates[pl.ds(expert, 1)], 0.0), axis=1, keepdims=True)
        rows = jnp.dot(dispatch[...], normed[...], preferred_element_type=f32).astype(bf16)
        taken[...] = rows
        taken_turned[...] = rows.T
        grads = jnp.dot(dispatch[...], grad[...], preferred_element_type=f32)
        given[...] = grads.astype(bf16)
        routed[...] = (weight * grads).astype(bf16)
        result[...] = jnp.zeros_like(result)
        back_sum[...] = jnp.zeros_like(back_sum)

    weights = jnp.concatenate([w_in[0, 0], w_in[0, 1]], axis=1)
    hidden = jnp.dot(taken[...], weights, preferred_element_type=f32)
    gate_value, up_value = hidden[:, :units], hidden[:, units:]
    silu_value, slope = silu_parts(gate_value)
    act = (silu_value * up_value).astype(bf16)
    act_grad = contract(routed[...], w_down[0])
    low = jnp.concatenate(
        [
            (act_grad * up_value * slope).astype(bf16),
            (act_grad * silu_value).astype(bf16),
        ],
        axis=1,
    )
    result[...] += jnp.dot(act, w_down[0], preferred_element_type=f32)
    back_sum[...] += contract(low, weights)
    in_grad = jnp.dot(taken_turned[...], low, preferred_element_type=f32).astype(bf16)
    w_in_grad[0, 0] = in_grad[:, :units]
    w_in_grad[0, 1] = in_grad[:, units:]
    w_down_grad[...] = transposed(act, routed[...]).astype(bf16)

    @pl.when(step == steps - 1)
    def _():
        places = lax.broadcasted_iota(jnp.int32, dispatch.shape, 0)
        chosen = places == slots[pl.ds(expert, 1)]
        weight = jnp.sum(jnp.where(chosen, gates[pl.ds(expert, 1)], 0.0), axis=1, keepdims=True)
        number = jnp.sum(result[...] * given[...].astype(f32), axis=1, keepdims=True)
        gate_grad[pl.ds(expert, 1)] = jnp.sum(
            jnp.where(chosen, number, 0.0), axis=0, keepdims=True
        )
        outward = transposed(dispatch[...], (weight * result[...]).astype(bf16))
        inward = transposed(dispatch[...], back_sum[...].astype(bf16))

        @pl.when(expert == 0)
        def _():
            branch_sum[...] = branch_in[...] + outward
            back_total[...] = back_in[...] + inward

        @pl.when(expert == EXP_DEV - 1)
        def _():
            branch[...] = (branch_sum[...] + outward).astype(bf16)
            back_grad[...] = (back_total[...] + inward).astype(bf16)


def experts(capacity, slots, gates, normed, grad, branch_in, back_in, w_in, w_down):
    units = 128
    steps = w_down.shape[1] // units
    whole = pl.BlockSpec(memory_space=VM)
    in_block = pl.BlockSpec((1, 2, D, units), lambda e, k: (e, 0, 0, k))
    down_out = pl.BlockSpec((units, D), lambda e, k: (k, e))
    down_block = pl.BlockSpec((1, units, D), lambda e, k: (e, k, 0))
    return pl.pallas_call(
        experts_body,
        name="experts",
        grid=(EXP_DEV, steps),
        out_shape=(
            shape_of((2 * TS, D), bf16),
            shape_of((2 * TS, D), bf16),
            shape_of((8, 2 * TS), f32),
            shape_of(w_in.shape, bf16),
            shape_of((w_down.shape[1], EXP_DEV * D), bf16),
        ),
        in_specs=[whole] * 6 + [in_block, down_block],
        out_specs=(whole, whole, whole, in_block, down_out),
        scratch_shapes=[
            pltpu.VMEM((capacity, 2 * TS), bf16),
            pltpu.VMEM((capacity, D), bf16),
            pltpu.VMEM((D, capacity), bf16),
            pltpu.VMEM((capacity, D), bf16),
            pltpu.VMEM((capacity, D), bf16),
            pltpu.VMEM((capacity, D), f32),
            pltpu.VMEM((capacity, D), f32),
            pltpu.VMEM((2 * TS, D), f32),
            pltpu.VMEM((2 * TS, D), f32),
        ],
        compiler_params=pltpu.CompilerParams(vmem_limit_bytes=VMEM_BYTES),
        cost_estimate=pl.CostEstimate(
            flops=40 * 10**9, bytes_accessed=80 * 10**6, transcendentals=10**6
        ),
    )(slots, gates, normed, grad, branch_in, back_in, w_in, w_down)


def rope_tables(positions, width):
    half_width = width // 2
    frequency = jnp.exp(
        -jnp.log(rope_base) * (2.0 * jnp.arange(half_width, dtype=jnp.float32) / width)
    )
    angles = positions.astype(jnp.float32)[:, None] * frequency[None, :]
    return (jnp.cos(angles), jnp.sin(angles))


def rotate(values, rope_cos, rope_sin):
    half_width = values.shape[-1] // 2
    first_half = values[..., :half_width]
    second_half = values[..., half_width:]
    return jnp.concatenate(
        [
            first_half * rope_cos - second_half * rope_sin,
            second_half * rope_cos + first_half * rope_sin,
        ],
        axis=-1,
    )


def rms_scale(values):
    return lax.rsqrt(jnp.mean(values * values, axis=-1, keepdims=True) + eps)


def product(left, right):
    return jnp.dot(left, right, preferred_element_type=jnp.float32)


def left_product(left, right):
    return lax.dot_general(
        left, right, (((0,), (0,)), ((), ())), preferred_element_type=jnp.float32
    )


def right_product(left, right):
    return lax.dot_general(
        left, right, (((1,), (1,)), ((), ())), preferred_element_type=jnp.float32
    )


def turned_product(left, right):
    return lax.dot_general(
        left, right, (((0,), (1,)), ((), ())), preferred_element_type=jnp.float32
    )


def einsum(text, *terms):
    return jnp.einsum(text, *terms, preferred_element_type=f32)


def to_blocks(term):
    return term.reshape(2, RING, 2, term.shape[0] // ROWS, term.shape[1])


def local(
    hidden_in,
    gain_first,
    query_down,
    query_gain,
    query_up,
    latent_down,
    latent_gain,
    latent_up,
    attention_out,
    gain_second,
    router,
    expert_gate,
    expert_up,
    expert_down,
    shared_gate,
    shared_up,
    shared_down,
    seq_lens,
    routes,
    out_grad,
):
    row_index = lax.axis_index("row")
    col_index = lax.axis_index("col")
    seq_count, local_len, col_width = hidden_in.shape
    row_total = seq_count * local_len
    experts_all = EXP_DEV * COLS
    most_rows = (5 * local_len * TOPK + 4 * experts_all - 1) // (4 * experts_all)
    capacity = seq_count * most_rows
    query_cols = QL // COLS
    kv_cols = (KL + DR) // COLS

    def here(values, axis=-1):
        width = values.shape[axis] // COLS
        return lax.dynamic_slice_in_dim(values, col_index * width, width, axis)

    (
        hidden_low,
        grad_full,
        down_all,
        query_up_all,
        latent_up_all,
        attention_out_all,
        shared_gate_all,
        shared_up_all,
        shared_down_all,
    ) = front(
        hidden_in.reshape(row_total, col_width),
        out_grad.reshape(row_total, col_width),
        jnp.concatenate([query_down, latent_down, router], axis=1),
        query_up,
        latent_up,
        attention_out,
        shared_gate,
        shared_up,
        shared_down,
    )
    expert_units = expert_gate.shape[2]
    expert_in, expert_down_late, hidden_low = lax.optimization_barrier(
        (
            jnp.stack([expert_gate, expert_up], axis=1).reshape(
                2 * EXP_DEV, D // ROWS, expert_units
            ),
            expert_down,
            hidden_low,
        )
    )
    expert_in_all = lax.all_gather(expert_in, "row", axis=1, tiled=True)
    expert_in_all = expert_in_all.reshape(EXP_DEV, 2, D, expert_units)
    expert_down_all = lax.all_gather(expert_down_late, "row", axis=1, tiled=True)

    hidden = hidden_low.astype(f32)
    scale_first = rms_scale(hidden)
    normed_first = (hidden * scale_first * gain_first).astype(bf16)
    latent_width = query_cols + kv_cols
    latent_weights = down_all[:, :latent_width]
    router_all = down_all[:, latent_width:]
    latent_here = turned_product(latent_weights, normed_first).astype(bf16)
    kv_pad = (-kv_cols) % 16
    query_latent, _, latent_all = latents(
        latent_here[:query_cols], jnp.pad(latent_here[query_cols:], ((0, kv_pad), (0, 0)))
    )
    kv_latent = lax.dynamic_index_in_dim(latent_all, row_index, 1, False)
    kv_latent = kv_latent[:, :kv_cols].reshape(KL + DR, row_total)
    latent_pad = ((0, 0), (0, kv_pad), (0, 0))
    every_cos, every_sin = rope_tables(jnp.arange(ROWS * local_len, dtype=jnp.int32), DR)
    kvt_all = expand(
        latent_all,
        jnp.pad(
            jnp.pad(latent_up_all, ((0, DR), (0, 0))).reshape(COLS, kv_cols, -1), latent_pad
        ).reshape(COLS * (kv_cols + kv_pad), -1).T,
        jnp.pad(
            jnp.pad(latent_gain, (0, DR)).reshape(COLS, kv_cols, 1), latent_pad
        ).reshape(COLS * (kv_cols + kv_pad), 1),
        every_cos.T,
        every_sin.T,
    )
    query_float = query_latent.astype(f32)
    query_scale = lax.rsqrt(jnp.mean(query_float * query_float, axis=0, keepdims=True) + eps)
    query_input = (query_float * query_scale * query_gain[:, None]).astype(bf16)
    latent_float = kv_latent[:KL].astype(f32)
    latent_scale = lax.rsqrt(jnp.mean(latent_float * latent_float, axis=0, keepdims=True) + eps)
    latent_input = (latent_float * latent_scale * latent_gain[:, None]).astype(bf16)
    positions = row_index * local_len + jnp.arange(local_len, dtype=jnp.int32)
    rope_cos, rope_sin = rope_tables(positions, DR)
    rope_cos = jnp.concatenate([rope_cos] * seq_count, axis=0)
    rope_sin = jnp.concatenate([rope_sin] * seq_count, axis=0)
    tile_cos = jnp.concatenate([rope_cos] * 4, axis=1)
    tile_sin = jnp.concatenate([-rope_sin, rope_sin] * 2, axis=1)
    split = DN + DR
    query_up_pack = jnp.concatenate(
        [query_up_all[:, :split], query_up_all[:, split + DN :], query_up_all[:, split : split + DN]],
        axis=1,
    )
    query_proj = left_product(query_input, query_up_pack)
    query_rope = query_proj[:, DN : 2 * DN]
    query_swap = jnp.concatenate(
        [query_rope[:, part : part + DR // 2] for part in (32, 0, 96, 64)], axis=1
    )
    query_pack = jnp.concatenate(
        [
            query_proj[:, :DN],
            query_rope * tile_cos + query_swap * tile_sin,
            query_proj[:, 2 * DN :],
        ],
        axis=1,
    ).astype(bf16)
    key_value = left_product(latent_input, latent_up_all).astype(bf16)
    key_rope = rotate(kv_latent[KL:].T.astype(f32), rope_cos, rope_sin).astype(bf16)
    near = jnp.concatenate(
        [
            key_value[:, :DN],
            key_rope,
            key_rope,
            key_value[:, 2 * DN : 3 * DN],
            key_value[:, DN : 2 * DN],
            key_value[:, 3 * DN :],
        ],
        axis=1,
    )

    attended_float, lse, lse_rows = attend(seq_lens, query_pack, kvt_all)
    attended = attended_float.astype(bf16)
    attention_part = product(attended, attention_out_all).astype(bf16)
    (attention_sum,) = sum_over_col("sum_attention", 4, attention_part, COL_CUT, ())

    residual_one = hidden + attention_sum.astype(f32)
    scale_second = rms_scale(residual_one)
    normed_second = (residual_one * scale_second * gain_second).astype(bf16)
    logits = turned_product(router_all, normed_second)
    sigmoid_all = jax.nn.sigmoid(logits)
    routes_turned = routes.reshape(row_total, TOPK).T
    chosen = jnp.sum(
        (
            routes_turned[:, None, :] == jnp.arange(experts_all, dtype=jnp.int32)[None, :, None]
        ).astype(f32),
        axis=0,
    )
    weighted_sig = sigmoid_all * chosen
    denominator = jnp.sum(weighted_sig, axis=0, keepdims=True)
    gate_weights = route_scale * weighted_sig / denominator
    gate_here = here(gate_weights, 0)
    member = here(chosen, 0).reshape(EXP_DEV * seq_count, local_len)
    before = jnp.triu(jnp.ones((local_len, local_len), bf16), 1)
    rank = product(member.astype(bf16), before).reshape(EXP_DEV, seq_count, local_len)
    rank = rank + (jnp.arange(seq_count, dtype=f32) * most_rows)[None, :, None]
    slots = jnp.where(member.reshape(rank.shape) > 0, rank, float(capacity))
    slots = slots.astype(jnp.int32).reshape(EXP_DEV, row_total)
    shared_branch, shared_back, shared_gate_grad, shared_up_grad, shared_down_grad = shared_experts(
        normed_second, grad_full, shared_gate_all, shared_up_all, shared_down_all
    )
    branch_part, normed_part, gate_grad_here, expert_in_part, expert_down_part = experts(
        capacity,
        slots,
        gate_here,
        normed_second,
        grad_full,
        shared_branch,
        shared_back,
        expert_in_all,
        expert_down_all,
    )
    expert_in_sum = lax.psum_scatter(
        expert_in_part.reshape(2 * EXP_DEV, D, expert_units),
        "row",
        scatter_dimension=1,
        tiled=True,
    )
    expert_down_sum = lax.psum_scatter(expert_down_part, "row", scatter_dimension=0, tiled=True)
    gate_grad_all = lax.dynamic_update_slice_in_dim(
        jnp.zeros((experts_all, row_total), f32), gate_grad_here[:EXP_DEV], col_index * EXP_DEV, 0
    )
    inner_sum = jnp.sum(gate_grad_all * gate_weights, axis=0, keepdims=True)
    logit_part = (
        sigmoid_all
        * (1.0 - sigmoid_all)
        * chosen
        / denominator
        * (route_scale * gate_grad_all - inner_sum)
    )
    normed_sum, logit_all, query_all = sum_over_col(
        "sum_normed",
        5,
        normed_part,
        COL_CUT,
        (("col", experts_all), ("row", CUT)),
        logit_part,
        query_pack,
    )
    logit_low = jnp.sum(logit_all, axis=0).astype(bf16)
    normed_grad = normed_sum.astype(f32) + turned_product(logit_low, router_all)
    router_grad = turned_product(normed_second, logit_low)
    weighted = normed_grad * gain_second
    residual_grad = (
        grad_full.astype(f32)
        + scale_second * weighted
        - residual_one
        * (scale_second * scale_second * scale_second)
        * jnp.mean(weighted * residual_one, axis=-1, keepdims=True)
    )
    gain_second_part = jnp.sum(here(normed_grad) * here(residual_one) * scale_second, axis=0)

    attention_grad = residual_grad.astype(bf16)
    attention_out_grad = einsum(
        "rk,rbn->bkn", attended, attention_grad.reshape(row_total, ROWS, D // ROWS)
    ).astype(bf16)
    attended_grad = right_product(attention_grad, attention_out_all).astype(bf16)
    delta = jnp.sum(
        (attended_grad.astype(f32) * attended_float).reshape(row_total, 2, DV), axis=-1
    )
    delta_lanes = jnp.repeat(delta, DV, axis=1)
    stats = jnp.concatenate([lse_rows[:2], delta.T, jnp.zeros((4, row_total), f32)], axis=0)
    attended_grad_all, stats_all, branch_here = back(attended_grad, stats, branch_part)
    block_out = (
        (here(residual_one) + branch_here).astype(bf16).reshape(seq_count, local_len, col_width)
    )
    dq, dk, dv = attend_back(
        seq_lens,
        query_pack,
        kvt_all,
        attended_grad,
        lse,
        delta_lanes,
        near,
        query_all,
        attended_grad_all,
        stats_all,
    )
    query_up_grad, latent_up_grad, query_in_grad, kv_part, numbers = project_back(
        dq,
        dk,
        dv,
        tile_cos,
        tile_sin,
        query_up_pack,
        latent_up_all,
        query_input,
        latent_input,
        query_latent,
        kv_latent[:KL],
        query_gain[:, None],
        latent_gain[:, None],
    )
    kv_part = jnp.pad(kv_part.reshape(COLS, kv_cols, row_total), latent_pad)
    shared_width = shared_gate.shape[1]
    (query_in_here, kv_in_here), numbers_all, summed = col_and_row(
        "sum_latents",
        7,
        "lead",
        (query_in_grad.reshape(COLS, query_cols, row_total), kv_part),
        ((query_cols, row_total), (kv_cols + kv_pad, row_total)),
        (128, 80),
        numbers,
        (attention_out_grad.reshape(2, RING, 2, col_width, D // ROWS),),
        (96,),
    )
    (attention_out_sum,) = summed
    kv_in_here = kv_in_here[:kv_cols]
    numbers_sum = jnp.sum(numbers_all, axis=0)
    query_mean = numbers_sum[:1] / QL
    latent_mean = numbers_sum[1:2] / KL
    query_float_here = here(query_float, 0)
    query_latent_here = (
        query_scale * query_in_here * here(query_gain)[:, None]
        - query_float_here * (query_scale * query_scale * query_scale) * query_mean
    )
    kv_float_here = here(kv_latent, 0).astype(f32)
    is_latent = (col_index * kv_cols + jnp.arange(kv_cols)) < KL
    latent_gain_here = here(jnp.concatenate([latent_gain, jnp.ones((DR,), f32)]))
    kv_latent_here = jnp.where(
        is_latent[:, None],
        latent_scale * kv_in_here * latent_gain_here[:, None]
        - kv_float_here * (latent_scale * latent_scale * latent_scale) * latent_mean,
        kv_in_here,
    )
    query_gain_part = jnp.sum(query_in_here * query_float_here * query_scale, axis=1)
    latent_gain_part = jnp.sum(kv_in_here * kv_float_here * latent_scale, axis=1)
    latent_here_grad = jnp.concatenate([query_latent_here, kv_latent_here], axis=0).astype(bf16)
    latent_down_grads = turned_product(normed_first, latent_here_grad)
    first_part = turned_product(latent_here_grad, latent_weights)
    first_number = jnp.sum(first_part * gain_first * hidden, axis=-1)
    first_numbers = jnp.concatenate([first_number[None], jnp.zeros((7, row_total), f32)], axis=0)
    (first_here,), first_numbers_all, summed = col_and_row(
        "sum_first",
        8,
        "lane",
        (first_part.astype(bf16),),
        ((row_total, col_width),),
        (384,),
        first_numbers,
        (
            to_blocks(
                jnp.concatenate([latent_down_grads.astype(bf16), router_grad.astype(bf16)], axis=1)
            ),
            to_blocks(query_up_grad),
            to_blocks(latent_up_grad),
            to_blocks(shared_gate_grad),
            to_blocks(shared_up_grad),
            shared_down_grad.reshape(2, RING, 2, shared_width, D // ROWS),
        ),
        (0, QL // ROWS, KL // ROWS, D // ROWS, 0, 0),
    )
    down_sum, query_up_sum, latent_up_sum, shared_gate_sum, shared_up_sum, shared_down_sum = summed
    query_up_sum = jnp.concatenate(
        [query_up_sum[:, :split], query_up_sum[:, 2 * DN :], query_up_sum[:, split : 2 * DN]], axis=1
    )
    first_mean = (jnp.sum(first_numbers_all[:, 0], axis=0) / D)[:, None]
    hidden_here = here(hidden)
    hidden_grad = (
        here(residual_grad)
        + scale_first * first_here * here(gain_first)
        - hidden_here * (scale_first * scale_first * scale_first) * first_mean
    ).reshape(seq_count, local_len, col_width)
    gain_first_part = jnp.sum(first_here * hidden_here * scale_first, axis=0)
    gains = jnp.concatenate(
        [
            gain_first_part,
            gain_second_part,
            query_gain_part,
            jnp.zeros((64,), f32),
            latent_gain_part,
            jnp.zeros((1024 - 768 - kv_cols,), f32),
        ]
    ).reshape(8, 128)
    gains_all = last(gains).reshape(COLS, 1024)
    expert_in_grad = expert_in_sum.reshape(EXP_DEV, 2, D // ROWS, expert_units).astype(f32)
    expert_down_grad = jnp.stack(
        [expert_down_sum[:, expert * D : (expert + 1) * D] for expert in range(EXP_DEV)], axis=0
    ).astype(f32)
    return (
        block_out,
        hidden_grad,
        gains_all[:, :col_width].reshape(D),
        down_sum[:, :query_cols],
        gains_all[:, 512 : 512 + query_cols].reshape(QL),
        query_up_sum,
        down_sum[:, query_cols:latent_width],
        gains_all[:, 768 : 768 + kv_cols].reshape(KL + DR)[:KL],
        latent_up_sum,
        attention_out_sum,
        gains_all[:, col_width : 2 * col_width].reshape(D),
        down_sum[:, latent_width:],
        expert_in_grad[:, 0],
        expert_in_grad[:, 1],
        expert_down_grad,
        shared_gate_sum,
        shared_up_sum,
        shared_down_sum,
    )


def solution(mesh):
    in_specs = (
        P(None, "row", "col"),
        P(),
        P("row", "col"),
        P(),
        P("row", "col"),
        P("row", "col"),
        P(),
        P("row", "col"),
        P("col", "row"),
        P(),
        P("row", None),
        P("col", "row", None),
        P("col", "row", None),
        P("col", "row", None),
        P("row", "col"),
        P("row", "col"),
        P("col", "row"),
        P(),
        P(None, "row", None),
        P(None, "row", "col"),
    )
    out_specs = (
        P(None, "row", "col"),
        P(None, "row", "col"),
        P(),
        P("row", "col"),
        P(),
        P("row", "col"),
        P("row", "col"),
        P(),
        P("row", "col"),
        P("col", "row"),
        P(),
        P("row", None),
        P("col", "row", None),
        P("col", "row", None),
        P("col", "row", None),
        P("row", "col"),
        P("row", "col"),
        P("col", "row"),
    )
    return jax.shard_map(local, mesh=mesh, in_specs=in_specs, out_specs=out_specs, check_vma=False)
```

```python
import functools
import math

import jax
import jax.numpy as jnp
from jax import lax
from jax.experimental import pallas as pl
from jax.experimental.pallas import tpu as pltpu
from jax.sharding import PartitionSpec as P

D = 2048
H = 16
DN = 128
DR = 64
DV = 128
QL = 1536
KL = 512
EXP_DEV = 2
TOPK = 6
ROWS = 16
COLS = 8
TS = 256
CUT = 208
COL_CUT = 400
LATENT_CUT = 5
KV_COLS = (KL + DR) // COLS

eps = 1e-06
route_scale = 2.446
rope_base = 50000.0
score_scale = 1.0 / math.sqrt(DN + DR)
score_bits = score_scale * math.log2(math.e)

bf16 = jnp.bfloat16
f32 = jnp.float32
ANY = pl.ANY
VM = pltpu.VMEM


def shape_of(shape, dtype):
    return jax.ShapeDtypeStruct(shape, dtype)

MESH = pl.DeviceIdType.MESH
RING = 4
VMEM_BYTES = 56 * 2**20


class Place:
    def __init__(self, axis):
        self.axis = axis
        self.index = lax.axis_index(axis)
        self.cores = 2 if axis == "row" else 1
        self.core = lax.rem(self.index, self.cores)
        self.ring = lax.rem(lax.div(self.index, self.cores), RING)
        self.pair = lax.div(self.index, self.cores * RING)

    def at(self, pair, ring, core=None):
        core = self.core if core is None else core
        return (pair * RING + ring) * self.cores + core

    def turn(self, step):
        return lax.rem(self.ring + step + RING, RING)

    def peers(self):
        found = [self.at(self.pair, self.turn(step)) for step in (1, 2, 3)]
        found.append(self.at(1 - self.pair, self.ring))
        if self.cores == 2:
            found.append(self.at(self.pair, self.ring, 1 - self.core))
        return found


class Net:
    def __init__(self, send_sems, recv_sems):
        self.send_sems, self.recv_sems = send_sems, recv_sems
        self.count = 0
        self.sent = []
        self.own = []

    def send(self, source, target, axis, index):
        number = self.count
        self.count += 1
        copy = pltpu.make_async_remote_copy(
            source,
            target,
            self.send_sems.at[number],
            self.recv_sems.at[number],
            device_id={axis: index},
            device_id_type=MESH,
        )
        copy.start()
        self.sent.append(copy)
        return number

    def receive(self, number, target, axis, index):
        pltpu.make_async_remote_copy(
            target,
            target,
            self.send_sems.at[number],
            self.recv_sems.at[number],
            device_id={axis: index},
            device_id_type=MESH,
        ).wait_recv()

    def local(self, source, target):
        number = self.count
        self.count += 1
        copy = pltpu.make_async_copy(source, target, self.send_sems.at[number])
        copy.start()
        self.own.append(copy)

    def settle(self):
        for copy in self.own:
            copy.wait()
        self.own = []

    def finish(self):
        for copy in self.sent:
            copy.wait_send()
        self.settle()


def greet(*places, everyone=False):
    barrier = pltpu.get_barrier_semaphore()
    count = 0
    for place in places:
        members = lax.axis_size(place.axis)
        all_peers = [lax.rem(place.index + step, members) for step in range(1, members)]
        for peer in all_peers if everyone else place.peers():
            pl.semaphore_signal(
                barrier, inc=1, device_id={place.axis: peer}, device_id_type=MESH
            )
            count += 1
    pl.semaphore_wait(barrier, count)


class Gather:
    def __init__(self, net, place, source, slot, rows, cut, relay=False, cross=None):
        self.net, self.place, self.source, self.slot = net, place, source, slot
        self.rows, self.cut, self.relay = rows, cut, relay
        self.first, self.second = (0, cut), (cut, rows - cut)
        self.crossed = []
        if place.cores == 2:
            partner = place.at(place.pair, place.ring, 1 - place.core)

            def other(pair, ring, low, count):
                return slot(place.at(pair, ring, 1 - place.core), low, count)

            cross = (place.axis, partner, other)
        self.cross = cross

    def _send(self, owner, part, peer, own=False):
        piece = self.slot(owner, *part)
        start = self.source.at[pl.ds(*part)] if own else piece
        return self.net.send(start, piece, self.place.axis, peer)

    def _receive(self, number, pair, ring, part, peer):
        place = self.place
        self.net.receive(number, self.slot(place.at(pair, ring), *part), place.axis, peer)

    def _cross(self, pair, ring, part, own=False):
        if self.cross is None:
            return
        piece = self.slot(self.place.at(pair, ring), *part)
        start = self.source.at[pl.ds(*part)] if own else piece
        number = self.net.send(start, piece, self.cross[0], self.cross[1])
        self.crossed.append((number, pair, ring, part))

    def _halves(self, part):
        low, count = part
        unit = 16 if count % 16 == 0 else 1
        half = max(count // 2 // unit, 1) * unit
        return (low, half), (low + half, count - half)

    def _relays(self, part):
        return self.relay and part[1] >= (32 if part[1] % 16 == 0 else 2)

    def _round(self, pair, part, own=False):
        place = self.place
        owner = place.at(pair, place.ring)
        steps = (1, 3) if self._relays(part) else (1, 3, 2)
        return {
            step: self._send(owner, part, place.at(place.pair, place.turn(step)), own)
            for step in steps
        }

    def _pass(self, numbers, pair, part, then):
        place = self.place
        passed = {}
        for step in (1, 3):
            ring = place.turn(-step)
            self._receive(numbers[step], pair, ring, part, place.at(place.pair, ring))
            if self._relays(part):
                half = self._halves(part)[step // 2]
                passed[step] = self._send(
                    place.at(pair, ring), half, place.at(place.pair, place.turn(step))
                )
            then(pair, ring, part)
        return passed

    def _meet(self, numbers, passed, pair, part, then):
        place = self.place
        far = place.turn(2)
        if self._relays(part):
            for step in (1, 3):
                half = self._halves(part)[step // 2]
                self._receive(
                    passed[step], pair, far, half, place.at(place.pair, place.turn(-step))
                )
        else:
            self._receive(numbers[2], pair, far, part, place.at(place.pair, far))
        then(pair, far, part)

    def start_first(self):
        place = self.place
        if self.cut:
            other = place.at(1 - place.pair, place.ring)
            self.across = self._send(place.index, self.first, other, True)
            self.near = self._round(place.pair, self.first, True)

    def start_second(self):
        place = self.place
        if self.second[1]:
            self.round = self._round(place.pair, self.second, True)
            other = place.at(1 - place.pair, place.ring)
            self.over = [(place.ring, self._send(place.index, self.second, other, True))]
        self._cross(place.pair, place.ring, (0, self.rows), True)
        self.net.local(self.source, self.slot(place.index, 0, self.rows))

    def start(self):
        self.start_first()
        self.start_second()

    def forward_first(self):
        place = self.place
        if self.cut:
            other = place.at(1 - place.pair, place.ring)
            self._receive(self.across, 1 - place.pair, place.ring, self.first, other)
            self.far = self._round(1 - place.pair, self.first)
            self._cross(1 - place.pair, place.ring, self.first)

    def _over(self, pair, ring, part):
        place = self.place
        other = place.at(1 - place.pair, place.ring)
        self.over.append((ring, self._send(place.at(pair, ring), part, other)))
        self._cross(pair, ring, part)

    def near_pass(self):
        place = self.place
        if self.second[1]:
            self.round_passed = self._pass(self.round, place.pair, self.second, self._over)
        if self.cut:
            self.near_passed = self._pass(self.near, place.pair, self.first, self._cross)

    def far_pass(self):
        if self.cut:
            pair = 1 - self.place.pair
            self.far_passed = self._pass(self.far, pair, self.first, self._cross)

    def near_meet(self):
        place = self.place
        if self.second[1]:
            self._meet(self.round, self.round_passed, place.pair, self.second, self._over)
        if self.cut:
            self._meet(self.near, self.near_passed, place.pair, self.first, self._cross)

    def far_meet(self):
        place = self.place
        if self.cut:
            self._meet(self.far, self.far_passed, 1 - place.pair, self.first, self._cross)
        if self.second[1]:
            other = place.at(1 - place.pair, place.ring)
            for ring, number in self.over:
                self._receive(number, 1 - place.pair, ring, self.second, other)
                self._cross(1 - place.pair, ring, self.second)

    def end(self):
        for number, pair, ring, part in self.crossed:
            axis, partner, other = self.cross
            self.net.receive(number, other(pair, ring, *part), axis, partner)


class Direct:
    def __init__(self, net, place, source, ref, count):
        self.net, self.place, self.source, self.ref, self.count = net, place, source, ref, count

    def start(self):
        place = self.place
        self.numbers = [
            self.net.send(
                self.source,
                self.ref.at[place.index],
                place.axis,
                lax.rem(place.index + step, self.count),
            )
            for step in range(1, self.count)
        ]
        self.net.local(self.source, self.ref.at[place.index])

    def land(self):
        place = self.place
        for step, number in zip(range(1, self.count), self.numbers):
            owner = lax.rem(place.index + self.count - step, self.count)
            self.net.receive(number, self.ref.at[owner], place.axis, owner)


STAGES = ("start", "forward_first", "near_pass", "far_pass", "near_meet", "far_meet", "end")


def run_stages(gathers, stages=STAGES):
    for stage in stages:
        for gather in gathers:
            getattr(gather, stage)()


def run_gathers(*gathers):
    run_stages(gathers)


def row_slots(ref, rows):
    return lambda owner, low, count: ref.at[
        pl.ds(pl.multiple_of(owner * rows + low, 16), count)
    ]


def lead_slots(ref):
    return lambda owner, low, count: ref.at[owner, pl.ds(low, count)]


def lane_slots(ref, width):
    return lambda owner, low, count: ref.at[
        pl.ds(low, count), pl.ds(pl.multiple_of(owner * width, 128), width)
    ]


class Scatter:
    def __init__(self, net, place, block, rows, cut, scratch, keep):
        self.net, self.place, self.block, self.rows, self.cut = net, place, block, rows, cut
        self.scratch, self.keep = scratch, keep
        self.first, self.second = (0, cut), (cut, rows - cut)

    @staticmethod
    def scratch_of(rows, cut, width, dtype=jnp.bfloat16):
        shapes = []
        if cut:
            shapes += [(3, 2, cut, width), (2, cut, width)]
        if rows - cut:
            shapes += [(4, rows - cut, width), (4, rows - cut, width), (3, rows - cut, width)]
        return [pltpu.VMEM(shape, dtype) for shape in shapes]

    def _refs(self):
        refs = list(self.scratch)
        first = refs[:2] if self.cut else None
        second = refs[-3:] if self.second[1] else None
        return first, second

    def _owner(self, pair, ring):
        return self.place.at(pair, ring)

    def start(self):
        place, net = self.place, self.net
        first, second = self._refs()
        if first:
            self.round = [
                [
                    net.send(
                        self.block(self._owner(pair, place.turn(step)), *self.first),
                        first[0].at[step - 1, pair],
                        place.axis,
                        place.at(place.pair, place.turn(step)),
                    )
                    for pair in (0, 1)
                ]
                for step in (1, 2, 3)
            ]
        if second:
            self.across = [
                net.send(
                    self.block(self._owner(1 - place.pair, ring), *self.second),
                    second[0].at[ring],
                    place.axis,
                    place.at(1 - place.pair, place.ring),
                )
                for ring in range(RING)
            ]

    def forward_second(self):
        place, net = self.place, self.net
        first, second = self._refs()
        if not second:
            return
        other = place.at(1 - place.pair, place.ring)
        for ring in range(RING):
            net.receive(self.across[ring], second[0].at[ring], place.axis, other)
        for ring in range(RING):
            total = (
                self.block(self._owner(place.pair, ring), *self.second)[...].astype(jnp.float32)
                + second[0][ring].astype(jnp.float32)
            )
            second[1][ring] = total.astype(second[1].dtype)
        self.last = [
            net.send(
                second[1].at[place.turn(step)],
                second[2].at[step - 1],
                place.axis,
                place.at(place.pair, place.turn(step)),
            )
            for step in (1, 2, 3)
        ]

    def forward_first(self):
        place, net = self.place, self.net
        first, second = self._refs()
        if not first:
            return
        for step in (1, 3, 2):
            owner = place.at(place.pair, place.turn(-step))
            for pair in (0, 1):
                net.receive(self.round[step - 1][pair], first[0].at[step - 1, pair], place.axis, owner)
        other = 1 - place.pair
        total = self.block(self._owner(other, place.ring), *self.first)[...].astype(jnp.float32)
        for step in range(3):
            total = total + first[0][step, other].astype(jnp.float32)
        first[1][0] = total.astype(first[1].dtype)
        self.over = net.send(
            first[1].at[0], first[1].at[1], place.axis, place.at(other, place.ring)
        )

    def end_first(self):
        place, net = self.place, self.net
        first, second = self._refs()
        if not first:
            return
        total = self.block(self._owner(place.pair, place.ring), *self.first)[...].astype(jnp.float32)
        for step in range(3):
            total = total + first[0][step, place.pair].astype(jnp.float32)
        other = place.at(1 - place.pair, place.ring)
        net.receive(self.over, first[1].at[1], place.axis, other)
        self.keep(self.first, total + first[1][1].astype(jnp.float32))

    def end_second(self):
        place, net = self.place, self.net
        first, second = self._refs()
        if not second:
            return
        total = (
            self.block(self._owner(place.pair, place.ring), *self.second)[...].astype(jnp.float32)
            + second[0][place.ring].astype(jnp.float32)
        )
        for step in (1, 3, 2):
            owner = place.at(place.pair, place.turn(-step))
            net.receive(self.last[step - 1], second[2].at[step - 1], place.axis, owner)
            total = total + second[2][step - 1].astype(jnp.float32)
        self.keep(self.second, total)


def comm_call(body, name, collective_id, out_shapes, in_spaces, out_spaces, copies, scratch=(), args=(), aliases=None):
    return pl.pallas_call(
        body,
        name=name,
        out_shape=out_shapes,
        in_specs=[pl.BlockSpec(memory_space=space) for space in in_spaces],
        out_specs=tuple(pl.BlockSpec(memory_space=space) for space in out_spaces),
        scratch_shapes=[
            pltpu.SemaphoreType.DMA((copies,)),
            pltpu.SemaphoreType.DMA((copies,)),
            *scratch,
        ],
        input_output_aliases=aliases or {},
        compiler_params=pltpu.CompilerParams(
            collective_id=collective_id, has_side_effects=True, vmem_limit_bytes=VMEM_BYTES
        ),
    )(*args)


def plane_slots(ref, plane):
    return lambda owner, low, count: ref.at[
        plane, pl.ds(pl.multiple_of(owner * (D // ROWS) + low, 16), count)
    ]


def plane_gather(net, row, source, ref, plane, cut):
    return Gather(net, row, source, plane_slots(ref, plane), D // ROWS, cut, True)


def front_body(hidden, grad, w1, qu, lu, ao, sg, su, sd, gate, down, *rest):
    hidden_all, grad_all, w1_all, qu_all, lu_all, ao_all, sg_all, su_all, sd_all = rest[:9]
    planes, down_chip, ss, rs, down_other = rest[9:]
    row, col = Place("row"), Place("col")
    greet(row, col)
    net = Net(ss, rs)
    partner = row.at(row.pair, row.ring, 1 - row.core)
    gathers = [
        Gather(net, col, hidden, lane_slots(hidden_all, D // COLS), 2 * TS, 2 * TS, True),
        *(
            Gather(net, row, term, row_slots(ref, term.shape[0]), term.shape[0], cut, True)
            for term, ref, cut in (
                (w1, w1_all, 128),
                (qu, qu_all, 96),
                (lu, lu_all, 32),
                (sg, sg_all, 128),
                (su, su_all, 96),
            )
        ),
        *(
            Gather(net, row, term, lane_slots(ref, term.shape[1]), term.shape[0], cut, True)
            for term, ref, cut in ((ao, ao_all, 192), (sd, sd_all, 256))
        ),
        plane_gather(net, row, gate.at[0], planes, 0, 64),
        Gather(net, col, grad, lane_slots(grad_all, D // COLS), 2 * TS, 2 * TS, True),
    ]
    number = net.send(down.at[1 - row.core], down_other, "row", partner)
    run_stages(gathers, STAGES[:1])
    net.receive(number, down_other, "row", partner)
    height = down_chip.shape[0] // 2
    own = down[row.core].astype(f32)[:height]
    given = down_other[...].astype(f32)[:height]
    even = row.core == 0
    down_chip[...] = jnp.concatenate(
        [jnp.where(even, own, given), jnp.where(even, given, own)], axis=0
    ).astype(bf16)
    run_stages(gathers, STAGES[1:])
    net.finish()


def stacked(term):
    return shape_of((ROWS * term.shape[0], term.shape[1]), term.dtype)


def side_by_side(term):
    return shape_of((term.shape[0], ROWS * term.shape[1]), term.dtype)


def front(hidden, grad, w1, qu, lu, ao, sg, su, sd, gate, down, units):
    return comm_call(
        front_body,
        "gather_front",
        1,
        (
            shape_of((2 * TS, D), bf16),
            shape_of((2 * TS, D), bf16),
            stacked(w1),
            stacked(qu),
            stacked(lu),
            side_by_side(ao),
            stacked(sg),
            stacked(su),
            side_by_side(sd),
            shape_of((2 * EXP_DEV, D, units), bf16),
            shape_of((2 * units // ROWS, D), bf16),
        ),
        [ANY] * 10 + [VM],
        [ANY] * 10 + [VM],
        256,
        [pltpu.VMEM(down.shape[1:], bf16)],
        (hidden, grad, w1, qu, lu, ao, sg, su, sd, gate, down),
    )


def latent_body(query, latent, gate, up, _, query_all, rows_all, latent_all, planes, ss, rs):
    row, col = Place("row"), Place("col")
    greet(row, col)
    net = Net(ss, rs)
    queries = Gather(
        net, col, query, row_slots(query_all, query.shape[0]), query.shape[0], 192, True
    )
    weights = [
        plane_gather(net, row, up.at[0], planes, 1, 96),
        plane_gather(net, row, gate.at[1], planes, 2, 96),
    ]
    rows = Gather(net, row, latent, lead_slots(rows_all), latent.shape[0], 48)
    half = ROWS // 2
    base = row.core * half
    partner = row.at(row.pair, row.ring, 1 - row.core)

    def slot(owner, low, count):
        return latent_all.at[owner, pl.ds(base + low, count)]

    def other(pair, ring, low, count):
        return latent_all.at[col.at(pair, ring), pl.ds(half - base + low, count)]

    every = Gather(
        net, col, rows_all.at[pl.ds(base, half)], slot, half, LATENT_CUT, True, ("row", partner, other)
    )
    run_stages((rows, queries), STAGES[:1])
    run_stages((rows,), STAGES[1:])
    net.settle()
    run_stages((every, *weights), STAGES[:1])
    run_stages((queries, every, *weights), STAGES[1:])
    net.finish()


def latents(query, latent, gate, up, planes):
    return comm_call(
        latent_body,
        "gather_latents",
        2,
        (
            shape_of((COLS * query.shape[0], query.shape[1]), bf16),
            shape_of((ROWS, *latent.shape), bf16),
            shape_of((COLS, ROWS, *latent.shape), bf16),
            shape_of(planes.shape, bf16),
        ),
        [ANY] * 5,
        [ANY] * 4,
        192,
        args=(query, latent, gate, up, planes),
        aliases={4: 3},
    )


def expand_body(latent, weight, gain, cos, sin, out):
    @pl.when(pl.program_id(0) <= lax.axis_index("row") + 1)
    def _():
        features = latent.shape[0] * latent.shape[2]
        values = latent[:, 0].reshape(features, latent.shape[3]).astype(f32)
        live = features - latent.shape[2] + 8
        square = jnp.sum(values[:live] * values[:live], axis=0, keepdims=True)
        scaled = (values * lax.rsqrt(square / KL + eps) * gain[...]).astype(bf16)
        found = jnp.dot(weight[...], scaled, preferred_element_type=f32).astype(bf16)
        turn_cos = jnp.concatenate([cos[...], cos[...]], axis=1)
        turn_sin = jnp.concatenate([sin[...], sin[...]], axis=1)
        first, second = values[live : live + 32], values[live + 32 : live + 64]
        rope = jnp.concatenate(
            [first * turn_cos - second * turn_sin, second * turn_cos + first * turn_sin], axis=0
        ).astype(bf16)
        out[0, 0:128] = found[0:128]
        out[0, 128:192] = rope
        out[0, 192:256] = rope
        out[0, 256:384] = found[256:384]
        out[0, 384:512] = found[128:256]
        out[0, 512:640] = found[384:512]


def expand(latent, weight, gain, cos, sin):
    cols, rows, height, width = latent.shape
    return pl.pallas_call(
        expand_body,
        name="expand_keys",
        grid=(rows,),
        out_shape=shape_of((rows, 640, width), bf16),
        in_specs=[
            pl.BlockSpec((cols, 1, height, width), lambda r: (0, r, 0, 0)),
            pl.BlockSpec(weight.shape, lambda r: (0, 0)),
            pl.BlockSpec(gain.shape, lambda r: (0, 0)),
            pl.BlockSpec((32, TS), lambda r: (0, r)),
            pl.BlockSpec((32, TS), lambda r: (0, r)),
        ],
        out_specs=pl.BlockSpec((1, 640, width), lambda r: (r, 0, 0)),
        compiler_params=pltpu.CompilerParams(vmem_limit_bytes=VMEM_BYTES),
        cost_estimate=pl.CostEstimate(
            flops=6 * 10**9, bytes_accessed=22 * 10**6, transcendentals=8192
        ),
    )(latent, weight, gain, cos, sin)


def sum_body(cut, kinds, term, *rest):
    count = len(kinds)
    extras, total_all, extras_all = rest[:count], rest[count], rest[count + 1 : 2 * count + 1]
    ss, rs, *scratch = rest[2 * count + 1 :]
    places = {"row": Place("row"), "col": Place("col")}
    greet(*(places[axis] for axis in sorted({"col", *(axis for axis, _ in kinds)})))
    net = Net(ss, rs)
    width = D // COLS
    mine = scratch[-1]

    def keep(part, value):
        mine[pl.ds(*part)] = value.astype(mine.dtype)

    col = places["col"]
    scatter = Scatter(net, col, lane_slots(term, width), 2 * TS, cut, scratch[:-1], keep)
    gather = Gather(net, col, mine, lane_slots(total_all, width), 2 * TS, cut, True)
    beside = [
        Gather(net, places[axis], extra, lead_slots(extra_all), extra.shape[0], extra_cut, True)
        for (axis, extra_cut), extra, extra_all in zip(kinds, extras, extras_all)
    ]
    scatter.start()
    run_stages(beside, STAGES[:1])
    scatter.forward_second()
    scatter.forward_first()
    run_stages(beside, STAGES[1:3])
    scatter.end_first()
    gather.start_first()
    scatter.end_second()
    gather.start_second()
    run_stages((gather,), STAGES[1:3])
    run_stages(beside, STAGES[3:])
    run_stages((gather,), STAGES[3:])
    net.finish()


def sum_over_col(name, collective_id, term, cut, kinds, *extras):
    counts = {"row": ROWS, "col": COLS}
    return comm_call(
        functools.partial(sum_body, cut, kinds),
        name,
        collective_id,
        (
            shape_of((2 * TS, D), bf16),
            *(
                shape_of((counts[axis], *extra.shape), extra.dtype)
                for (axis, _), extra in zip(kinds, extras)
            ),
        ),
        [VM] + [ANY] * len(extras),
        [ANY] * (1 + len(extras)),
        128,
        [*Scatter.scratch_of(2 * TS, cut, D // COLS), pltpu.VMEM((2 * TS, D // COLS), bf16)],
        (term, *extras),
    )


def attention_sum_body(term, up, down, _, total_all, planes, down_all, ss, rs, *scratch):
    row, col = Place("row"), Place("col")
    greet(row, col)
    net = Net(ss, rs)
    width = D // COLS
    mine = scratch[-1]

    def keep(part, value):
        mine[pl.ds(*part)] = value.astype(mine.dtype)

    height = down.shape[0]

    def down_slot(owner, low, count):
        place = pl.multiple_of(lax.div(owner, 2) * height + low, 16)
        return down_all.at[lax.rem(owner, 2), pl.ds(place, count)]

    scatter = Scatter(net, col, lane_slots(term, width), 2 * TS, 2 * TS, scratch[:-1], keep)
    gather = Gather(net, col, mine, lane_slots(total_all, width), 2 * TS, 2 * TS, True)
    weights = [
        plane_gather(net, row, up.at[1], planes, 3, 96),
        Gather(net, row, down, down_slot, height, 112, True),
    ]
    scatter.start()
    run_stages(weights, STAGES[:1])
    scatter.forward_first()
    run_stages(weights, STAGES[1:2])
    scatter.end_first()
    gather.start()
    run_stages(weights, STAGES[2:3])
    run_stages((gather,), STAGES[1:3])
    run_stages(weights, STAGES[3:4])
    run_stages((gather,), STAGES[3:5])
    run_stages(weights, STAGES[4:5])
    run_stages((gather, *weights), STAGES[5:])
    net.finish()


def attention_sum_over_col(term, up, down, planes):
    return comm_call(
        attention_sum_body,
        "sum_attention",
        4,
        (
            shape_of((2 * TS, D), bf16),
            shape_of(planes.shape, bf16),
            shape_of((EXP_DEV, ROWS // 2 * down.shape[0], D), bf16),
        ),
        [VM, ANY, ANY, ANY],
        [ANY] * 3,
        128,
        [*Scatter.scratch_of(2 * TS, 2 * TS, D // COLS), pltpu.VMEM((2 * TS, D // COLS), bf16)],
        (term, up, down, planes),
        aliases={3: 1},
    )


def back_body(grad, stats, branch, grad_all, stats_all, branch_sum, ss, rs, *scratch):
    row, col = Place("row"), Place("col")
    greet(row, col)
    net = Net(ss, rs)

    def keep(part, value):
        branch_sum[pl.ds(*part)] = value

    scatter = Scatter(net, col, lane_slots(branch, D // COLS), 2 * TS, COL_CUT, scratch, keep)
    gathers = (
        Gather(net, row, grad, lead_slots(grad_all), 2 * TS, 96, True),
        Gather(net, row, stats, lead_slots(stats_all), stats.shape[0], stats.shape[0]),
    )
    run_stages(gathers, STAGES[:1])
    scatter.start()
    run_stages(gathers, STAGES[1:3])
    scatter.forward_second()
    scatter.forward_first()
    run_stages(gathers, STAGES[3:6])
    scatter.end_first()
    scatter.end_second()
    run_stages(gathers, STAGES[6:])
    net.finish()


def back(grad, stats, branch):
    return comm_call(
        back_body,
        "gather_back",
        6,
        (
            shape_of((ROWS, *grad.shape), bf16),
            shape_of((ROWS, *stats.shape), f32),
            shape_of((2 * TS, D // COLS), f32),
        ),
        [ANY, ANY, VM],
        [ANY, ANY, VM],
        96,
        Scatter.scratch_of(2 * TS, COL_CUT, D // COLS),
        (grad, stats, branch),
    )


class RowScatter:
    def __init__(self, net, place, term, cut, scratch, keep):
        self.net, self.place, self.term = net, place, term
        self.arrived, self.summed = scratch[:2]
        rows = term.shape[3]

        def block(owner, low, count):
            return self.summed.at[lax.div(owner, 2), pl.ds(low, count)]

        self.inner = Scatter(net, place, block, rows, cut, scratch[2:], keep)

    @staticmethod
    def scratch_of(rows, cut, width):
        return [
            pltpu.VMEM((2, RING, rows, width), bf16),
            pltpu.VMEM((2 * RING, rows, width), bf16),
            *Scatter.scratch_of(rows, cut, width),
        ]

    def start(self):
        place = self.place
        self.partner = place.at(place.pair, place.ring, 1 - place.core)
        self.number = self.net.send(
            self.term.at[:, :, 1 - place.core], self.arrived, place.axis, self.partner
        )

    def middle(self):
        place = self.place
        self.net.receive(self.number, self.arrived, place.axis, self.partner)
        for pair in range(2):
            for ring in range(RING):
                self.summed[pair * RING + ring] = (
                    self.term[pair, ring, place.core].astype(f32)
                    + self.arrived[pair, ring].astype(f32)
                ).astype(bf16)
        self.inner.start()


def run_scatters(scatters):
    for scatter in scatters:
        scatter.forward_second()
    for scatter in scatters:
        scatter.forward_first()
    for scatter in scatters:
        scatter.end_first()
    for scatter in scatters:
        scatter.end_second()


def keep_in(ref):
    def keep(part, value):
        ref[pl.ds(*part)] = value

    return keep


def block_slots(ref):
    return lambda owner, low, count: ref.at[owner, pl.ds(low, count)]


def rows_sum(net, place, terms, cuts, totals, scratch):
    parts = []
    for term, cut, total in zip(terms, cuts, totals):
        count = len(RowScatter.scratch_of(term.shape[3], cut, term.shape[4]))
        parts.append(RowScatter(net, place, term, cut, scratch[:count], keep_in(total)))
        scratch = scratch[count:]
    return parts


def rows_scratch(terms, cuts):
    found = []
    for term, cut in zip(terms, cuts):
        found += RowScatter.scratch_of(term.shape[3], cut, term.shape[4])
    return found


def col_and_row_body(col_cuts, row_cuts, slots, *rest):
    cols, rows = len(col_cuts), len(row_cuts)
    col_terms, rest = rest[:cols], rest[cols:]
    extra, rest = rest[0], rest[1:]
    row_terms, rest = rest[:rows], rest[rows:]
    col_totals, rest = rest[:cols], rest[cols:]
    extra_all, rest = rest[0], rest[1:]
    row_totals, rest = rest[:rows], rest[rows:]
    ss, rs, *scratch = rest
    row, col = Place("row"), Place("col")
    greet(row, col)
    net = Net(ss, rs)
    scatters = []
    for term, cut, total in zip(col_terms, col_cuts, col_totals):
        height, width = total.shape
        block = lane_slots(term, width) if slots == "lane" else block_slots(term)
        count = len(Scatter.scratch_of(height, cut, width))
        scatters.append(Scatter(net, col, block, height, cut, scratch[:count], keep_in(total)))
        scratch = scratch[count:]
    beside = Gather(net, col, extra, lead_slots(extra_all), extra.shape[0], extra.shape[0])
    parts = rows_sum(net, row, row_terms, row_cuts, row_totals, scratch)
    for part in parts:
        part.start()
    for scatter in scatters:
        scatter.start()
    beside.start()
    for part in parts:
        part.middle()
    run_stages((beside,), STAGES[1:2])
    run_scatters(scatters + [part.inner for part in parts])
    run_stages((beside,), STAGES[2:])
    net.finish()


def col_and_row(name, collective_id, slots, col_terms, col_shapes, col_cuts, extra, row_terms, row_cuts):
    scratch = []
    for shape, cut in zip(col_shapes, col_cuts):
        scratch += Scatter.scratch_of(shape[0], cut, shape[1])
    found = comm_call(
        functools.partial(col_and_row_body, tuple(col_cuts), tuple(row_cuts), slots),
        name,
        collective_id,
        (
            *(shape_of(shape, f32) for shape in col_shapes),
            shape_of((COLS, *extra.shape), f32),
            *(shape_of(term.shape[3:], f32) for term in row_terms),
        ),
        [*([VM] * len(col_terms)), ANY, *([VM] * len(row_terms))],
        [*([VM] * len(col_terms)), ANY, *([VM] * len(row_terms))],
        128,
        [*scratch, *rows_scratch(row_terms, row_cuts)],
        (*col_terms, extra, *row_terms),
    )
    count = len(col_terms)
    return found[:count], found[count], found[count + 1 :]


def last_body(gains, gains_all, ss, rs, gains_rows, gains_mine):
    row, col = Place("row"), Place("col")
    greet(row, col, everyone=True)
    net = Net(ss, rs)
    beside = Direct(net, row, gains, gains_rows, ROWS)
    beside.start()
    beside.land()
    net.settle()
    total = gains_rows[0]
    for index in range(1, ROWS):
        total = total + gains_rows[index]
    gains_mine[...] = total
    spread = Direct(net, col, gains_mine, gains_all, COLS)
    spread.start()
    spread.land()
    net.finish()


def last(gains):
    return comm_call(
        last_body,
        "sum_last",
        9,
        (shape_of((COLS, 8, 128), f32),),
        [VM],
        [VM],
        64,
        [pltpu.VMEM((ROWS, 8, 128), f32), pltpu.VMEM((8, 128), f32)],
        (gains,),
    )[0]


def contract(left, right):
    return lax.dot_general(left, right, (((1,), (1,)), ((), ())), preferred_element_type=f32)


def masked_queries(pack):
    lanes = lax.broadcasted_iota(jnp.int32, (pack.shape[0], 256), 1)
    zero = jnp.zeros((), pack.dtype)
    return (
        jnp.where(lanes < 192, pack[:, :256], zero),
        jnp.where(lanes >= 64, pack[:, 128:], zero),
    )


def attend_body(lens, query, kvt, out, lse, lse_rows, scores):
    seq = pl.program_id(0)
    mine = lax.axis_index("row")
    live = lens[seq]
    steps = lax.div(jnp.minimum(mine + 1, lax.div(live + TS - 1, TS)) + 1, 2)
    places = mine * TS + lax.broadcasted_iota(jnp.int32, (TS, 1), 0)
    limit = jnp.minimum(places + 1, live)
    offsets = lax.broadcasted_iota(jnp.int32, (TS, TS), 1)
    queries = masked_queries(query[...])

    def first(step, tops):
        tops = list(tops)
        for half in range(2):
            index = 2 * step + half
            valid = offsets < limit - index * TS
            for head in range(2):
                key = kvt[index, head * 128 : head * 128 + 256]
                value = jnp.dot(queries[head], key, preferred_element_type=f32)
                value = jnp.where(valid, value, -1e30)
                scores[head, index] = value
                tops[head] = jnp.maximum(
                    tops[head], jnp.maximum(value[:, :128], value[:, 128:])
                )
        return tuple(tops)

    tops = lax.fori_loop(0, steps, first, (jnp.full((TS, 128), -1e30, f32),) * 2)
    tops = [jnp.max(top, axis=1, keepdims=True) * score_bits for top in tops]

    def second(step, carried):
        found = []
        for head in range(2):
            sums, total = carried[head]
            for half in range(2):
                index = 2 * step + half
                weight = jnp.exp2(scores[head, index] * score_bits - tops[head])
                sums = sums + (weight[:, :128] + weight[:, 128:])
                value = kvt[index, 384 + head * 128 : 512 + head * 128]
                total = total + contract(weight.astype(bf16), value)
            found.append((sums, total))
        return tuple(found)

    zero = jnp.zeros((TS, 128), f32)
    carried = lax.fori_loop(0, steps, second, ((zero, zero),) * 2)
    for head in range(2):
        sums, total = carried[head]
        whole = jnp.sum(sums, axis=1, keepdims=True)
        lanes = pl.ds(head * 128, 128)
        out[:, lanes] = total / whole
        value = jnp.broadcast_to(tops[head] + jnp.log2(whole), (TS, 128))
        lse[:, lanes] = value
        lse_rows[head : head + 1] = value.T[:1]


def attend(lens, query, kvt):
    return pl.pallas_call(
        attend_body,
        name="attend",
        grid=(2,),
        out_shape=(
            shape_of((2 * TS, 256), f32),
            shape_of((2 * TS, 256), f32),
            shape_of((8, 2 * TS), f32),
        ),
        in_specs=[
            pl.BlockSpec(memory_space=pltpu.SMEM),
            pl.BlockSpec((TS, 384), lambda s: (s, 0)),
            pl.BlockSpec((ROWS, 640, TS), lambda s: (0, 0, s)),
        ],
        out_specs=(
            pl.BlockSpec((TS, 256), lambda s: (s, 0)),
            pl.BlockSpec((TS, 256), lambda s: (s, 0)),
            pl.BlockSpec((8, TS), lambda s: (0, s)),
        ),
        scratch_shapes=[pltpu.VMEM((2, ROWS, TS, TS), f32)],
        compiler_params=pltpu.CompilerParams(vmem_limit_bytes=VMEM_BYTES),
        cost_estimate=pl.CostEstimate(
            flops=6 * 10**9, bytes_accessed=12 * 10**6, transcendentals=4 * 10**6
        ),
    )(lens, query, kvt)


def attend_back_body(lens, query, kvt, grad, lse, delta, near, query_all, grad_all, stats, dq, dk, dv):
    seq = pl.program_id(0)
    mine = lax.axis_index("row")
    live = lens[seq]
    width = 2 * TS
    steps = lax.div(jnp.minimum(mine + 1, lax.div(live + TS - 1, TS)) + 1, 2)
    places = mine * TS + lax.broadcasted_iota(jnp.int32, (TS, 1), 0)
    limit = jnp.minimum(places + 1, live)
    narrow = lax.broadcasted_iota(jnp.int32, (TS, TS), 1)
    wide = lax.broadcasted_iota(jnp.int32, (TS, width), 1)
    queries = masked_queries(query[...])

    def queries_step(step, carried):
        totals = list(carried)
        for half in range(2):
            index = 2 * step + half
            valid = narrow < limit - index * TS
            for head in range(2):
                key = kvt[index, head * 128 : head * 128 + 256]
                value = kvt[index, 384 + head * 128 : 512 + head * 128]
                lanes = pl.ds(head * 128, 128)
                score = jnp.dot(queries[head], key, preferred_element_type=f32)
                score = score * score_bits - lse[:, lanes][:, :1]
                weight = jnp.exp2(jnp.where(valid, score, -1e30))
                slope = jnp.dot(grad[:, lanes], value, preferred_element_type=f32)
                low = (weight * (slope - delta[:, lanes][:, :1])).astype(bf16)
                totals[head] = totals[head] + contract(low, key)
        return tuple(totals)

    totals = lax.fori_loop(0, steps, queries_step, (jnp.zeros((TS, 256), f32),) * 2)
    edge = lax.broadcasted_iota(jnp.int32, (TS, 128), 1) < DR
    dq[:, 0:128] = totals[0][:, :128] * score_scale
    dq[:, 128:256] = jnp.where(edge, totals[0][:, 128:], totals[1][:, :128]) * score_scale
    dq[:, 256:384] = totals[1][:, 128:] * score_scale

    bar = jnp.where(places < live, places, 2 * ROWS * TS)
    keys = masked_queries(near[:, :384])

    def keys_step(step, carried):
        valid = wide >= bar - step * width
        queries = query_all[pl.ds(2 * step, 2)].reshape(width, query_all.shape[2])
        grads = grad_all[pl.ds(2 * step, 2)].reshape(width, 256)
        numbers = stats[pl.ds(2 * step, 2)]
        numbers = jnp.concatenate([numbers[0], numbers[1]], axis=1)
        found = []
        for head in range(2):
            key_total, value_total = carried[head]
            asked = queries[:, head * 128 : head * 128 + 256]
            given = grads[:, head * 128 : head * 128 + 128]
            score = contract(keys[head], asked) * score_bits - numbers[head : head + 1]
            weight = jnp.exp2(jnp.where(valid, score, -1e30))
            value_total = value_total + jnp.dot(
                weight.astype(bf16), given, preferred_element_type=f32
            )
            value = near[:, 384 + head * 128 : 512 + head * 128]
            slope = contract(value, given) - numbers[2 + head : 3 + head]
            low = (weight * slope).astype(bf16)
            key_total = key_total + jnp.dot(low, asked, preferred_element_type=f32)
            found.append((key_total, value_total))
        return tuple(found)

    zero = (jnp.zeros((TS, 256), f32), jnp.zeros((TS, 128), f32))
    last_step = jnp.where(mine * TS < live, ROWS // 2, 0)
    totals = lax.fori_loop(lax.div(mine, 2), last_step, keys_step, (zero, zero))
    dk[:, 0:128] = totals[0][0][:, :128] * score_scale
    dk[:, 128:256] = jnp.where(edge, totals[0][0][:, 128:], totals[1][0][:, :128]) * score_scale
    dk[:, 256:384] = totals[1][0][:, 128:] * score_scale
    dv[:, 0:128] = totals[0][1]
    dv[:, 128:256] = totals[1][1]


def attend_back(lens, query, kvt, grad, lse, delta, near, query_all, grad_all, stats):
    def lanes(width):
        return pl.BlockSpec((TS, width), lambda s: (s, 0))

    return pl.pallas_call(
        attend_back_body,
        name="attend_back",
        grid=(2,),
        out_shape=(
            shape_of((2 * TS, 384), f32),
            shape_of((2 * TS, 384), f32),
            shape_of((2 * TS, 256), f32),
        ),
        in_specs=[
            pl.BlockSpec(memory_space=pltpu.SMEM),
            lanes(384),
            pl.BlockSpec((ROWS, 640, TS), lambda s: (0, 0, s)),
            lanes(256),
            lanes(256),
            lanes(256),
            lanes(640),
            pl.BlockSpec((ROWS, TS, query_all.shape[2]), lambda s: (0, s, 0)),
            pl.BlockSpec((ROWS, TS, 256), lambda s: (0, s, 0)),
            pl.BlockSpec((ROWS, 8, TS), lambda s: (0, 0, s)),
        ],
        out_specs=(lanes(384), lanes(384), lanes(256)),
        compiler_params=pltpu.CompilerParams(vmem_limit_bytes=VMEM_BYTES),
        cost_estimate=pl.CostEstimate(
            flops=12 * 10**9, bytes_accessed=24 * 10**6, transcendentals=8 * 10**6
        ),
    )(lens, query, kvt, grad, lse, delta, near, query_all, grad_all, stats)


def project_back_body(
    dq, dk, dv, cos, sin, query_up, latent_up, query_in, latent_in, query_raw, latent_raw,
    query_gain, latent_gain, query_up_grad, latent_up_grad, query_grad, latent_grad, numbers,
):
    def turn_back(tile):
        return tile * cos[...] - swap_halves(tile) * sin[...]

    queries = jnp.concatenate(
        [dq[:, :128], turn_back(dq[:, 128:256]), dq[:, 256:]], axis=1
    ).astype(bf16)
    middle = dk[:, 128:256]
    middle = middle + pltpu.roll(middle, DR, 1)
    rope = turn_back(middle)
    pairs = jnp.concatenate(
        [dk[:, :128], dv[:, :128], dk[:, 256:], dv[:, 128:]], axis=1
    ).astype(bf16)
    query_up_grad[...] = jnp.dot(query_in[...], queries, preferred_element_type=f32).astype(bf16)
    latent_up_grad[...] = jnp.dot(latent_in[...], pairs, preferred_element_type=f32).astype(bf16)
    back = contract(query_up[...], queries)
    query_grad[...] = back.astype(bf16)
    numbers[...] = jnp.zeros_like(numbers)
    numbers[0:1] = jnp.sum(back * query_gain[...] * query_raw[...].astype(f32), axis=0, keepdims=True)
    back = contract(latent_up[...], pairs)
    numbers[1:2] = jnp.sum(
        back * latent_gain[...] * latent_raw[...].astype(f32), axis=0, keepdims=True
    )
    latent_grad[:KL] = back.astype(bf16)
    latent_grad[KL:] = rope.T[:DR].astype(bf16)


def project_back(*terms):
    query_up, latent_up, query_in, latent_in = terms[5:9]
    return pl.pallas_call(
        project_back_body,
        name="project_back",
        out_shape=(
            shape_of(query_up.shape, bf16),
            shape_of(latent_up.shape, bf16),
            shape_of(query_in.shape, bf16),
            shape_of((KL + DR, 2 * TS), bf16),
            shape_of((8, 2 * TS), f32),
        ),
        in_specs=[pl.BlockSpec(memory_space=VM)] * len(terms),
        out_specs=(pl.BlockSpec(memory_space=VM),) * 5,
        compiler_params=pltpu.CompilerParams(vmem_limit_bytes=VMEM_BYTES),
        cost_estimate=pl.CostEstimate(
            flops=2 * 10**9, bytes_accessed=16 * 10**6, transcendentals=0
        ),
    )(*terms)


def silu_parts(gate_value):
    sigmoid_value = 1.0 / (1.0 + jnp.exp(-gate_value))
    return (gate_value * sigmoid_value, sigmoid_value * (1.0 + gate_value * (1.0 - sigmoid_value)))


def transposed(left, right):
    return lax.dot_general(left, right, (((0,), (0,)), ((), ())), preferred_element_type=f32)


def shared_body(normed, grad, gate, up, down, branch, back_grad, weight_grad):
    normed_value, grad_value = normed[...], grad[...]
    gate_value = jnp.dot(normed_value, gate[...], preferred_element_type=f32)
    up_value = jnp.dot(normed_value, up[...], preferred_element_type=f32)
    silu_value, slope = silu_parts(gate_value)
    act = (silu_value * up_value).astype(bf16)
    act_grad = contract(grad_value, down[...])
    gate_low = (act_grad * up_value * slope).astype(bf16)
    up_low = (act_grad * silu_value).astype(bf16)
    branch[...] = jnp.dot(act, down[...], preferred_element_type=f32)
    back_grad[...] = contract(gate_low, gate[...]) + contract(up_low, up[...])
    lanes = weight_grad.shape[1] // 3
    blank = jnp.zeros((gate_low.shape[0], lanes - gate_low.shape[1]), bf16)
    parts = ((normed_value, gate_low), (normed_value, up_low), (grad_value, act))
    for index, (left, right) in enumerate(parts):
        right = jnp.concatenate([right, blank], axis=1)
        weight_grad[:, index * lanes : (index + 1) * lanes] = transposed(left, right).astype(bf16)


def shared_experts(normed, grad, gate, up, down):
    units = gate.shape[1]
    return pl.pallas_call(
        shared_body,
        name="shared_experts",
        out_shape=(
            shape_of((2 * TS, D), f32),
            shape_of((2 * TS, D), f32),
            shape_of((D, 3 * (units + (-units) % 128)), bf16),
        ),
        in_specs=[pl.BlockSpec(memory_space=VM)] * 5,
        out_specs=(pl.BlockSpec(memory_space=VM),) * 3,
        compiler_params=pltpu.CompilerParams(vmem_limit_bytes=VMEM_BYTES),
        cost_estimate=pl.CostEstimate(
            flops=8 * 10**9, bytes_accessed=24 * 10**6, transcendentals=10**6
        ),
    )(normed, grad, gate, up, down)


def experts_body(
    slots, gates, normed, grad, branch_in, back_in, w_in, w_down,
    branch, back_grad, gate_grad, w_in_grad, w_down_grad,
    dispatch, taken, taken_turned, given, routed, result, back_sum, branch_sum, back_total,
):
    expert, step = pl.program_id(0), pl.program_id(1)
    steps = pl.num_programs(1)
    capacity = dispatch.shape[0]
    units = w_down.shape[1]

    @pl.when(step == 0)
    def _():
        places = lax.broadcasted_iota(jnp.int32, dispatch.shape, 0)
        chosen = places == slots[pl.ds(expert, 1)]
        dispatch[...] = chosen.astype(bf16)
        weight = jnp.sum(jnp.where(chosen, gates[pl.ds(expert, 1)], 0.0), axis=1, keepdims=True)
        rows = jnp.dot(dispatch[...], normed[...], preferred_element_type=f32).astype(bf16)
        taken[...] = rows
        taken_turned[...] = rows.T
        grads = jnp.dot(dispatch[...], grad[...], preferred_element_type=f32)
        given[...] = grads.astype(bf16)
        routed[...] = (weight * grads).astype(bf16)
        result[...] = jnp.zeros_like(result)
        back_sum[...] = jnp.zeros_like(back_sum)

    weights = jnp.concatenate([w_in[0, 0], w_in[0, 1]], axis=1)
    hidden = jnp.dot(taken[...], weights, preferred_element_type=f32)
    gate_value, up_value = hidden[:, :units], hidden[:, units:]
    silu_value, slope = silu_parts(gate_value)
    act = (silu_value * up_value).astype(bf16)
    act_grad = contract(routed[...], w_down[0])
    low = jnp.concatenate(
        [
            (act_grad * up_value * slope).astype(bf16),
            (act_grad * silu_value).astype(bf16),
        ],
        axis=1,
    )
    result[...] += jnp.dot(act, w_down[0], preferred_element_type=f32)
    back_sum[...] += contract(low, weights)
    in_grad = jnp.dot(taken_turned[...], low, preferred_element_type=f32).astype(bf16)
    w_in_grad[0, 0] = in_grad[:, :units]
    w_in_grad[0, 1] = in_grad[:, units:]
    w_down_grad[...] = transposed(act, routed[...]).astype(bf16)

    @pl.when(step == steps - 1)
    def _():
        places = lax.broadcasted_iota(jnp.int32, dispatch.shape, 0)
        chosen = places == slots[pl.ds(expert, 1)]
        weight = jnp.sum(jnp.where(chosen, gates[pl.ds(expert, 1)], 0.0), axis=1, keepdims=True)
        number = jnp.sum(result[...] * given[...].astype(f32), axis=1, keepdims=True)
        gate_grad[pl.ds(expert, 1)] = jnp.sum(
            jnp.where(chosen, number, 0.0), axis=0, keepdims=True
        )
        outward = transposed(dispatch[...], (weight * result[...]).astype(bf16))
        inward = transposed(dispatch[...], back_sum[...].astype(bf16))

        @pl.when(expert == 0)
        def _():
            branch_sum[...] = branch_in[...] + outward
            back_total[...] = back_in[...] + inward

        @pl.when(expert == EXP_DEV - 1)
        def _():
            branch[...] = (branch_sum[...] + outward).astype(bf16)
            back_grad[...] = (back_total[...] + inward).astype(bf16)


def experts(capacity, slots, gates, normed, grad, branch_in, back_in, w_in, w_down):
    units = 128
    steps = w_down.shape[1] // units
    whole = pl.BlockSpec(memory_space=VM)
    in_block = pl.BlockSpec((1, 2, D, units), lambda e, k: (e, 0, 0, k))
    down_out = pl.BlockSpec((units, D), lambda e, k: (k, e))
    down_block = pl.BlockSpec((1, units, D), lambda e, k: (e, k, 0))
    return pl.pallas_call(
        experts_body,
        name="experts",
        grid=(EXP_DEV, steps),
        out_shape=(
            shape_of((2 * TS, D), bf16),
            shape_of((2 * TS, D), bf16),
            shape_of((8, 2 * TS), f32),
            shape_of(w_in.shape, bf16),
            shape_of((w_down.shape[1], EXP_DEV * D), bf16),
        ),
        in_specs=[whole] * 6 + [in_block, down_block],
        out_specs=(whole, whole, whole, in_block, down_out),
        scratch_shapes=[
            pltpu.VMEM((capacity, 2 * TS), bf16),
            pltpu.VMEM((capacity, D), bf16),
            pltpu.VMEM((D, capacity), bf16),
            pltpu.VMEM((capacity, D), bf16),
            pltpu.VMEM((capacity, D), bf16),
            pltpu.VMEM((capacity, D), f32),
            pltpu.VMEM((capacity, D), f32),
            pltpu.VMEM((2 * TS, D), f32),
            pltpu.VMEM((2 * TS, D), f32),
        ],
        compiler_params=pltpu.CompilerParams(vmem_limit_bytes=VMEM_BYTES),
        cost_estimate=pl.CostEstimate(
            flops=40 * 10**9, bytes_accessed=80 * 10**6, transcendentals=10**6
        ),
    )(slots, gates, normed, grad, branch_in, back_in, w_in, w_down)


def second_back_body(
    normed_sum, logits, router, hidden, attention, grad, gain, out_weight, attended,
    attended_grad, delta, delta_rows, out_grad, residual_here, router_grad, gain_grad, whole,
):
    total = logits[0]
    for index in range(1, COLS):
        total = total + logits[index]
    logit_low = total.T.astype(bf16)
    spare = jnp.zeros((2 * TS, router.shape[1] - 256 - logit_low.shape[1]), f32)
    wide = jnp.concatenate([spare, total.T], axis=1).astype(bf16)
    normed_grad = normed_sum[...].astype(f32) + contract(wide, router[:, 256:])
    residual = hidden[...].astype(f32) + attention[...].astype(f32)
    scale = lax.rsqrt(jnp.mean(residual * residual, axis=1, keepdims=True) + eps)
    normed = residual * scale
    router_grad[...] = transposed((normed * gain[...]).astype(bf16), logit_low).astype(bf16)
    gain_grad[...] = jnp.broadcast_to(
        jnp.sum(normed_grad * normed, axis=0, keepdims=True), gain_grad.shape
    )
    weighted = normed_grad * gain[...]
    inner = jnp.mean(weighted * residual, axis=1, keepdims=True)
    residual_grad = (
        grad[...].astype(f32) + scale * weighted - residual * (scale * scale * scale * inner)
    )
    whole[...] = residual_grad
    width = residual_here.shape[1]
    first = pl.multiple_of(lax.axis_index("col") * width, 128)
    residual_here[...] = whole[:, pl.ds(first, width)]
    low = residual_grad.astype(bf16)
    found = contract(low, out_weight[...]).astype(bf16)
    attended_grad[...] = found
    weights = transposed(attended[...].astype(bf16), low).astype(bf16)
    for index in range(ROWS):
        out_grad[index] = weights[:, index * 128 : (index + 1) * 128]
    numbers = found.astype(f32) * attended[...]
    delta_rows[...] = jnp.zeros_like(delta_rows)
    for head in range(2):
        lanes = slice(head * 128, head * 128 + 128)
        number = jnp.sum(numbers[:, lanes], axis=1, keepdims=True)
        number = jnp.broadcast_to(number, (2 * TS, 128))
        delta[:, lanes] = number
        delta_rows[head : head + 1] = number.T[:1]


def second_back(*terms):
    rows = 2 * TS
    outs = (
        shape_of((rows, 256), bf16),
        shape_of((rows, 256), f32),
        shape_of((8, rows), f32),
        shape_of((ROWS, 256, D // ROWS), bf16),
        shape_of((rows, D // COLS), f32),
        shape_of((D, 16), bf16),
        shape_of((8, D), f32),
    )
    return pl.pallas_call(
        second_back_body,
        name="second_back",
        out_shape=outs,
        in_specs=[pl.BlockSpec(memory_space=VM)] * len(terms),
        out_specs=(pl.BlockSpec(memory_space=VM),) * len(outs),
        scratch_shapes=[pltpu.VMEM((rows, D), f32)],
        compiler_params=pltpu.CompilerParams(vmem_limit_bytes=VMEM_BYTES),
        cost_estimate=pl.CostEstimate(
            flops=2 * 10**9, bytes_accessed=16 * 10**6, transcendentals=512
        ),
    )(*terms)


def first_project_body(hidden, gain, weight, normed, query, latent):
    values = hidden[...].astype(f32)
    scale = lax.rsqrt(jnp.mean(values * values, axis=1, keepdims=True) + eps)
    low = (values * scale * gain[...]).astype(bf16)
    normed[...] = low
    found = jnp.dot(low, weight[...], preferred_element_type=f32).T
    height = query.shape[0]
    live = KV_COLS
    query[...] = found[:height].astype(bf16)
    blank = jnp.zeros((latent.shape[0] - live, found.shape[1]), f32)
    latent[...] = jnp.concatenate([found[height : height + live], blank], axis=0).astype(bf16)


def simple_call(body, name, outs, terms, flops, moved, scratch=()):
    return pl.pallas_call(
        body,
        name=name,
        out_shape=outs,
        in_specs=[pl.BlockSpec(memory_space=VM)] * len(terms),
        out_specs=(pl.BlockSpec(memory_space=VM),) * len(outs),
        scratch_shapes=list(scratch),
        compiler_params=pltpu.CompilerParams(vmem_limit_bytes=VMEM_BYTES),
        cost_estimate=pl.CostEstimate(flops=flops, bytes_accessed=moved, transcendentals=0),
    )(*terms)


def first_project(hidden, gain, weight):
    outs = (
        shape_of((2 * TS, D), bf16),
        shape_of((QL // COLS, 2 * TS), bf16),
        shape_of((KV_COLS + (-KV_COLS) % 16, 2 * TS), bf16),
    )
    return simple_call(
        first_project_body, "first_project", outs, (hidden, gain, weight), 10**9, 6 * 10**6
    )


def swap_halves(tile):
    lane = lax.broadcasted_iota(jnp.int32, tile.shape, 1)
    lower = lax.rem(lane, DR) < DR // 2
    return jnp.where(lower, pltpu.roll(tile, 128 - DR // 2, 1), pltpu.roll(tile, DR // 2, 1))


def project_body(
    query_raw, latent_raw, query_gain, latent_gain, query_up, latent_up, cos, sin,
    query_in, latent_in, query, near,
):
    def normed(values, gain):
        scale = lax.rsqrt(jnp.mean(values * values, axis=0, keepdims=True) + eps)
        return (values * scale * gain).astype(bf16)

    low = normed(query_raw[...].astype(f32), query_gain[...])
    query_in[...] = low
    found = transposed(low, query_up[...])
    middle = found[:, 128:256]
    query[:, :128] = found[:, :128].astype(bf16)
    query[:, 128:256] = (middle * cos[...] + swap_halves(middle) * sin[...]).astype(bf16)
    query[:, 256:] = found[:, 256:].astype(bf16)
    raw = latent_raw[...].astype(f32)
    low = normed(raw[:KL], latent_gain[...])
    latent_in[...] = low
    found = transposed(low, latent_up[...]).astype(bf16)
    rope = jnp.concatenate([raw[KL:], raw[KL:]], axis=0).T
    near[:, :128] = found[:, :128]
    near[:, 128:256] = (rope * cos[...] + swap_halves(rope) * sin[...]).astype(bf16)
    near[:, 256:384] = found[:, 256:384]
    near[:, 384:512] = found[:, 128:256]
    near[:, 512:] = found[:, 384:]


def project(*terms):
    outs = (
        shape_of((QL, 2 * TS), bf16),
        shape_of((KL, 2 * TS), bf16),
        shape_of((2 * TS, 384), bf16),
        shape_of((2 * TS, 640), bf16),
    )
    return simple_call(project_body, "project", outs, terms, 2 * 10**9, 8 * 10**6)


def latent_back_body(
    query_sum, kv_sum, numbers, query_raw, kv_raw, query_gain, kv_gain, live, query_square, kv_square,
    normed, weight, gain, hidden, router_grad,
    first_part, first_numbers, down_grad, query_gain_grad, kv_gain_grad,
):
    total = numbers[0]
    for index in range(1, COLS):
        total = total + numbers[index]
    query_scale = lax.rsqrt(query_square[:1] + eps)
    kv_scale = lax.rsqrt(kv_square[:1] + eps)
    query_raw_value = query_raw[...].astype(f32)
    kv_raw_value = kv_raw[...].astype(f32)
    query_value = query_sum[...]
    kv_value = kv_sum[: kv_raw.shape[0]]
    query_normed, kv_normed = query_raw_value * query_scale, kv_raw_value * kv_scale
    query_gain_grad[...] = jnp.sum(query_value * query_normed, axis=1, keepdims=True)
    kv_gain_grad[...] = jnp.sum(kv_value * kv_normed, axis=1, keepdims=True)
    query_low = query_scale * (query_value * query_gain[...]) - query_normed * (
        query_scale * query_scale * (total[0:1] / QL)
    )
    kv_low = kv_scale * (kv_value * kv_gain[...]) - kv_normed * (
        kv_scale * kv_scale * (total[1:2] / KL)
    )
    kv_low = jnp.where(live[...] > 0, kv_low, kv_value)
    both = jnp.concatenate([query_low, kv_low], axis=0)
    turned = both.T.astype(bf16)
    width = turned.shape[1]
    part = contract(turned, weight[:, :width])
    first_part[...] = part.astype(bf16)
    number = jnp.sum(part * gain[...] * hidden[...].astype(f32), axis=1, keepdims=True)
    first_numbers[...] = jnp.broadcast_to(number, (2 * TS, 128)).T[:8]
    grads = transposed(normed[...], turned).astype(bf16)
    down_grad[:, :width] = grads
    down_grad[:, width:] = router_grad[...]


def latent_back(*terms):
    query_rows, kv_rows = terms[3].shape[0], terms[4].shape[0]
    outs = (
        shape_of((2 * TS, D), bf16),
        shape_of((8, 2 * TS), f32),
        shape_of(terms[11].shape, bf16),
        shape_of((query_rows, 1), f32),
        shape_of((kv_rows, 1), f32),
    )
    return simple_call(latent_back_body, "latent_back", outs, terms, 2 * 10**9, 10**7)


def rope_tables(positions, width):
    half_width = width // 2
    frequency = jnp.exp(
        -jnp.log(rope_base) * (2.0 * jnp.arange(half_width, dtype=jnp.float32) / width)
    )
    angles = positions.astype(jnp.float32)[:, None] * frequency[None, :]
    return (jnp.cos(angles), jnp.sin(angles))


def rms_scale(values):
    return lax.rsqrt(jnp.mean(values * values, axis=-1, keepdims=True) + eps)


def product(left, right):
    return jnp.dot(left, right, preferred_element_type=jnp.float32)


def left_product(left, right):
    return lax.dot_general(
        left, right, (((0,), (0,)), ((), ())), preferred_element_type=jnp.float32
    )


def right_product(left, right):
    return lax.dot_general(
        left, right, (((1,), (1,)), ((), ())), preferred_element_type=jnp.float32
    )


def turned_product(left, right):
    return lax.dot_general(
        left, right, (((0,), (1,)), ((), ())), preferred_element_type=jnp.float32
    )


def einsum(text, *terms):
    return jnp.einsum(text, *terms, preferred_element_type=f32)


def to_blocks(term):
    return term.reshape(2, RING, 2, term.shape[0] // ROWS, term.shape[1])


def local(
    hidden_in,
    gain_first,
    query_down,
    query_gain,
    query_up,
    latent_down,
    latent_gain,
    latent_up,
    attention_out,
    gain_second,
    router,
    expert_gate,
    expert_up,
    expert_down,
    shared_gate,
    shared_up,
    shared_down,
    seq_lens,
    routes,
    out_grad,
):
    row_index = lax.axis_index("row")
    col_index = lax.axis_index("col")
    seq_count, local_len, col_width = hidden_in.shape
    row_total = seq_count * local_len
    experts_all = EXP_DEV * COLS
    most_rows = (5 * local_len * TOPK + 4 * experts_all - 1) // (4 * experts_all)
    capacity = seq_count * most_rows
    query_cols = QL // COLS
    kv_cols = (KL + DR) // COLS

    def here(values, axis=-1):
        width = values.shape[axis] // COLS
        return lax.dynamic_slice_in_dim(values, col_index * width, width, axis)

    (
        hidden_low,
        grad_full,
        down_all,
        query_up_all,
        latent_up_all,
        attention_out_all,
        shared_gate_all,
        shared_up_all,
        shared_down_all,
        planes,
        down_chip,
    ) = front(
        hidden_in.reshape(row_total, col_width),
        out_grad.reshape(row_total, col_width),
        jnp.concatenate([query_down, latent_down, router], axis=1),
        query_up,
        latent_up,
        attention_out,
        shared_gate,
        shared_up,
        shared_down,
        expert_gate,
        jnp.pad(expert_down, ((0, 0), (0, (-expert_down.shape[1]) % 16), (0, 0))),
        expert_gate.shape[2],
    )
    expert_units = expert_gate.shape[2]
    latent_width = query_cols + kv_cols
    router_all = down_all[:, latent_width:]
    kv_pad = (-kv_cols) % 16
    normed_first, query_here, latent_here = first_project(hidden_low, gain_first[None], down_all)
    query_latent, _, latent_all, planes = latents(
        query_here,
        latent_here,
        expert_gate,
        expert_up,
        planes,
    )
    kv_latent = lax.dynamic_index_in_dim(latent_all, row_index, 1, False)
    kv_latent = kv_latent[:, :kv_cols].reshape(KL + DR, row_total)
    latent_pad = ((0, 0), (0, kv_pad), (0, 0))
    every_cos, every_sin = rope_tables(jnp.arange(ROWS * local_len, dtype=jnp.int32), DR)
    kvt_all = expand(
        latent_all,
        jnp.pad(
            jnp.pad(latent_up_all, ((0, DR), (0, 0))).reshape(COLS, kv_cols, -1), latent_pad
        ).reshape(COLS * (kv_cols + kv_pad), -1).T,
        jnp.pad(
            jnp.pad(latent_gain, (0, DR)).reshape(COLS, kv_cols, 1), latent_pad
        ).reshape(COLS * (kv_cols + kv_pad), 1),
        every_cos.T,
        every_sin.T,
    )
    lane = jnp.arange(2 * DR, dtype=jnp.int32)[None, :]
    position = row_index * local_len + jnp.arange(row_total, dtype=jnp.int32) % local_len
    frequency = jnp.exp(-math.log(rope_base) * (2.0 / DR) * (lane % (DR // 2)).astype(f32))
    angles = position.astype(f32)[:, None] * frequency
    tile_cos = jnp.cos(angles)
    tile_sin = jnp.where(lane % DR < DR // 2, -1.0, 1.0) * jnp.sin(angles)
    split = DN + DR
    query_up_pack = jnp.concatenate(
        [query_up_all[:, :split], query_up_all[:, split + DN :], query_up_all[:, split : split + DN]],
        axis=1,
    )
    query_input, latent_input, query_pack, near = project(
        query_latent,
        kv_latent,
        query_gain[:, None],
        latent_gain[:, None],
        query_up_pack,
        latent_up_all,
        tile_cos,
        tile_sin,
    )
    attended_float, lse, lse_rows = attend(seq_lens, query_pack, kvt_all)
    attended = attended_float.astype(bf16)
    attention_part = product(attended, attention_out_all).astype(bf16)
    attention_sum, planes, expert_down_all = attention_sum_over_col(
        attention_part, expert_up, down_chip, planes
    )
    expert_in_all = planes.reshape(EXP_DEV, 2, D, expert_units)
    attention_sum, query_late = lax.optimization_barrier((attention_sum, query_pack))
    query_all = lax.all_gather(query_late, "row", axis=0, tiled=False)

    residual_one = hidden_low.astype(f32) + attention_sum.astype(f32)
    scale_second = rms_scale(residual_one)
    normed_second = (residual_one * scale_second * gain_second).astype(bf16)
    logits = turned_product(router_all, normed_second)
    sigmoid_all = jax.nn.sigmoid(logits)
    routes_turned = routes.reshape(row_total, TOPK).T
    chosen = jnp.sum(
        (
            routes_turned[:, None, :] == jnp.arange(experts_all, dtype=jnp.int32)[None, :, None]
        ).astype(f32),
        axis=0,
    )
    weighted_sig = sigmoid_all * chosen
    denominator = jnp.sum(weighted_sig, axis=0, keepdims=True)
    gate_weights = route_scale * weighted_sig / denominator
    gate_here = here(gate_weights, 0)
    member = here(chosen, 0).reshape(EXP_DEV * seq_count, local_len)
    before = jnp.triu(jnp.ones((local_len, local_len), bf16), 1)
    rank = product(member.astype(bf16), before).reshape(EXP_DEV, seq_count, local_len)
    rank = rank + (jnp.arange(seq_count, dtype=f32) * most_rows)[None, :, None]
    slots = jnp.where(member.reshape(rank.shape) > 0, rank, float(capacity))
    slots = slots.astype(jnp.int32).reshape(EXP_DEV, row_total)
    shared_branch, shared_back, shared_grad = shared_experts(
        normed_second, grad_full, shared_gate_all, shared_up_all, shared_down_all
    )
    branch_part, normed_part, gate_grad_here, expert_in_part, expert_down_part = experts(
        capacity,
        slots,
        gate_here,
        normed_second,
        grad_full,
        shared_branch,
        shared_back,
        expert_in_all,
        expert_down_all,
    )
    expert_in_sum = lax.psum_scatter(
        expert_in_part.reshape(2 * EXP_DEV, D, expert_units),
        "row",
        scatter_dimension=1,
        tiled=True,
    )
    expert_down_sum = lax.psum_scatter(expert_down_part, "row", scatter_dimension=0, tiled=True)
    gate_grad_all = lax.dynamic_update_slice_in_dim(
        jnp.zeros((experts_all, row_total), f32), gate_grad_here[:EXP_DEV], col_index * EXP_DEV, 0
    )
    inner_sum = jnp.sum(gate_grad_all * gate_weights, axis=0, keepdims=True)
    logit_part = (
        sigmoid_all
        * (1.0 - sigmoid_all)
        * chosen
        / denominator
        * (route_scale * gate_grad_all - inner_sum)
    )
    normed_sum, logit_all = sum_over_col(
        "sum_normed", 5, normed_part, COL_CUT, (("col", experts_all),), logit_part
    )
    (
        attended_grad,
        delta,
        delta_rows,
        attention_out_grad,
        residual_here,
        router_grad,
        gain_second_grad,
    ) = second_back(
        normed_sum,
        logit_all,
        down_all,
        hidden_low,
        attention_sum,
        grad_full,
        gain_second[None],
        attention_out_all,
        attended_float,
    )
    gain_second_part = here(gain_second_grad[0])
    stats = jnp.concatenate([lse_rows[:2], delta_rows[:2], lse_rows[:4]], axis=0)
    attended_grad_all, stats_all, branch_here = back(attended_grad, stats, branch_part)
    hidden_here = here(hidden_low).astype(f32)
    attended_here = here(attention_sum).astype(f32)
    block_out = (
        (hidden_here + attended_here + branch_here).astype(bf16).reshape(seq_count, local_len, col_width)
    )
    dq, dk, dv = attend_back(
        seq_lens,
        query_pack,
        kvt_all,
        attended_grad,
        lse,
        delta,
        near,
        query_all,
        attended_grad_all,
        stats_all,
    )
    query_up_grad, latent_up_grad, query_in_grad, kv_part, numbers = project_back(
        dq,
        dk,
        dv,
        tile_cos,
        tile_sin,
        query_up_pack,
        latent_up_all,
        query_input,
        latent_input,
        query_latent,
        kv_latent[:KL],
        query_gain[:, None],
        latent_gain[:, None],
    )
    kv_part = jnp.pad(kv_part.reshape(COLS, kv_cols, row_total), latent_pad)
    shared_width = shared_gate.shape[1]
    (query_in_here, kv_in_here), numbers_all, summed = col_and_row(
        "sum_latents",
        7,
        "lead",
        (query_in_grad.reshape(COLS, query_cols, row_total), kv_part),
        ((query_cols, row_total), (kv_cols + kv_pad, row_total)),
        (128, 80),
        numbers,
        (attention_out_grad.reshape(2, RING, 2, col_width, D // ROWS),),
        (96,),
    )
    (attention_out_sum,) = summed
    is_latent = (col_index * kv_cols + jnp.arange(kv_cols)) < KL
    latent_gain_here = here(jnp.concatenate([latent_gain, jnp.ones((DR,), f32)]))
    query_square, kv_square = (
        jnp.broadcast_to(
            jnp.mean(jnp.square(values.astype(f32)), axis=0, keepdims=True), (8, row_total)
        )
        for values in (query_latent, kv_latent[:KL])
    )
    first_part, first_numbers, down_grads, query_gain_part, latent_gain_part = latent_back(
        query_in_here,
        kv_in_here,
        numbers_all,
        here(query_latent, 0),
        here(kv_latent, 0),
        here(query_gain)[:, None],
        latent_gain_here[:, None],
        is_latent.astype(f32)[:, None],
        query_square,
        kv_square,
        normed_first,
        down_all,
        gain_first[None],
        hidden_low,
        router_grad,
    )
    (first_here,), first_numbers_all, summed = col_and_row(
        "sum_first",
        8,
        "lane",
        (first_part,),
        ((row_total, col_width),),
        (384,),
        first_numbers,
        (
            to_blocks(down_grads),
            to_blocks(query_up_grad),
            to_blocks(latent_up_grad),
            to_blocks(shared_grad),
        ),
        (0, QL // ROWS, KL // ROWS, 64),
    )
    down_sum, query_up_sum, latent_up_sum, shared_sum = summed
    shared_lanes = shared_sum.shape[1] // 3
    shared_gate_sum, shared_up_sum, shared_down_sum = (
        shared_sum[:, part * shared_lanes : part * shared_lanes + shared_width]
        for part in range(3)
    )
    query_up_sum = jnp.concatenate(
        [query_up_sum[:, :split], query_up_sum[:, 2 * DN :], query_up_sum[:, split : 2 * DN]], axis=1
    )
    first_mean = (jnp.sum(first_numbers_all[:, 0], axis=0) / D)[:, None]
    scale_first = rms_scale(hidden_low.astype(f32))
    hidden_grad = (
        residual_here
        + scale_first * first_here * here(gain_first)
        - hidden_here * (scale_first * scale_first * scale_first) * first_mean
    ).reshape(seq_count, local_len, col_width)
    gain_first_part = jnp.sum(first_here * hidden_here * scale_first, axis=0)
    gains = jnp.concatenate(
        [
            gain_first_part,
            gain_second_part,
            query_gain_part[:, 0],
            jnp.zeros((64,), f32),
            latent_gain_part[:, 0],
            jnp.zeros((1024 - 768 - kv_cols,), f32),
        ]
    ).reshape(8, 128)
    gains_all = last(gains).reshape(COLS, 1024)
    expert_in_grad = expert_in_sum.reshape(EXP_DEV, 2, D // ROWS, expert_units).astype(f32)
    expert_down_grad = jnp.stack(
        [expert_down_sum[:, expert * D : (expert + 1) * D] for expert in range(EXP_DEV)], axis=0
    ).astype(f32)
    return (
        block_out,
        hidden_grad,
        gains_all[:, :col_width].reshape(D),
        down_sum[:, :query_cols],
        gains_all[:, 512 : 512 + query_cols].reshape(QL),
        query_up_sum,
        down_sum[:, query_cols:latent_width],
        gains_all[:, 768 : 768 + kv_cols].reshape(KL + DR)[:KL],
        latent_up_sum,
        attention_out_sum,
        gains_all[:, col_width : 2 * col_width].reshape(D),
        down_sum[:, latent_width:],
        expert_in_grad[:, 0],
        expert_in_grad[:, 1],
        expert_down_grad,
        shared_gate_sum,
        shared_up_sum,
        shared_down_sum.T,
    )


def solution(mesh):
    in_specs = (
        P(None, "row", "col"),
        P(),
        P("row", "col"),
        P(),
        P("row", "col"),
        P("row", "col"),
        P(),
        P("row", "col"),
        P("col", "row"),
        P(),
        P("row", None),
        P("col", "row", None),
        P("col", "row", None),
        P("col", "row", None),
        P("row", "col"),
        P("row", "col"),
        P("col", "row"),
        P(),
        P(None, "row", None),
        P(None, "row", "col"),
    )
    out_specs = (
        P(None, "row", "col"),
        P(None, "row", "col"),
        P(),
        P("row", "col"),
        P(),
        P("row", "col"),
        P("row", "col"),
        P(),
        P("row", "col"),
        P("col", "row"),
        P(),
        P("row", None),
        P("col", "row", None),
        P("col", "row", None),
        P("col", "row", None),
        P("row", "col"),
        P("row", "col"),
        P("col", "row"),
    )
    return jax.shard_map(local, mesh=mesh, in_specs=in_specs, out_specs=out_specs, check_vma=False)
```

```python
import functools
import math

import jax
import jax.numpy as jnp
from jax import lax
from jax.experimental import pallas as pl
from jax.experimental.pallas import tpu as pltpu
from jax.sharding import PartitionSpec as P

D = 2048
H = 16
DN = 128
DR = 64
DV = 128
QL = 1536
KL = 512
EXP_DEV = 2
TOPK = 6
ROWS = 16
COLS = 8
TS = 256
CUT = 208
COL_CUT = 400
LATENT_CUT = 5
FIRST_CUT = 384
DOWN_CUT = 112
SUM_CUT = 208
NORMED_CUT = 208
KV_COLS = (KL + DR) // COLS
SHARED_UNITS = 352

eps = 1e-06
route_scale = 2.446
rope_base = 50000.0
score_scale = 1.0 / math.sqrt(DN + DR)
score_bits = score_scale * math.log2(math.e)

bf16 = jnp.bfloat16
f32 = jnp.float32
ANY = pl.ANY
VM = pltpu.VMEM


def shape_of(shape, dtype):
    return jax.ShapeDtypeStruct(shape, dtype)

MESH = pl.DeviceIdType.MESH
RING = 4
VMEM_BYTES = 56 * 2**20


class Place:
    def __init__(self, axis):
        self.axis = axis
        self.index = lax.axis_index(axis)
        self.cores = 2 if axis == "row" else 1
        self.core = lax.rem(self.index, self.cores)
        self.ring = lax.rem(lax.div(self.index, self.cores), RING)
        self.pair = lax.div(self.index, self.cores * RING)

    def at(self, pair, ring, core=None):
        core = self.core if core is None else core
        return (pair * RING + ring) * self.cores + core

    def turn(self, step):
        return lax.rem(self.ring + step + RING, RING)

    def peers(self):
        found = [self.at(self.pair, self.turn(step)) for step in (1, 2, 3)]
        found.append(self.at(1 - self.pair, self.ring))
        if self.cores == 2:
            found.append(self.at(self.pair, self.ring, 1 - self.core))
        return found


class Net:
    def __init__(self, send_sems, recv_sems):
        self.send_sems, self.recv_sems = send_sems, recv_sems
        self.count = 0
        self.sent = []
        self.own = []

    def send(self, source, target, axis, index):
        number = self.count
        self.count += 1
        copy = pltpu.make_async_remote_copy(
            source,
            target,
            self.send_sems.at[number],
            self.recv_sems.at[number],
            device_id={axis: index},
            device_id_type=MESH,
        )
        copy.start()
        self.sent.append(copy)
        return number

    def receive(self, number, target, axis, index):
        pltpu.make_async_remote_copy(
            target,
            target,
            self.send_sems.at[number],
            self.recv_sems.at[number],
            device_id={axis: index},
            device_id_type=MESH,
        ).wait_recv()

    def local(self, source, target):
        number = self.count
        self.count += 1
        copy = pltpu.make_async_copy(source, target, self.send_sems.at[number])
        copy.start()
        self.own.append(copy)

    def settle(self):
        for copy in self.own:
            copy.wait()
        self.own = []

    def finish(self):
        for copy in self.sent:
            copy.wait_send()
        self.settle()


def greet(*places, everyone=False):
    barrier = pltpu.get_barrier_semaphore()
    count = 0
    for place in places:
        members = lax.axis_size(place.axis)
        all_peers = [lax.rem(place.index + step, members) for step in range(1, members)]
        for peer in all_peers if everyone else place.peers():
            pl.semaphore_signal(
                barrier, inc=1, device_id={place.axis: peer}, device_id_type=MESH
            )
            count += 1
    pl.semaphore_wait(barrier, count)


class Gather:
    def __init__(self, net, place, source, slot, rows, cut, relay=False, cross=None):
        self.net, self.place, self.source, self.slot = net, place, source, slot
        self.rows, self.cut, self.relay = rows, cut, relay
        self.first, self.second = (0, cut), (cut, rows - cut)
        self.crossed = []
        if place.cores == 2:
            partner = place.at(place.pair, place.ring, 1 - place.core)

            def other(pair, ring, low, count):
                return slot(place.at(pair, ring, 1 - place.core), low, count)

            cross = (place.axis, partner, other)
        self.cross = cross

    def _send(self, owner, part, peer, own=False):
        piece = self.slot(owner, *part)
        start = self.source.at[pl.ds(*part)] if own else piece
        return self.net.send(start, piece, self.place.axis, peer)

    def _receive(self, number, pair, ring, part, peer):
        place = self.place
        self.net.receive(number, self.slot(place.at(pair, ring), *part), place.axis, peer)

    def _cross(self, pair, ring, part, own=False):
        if self.cross is None:
            return
        piece = self.slot(self.place.at(pair, ring), *part)
        start = self.source.at[pl.ds(*part)] if own else piece
        number = self.net.send(start, piece, self.cross[0], self.cross[1])
        self.crossed.append((number, pair, ring, part))

    def _halves(self, part):
        low, count = part
        unit = 16 if count % 16 == 0 else 1
        half = max(count // 2 // unit, 1) * unit
        return (low, half), (low + half, count - half)

    def _relays(self, part):
        return self.relay and part[1] >= (32 if part[1] % 16 == 0 else 2)

    def _round(self, pair, part, own=False):
        place = self.place
        owner = place.at(pair, place.ring)
        steps = (1, 3) if self._relays(part) else (1, 3, 2)
        return {
            step: self._send(owner, part, place.at(place.pair, place.turn(step)), own)
            for step in steps
        }

    def _pass(self, numbers, pair, part, then):
        place = self.place
        passed = {}
        for step in (1, 3):
            ring = place.turn(-step)
            self._receive(numbers[step], pair, ring, part, place.at(place.pair, ring))
            if self._relays(part):
                half = self._halves(part)[step // 2]
                passed[step] = self._send(
                    place.at(pair, ring), half, place.at(place.pair, place.turn(step))
                )
            then(pair, ring, part)
        return passed

    def _meet(self, numbers, passed, pair, part, then):
        place = self.place
        far = place.turn(2)
        if self._relays(part):
            for step in (1, 3):
                half = self._halves(part)[step // 2]
                self._receive(
                    passed[step], pair, far, half, place.at(place.pair, place.turn(-step))
                )
        else:
            self._receive(numbers[2], pair, far, part, place.at(place.pair, far))
        then(pair, far, part)

    def start_first(self):
        place = self.place
        if self.cut:
            other = place.at(1 - place.pair, place.ring)
            self.across = self._send(place.index, self.first, other, True)
            self.near = self._round(place.pair, self.first, True)

    def start_second(self):
        place = self.place
        if self.second[1]:
            self.round = self._round(place.pair, self.second, True)
            other = place.at(1 - place.pair, place.ring)
            self.over = [(place.ring, self._send(place.index, self.second, other, True))]
        self._cross(place.pair, place.ring, (0, self.rows), True)
        self.net.local(self.source, self.slot(place.index, 0, self.rows))

    def start(self):
        self.start_first()
        self.start_second()

    def forward_first(self):
        place = self.place
        if self.cut:
            other = place.at(1 - place.pair, place.ring)
            self._receive(self.across, 1 - place.pair, place.ring, self.first, other)
            self.far = self._round(1 - place.pair, self.first)
            self._cross(1 - place.pair, place.ring, self.first)

    def _over(self, pair, ring, part):
        place = self.place
        other = place.at(1 - place.pair, place.ring)
        self.over.append((ring, self._send(place.at(pair, ring), part, other)))
        self._cross(pair, ring, part)

    def near_pass(self):
        place = self.place
        if self.second[1]:
            self.round_passed = self._pass(self.round, place.pair, self.second, self._over)
        if self.cut:
            self.near_passed = self._pass(self.near, place.pair, self.first, self._cross)

    def far_pass(self):
        if self.cut:
            pair = 1 - self.place.pair
            self.far_passed = self._pass(self.far, pair, self.first, self._cross)

    def near_meet(self):
        place = self.place
        if self.second[1]:
            self._meet(self.round, self.round_passed, place.pair, self.second, self._over)
        if self.cut:
            self._meet(self.near, self.near_passed, place.pair, self.first, self._cross)

    def far_meet(self):
        place = self.place
        if self.cut:
            self._meet(self.far, self.far_passed, 1 - place.pair, self.first, self._cross)
        if self.second[1]:
            other = place.at(1 - place.pair, place.ring)
            for ring, number in self.over:
                self._receive(number, 1 - place.pair, ring, self.second, other)
                self._cross(1 - place.pair, ring, self.second)

    def end(self):
        for number, pair, ring, part in self.crossed:
            axis, partner, other = self.cross
            self.net.receive(number, other(pair, ring, *part), axis, partner)


class Direct:
    def __init__(self, net, place, source, ref, count):
        self.net, self.place, self.source, self.ref, self.count = net, place, source, ref, count

    def start(self):
        place = self.place
        self.numbers = [
            self.net.send(
                self.source,
                self.ref.at[place.index],
                place.axis,
                lax.rem(place.index + step, self.count),
            )
            for step in range(1, self.count)
        ]
        self.net.local(self.source, self.ref.at[place.index])

    def land(self):
        place = self.place
        for step, number in zip(range(1, self.count), self.numbers):
            owner = lax.rem(place.index + self.count - step, self.count)
            self.net.receive(number, self.ref.at[owner], place.axis, owner)


STAGES = ("start", "forward_first", "near_pass", "far_pass", "near_meet", "far_meet", "end")


def run_stages(gathers, stages=STAGES):
    for stage in stages:
        for gather in gathers:
            getattr(gather, stage)()


def run_gathers(*gathers):
    run_stages(gathers)


def row_slots(ref, rows):
    return lambda owner, low, count: ref.at[
        pl.ds(pl.multiple_of(owner * rows + low, 16), count)
    ]


def lead_slots(ref):
    return lambda owner, low, count: ref.at[owner, pl.ds(low, count)]


def lane_slots(ref, width):
    return lambda owner, low, count: ref.at[
        pl.ds(low, count), pl.ds(pl.multiple_of(owner * width, 128), width)
    ]


class Scatter:
    def __init__(self, net, place, block, rows, cut, scratch, keep):
        self.net, self.place, self.block, self.rows, self.cut = net, place, block, rows, cut
        self.scratch, self.keep = scratch, keep
        self.first, self.second = (0, cut), (cut, rows - cut)

    @staticmethod
    def scratch_of(rows, cut, width, dtype=jnp.bfloat16):
        shapes = []
        if cut:
            shapes += [(3, 2, cut, width), (2, cut, width)]
        if rows - cut:
            shapes += [(4, rows - cut, width), (4, rows - cut, width), (3, rows - cut, width)]
        return [pltpu.VMEM(shape, dtype) for shape in shapes]

    def _refs(self):
        refs = list(self.scratch)
        first = refs[:2] if self.cut else None
        second = refs[-3:] if self.second[1] else None
        return first, second

    def _owner(self, pair, ring):
        return self.place.at(pair, ring)

    def start(self):
        place, net = self.place, self.net
        first, second = self._refs()
        if first:
            self.round = [
                [
                    net.send(
                        self.block(self._owner(pair, place.turn(step)), *self.first),
                        first[0].at[step - 1, pair],
                        place.axis,
                        place.at(place.pair, place.turn(step)),
                    )
                    for pair in (0, 1)
                ]
                for step in (1, 2, 3)
            ]
        if second:
            self.across = [
                net.send(
                    self.block(self._owner(1 - place.pair, ring), *self.second),
                    second[0].at[ring],
                    place.axis,
                    place.at(1 - place.pair, place.ring),
                )
                for ring in range(RING)
            ]

    def forward_second(self):
        place, net = self.place, self.net
        first, second = self._refs()
        if not second:
            return
        other = place.at(1 - place.pair, place.ring)
        for ring in range(RING):
            net.receive(self.across[ring], second[0].at[ring], place.axis, other)
        for ring in range(RING):
            total = (
                self.block(self._owner(place.pair, ring), *self.second)[...].astype(jnp.float32)
                + second[0][ring].astype(jnp.float32)
            )
            second[1][ring] = total.astype(second[1].dtype)
        self.last = [
            net.send(
                second[1].at[place.turn(step)],
                second[2].at[step - 1],
                place.axis,
                place.at(place.pair, place.turn(step)),
            )
            for step in (1, 2, 3)
        ]

    def forward_first(self):
        place, net = self.place, self.net
        first, second = self._refs()
        if not first:
            return
        for step in (1, 3, 2):
            owner = place.at(place.pair, place.turn(-step))
            for pair in (0, 1):
                net.receive(self.round[step - 1][pair], first[0].at[step - 1, pair], place.axis, owner)
        other = 1 - place.pair
        total = self.block(self._owner(other, place.ring), *self.first)[...].astype(jnp.float32)
        for step in range(3):
            total = total + first[0][step, other].astype(jnp.float32)
        first[1][0] = total.astype(first[1].dtype)
        self.over = net.send(
            first[1].at[0], first[1].at[1], place.axis, place.at(other, place.ring)
        )

    def end_first(self):
        place, net = self.place, self.net
        first, second = self._refs()
        if not first:
            return
        total = self.block(self._owner(place.pair, place.ring), *self.first)[...].astype(jnp.float32)
        for step in range(3):
            total = total + first[0][step, place.pair].astype(jnp.float32)
        other = place.at(1 - place.pair, place.ring)
        net.receive(self.over, first[1].at[1], place.axis, other)
        self.keep(self.first, total + first[1][1].astype(jnp.float32))

    def end_second(self):
        place, net = self.place, self.net
        first, second = self._refs()
        if not second:
            return
        total = (
            self.block(self._owner(place.pair, place.ring), *self.second)[...].astype(jnp.float32)
            + second[0][place.ring].astype(jnp.float32)
        )
        for step in (1, 3, 2):
            owner = place.at(place.pair, place.turn(-step))
            net.receive(self.last[step - 1], second[2].at[step - 1], place.axis, owner)
            total = total + second[2][step - 1].astype(jnp.float32)
        self.keep(self.second, total)


def comm_call(body, name, collective_id, out_shapes, in_spaces, out_spaces, copies, scratch=(), args=(), aliases=None):
    return pl.pallas_call(
        body,
        name=name,
        out_shape=out_shapes,
        in_specs=[pl.BlockSpec(memory_space=space) for space in in_spaces],
        out_specs=tuple(pl.BlockSpec(memory_space=space) for space in out_spaces),
        scratch_shapes=[
            pltpu.SemaphoreType.DMA((copies,)),
            pltpu.SemaphoreType.DMA((copies,)),
            *scratch,
        ],
        input_output_aliases=aliases or {},
        compiler_params=pltpu.CompilerParams(
            collective_id=collective_id, has_side_effects=True, vmem_limit_bytes=VMEM_BYTES
        ),
    )(*args)


def plane_slots(ref, plane):
    return lambda owner, low, count: ref.at[
        plane, pl.ds(pl.multiple_of(owner * (D // ROWS) + low, 16), count)
    ]


def plane_gather(net, row, source, ref, plane, cut):
    return Gather(net, row, source, plane_slots(ref, plane), D // ROWS, cut, True)


def front_body(hidden, grad, w1, qu, lu, ao, sg, su, sd, gate, down, *rest):
    hidden_all, grad_all, w1_all, qu_all, lu_all, ao_all, sg_all, su_all, sd_all = rest[:9]
    planes, down_chip, ss, rs, down_other = rest[9:]
    row, col = Place("row"), Place("col")
    greet(row, col)
    net = Net(ss, rs)
    partner = row.at(row.pair, row.ring, 1 - row.core)
    gathers = [
        Gather(net, col, hidden, lane_slots(hidden_all, D // COLS), 2 * TS, 2 * TS, True),
        *(
            Gather(net, row, term, row_slots(ref, term.shape[0]), term.shape[0], cut, True)
            for term, ref, cut in (
                (w1, w1_all, 128),
                (qu, qu_all, 96),
                (lu, lu_all, 32),
            )
        ),
        *(
            Gather(net, row, term, lane_slots(ref, term.shape[1]), term.shape[0], cut, True)
            for term, ref, cut in (
                (ao, ao_all, 192),
                (sg, sg_all, 352),
                (su, su_all, 256),
                (sd, sd_all, 256),
            )
        ),
        plane_gather(net, row, gate.at[0], planes, 0, 64),
        Gather(net, col, grad, lane_slots(grad_all, D // COLS), 2 * TS, 2 * TS, True),
    ]
    number = net.send(down.at[1 - row.core], down_other, "row", partner)
    run_stages(gathers, STAGES[:1])
    net.receive(number, down_other, "row", partner)
    height = down_chip.shape[0] // 2
    own = down[row.core].astype(f32)[:height]
    given = down_other[...].astype(f32)[:height]
    even = row.core == 0
    down_chip[...] = jnp.concatenate(
        [jnp.where(even, own, given), jnp.where(even, given, own)], axis=0
    ).astype(bf16)
    run_stages(gathers, STAGES[1:])
    net.finish()


def stacked(term):
    return shape_of((ROWS * term.shape[0], term.shape[1]), term.dtype)


def side_by_side(term):
    return shape_of((term.shape[0], ROWS * term.shape[1]), term.dtype)


def front(hidden, grad, w1, qu, lu, ao, sg, su, sd, gate, down, units):
    return comm_call(
        front_body,
        "gather_front",
        1,
        (
            shape_of((2 * TS, D), bf16),
            shape_of((2 * TS, D), bf16),
            stacked(w1),
            stacked(qu),
            stacked(lu),
            side_by_side(ao),
            side_by_side(sg),
            side_by_side(su),
            side_by_side(sd),
            shape_of((2 * EXP_DEV, D, units), bf16),
            shape_of((2 * units // ROWS, D), bf16),
        ),
        [ANY] * 10 + [VM],
        [ANY] * 10 + [VM],
        256,
        [pltpu.VMEM(down.shape[1:], bf16)],
        (hidden, grad, w1, qu, lu, ao, sg, su, sd, gate, down),
    )


def latent_body(query, latent, gate, up, _, query_all, rows_all, latent_all, planes, ss, rs):
    row, col = Place("row"), Place("col")
    greet(row, col)
    net = Net(ss, rs)
    queries = Gather(
        net, col, query, row_slots(query_all, query.shape[0]), query.shape[0], 192, True
    )
    weights = [
        plane_gather(net, row, up.at[0], planes, 1, 96),
        plane_gather(net, row, gate.at[1], planes, 2, 96),
    ]
    rows = Gather(net, row, latent, lead_slots(rows_all), latent.shape[0], 48)
    half = ROWS // 2
    base = row.core * half
    partner = row.at(row.pair, row.ring, 1 - row.core)

    def slot(owner, low, count):
        return latent_all.at[owner, pl.ds(base + low, count)]

    def other(pair, ring, low, count):
        return latent_all.at[col.at(pair, ring), pl.ds(half - base + low, count)]

    every = Gather(
        net, col, rows_all.at[pl.ds(base, half)], slot, half, LATENT_CUT, True, ("row", partner, other)
    )
    run_stages((rows, queries), STAGES[:1])
    run_stages((rows,), STAGES[1:])
    net.settle()
    run_stages((every, *weights), STAGES[:1])
    run_stages((queries, every, *weights), STAGES[1:])
    net.finish()


def latents(query, latent, gate, up, planes):
    return comm_call(
        latent_body,
        "gather_latents",
        2,
        (
            shape_of((COLS * query.shape[0], query.shape[1]), bf16),
            shape_of((ROWS, *latent.shape), bf16),
            shape_of((COLS, ROWS, *latent.shape), bf16),
            shape_of(planes.shape, bf16),
        ),
        [ANY] * 5,
        [ANY] * 4,
        192,
        args=(query, latent, gate, up, planes),
        aliases={4: 3},
    )


def expand_body(latent, weight, gain, cos, sin, start_cos, start_sin, out):
    @pl.when(pl.program_id(0) <= lax.axis_index("row") + 1)
    def _():
        features = latent.shape[0] * latent.shape[2]
        values = latent[:, 0].reshape(features, latent.shape[3]).astype(f32)
        live = features - latent.shape[2] + 8
        square = jnp.sum(values[:live] * values[:live], axis=0, keepdims=True)
        scaled = (values * lax.rsqrt(square / KL + eps) * gain[...]).astype(bf16)
        found = jnp.dot(weight[...], scaled, preferred_element_type=f32).astype(bf16)
        turn_cos = cos[...] * start_cos[0] - sin[...] * start_sin[0]
        turn_sin = sin[...] * start_cos[0] + cos[...] * start_sin[0]
        turn_cos = jnp.concatenate([turn_cos, turn_cos], axis=1)
        turn_sin = jnp.concatenate([turn_sin, turn_sin], axis=1)
        first, second = values[live : live + 32], values[live + 32 : live + 64]
        rope = jnp.concatenate(
            [first * turn_cos - second * turn_sin, second * turn_cos + first * turn_sin], axis=0
        ).astype(bf16)
        out[0, 0:128] = found[0:128]
        out[0, 128:192] = rope
        out[0, 192:256] = rope
        out[0, 256:384] = found[256:384]
        out[0, 384:512] = found[128:256]
        out[0, 512:640] = found[384:512]


def expand(latent, weight, gain, cos, sin, start_cos, start_sin):
    cols, rows, height, width = latent.shape
    return pl.pallas_call(
        expand_body,
        name="expand_keys",
        grid=(rows,),
        out_shape=shape_of((rows, 640, width), bf16),
        in_specs=[
            pl.BlockSpec((cols, 1, height, width), lambda r: (0, r, 0, 0)),
            pl.BlockSpec(weight.shape, lambda r: (0, 0)),
            pl.BlockSpec(gain.shape, lambda r: (0, 0)),
            pl.BlockSpec((32, TS), lambda r: (0, 0)),
            pl.BlockSpec((32, TS), lambda r: (0, 0)),
            pl.BlockSpec((1, 32, 1), lambda r: (r, 0, 0)),
            pl.BlockSpec((1, 32, 1), lambda r: (r, 0, 0)),
        ],
        out_specs=pl.BlockSpec((1, 640, width), lambda r: (r, 0, 0)),
        compiler_params=pltpu.CompilerParams(vmem_limit_bytes=VMEM_BYTES),
        cost_estimate=pl.CostEstimate(
            flops=6 * 10**9, bytes_accessed=22 * 10**6, transcendentals=8192
        ),
    )(latent, weight, gain, cos, sin, start_cos, start_sin)


class ColSum:
    def __init__(self, net, col, term, total, cut, scratch):
        width = D // COLS
        *scratch, mine = scratch
        count = len(Scatter.scratch_of(TS, cut, width))
        self.parts = []
        for chunk in range(2):
            first = chunk * TS

            def block(owner, low, rows, first=first):
                return lane_slots(term, width)(owner, first + low, rows)

            def slot(owner, low, rows, first=first):
                return lane_slots(total, width)(owner, first + low, rows)

            def keep(part, value, chunk=chunk):
                mine[chunk, pl.ds(*part)] = value.astype(mine.dtype)

            part_scratch = scratch[chunk * count : (chunk + 1) * count]
            self.parts.append(
                (
                    Scatter(net, col, block, TS, cut, part_scratch, keep),
                    Gather(net, col, mine.at[chunk], slot, TS, cut, True),
                )
            )

    @staticmethod
    def scratch_of(cut):
        return [
            *Scatter.scratch_of(TS, cut, D // COLS),
            *Scatter.scratch_of(TS, cut, D // COLS),
            pltpu.VMEM((2, TS, D // COLS), bf16),
        ]

    def start(self):
        for scatter, _ in self.parts:
            scatter.start()

    def summed(self, chunk):
        scatter, gather = self.parts[chunk]
        scatter.forward_second()
        scatter.forward_first()
        scatter.end_first()
        gather.start_first()
        scatter.end_second()
        gather.start_second()

    def sent(self, chunk, stages):
        run_stages((self.parts[chunk][1],), stages)


def sum_body(cut, extra_cut, term, extra, total_all, extra_all, ss, rs, *scratch):
    col = Place("col")
    greet(col)
    net = Net(ss, rs)
    total = ColSum(net, col, term, total_all, cut, scratch)
    beside = Gather(net, col, extra, lead_slots(extra_all), extra.shape[0], extra_cut, True)
    total.start()
    run_stages((beside,), STAGES[:1])
    total.summed(0)
    run_stages((beside,), STAGES[1:3])
    total.sent(0, STAGES[1:2])
    total.summed(1)
    total.sent(0, STAGES[2:4])
    total.sent(1, STAGES[1:4])
    total.sent(0, STAGES[4:])
    run_stages((beside,), STAGES[3:])
    total.sent(1, STAGES[4:])
    net.finish()


def sum_over_col(name, collective_id, term, cut, extra, extra_cut):
    return comm_call(
        functools.partial(sum_body, cut, extra_cut),
        name,
        collective_id,
        (shape_of((2 * TS, D), bf16), shape_of((COLS, *extra.shape), extra.dtype)),
        [VM, ANY],
        [ANY, ANY],
        160,
        ColSum.scratch_of(cut),
        (term, extra),
    )


def attention_sum_body(cut, term, up, down, _, total_all, planes, down_all, ss, rs, *scratch):
    row, col = Place("row"), Place("col")
    greet(row, col)
    net = Net(ss, rs)
    height = down.shape[0]

    def down_slot(owner, low, count):
        place = pl.multiple_of(lax.div(owner, 2) * height + low, 16)
        return down_all.at[lax.rem(owner, 2), pl.ds(place, count)]

    total = ColSum(net, col, term, total_all, cut, scratch)
    weights = (
        plane_gather(net, row, up.at[1], planes, 3, 96),
        Gather(net, row, down, down_slot, height, DOWN_CUT, True),
    )
    total.start()
    run_stages(weights, STAGES[:1])
    total.summed(0)
    run_stages(weights, STAGES[1:2])
    total.sent(0, STAGES[1:2])
    total.summed(1)
    run_stages(weights, STAGES[2:3])
    total.sent(0, STAGES[2:4])
    total.sent(1, STAGES[1:2])
    run_stages(weights, STAGES[3:4])
    total.sent(1, STAGES[2:4])
    total.sent(0, STAGES[4:])
    run_stages(weights, STAGES[4:5])
    total.sent(1, STAGES[4:])
    run_stages(weights, STAGES[5:])
    net.finish()


def attention_sum_over_col(term, up, down, planes, cut):
    return comm_call(
        functools.partial(attention_sum_body, cut),
        "sum_attention",
        4,
        (
            shape_of((2 * TS, D), bf16),
            shape_of(planes.shape, bf16),
            shape_of((EXP_DEV, ROWS // 2 * down.shape[0], D), bf16),
        ),
        [VM, ANY, ANY, ANY],
        [ANY] * 3,
        160,
        ColSum.scratch_of(cut),
        (term, up, down, planes),
        aliases={3: 1},
    )


def back_body(grad, stats, branch, grad_all, stats_all, branch_sum, ss, rs, *scratch):
    row, col = Place("row"), Place("col")
    greet(row, col)
    net = Net(ss, rs)

    def keep(part, value):
        branch_sum[pl.ds(*part)] = value

    scatter = Scatter(net, col, lane_slots(branch, D // COLS), 2 * TS, COL_CUT, scratch, keep)
    gathers = (
        Gather(net, row, grad, lead_slots(grad_all), 2 * TS, 96, True),
        Gather(net, row, stats, lead_slots(stats_all), stats.shape[0], stats.shape[0]),
    )
    run_stages(gathers, STAGES[:1])
    scatter.start()
    run_stages(gathers, STAGES[1:3])
    scatter.forward_second()
    scatter.forward_first()
    run_stages(gathers, STAGES[3:6])
    scatter.end_first()
    scatter.end_second()
    run_stages(gathers, STAGES[6:])
    net.finish()


def back(grad, stats, branch):
    return comm_call(
        back_body,
        "gather_back",
        6,
        (
            shape_of((ROWS, *grad.shape), bf16),
            shape_of((ROWS, *stats.shape), f32),
            shape_of((2 * TS, D // COLS), f32),
        ),
        [ANY, ANY, VM],
        [ANY, ANY, VM],
        96,
        Scatter.scratch_of(2 * TS, COL_CUT, D // COLS),
        (grad, stats, branch),
    )


class RowScatter:
    def __init__(self, net, place, term, cut, scratch, keep):
        self.net, self.place, self.term = net, place, term
        self.arrived, self.summed = scratch[:2]
        rows = term.shape[3]

        def block(owner, low, count):
            return self.summed.at[lax.div(owner, 2), pl.ds(low, count)]

        self.inner = Scatter(net, place, block, rows, cut, scratch[2:], keep)

    @staticmethod
    def scratch_of(rows, cut, width):
        return [
            pltpu.VMEM((2, RING, rows, width), bf16),
            pltpu.VMEM((2 * RING, rows, width), bf16),
            *Scatter.scratch_of(rows, cut, width),
        ]

    def start(self):
        place = self.place
        self.partner = place.at(place.pair, place.ring, 1 - place.core)
        self.number = self.net.send(
            self.term.at[:, :, 1 - place.core], self.arrived, place.axis, self.partner
        )

    def middle(self):
        place = self.place
        self.net.receive(self.number, self.arrived, place.axis, self.partner)
        for pair in range(2):
            for ring in range(RING):
                self.summed[pair * RING + ring] = (
                    self.term[pair, ring, place.core].astype(f32)
                    + self.arrived[pair, ring].astype(f32)
                ).astype(bf16)
        self.inner.start()


def run_scatters(scatters):
    for scatter in scatters:
        scatter.forward_second()
    for scatter in scatters:
        scatter.forward_first()
    for scatter in scatters:
        scatter.end_first()
    for scatter in scatters:
        scatter.end_second()


def keep_in(ref):
    def keep(part, value):
        ref[pl.ds(*part)] = value

    return keep


def block_slots(ref):
    return lambda owner, low, count: ref.at[owner, pl.ds(low, count)]


def rows_sum(net, place, terms, cuts, totals, scratch):
    parts = []
    for term, cut, total in zip(terms, cuts, totals):
        count = len(RowScatter.scratch_of(term.shape[3], cut, term.shape[4]))
        parts.append(RowScatter(net, place, term, cut, scratch[:count], keep_in(total)))
        scratch = scratch[count:]
    return parts


def rows_scratch(terms, cuts):
    found = []
    for term, cut in zip(terms, cuts):
        found += RowScatter.scratch_of(term.shape[3], cut, term.shape[4])
    return found


def col_and_row_body(col_cuts, row_cuts, slots, *rest):
    cols, rows = len(col_cuts), len(row_cuts)
    col_terms, rest = rest[:cols], rest[cols:]
    extra, rest = rest[0], rest[1:]
    row_terms, rest = rest[:rows], rest[rows:]
    col_totals, rest = rest[:cols], rest[cols:]
    extra_all, rest = rest[0], rest[1:]
    row_totals, rest = rest[:rows], rest[rows:]
    ss, rs, *scratch = rest
    row, col = Place("row"), Place("col")
    greet(row, col)
    net = Net(ss, rs)
    scatters = []
    for term, cut, total in zip(col_terms, col_cuts, col_totals):
        height, width = total.shape
        block = lane_slots(term, width) if slots == "lane" else block_slots(term)
        count = len(Scatter.scratch_of(height, cut, width))
        scatters.append(Scatter(net, col, block, height, cut, scratch[:count], keep_in(total)))
        scratch = scratch[count:]
    beside = Gather(net, col, extra, lead_slots(extra_all), extra.shape[0], extra.shape[0])
    parts = rows_sum(net, row, row_terms, row_cuts, row_totals, scratch)
    for part in parts:
        part.start()
    for scatter in scatters:
        scatter.start()
    beside.start()
    for part in parts:
        part.middle()
    run_stages((beside,), STAGES[1:2])
    run_scatters(scatters + [part.inner for part in parts])
    run_stages((beside,), STAGES[2:])
    net.finish()


def col_and_row(name, collective_id, slots, col_terms, col_shapes, col_cuts, extra, row_terms, row_cuts):
    scratch = []
    for shape, cut in zip(col_shapes, col_cuts):
        scratch += Scatter.scratch_of(shape[0], cut, shape[1])
    found = comm_call(
        functools.partial(col_and_row_body, tuple(col_cuts), tuple(row_cuts), slots),
        name,
        collective_id,
        (
            *(shape_of(shape, f32) for shape in col_shapes),
            shape_of((COLS, *extra.shape), f32),
            *(shape_of(term.shape[3:], f32) for term in row_terms),
        ),
        [*([VM] * len(col_terms)), ANY, *([VM] * len(row_terms))],
        [*([VM] * len(col_terms)), ANY, *([VM] * len(row_terms))],
        128,
        [*scratch, *rows_scratch(row_terms, row_cuts)],
        (*col_terms, extra, *row_terms),
    )
    count = len(col_terms)
    return found[:count], found[count], found[count + 1 :]


def first_sum_body(row_cuts, term, extra, normed, gains, *rest):
    rows = len(row_cuts)
    row_terms, rest = rest[:rows], rest[rows:]
    total, extra_all, gains_all, rest = *rest[:3], rest[3:]
    row_totals, rest = rest[:rows], rest[rows:]
    ss, rs, gains_rows, gains_mine, *scratch = rest
    row, col = Place("row"), Place("col")
    greet(row, col, everyone=True)
    net = Net(ss, rs)
    height, width = total.shape
    count = len(Scatter.scratch_of(height, FIRST_CUT, width))
    scatter = Scatter(
        net, col, lane_slots(term, width), height, FIRST_CUT, scratch[:count], keep_in(total)
    )
    beside = Direct(net, col, extra, extra_all, COLS)
    parts = rows_sum(net, row, row_terms, row_cuts, row_totals, scratch[count:])
    inner = [part.inner for part in parts]
    scatter.start()
    for part in parts:
        part.start()
    beside.start()
    for part in parts:
        part.middle()
    scatter.forward_second()
    scatter.forward_first()
    for part in inner:
        part.forward_second()
    for part in inner:
        part.forward_first()
    scatter.end_first()
    scatter.end_second()
    gain = jnp.sum(total[...] * normed[...], axis=0, keepdims=True)
    gains_mine[...] = gains[...]
    gains_mine[0:1] = gain[:, :128]
    gains_mine[1:2] = gain[:, 128:]
    every = Direct(net, row, gains_mine, gains_rows, ROWS)
    every.start()
    for part in inner:
        part.end_first()
    beside.land()
    every.land()
    net.settle()
    found = gains_rows[0]
    for index in range(1, ROWS):
        found = found + gains_rows[index]
    gains_rows[ROWS] = found
    spread = Direct(net, col, gains_rows.at[ROWS], gains_all, COLS)
    spread.start()
    for part in inner:
        part.end_second()
    spread.land()
    net.finish()


def first_sum(term, extra, normed, gains, row_terms, row_cuts):
    width = D // COLS
    found = comm_call(
        functools.partial(first_sum_body, tuple(row_cuts)),
        "sum_first",
        8,
        (
            shape_of((2 * TS, width), f32),
            shape_of((COLS, *extra.shape), f32),
            shape_of((COLS, 8, 128), f32),
            *(shape_of(term.shape[3:], f32) for term in row_terms),
        ),
        [VM] * (4 + len(row_terms)),
        [VM] * (3 + len(row_terms)),
        160,
        [
            pltpu.VMEM((ROWS + 1, 8, 128), f32),
            pltpu.VMEM((8, 128), f32),
            *Scatter.scratch_of(2 * TS, FIRST_CUT, width),
            *rows_scratch(row_terms, row_cuts),
        ],
        (term, extra, normed, gains, *row_terms),
    )
    return found[:3], found[3:]


def contract(left, right):
    return lax.dot_general(left, right, (((1,), (1,)), ((), ())), preferred_element_type=f32)


def masked_queries(pack):
    lanes = lax.broadcasted_iota(jnp.int32, (pack.shape[0], 256), 1)
    zero = jnp.zeros((), pack.dtype)
    return (
        jnp.where(lanes < 192, pack[:, :256], zero),
        jnp.where(lanes >= 64, pack[:, 128:], zero),
    )


def attend_body(lens, query, kvt, out, lse, lse_rows, scores):
    seq = pl.program_id(0)
    mine = lax.axis_index("row")
    live = lens[seq]
    steps = lax.div(jnp.minimum(mine + 1, lax.div(live + TS - 1, TS)) + 1, 2)
    places = mine * TS + lax.broadcasted_iota(jnp.int32, (TS, 1), 0)
    limit = jnp.minimum(places + 1, live)
    offsets = lax.broadcasted_iota(jnp.int32, (TS, TS), 1)
    queries = masked_queries(query[...])

    def first(step, tops):
        tops = list(tops)
        for half in range(2):
            index = 2 * step + half
            valid = offsets < limit - index * TS
            for head in range(2):
                key = kvt[index, head * 128 : head * 128 + 256]
                value = jnp.dot(queries[head], key, preferred_element_type=f32)
                value = jnp.where(valid, value, -1e30)
                scores[head, index] = value
                tops[head] = jnp.maximum(
                    tops[head], jnp.maximum(value[:, :128], value[:, 128:])
                )
        return tuple(tops)

    tops = lax.fori_loop(0, steps, first, (jnp.full((TS, 128), -1e30, f32),) * 2)
    tops = [jnp.max(top, axis=1, keepdims=True) * score_bits for top in tops]

    def second(step, carried):
        found = []
        for head in range(2):
            sums, total = carried[head]
            for half in range(2):
                index = 2 * step + half
                weight = jnp.exp2(scores[head, index] * score_bits - tops[head])
                sums = sums + (weight[:, :128] + weight[:, 128:])
                value = kvt[index, 384 + head * 128 : 512 + head * 128]
                total = total + contract(weight.astype(bf16), value)
            found.append((sums, total))
        return tuple(found)

    zero = jnp.zeros((TS, 128), f32)
    carried = lax.fori_loop(0, steps, second, ((zero, zero),) * 2)
    for head in range(2):
        sums, total = carried[head]
        whole = jnp.sum(sums, axis=1, keepdims=True)
        lanes = pl.ds(head * 128, 128)
        out[:, lanes] = total / whole
        value = jnp.broadcast_to(tops[head] + jnp.log2(whole), (TS, 128))
        lse[:, lanes] = value
        lse_rows[head : head + 1] = value.T[:1]


def attend(lens, query, kvt):
    return pl.pallas_call(
        attend_body,
        name="attend",
        grid=(2,),
        out_shape=(
            shape_of((2 * TS, 256), f32),
            shape_of((2 * TS, 256), f32),
            shape_of((8, 2 * TS), f32),
        ),
        in_specs=[
            pl.BlockSpec(memory_space=pltpu.SMEM),
            pl.BlockSpec((TS, 384), lambda s: (s, 0)),
            pl.BlockSpec((ROWS, 640, TS), lambda s: (0, 0, s)),
        ],
        out_specs=(
            pl.BlockSpec((TS, 256), lambda s: (s, 0)),
            pl.BlockSpec((TS, 256), lambda s: (s, 0)),
            pl.BlockSpec((8, TS), lambda s: (0, s)),
        ),
        scratch_shapes=[pltpu.VMEM((2, ROWS, TS, TS), f32)],
        compiler_params=pltpu.CompilerParams(vmem_limit_bytes=VMEM_BYTES),
        cost_estimate=pl.CostEstimate(
            flops=6 * 10**9, bytes_accessed=12 * 10**6, transcendentals=4 * 10**6
        ),
    )(lens, query, kvt)


def attend_back_body(lens, query, kvt, grad, lse, delta, near, query_all, grad_all, stats, dq, dk, dv):
    seq = pl.program_id(0)
    mine = lax.axis_index("row")
    live = lens[seq]
    width = 2 * TS
    steps = lax.div(jnp.minimum(mine + 1, lax.div(live + TS - 1, TS)) + 1, 2)
    places = mine * TS + lax.broadcasted_iota(jnp.int32, (TS, 1), 0)
    limit = jnp.minimum(places + 1, live)
    narrow = lax.broadcasted_iota(jnp.int32, (TS, TS), 1)
    wide = lax.broadcasted_iota(jnp.int32, (TS, width), 1)
    queries = masked_queries(query[...])

    def queries_step(step, carried):
        totals = list(carried)
        for half in range(2):
            index = 2 * step + half
            valid = narrow < limit - index * TS
            for head in range(2):
                key = kvt[index, head * 128 : head * 128 + 256]
                value = kvt[index, 384 + head * 128 : 512 + head * 128]
                lanes = pl.ds(head * 128, 128)
                score = jnp.dot(queries[head], key, preferred_element_type=f32)
                score = score * score_bits - lse[:, lanes][:, :1]
                weight = jnp.exp2(jnp.where(valid, score, -1e30))
                slope = jnp.dot(grad[:, lanes], value, preferred_element_type=f32)
                low = (weight * (slope - delta[:, lanes][:, :1])).astype(bf16)
                totals[head] = totals[head] + contract(low, key)
        return tuple(totals)

    totals = lax.fori_loop(0, steps, queries_step, (jnp.zeros((TS, 256), f32),) * 2)
    edge = lax.broadcasted_iota(jnp.int32, (TS, 128), 1) < DR
    dq[:, 0:128] = totals[0][:, :128] * score_scale
    dq[:, 128:256] = jnp.where(edge, totals[0][:, 128:], totals[1][:, :128]) * score_scale
    dq[:, 256:384] = totals[1][:, 128:] * score_scale

    bar = jnp.where(places < live, places, 2 * ROWS * TS)
    keys = masked_queries(near[:, :384])

    def keys_step(step, carried):
        valid = wide >= bar - step * width
        queries = query_all[pl.ds(2 * step, 2)].reshape(width, query_all.shape[2])
        grads = grad_all[pl.ds(2 * step, 2)].reshape(width, 256)
        numbers = stats[pl.ds(2 * step, 2)]
        numbers = jnp.concatenate([numbers[0], numbers[1]], axis=1)
        found = []
        for head in range(2):
            key_total, value_total = carried[head]
            asked = queries[:, head * 128 : head * 128 + 256]
            given = grads[:, head * 128 : head * 128 + 128]
            score = contract(keys[head], asked) * score_bits - numbers[head : head + 1]
            weight = jnp.exp2(jnp.where(valid, score, -1e30))
            value_total = value_total + jnp.dot(
                weight.astype(bf16), given, preferred_element_type=f32
            )
            value = near[:, 384 + head * 128 : 512 + head * 128]
            slope = contract(value, given) - numbers[2 + head : 3 + head]
            low = (weight * slope).astype(bf16)
            key_total = key_total + jnp.dot(low, asked, preferred_element_type=f32)
            found.append((key_total, value_total))
        return tuple(found)

    zero = (jnp.zeros((TS, 256), f32), jnp.zeros((TS, 128), f32))
    last_step = jnp.where(mine * TS < live, ROWS // 2, 0)
    totals = lax.fori_loop(lax.div(mine, 2), last_step, keys_step, (zero, zero))
    dk[:, 0:128] = totals[0][0][:, :128] * score_scale
    dk[:, 128:256] = jnp.where(edge, totals[0][0][:, 128:], totals[1][0][:, :128]) * score_scale
    dk[:, 256:384] = totals[1][0][:, 128:] * score_scale
    dv[:, 0:128] = totals[0][1]
    dv[:, 128:256] = totals[1][1]


def attend_back(lens, query, kvt, grad, lse, delta, near, query_all, grad_all, stats):
    def lanes(width):
        return pl.BlockSpec((TS, width), lambda s: (s, 0))

    return pl.pallas_call(
        attend_back_body,
        name="attend_back",
        grid=(2,),
        out_shape=(
            shape_of((2 * TS, 384), f32),
            shape_of((2 * TS, 384), f32),
            shape_of((2 * TS, 256), f32),
        ),
        in_specs=[
            pl.BlockSpec(memory_space=pltpu.SMEM),
            lanes(384),
            pl.BlockSpec((ROWS, 640, TS), lambda s: (0, 0, s)),
            lanes(256),
            lanes(256),
            lanes(256),
            lanes(640),
            pl.BlockSpec((ROWS, TS, query_all.shape[2]), lambda s: (0, s, 0)),
            pl.BlockSpec((ROWS, TS, 256), lambda s: (0, s, 0)),
            pl.BlockSpec((ROWS, 8, TS), lambda s: (0, 0, s)),
        ],
        out_specs=(lanes(384), lanes(384), lanes(256)),
        compiler_params=pltpu.CompilerParams(vmem_limit_bytes=VMEM_BYTES),
        cost_estimate=pl.CostEstimate(
            flops=12 * 10**9, bytes_accessed=24 * 10**6, transcendentals=8 * 10**6
        ),
    )(lens, query, kvt, grad, lse, delta, near, query_all, grad_all, stats)


def project_back_body(
    dq, dk, dv, cos, sin, query_up, latent_up, query_in, latent_in, query_raw, latent_raw,
    query_gain, latent_gain, query_up_grad, latent_up_grad, query_grad, latent_grad, numbers,
):
    def turn_back(tile):
        return tile * cos[...] - swap_halves(tile) * sin[...]

    queries = jnp.concatenate(
        [dq[:, :128], turn_back(dq[:, 128:256]), dq[:, 256:]], axis=1
    ).astype(bf16)
    middle = dk[:, 128:256]
    middle = middle + pltpu.roll(middle, DR, 1)
    rope = turn_back(middle)
    pairs = jnp.concatenate(
        [dk[:, :128], dv[:, :128], dk[:, 256:], dv[:, 128:]], axis=1
    ).astype(bf16)
    query_up_grad[...] = jnp.dot(query_in[...], queries, preferred_element_type=f32).astype(bf16)
    latent_up_grad[...] = jnp.dot(latent_in[...], pairs, preferred_element_type=f32).astype(bf16)
    back = contract(query_up[...], queries)
    query_grad[...] = back.astype(bf16)
    numbers[...] = jnp.zeros_like(numbers)
    numbers[0:1] = jnp.sum(back * query_gain[...] * query_raw[...].astype(f32), axis=0, keepdims=True)
    back = contract(latent_up[...], pairs)
    numbers[1:2] = jnp.sum(
        back * latent_gain[...] * latent_raw[...].astype(f32), axis=0, keepdims=True
    )
    latent_grad[:KL] = back.astype(bf16)
    latent_grad[KL:] = rope.T[:DR].astype(bf16)


def project_back(*terms):
    query_up, latent_up, query_in, latent_in = terms[5:9]
    return pl.pallas_call(
        project_back_body,
        name="project_back",
        out_shape=(
            shape_of(query_up.shape, bf16),
            shape_of(latent_up.shape, bf16),
            shape_of(query_in.shape, bf16),
            shape_of((KL + DR, 2 * TS), bf16),
            shape_of((8, 2 * TS), f32),
        ),
        in_specs=[pl.BlockSpec(memory_space=VM)] * len(terms),
        out_specs=(pl.BlockSpec(memory_space=VM),) * 5,
        compiler_params=pltpu.CompilerParams(vmem_limit_bytes=VMEM_BYTES),
        cost_estimate=pl.CostEstimate(
            flops=2 * 10**9, bytes_accessed=16 * 10**6, transcendentals=0
        ),
    )(*terms)


def silu_parts(gate_value):
    sigmoid_value = 1.0 / (1.0 + jnp.exp(-gate_value))
    return (gate_value * sigmoid_value, sigmoid_value * (1.0 + gate_value * (1.0 - sigmoid_value)))


def transposed(left, right):
    return lax.dot_general(left, right, (((0,), (0,)), ((), ())), preferred_element_type=f32)


def shared_body(normed, grad, gate, up, down, branch, back_grad, weight_grad):
    normed_value, grad_value = normed[...], grad[...]
    gate_value = contract(normed_value, gate[...])
    up_value = contract(normed_value, up[...])
    silu_value, slope = silu_parts(gate_value)
    act = (silu_value * up_value).astype(bf16)
    act_grad = contract(grad_value, down[...])
    gate_low = (act_grad * up_value * slope).astype(bf16)
    up_low = (act_grad * silu_value).astype(bf16)
    branch[...] = jnp.dot(act, down[...], preferred_element_type=f32)
    back_grad[...] = jnp.dot(gate_low, gate[...], preferred_element_type=f32) + jnp.dot(
        up_low, up[...], preferred_element_type=f32
    )
    lanes = weight_grad.shape[1] // 3
    blank = jnp.zeros((gate_low.shape[0], lanes - gate_low.shape[1]), bf16)
    parts = ((normed_value, gate_low), (normed_value, up_low), (grad_value, act))
    for index, (left, right) in enumerate(parts):
        right = jnp.concatenate([right, blank], axis=1)
        weight_grad[:, index * lanes : (index + 1) * lanes] = transposed(left, right).astype(bf16)


def shared_experts(normed, grad, gate, up, down):
    units = gate.shape[0]
    return pl.pallas_call(
        shared_body,
        name="shared_experts",
        out_shape=(
            shape_of((2 * TS, D), f32),
            shape_of((2 * TS, D), f32),
            shape_of((D, 3 * (units + (-units) % 128)), bf16),
        ),
        in_specs=[pl.BlockSpec(memory_space=VM)] * 5,
        out_specs=(pl.BlockSpec(memory_space=VM),) * 3,
        compiler_params=pltpu.CompilerParams(vmem_limit_bytes=VMEM_BYTES),
        cost_estimate=pl.CostEstimate(
            flops=8 * 10**9, bytes_accessed=24 * 10**6, transcendentals=10**6
        ),
    )(normed, grad, gate, up, down)


def experts_body(
    slots, gates, normed, grad, branch_in, back_in, w_in, w_down,
    branch, back_grad, gate_grad, sums,
    dispatch, taken, taken_turned, given, routed, result, back_sum, branch_sum, back_total,
    act_turned, staged, down_staged, sems,
):
    expert, step = pl.program_id(0), pl.program_id(1)
    steps = pl.num_programs(1)
    capacity = dispatch.shape[0]
    units = w_down.shape[1]
    height = D // ROWS
    number = expert * steps + step
    slot = lax.rem(number, 2)
    down_rows = act_turned.shape[0] // ROWS

    def in_copy(slot, expert, step):
        target = sums.at[
            :,
            pl.ds(pl.multiple_of(expert * 2 * height, 2 * height), 2 * height),
            pl.ds(pl.multiple_of(step * units, units), units),
        ]
        return pltpu.make_async_copy(staged.at[slot], target, sems.at[slot])

    def down_copy(expert):
        first = pl.multiple_of(2 * EXP_DEV * height + expert * height, height)
        return pltpu.make_async_copy(down_staged, sums.at[:, pl.ds(first, height)], sems.at[2])

    @pl.when(step == 0)
    def _():
        places = lax.broadcasted_iota(jnp.int32, dispatch.shape, 0)
        chosen = places == slots[pl.ds(expert, 1)]
        dispatch[...] = chosen.astype(bf16)
        weight = jnp.sum(jnp.where(chosen, gates[pl.ds(expert, 1)], 0.0), axis=1, keepdims=True)
        rows = jnp.dot(dispatch[...], normed[...], preferred_element_type=f32).astype(bf16)
        taken[...] = rows
        taken_turned[...] = rows.T
        grads = jnp.dot(dispatch[...], grad[...], preferred_element_type=f32)
        given[...] = grads.astype(bf16)
        routed[...] = (weight * grads).astype(bf16)
        result[...] = jnp.zeros_like(result)
        back_sum[...] = jnp.zeros_like(back_sum)

    weights = jnp.concatenate([w_in[0], w_in[1]], axis=1)
    hidden = jnp.dot(taken[...], weights, preferred_element_type=f32)
    gate_value, up_value = hidden[:, :units], hidden[:, units:]
    silu_value, slope = silu_parts(gate_value)
    act = (silu_value * up_value).astype(bf16)
    act_turned[pl.ds(pl.multiple_of(step * units, units), units)] = act.T
    act_grad = contract(routed[...], w_down[0])
    low = jnp.concatenate(
        [
            (act_grad * up_value * slope).astype(bf16),
            (act_grad * silu_value).astype(bf16),
        ],
        axis=1,
    )
    result[...] += jnp.dot(act, w_down[0], preferred_element_type=f32)
    back_sum[...] += contract(low, weights)
    in_grad = jnp.dot(taken_turned[...], low, preferred_element_type=f32).astype(bf16)

    @pl.when(number >= 2)
    def _():
        in_copy(slot, expert, step).wait()

    staged[slot, :, :height] = in_grad[:, :units].reshape(ROWS, height, units)
    staged[slot, :, height:] = in_grad[:, units:].reshape(ROWS, height, units)
    in_copy(slot, expert, step).start()

    @pl.when(step == steps - 1)
    def _():
        places = lax.broadcasted_iota(jnp.int32, dispatch.shape, 0)
        chosen = places == slots[pl.ds(expert, 1)]
        weight = jnp.sum(jnp.where(chosen, gates[pl.ds(expert, 1)], 0.0), axis=1, keepdims=True)
        number = jnp.sum(result[...] * given[...].astype(f32), axis=1, keepdims=True)
        gate_grad[pl.ds(expert, 1)] = jnp.sum(
            jnp.where(chosen, number, 0.0), axis=0, keepdims=True
        )

        @pl.when(expert > 0)
        def _():
            down_copy(expert).wait()

        def down_step(part, carried):
            columns = pl.ds(pl.multiple_of(part * 256, 256), 256)
            value = jnp.dot(act_turned[...], routed[:, columns], preferred_element_type=f32)
            for owner in range(ROWS):
                block = value[owner * down_rows : (owner + 1) * down_rows]
                bands = [
                    jnp.concatenate(
                        [
                            block[low : low + 8, half * 128 : half * 128 + 128]
                            for low in range(0, down_rows, 8)
                        ],
                        axis=1,
                    )
                    for half in range(2)
                ]
                rows = pl.ds(pl.multiple_of(part * 16, 16), 16)
                down_staged[owner, rows] = jnp.concatenate(bands, axis=0).astype(bf16)
            return carried

        lax.fori_loop(0, D // 256, down_step, 0)
        down_copy(expert).start()
        outward = transposed(dispatch[...], (weight * result[...]).astype(bf16))
        inward = transposed(dispatch[...], back_sum[...].astype(bf16))

        @pl.when(expert == 0)
        def _():
            branch_sum[...] = branch_in[...] + outward
            back_total[...] = back_in[...] + inward

        @pl.when(expert == EXP_DEV - 1)
        def _():
            branch[...] = (branch_sum[...] + outward).astype(bf16)
            back_grad[...] = (back_total[...] + inward).astype(bf16)
            in_copy(1 - slot, expert, step).wait()
            in_copy(slot, expert, step).wait()
            down_copy(expert).wait()


def experts(capacity, slots, gates, normed, grad, branch_in, back_in, planes, w_down):
    units = 128
    hidden_units = w_down.shape[1]
    steps = hidden_units // units
    height = D // ROWS
    whole = pl.BlockSpec(memory_space=VM)
    in_block = pl.BlockSpec((2, D, units), lambda e, k: (e, 0, k))
    down_block = pl.BlockSpec((1, units, D), lambda e, k: (e, k, 0))
    return pl.pallas_call(
        experts_body,
        name="experts",
        grid=(EXP_DEV, steps),
        out_shape=(
            shape_of((2 * TS, D), bf16),
            shape_of((2 * TS, D), bf16),
            shape_of((8, 2 * TS), f32),
            shape_of((ROWS, 3 * EXP_DEV * height, hidden_units), bf16),
        ),
        in_specs=[whole] * 6 + [in_block, down_block],
        out_specs=(whole, whole, whole, pl.BlockSpec(memory_space=ANY)),
        scratch_shapes=[
            pltpu.VMEM((capacity, 2 * TS), bf16),
            pltpu.VMEM((capacity, D), bf16),
            pltpu.VMEM((D, capacity), bf16),
            pltpu.VMEM((capacity, D), bf16),
            pltpu.VMEM((capacity, D), bf16),
            pltpu.VMEM((capacity, D), f32),
            pltpu.VMEM((capacity, D), f32),
            pltpu.VMEM((2 * TS, D), f32),
            pltpu.VMEM((2 * TS, D), f32),
            pltpu.VMEM((hidden_units, capacity), bf16),
            pltpu.VMEM((2, ROWS, 2 * height, units), bf16),
            pltpu.VMEM((ROWS, height, hidden_units), bf16),
            pltpu.SemaphoreType.DMA((3,)),
        ],
        compiler_params=pltpu.CompilerParams(vmem_limit_bytes=VMEM_BYTES),
        cost_estimate=pl.CostEstimate(
            flops=40 * 10**9, bytes_accessed=80 * 10**6, transcendentals=10**6
        ),
    )(slots, gates, normed, grad, branch_in, back_in, planes, w_down)


def finish_body(
    sums, down_sum, query_up_sum, gains, shared_sum, first, numbers, residual, normed, scale, gain,
    gate, up, down, query_down, latent_down, router, query_up, gain_first, gain_second, query_gain,
    latent_gain, shared_gate, shared_up, shared_down, hidden_grad,
):
    height = gate.shape[1]
    rows = down.shape[1]
    for expert in range(EXP_DEV):
        low = 2 * expert * height
        gate[expert] = sums[low : low + height].astype(f32)
        up[expert] = sums[low + height : low + 2 * height].astype(f32)
        low = (2 * EXP_DEV + expert) * height
        value = sums[low : low + height].astype(f32)
        for column in range(D // 128):
            band = value[column * 8 : column * 8 + 8]
            down[expert, :, column * 128 : column * 128 + 128] = jnp.concatenate(
                [band[:, tile * 128 : tile * 128 + 128] for tile in range(rows // 8)], axis=0
            )
    turned = down_sum[...].T
    query_rows, latent_rows = query_down.shape[0], latent_down.shape[0]
    query_down[...] = turned[:query_rows]
    latent_down[...] = turned[query_rows : query_rows + latent_rows]
    router[...] = turned[query_rows + latent_rows :]
    query_up[...] = jnp.concatenate(
        [query_up_sum[:, :192], query_up_sum[:, 256:], query_up_sum[:, 192:256]], axis=1
    )
    for col in range(COLS):
        gain_first[2 * col : 2 * col + 2] = gains[col, 0:2]
        gain_second[2 * col : 2 * col + 2] = gains[col, 2:4]
        query_gain[col : col + 1, :128] = gains[col, 4:5]
        query_gain[col : col + 1, 128:] = gains[col, 5:6, : query_rows - 128]
        latent_gain[col : col + 1] = gains[col, 6:7, :latent_rows]
    units = shared_gate.shape[0]
    lanes = shared_sum.shape[1] // 3
    for index, ref in enumerate((shared_gate, shared_up, shared_down)):
        part = shared_sum[:, index * lanes : (index + 1) * lanes].astype(f32)
        ref[...] = part.T[:units]
    total = numbers[0]
    for index in range(1, COLS):
        total = total + numbers[index]
    mean = total.T[:, :1] / D
    hidden_grad[...] = residual[...] + scale[...] * (
        first[...] * gain[...] - normed[...] * (scale[...] * mean)
    )


def finish(*terms):
    height, units = D // ROWS, terms[0].shape[1]
    query_rows = QL // COLS
    outs = (
        shape_of((EXP_DEV, height, units), f32),
        shape_of((EXP_DEV, height, units), f32),
        shape_of((EXP_DEV, units // ROWS, D), f32),
        shape_of((query_rows, height), f32),
        shape_of((KV_COLS, height), f32),
        shape_of((terms[1].shape[1] - query_rows - KV_COLS, height), f32),
        shape_of(terms[2].shape, f32),
        shape_of((2 * COLS, 128), f32),
        shape_of((2 * COLS, 128), f32),
        shape_of((COLS, query_rows), f32),
        shape_of((COLS, KV_COLS), f32),
        *((shape_of((SHARED_UNITS, height), f32),) * 3),
        shape_of(terms[5].shape, f32),
    )
    return simple_call(finish_body, "finish", outs, terms, 0, 12 * 10**6)


def second_back_body(
    normed_sum, logits, router, hidden, attention, grad, gain, out_weight, attended,
    attended_grad, delta, delta_rows, out_grad, residual_here, router_grad, gain_grad, whole,
):
    total = logits[0]
    for index in range(1, COLS):
        total = total + logits[index]
    logit_low = total.T.astype(bf16)
    spare = jnp.zeros((2 * TS, router.shape[1] - 256 - logit_low.shape[1]), f32)
    wide = jnp.concatenate([spare, total.T], axis=1).astype(bf16)
    normed_grad = normed_sum[...].astype(f32) + contract(wide, router[:, 256:])
    residual = hidden[...].astype(f32) + attention[...].astype(f32)
    scale = lax.rsqrt(jnp.mean(residual * residual, axis=1, keepdims=True) + eps)
    normed = residual * scale
    router_grad[...] = transposed((normed * gain[...]).astype(bf16), logit_low).astype(bf16)
    gain_grad[...] = jnp.broadcast_to(
        jnp.sum(normed_grad * normed, axis=0, keepdims=True), gain_grad.shape
    )
    weighted = normed_grad * gain[...]
    inner = jnp.mean(weighted * residual, axis=1, keepdims=True)
    residual_grad = (
        grad[...].astype(f32) + scale * weighted - residual * (scale * scale * scale * inner)
    )
    whole[...] = residual_grad
    width = residual_here.shape[1]
    first = pl.multiple_of(lax.axis_index("col") * width, 128)
    residual_here[...] = whole[:, pl.ds(first, width)]
    low = residual_grad.astype(bf16)
    found = contract(low, out_weight[...]).astype(bf16)
    attended_grad[...] = found
    weights = transposed(attended[...].astype(bf16), low).astype(bf16)
    for index in range(ROWS):
        out_grad[index] = weights[:, index * 128 : (index + 1) * 128]
    numbers = found.astype(f32) * attended[...]
    delta_rows[...] = jnp.zeros_like(delta_rows)
    for head in range(2):
        lanes = slice(head * 128, head * 128 + 128)
        number = jnp.sum(numbers[:, lanes], axis=1, keepdims=True)
        number = jnp.broadcast_to(number, (2 * TS, 128))
        delta[:, lanes] = number
        delta_rows[head : head + 1] = number.T[:1]


def second_back(*terms):
    rows = 2 * TS
    outs = (
        shape_of((rows, 256), bf16),
        shape_of((rows, 256), f32),
        shape_of((8, rows), f32),
        shape_of((ROWS, 256, D // ROWS), bf16),
        shape_of((rows, D // COLS), f32),
        shape_of((D, 16), bf16),
        shape_of((8, D), f32),
    )
    return pl.pallas_call(
        second_back_body,
        name="second_back",
        out_shape=outs,
        in_specs=[pl.BlockSpec(memory_space=VM)] * len(terms),
        out_specs=(pl.BlockSpec(memory_space=VM),) * len(outs),
        scratch_shapes=[pltpu.VMEM((rows, D), f32)],
        compiler_params=pltpu.CompilerParams(vmem_limit_bytes=VMEM_BYTES),
        cost_estimate=pl.CostEstimate(
            flops=2 * 10**9, bytes_accessed=16 * 10**6, transcendentals=512
        ),
    )(*terms)


def first_project_body(hidden, gain, weight, normed, query, latent):
    values = hidden[...].astype(f32)
    scale = lax.rsqrt(jnp.mean(values * values, axis=1, keepdims=True) + eps)
    low = (values * scale * gain[...]).astype(bf16)
    normed[...] = low
    found = jnp.dot(low, weight[...], preferred_element_type=f32).T
    height = query.shape[0]
    live = KV_COLS
    query[...] = found[:height].astype(bf16)
    blank = jnp.zeros((latent.shape[0] - live, found.shape[1]), f32)
    latent[...] = jnp.concatenate([found[height : height + live], blank], axis=0).astype(bf16)


def simple_call(body, name, outs, terms, flops, moved, scratch=()):
    return pl.pallas_call(
        body,
        name=name,
        out_shape=outs,
        in_specs=[pl.BlockSpec(memory_space=VM)] * len(terms),
        out_specs=(pl.BlockSpec(memory_space=VM),) * len(outs),
        scratch_shapes=list(scratch),
        compiler_params=pltpu.CompilerParams(vmem_limit_bytes=VMEM_BYTES),
        cost_estimate=pl.CostEstimate(flops=flops, bytes_accessed=moved, transcendentals=0),
    )(*terms)


def first_project(hidden, gain, weight):
    outs = (
        shape_of((2 * TS, D), bf16),
        shape_of((QL // COLS, 2 * TS), bf16),
        shape_of((KV_COLS + (-KV_COLS) % 16, 2 * TS), bf16),
    )
    return simple_call(
        first_project_body, "first_project", outs, (hidden, gain, weight), 10**9, 6 * 10**6
    )


def swap_halves(tile):
    lane = lax.broadcasted_iota(jnp.int32, tile.shape, 1)
    lower = lax.rem(lane, DR) < DR // 2
    return jnp.where(lower, pltpu.roll(tile, 128 - DR // 2, 1), pltpu.roll(tile, DR // 2, 1))


def project_body(
    query_raw, latent_raw, query_gain, latent_gain, query_up, latent_up, cos, sin,
    query_in, latent_in, query, near,
):
    def normed(values, gain):
        scale = lax.rsqrt(jnp.mean(values * values, axis=0, keepdims=True) + eps)
        return (values * scale * gain).astype(bf16)

    low = normed(query_raw[...].astype(f32), query_gain[...])
    query_in[...] = low
    found = transposed(low, query_up[...])
    middle = found[:, 128:256]
    query[:, :128] = found[:, :128].astype(bf16)
    query[:, 128:256] = (middle * cos[...] + swap_halves(middle) * sin[...]).astype(bf16)
    query[:, 256:] = found[:, 256:].astype(bf16)
    raw = latent_raw[...].astype(f32)
    low = normed(raw[:KL], latent_gain[...])
    latent_in[...] = low
    found = transposed(low, latent_up[...]).astype(bf16)
    rope = jnp.concatenate([raw[KL:], raw[KL:]], axis=0).T
    near[:, :128] = found[:, :128]
    near[:, 128:256] = (rope * cos[...] + swap_halves(rope) * sin[...]).astype(bf16)
    near[:, 256:384] = found[:, 256:384]
    near[:, 384:512] = found[:, 128:256]
    near[:, 512:] = found[:, 384:]


def project(*terms):
    outs = (
        shape_of((QL, 2 * TS), bf16),
        shape_of((KL, 2 * TS), bf16),
        shape_of((2 * TS, 384), bf16),
        shape_of((2 * TS, 640), bf16),
    )
    return simple_call(project_body, "project", outs, terms, 2 * 10**9, 8 * 10**6)


def latent_back_body(
    query_sum, kv_sum, numbers, query_raw, kv_raw, query_gain, kv_gain, live, query_square, kv_square,
    normed, weight, gain, hidden, router_grad,
    first_part, first_numbers, down_grad, query_gain_grad, kv_gain_grad,
):
    total = numbers[0]
    for index in range(1, COLS):
        total = total + numbers[index]
    query_scale = lax.rsqrt(query_square[:1] + eps)
    kv_scale = lax.rsqrt(kv_square[:1] + eps)
    query_raw_value = query_raw[...].astype(f32)
    kv_raw_value = kv_raw[...].astype(f32)
    query_value = query_sum[...]
    kv_value = kv_sum[: kv_raw.shape[0]]
    query_normed, kv_normed = query_raw_value * query_scale, kv_raw_value * kv_scale
    query_gain_grad[...] = jnp.sum(query_value * query_normed, axis=1, keepdims=True)
    kv_gain_grad[...] = jnp.sum(kv_value * kv_normed, axis=1, keepdims=True)
    query_low = query_scale * (query_value * query_gain[...]) - query_normed * (
        query_scale * query_scale * (total[0:1] / QL)
    )
    kv_low = kv_scale * (kv_value * kv_gain[...]) - kv_normed * (
        kv_scale * kv_scale * (total[1:2] / KL)
    )
    kv_low = jnp.where(live[...] > 0, kv_low, kv_value)
    both = jnp.concatenate([query_low, kv_low], axis=0)
    turned = both.T.astype(bf16)
    width = turned.shape[1]
    part = contract(turned, weight[:, :width])
    first_part[...] = part.astype(bf16)
    number = jnp.sum(part * gain[...] * hidden[...].astype(f32), axis=1, keepdims=True)
    first_numbers[...] = jnp.broadcast_to(number, (2 * TS, 128)).T[:8]
    grads = transposed(normed[...], turned).astype(bf16)
    down_grad[:, :width] = grads
    down_grad[:, width:] = router_grad[...]


def latent_back(*terms):
    query_rows, kv_rows = terms[3].shape[0], terms[4].shape[0]
    outs = (
        shape_of((2 * TS, D), bf16),
        shape_of((8, 2 * TS), f32),
        shape_of(terms[11].shape, bf16),
        shape_of((query_rows, 1), f32),
        shape_of((kv_rows, 1), f32),
    )
    return simple_call(latent_back_body, "latent_back", outs, terms, 2 * 10**9, 10**7)


def rope_tables(positions, width):
    half_width = width // 2
    frequency = jnp.exp(
        -jnp.log(rope_base) * (2.0 * jnp.arange(half_width, dtype=jnp.float32) / width)
    )
    angles = positions.astype(jnp.float32)[:, None] * frequency[None, :]
    return (jnp.cos(angles), jnp.sin(angles))


def rms_scale(values):
    return lax.rsqrt(jnp.mean(values * values, axis=-1, keepdims=True) + eps)


def product(left, right):
    return jnp.dot(left, right, preferred_element_type=jnp.float32)


def left_product(left, right):
    return lax.dot_general(
        left, right, (((0,), (0,)), ((), ())), preferred_element_type=jnp.float32
    )


def right_product(left, right):
    return lax.dot_general(
        left, right, (((1,), (1,)), ((), ())), preferred_element_type=jnp.float32
    )


def turned_product(left, right):
    return lax.dot_general(
        left, right, (((0,), (1,)), ((), ())), preferred_element_type=jnp.float32
    )


def einsum(text, *terms):
    return jnp.einsum(text, *terms, preferred_element_type=f32)


def to_blocks(term):
    return term.reshape(2, RING, 2, term.shape[0] // ROWS, term.shape[1])


def local(
    hidden_in,
    gain_first,
    query_down,
    query_gain,
    query_up,
    latent_down,
    latent_gain,
    latent_up,
    attention_out,
    gain_second,
    router,
    expert_gate,
    expert_up,
    expert_down,
    shared_gate,
    shared_up,
    shared_down,
    seq_lens,
    routes,
    out_grad,
):
    row_index = lax.axis_index("row")
    col_index = lax.axis_index("col")
    seq_count, local_len, col_width = hidden_in.shape
    row_total = seq_count * local_len
    experts_all = EXP_DEV * COLS
    most_rows = (5 * local_len * TOPK + 4 * experts_all - 1) // (4 * experts_all)
    capacity = seq_count * most_rows
    query_cols = QL // COLS
    kv_cols = (KL + DR) // COLS

    def here(values, axis=-1):
        width = values.shape[axis] // COLS
        return lax.dynamic_slice_in_dim(values, col_index * width, width, axis)

    (
        hidden_low,
        grad_full,
        down_all,
        query_up_all,
        latent_up_all,
        attention_out_all,
        shared_gate_all,
        shared_up_all,
        shared_down_all,
        planes,
        down_chip,
    ) = front(
        hidden_in.reshape(row_total, col_width),
        out_grad.reshape(row_total, col_width),
        jnp.concatenate([query_down, latent_down, router], axis=1),
        query_up,
        latent_up,
        attention_out,
        shared_gate.T,
        shared_up.T,
        shared_down,
        expert_gate,
        jnp.pad(expert_down, ((0, 0), (0, (-expert_down.shape[1]) % 16), (0, 0))),
        expert_gate.shape[2],
    )
    expert_units = expert_gate.shape[2]
    latent_width = query_cols + kv_cols
    router_all = down_all[:, latent_width:]
    kv_pad = (-kv_cols) % 16
    normed_first, query_here, latent_here = first_project(hidden_low, gain_first[None], down_all)
    query_latent, _, latent_all, planes = latents(
        query_here,
        latent_here,
        expert_gate,
        expert_up,
        planes,
    )
    kv_latent = lax.dynamic_index_in_dim(latent_all, row_index, 1, False)
    kv_latent = kv_latent[:, :kv_cols].reshape(KL + DR, row_total)
    latent_pad = ((0, 0), (0, kv_pad), (0, 0))
    within_cos, within_sin = rope_tables(jnp.arange(local_len, dtype=jnp.int32), DR)
    start_cos, start_sin = rope_tables(jnp.arange(ROWS, dtype=jnp.int32) * local_len, DR)
    kvt_all = expand(
        latent_all,
        jnp.pad(
            jnp.pad(latent_up_all, ((0, DR), (0, 0))).reshape(COLS, kv_cols, -1), latent_pad
        ).reshape(COLS * (kv_cols + kv_pad), -1).T,
        jnp.pad(
            jnp.pad(latent_gain, (0, DR)).reshape(COLS, kv_cols, 1), latent_pad
        ).reshape(COLS * (kv_cols + kv_pad), 1),
        within_cos.T,
        within_sin.T,
        start_cos[:, :, None],
        start_sin[:, :, None],
    )
    lane = jnp.arange(2 * DR, dtype=jnp.int32)[None, :]
    position = row_index * local_len + jnp.arange(row_total, dtype=jnp.int32) % local_len
    frequency = jnp.exp(-math.log(rope_base) * (2.0 / DR) * (lane % (DR // 2)).astype(f32))
    angles = position.astype(f32)[:, None] * frequency
    tile_cos = jnp.cos(angles)
    tile_sin = jnp.where(lane % DR < DR // 2, -1.0, 1.0) * jnp.sin(angles)
    split = DN + DR
    query_up_pack = jnp.concatenate(
        [query_up_all[:, :split], query_up_all[:, split + DN :], query_up_all[:, split : split + DN]],
        axis=1,
    )
    query_input, latent_input, query_pack, near = project(
        query_latent,
        kv_latent,
        query_gain[:, None],
        latent_gain[:, None],
        query_up_pack,
        latent_up_all,
        tile_cos,
        tile_sin,
    )
    attended_float, lse, lse_rows = attend(seq_lens, query_pack, kvt_all)
    attended = attended_float.astype(bf16)
    attention_part = product(attended, attention_out_all).astype(bf16)
    attention_sum, planes, expert_down_all = attention_sum_over_col(
        attention_part, expert_up, down_chip, planes, SUM_CUT
    )
    query_all = lax.all_gather(query_pack, "row", axis=0, tiled=False)

    residual_one = hidden_low.astype(f32) + attention_sum.astype(f32)
    scale_second = rms_scale(residual_one)
    normed_second = (residual_one * scale_second * gain_second).astype(bf16)
    logits = turned_product(router_all, normed_second)
    sigmoid_all = jax.nn.sigmoid(logits)
    routes_turned = routes.reshape(row_total, TOPK).T
    chosen = jnp.sum(
        (
            routes_turned[:, None, :] == jnp.arange(experts_all, dtype=jnp.int32)[None, :, None]
        ).astype(f32),
        axis=0,
    )
    weighted_sig = sigmoid_all * chosen
    denominator = jnp.sum(weighted_sig, axis=0, keepdims=True)
    gate_weights = route_scale * weighted_sig / denominator
    gate_here = here(gate_weights, 0)
    member = here(chosen, 0).reshape(EXP_DEV * seq_count, local_len)
    before = jnp.triu(jnp.ones((local_len, local_len), bf16), 1)
    rank = product(member.astype(bf16), before).reshape(EXP_DEV, seq_count, local_len)
    rank = rank + (jnp.arange(seq_count, dtype=f32) * most_rows)[None, :, None]
    slots = jnp.where(member.reshape(rank.shape) > 0, rank, float(capacity))
    slots = slots.astype(jnp.int32).reshape(EXP_DEV, row_total)
    normed_shared, query_all = lax.optimization_barrier((normed_second, query_all))
    shared_branch, shared_back, shared_grad = shared_experts(
        normed_shared, grad_full, shared_gate_all, shared_up_all, shared_down_all
    )
    branch_part, normed_part, gate_grad_here, expert_part = experts(
        capacity,
        slots,
        gate_here,
        normed_second,
        grad_full,
        shared_branch,
        shared_back,
        planes,
        expert_down_all,
    )
    shared_sum = lax.psum_scatter(shared_grad, "row", scatter_dimension=0, tiled=True)
    expert_sum = lax.psum_scatter(
        expert_part.reshape(-1, expert_units), "row", scatter_dimension=0, tiled=True
    )
    gate_grad_all = lax.dynamic_update_slice_in_dim(
        jnp.zeros((experts_all, row_total), f32), gate_grad_here[:EXP_DEV], col_index * EXP_DEV, 0
    )
    inner_sum = jnp.sum(gate_grad_all * gate_weights, axis=0, keepdims=True)
    logit_part = (
        sigmoid_all
        * (1.0 - sigmoid_all)
        * chosen
        / denominator
        * (route_scale * gate_grad_all - inner_sum)
    )
    normed_sum, logit_all = sum_over_col(
        "sum_normed", 5, normed_part, NORMED_CUT, logit_part, experts_all
    )
    (
        attended_grad,
        delta,
        delta_rows,
        attention_out_grad,
        residual_here,
        router_grad,
        gain_second_grad,
    ) = second_back(
        normed_sum,
        logit_all,
        down_all,
        hidden_low,
        attention_sum,
        grad_full,
        gain_second[None],
        attention_out_all,
        attended_float,
    )
    gain_second_part = here(gain_second_grad[0])
    stats = jnp.concatenate([lse_rows[:2], delta_rows[:2], lse_rows[:4]], axis=0)
    attended_grad_all, stats_all, branch_here = back(attended_grad, stats, branch_part)
    hidden_here = here(hidden_low).astype(f32)
    attended_here = here(attention_sum).astype(f32)
    block_out = (
        (hidden_here + attended_here + branch_here).astype(bf16).reshape(seq_count, local_len, col_width)
    )
    dq, dk, dv = attend_back(
        seq_lens,
        query_pack,
        kvt_all,
        attended_grad,
        lse,
        delta,
        near,
        query_all,
        attended_grad_all,
        stats_all,
    )
    query_up_grad, latent_up_grad, query_in_grad, kv_part, numbers = project_back(
        dq,
        dk,
        dv,
        tile_cos,
        tile_sin,
        query_up_pack,
        latent_up_all,
        query_input,
        latent_input,
        query_latent,
        kv_latent[:KL],
        query_gain[:, None],
        latent_gain[:, None],
    )
    kv_part = jnp.pad(kv_part.reshape(COLS, kv_cols, row_total), latent_pad)
    shared_width = shared_gate.shape[1]
    (query_in_here, kv_in_here), numbers_all, summed = col_and_row(
        "sum_latents",
        7,
        "lead",
        (query_in_grad.reshape(COLS, query_cols, row_total), kv_part),
        ((query_cols, row_total), (kv_cols + kv_pad, row_total)),
        (128, 80),
        numbers,
        (attention_out_grad.reshape(2, RING, 2, col_width, D // ROWS),),
        (96,),
    )
    (attention_out_sum,) = summed
    is_latent = (col_index * kv_cols + jnp.arange(kv_cols)) < KL
    latent_gain_here = here(jnp.concatenate([latent_gain, jnp.ones((DR,), f32)]))
    query_square, kv_square = (
        jnp.broadcast_to(
            jnp.mean(jnp.square(values.astype(f32)), axis=0, keepdims=True), (8, row_total)
        )
        for values in (query_latent, kv_latent[:KL])
    )
    first_part, first_numbers, down_grads, query_gain_part, latent_gain_part = latent_back(
        query_in_here,
        kv_in_here,
        numbers_all,
        here(query_latent, 0),
        here(kv_latent, 0),
        here(query_gain)[:, None],
        latent_gain_here[:, None],
        is_latent.astype(f32)[:, None],
        query_square,
        kv_square,
        normed_first,
        down_all,
        gain_first[None],
        hidden_low,
        router_grad,
    )
    scale_first = rms_scale(hidden_low.astype(f32))
    normed_here = hidden_here * scale_first
    gains = jnp.concatenate(
        [
            jnp.zeros((col_width,), f32),
            gain_second_part,
            query_gain_part[:, 0],
            jnp.zeros((64,), f32),
            latent_gain_part[:, 0],
            jnp.zeros((1024 - 768 - kv_cols,), f32),
        ]
    ).reshape(8, 128)
    (first_here, first_numbers_all, gains_all), summed = first_sum(
        first_part,
        first_numbers,
        normed_here,
        gains,
        (to_blocks(down_grads), to_blocks(query_up_grad), to_blocks(latent_up_grad)),
        (0, QL // ROWS, KL // ROWS),
    )
    down_sum, query_up_sum, latent_up_sum = summed
    (
        expert_gate_grad,
        expert_up_grad,
        expert_down_grad,
        query_down_grad,
        latent_down_grad,
        router_grad,
        query_up_grad,
        gain_first_grad,
        gain_second_grad,
        query_gain_grad,
        latent_gain_grad,
        shared_gate_grad,
        shared_up_grad,
        shared_down_grad,
        hidden_grad,
    ) = finish(
        expert_sum,
        down_sum,
        query_up_sum,
        gains_all,
        shared_sum,
        first_here,
        first_numbers_all,
        residual_here,
        normed_here,
        scale_first,
        here(gain_first)[None],
    )
    return (
        block_out,
        hidden_grad.reshape(seq_count, local_len, col_width),
        gain_first_grad.reshape(D),
        query_down_grad.T,
        query_gain_grad.reshape(QL),
        query_up_grad,
        latent_down_grad.T,
        latent_gain_grad.reshape(KL + DR)[:KL],
        latent_up_sum,
        attention_out_sum,
        gain_second_grad.reshape(D),
        router_grad.T,
        expert_gate_grad,
        expert_up_grad,
        expert_down_grad,
        shared_gate_grad.T,
        shared_up_grad.T,
        shared_down_grad,
    )


def solution(mesh):
    in_specs = (
        P(None, "row", "col"),
        P(),
        P("row", "col"),
        P(),
        P("row", "col"),
        P("row", "col"),
        P(),
        P("row", "col"),
        P("col", "row"),
        P(),
        P("row", None),
        P("col", "row", None),
        P("col", "row", None),
        P("col", "row", None),
        P("row", "col"),
        P("row", "col"),
        P("col", "row"),
        P(),
        P(None, "row", None),
        P(None, "row", "col"),
    )
    out_specs = (
        P(None, "row", "col"),
        P(None, "row", "col"),
        P(),
        P("row", "col"),
        P(),
        P("row", "col"),
        P("row", "col"),
        P(),
        P("row", "col"),
        P("col", "row"),
        P(),
        P("row", None),
        P("col", "row", None),
        P("col", "row", None),
        P("col", "row", None),
        P("row", "col"),
        P("row", "col"),
        P("col", "row"),
    )
    return jax.shard_map(local, mesh=mesh, in_specs=in_specs, out_specs=out_specs, check_vma=False)
```

```python
import functools
import math

import jax
import jax.numpy as jnp
from jax import lax
from jax.experimental import pallas as pl
from jax.experimental.pallas import tpu as pltpu
from jax.sharding import PartitionSpec as P

D = 2048
H = 16
DN = 128
DR = 64
DV = 128
QL = 1536
KL = 512
EXP_DEV = 2
TOPK = 6
ROWS = 16
COLS = 8
TS = 256
CUT = 208
COL_CUT = 400
LATENT_CUT = 5
FIRST_CUT = 384
DOWN_CUT = 112
SUM_CUT = 208
NORMED_CUT = 208
KV_COLS = (KL + DR) // COLS
SHARED_UNITS = 352

eps = 1e-06
route_scale = 2.446
rope_base = 50000.0
score_scale = 1.0 / math.sqrt(DN + DR)
score_bits = score_scale * math.log2(math.e)

bf16 = jnp.bfloat16
f32 = jnp.float32
ANY = pl.ANY
VM = pltpu.VMEM


def shape_of(shape, dtype):
    return jax.ShapeDtypeStruct(shape, dtype)

MESH = pl.DeviceIdType.MESH
RING = 4
VMEM_BYTES = 56 * 2**20


class Place:
    def __init__(self, axis):
        self.axis = axis
        self.index = lax.axis_index(axis)
        self.cores = 2 if axis == "row" else 1
        self.core = lax.rem(self.index, self.cores)
        self.ring = lax.rem(lax.div(self.index, self.cores), RING)
        self.pair = lax.div(self.index, self.cores * RING)

    def at(self, pair, ring, core=None):
        core = self.core if core is None else core
        return (pair * RING + ring) * self.cores + core

    def turn(self, step):
        return lax.rem(self.ring + step + RING, RING)

    def peers(self):
        found = [self.at(self.pair, self.turn(step)) for step in (1, 2, 3)]
        found.append(self.at(1 - self.pair, self.ring))
        if self.cores == 2:
            found.append(self.at(self.pair, self.ring, 1 - self.core))
        return found


class Net:
    def __init__(self, send_sems, recv_sems):
        self.send_sems, self.recv_sems = send_sems, recv_sems
        self.count = 0
        self.sent = []
        self.own = []

    def send(self, source, target, axis, index):
        number = self.count
        self.count += 1
        copy = pltpu.make_async_remote_copy(
            source,
            target,
            self.send_sems.at[number],
            self.recv_sems.at[number],
            device_id={axis: index},
            device_id_type=MESH,
        )
        copy.start()
        self.sent.append(copy)
        return number

    def receive(self, number, target, axis, index):
        pltpu.make_async_remote_copy(
            target,
            target,
            self.send_sems.at[number],
            self.recv_sems.at[number],
            device_id={axis: index},
            device_id_type=MESH,
        ).wait_recv()

    def local(self, source, target):
        number = self.count
        self.count += 1
        copy = pltpu.make_async_copy(source, target, self.send_sems.at[number])
        copy.start()
        self.own.append(copy)

    def settle(self):
        for copy in self.own:
            copy.wait()
        self.own = []

    def finish(self):
        for copy in self.sent:
            copy.wait_send()
        self.settle()


def greet(*places, everyone=False):
    barrier = pltpu.get_barrier_semaphore()
    count = 0
    for place in places:
        members = lax.axis_size(place.axis)
        all_peers = [lax.rem(place.index + step, members) for step in range(1, members)]
        for peer in all_peers if everyone else place.peers():
            pl.semaphore_signal(
                barrier, inc=1, device_id={place.axis: peer}, device_id_type=MESH
            )
            count += 1
    pl.semaphore_wait(barrier, count)


class Gather:
    def __init__(self, net, place, source, slot, rows, cut, relay=False, cross=None):
        self.net, self.place, self.source, self.slot = net, place, source, slot
        self.rows, self.cut, self.relay = rows, cut, relay
        self.first, self.second = (0, cut), (cut, rows - cut)
        self.crossed = []
        if place.cores == 2:
            partner = place.at(place.pair, place.ring, 1 - place.core)

            def other(pair, ring, low, count):
                return slot(place.at(pair, ring, 1 - place.core), low, count)

            cross = (place.axis, partner, other)
        self.cross = cross

    def _send(self, owner, part, peer, own=False):
        piece = self.slot(owner, *part)
        start = self.source.at[pl.ds(*part)] if own else piece
        return self.net.send(start, piece, self.place.axis, peer)

    def _receive(self, number, pair, ring, part, peer):
        place = self.place
        self.net.receive(number, self.slot(place.at(pair, ring), *part), place.axis, peer)

    def _cross(self, pair, ring, part, own=False):
        if self.cross is None:
            return
        piece = self.slot(self.place.at(pair, ring), *part)
        start = self.source.at[pl.ds(*part)] if own else piece
        number = self.net.send(start, piece, self.cross[0], self.cross[1])
        self.crossed.append((number, pair, ring, part))

    def _halves(self, part):
        low, count = part
        unit = 16 if count % 16 == 0 else 1
        half = max(count // 2 // unit, 1) * unit
        return (low, half), (low + half, count - half)

    def _relays(self, part):
        return self.relay and part[1] >= (32 if part[1] % 16 == 0 else 2)

    def _round(self, pair, part, own=False):
        place = self.place
        owner = place.at(pair, place.ring)
        steps = (1, 3) if self._relays(part) else (1, 3, 2)
        return {
            step: self._send(owner, part, place.at(place.pair, place.turn(step)), own)
            for step in steps
        }

    def _pass(self, numbers, pair, part, then):
        place = self.place
        passed = {}
        for step in (1, 3):
            ring = place.turn(-step)
            self._receive(numbers[step], pair, ring, part, place.at(place.pair, ring))
            if self._relays(part):
                half = self._halves(part)[step // 2]
                passed[step] = self._send(
                    place.at(pair, ring), half, place.at(place.pair, place.turn(step))
                )
            then(pair, ring, part)
        return passed

    def _meet(self, numbers, passed, pair, part, then):
        place = self.place
        far = place.turn(2)
        if self._relays(part):
            for step in (1, 3):
                half = self._halves(part)[step // 2]
                self._receive(
                    passed[step], pair, far, half, place.at(place.pair, place.turn(-step))
                )
        else:
            self._receive(numbers[2], pair, far, part, place.at(place.pair, far))
        then(pair, far, part)

    def start_first(self):
        place = self.place
        if self.cut:
            other = place.at(1 - place.pair, place.ring)
            self.across = self._send(place.index, self.first, other, True)
            self.near = self._round(place.pair, self.first, True)

    def start_second(self):
        place = self.place
        if self.second[1]:
            self.round = self._round(place.pair, self.second, True)
            other = place.at(1 - place.pair, place.ring)
            self.over = [(place.ring, self._send(place.index, self.second, other, True))]
        self._cross(place.pair, place.ring, (0, self.rows), True)
        self.net.local(self.source, self.slot(place.index, 0, self.rows))

    def start(self):
        self.start_first()
        self.start_second()

    def forward_first(self):
        place = self.place
        if self.cut:
            other = place.at(1 - place.pair, place.ring)
            self._receive(self.across, 1 - place.pair, place.ring, self.first, other)
            self.far = self._round(1 - place.pair, self.first)
            self._cross(1 - place.pair, place.ring, self.first)

    def _over(self, pair, ring, part):
        place = self.place
        other = place.at(1 - place.pair, place.ring)
        self.over.append((ring, self._send(place.at(pair, ring), part, other)))
        self._cross(pair, ring, part)

    def near_pass(self):
        place = self.place
        if self.second[1]:
            self.round_passed = self._pass(self.round, place.pair, self.second, self._over)
        if self.cut:
            self.near_passed = self._pass(self.near, place.pair, self.first, self._cross)

    def far_pass(self):
        if self.cut:
            pair = 1 - self.place.pair
            self.far_passed = self._pass(self.far, pair, self.first, self._cross)

    def near_meet(self):
        place = self.place
        if self.second[1]:
            self._meet(self.round, self.round_passed, place.pair, self.second, self._over)
        if self.cut:
            self._meet(self.near, self.near_passed, place.pair, self.first, self._cross)

    def far_meet(self):
        place = self.place
        if self.cut:
            self._meet(self.far, self.far_passed, 1 - place.pair, self.first, self._cross)
        if self.second[1]:
            other = place.at(1 - place.pair, place.ring)
            for ring, number in self.over:
                self._receive(number, 1 - place.pair, ring, self.second, other)
                self._cross(1 - place.pair, ring, self.second)

    def end(self):
        for number, pair, ring, part in self.crossed:
            axis, partner, other = self.cross
            self.net.receive(number, other(pair, ring, *part), axis, partner)


class Direct:
    def __init__(self, net, place, source, ref, count):
        self.net, self.place, self.source, self.ref, self.count = net, place, source, ref, count

    def start(self):
        place = self.place
        self.numbers = [
            self.net.send(
                self.source,
                self.ref.at[place.index],
                place.axis,
                lax.rem(place.index + step, self.count),
            )
            for step in range(1, self.count)
        ]
        self.net.local(self.source, self.ref.at[place.index])

    def land(self):
        place = self.place
        for step, number in zip(range(1, self.count), self.numbers):
            owner = lax.rem(place.index + self.count - step, self.count)
            self.net.receive(number, self.ref.at[owner], place.axis, owner)


STAGES = ("start", "forward_first", "near_pass", "far_pass", "near_meet", "far_meet", "end")


def run_stages(gathers, stages=STAGES):
    for stage in stages:
        for gather in gathers:
            getattr(gather, stage)()


def run_gathers(*gathers):
    run_stages(gathers)


def row_slots(ref, rows):
    return lambda owner, low, count: ref.at[
        pl.ds(pl.multiple_of(owner * rows + low, 16), count)
    ]


def lead_slots(ref):
    return lambda owner, low, count: ref.at[owner, pl.ds(low, count)]


def lane_slots(ref, width):
    return lambda owner, low, count: ref.at[
        pl.ds(low, count), pl.ds(pl.multiple_of(owner * width, 128), width)
    ]


class Scatter:
    def __init__(self, net, place, block, rows, cut, scratch, keep):
        self.net, self.place, self.block, self.rows, self.cut = net, place, block, rows, cut
        self.scratch, self.keep = scratch, keep
        self.first, self.second = (0, cut), (cut, rows - cut)

    @staticmethod
    def scratch_of(rows, cut, width, dtype=jnp.bfloat16):
        shapes = []
        if cut:
            shapes += [(3, 2, cut, width), (2, cut, width)]
        if rows - cut:
            shapes += [(4, rows - cut, width), (4, rows - cut, width), (3, rows - cut, width)]
        return [pltpu.VMEM(shape, dtype) for shape in shapes]

    def _refs(self):
        refs = list(self.scratch)
        first = refs[:2] if self.cut else None
        second = refs[-3:] if self.second[1] else None
        return first, second

    def _owner(self, pair, ring):
        return self.place.at(pair, ring)

    def start(self):
        place, net = self.place, self.net
        first, second = self._refs()
        if first:
            self.round = [
                [
                    net.send(
                        self.block(self._owner(pair, place.turn(step)), *self.first),
                        first[0].at[step - 1, pair],
                        place.axis,
                        place.at(place.pair, place.turn(step)),
                    )
                    for pair in (0, 1)
                ]
                for step in (1, 2, 3)
            ]
        if second:
            self.across = [
                net.send(
                    self.block(self._owner(1 - place.pair, ring), *self.second),
                    second[0].at[ring],
                    place.axis,
                    place.at(1 - place.pair, place.ring),
                )
                for ring in range(RING)
            ]

    def forward_second(self):
        place, net = self.place, self.net
        first, second = self._refs()
        if not second:
            return
        other = place.at(1 - place.pair, place.ring)
        for ring in range(RING):
            net.receive(self.across[ring], second[0].at[ring], place.axis, other)
        for ring in range(RING):
            total = (
                self.block(self._owner(place.pair, ring), *self.second)[...].astype(jnp.float32)
                + second[0][ring].astype(jnp.float32)
            )
            second[1][ring] = total.astype(second[1].dtype)
        self.last = [
            net.send(
                second[1].at[place.turn(step)],
                second[2].at[step - 1],
                place.axis,
                place.at(place.pair, place.turn(step)),
            )
            for step in (1, 2, 3)
        ]

    def forward_first(self):
        place, net = self.place, self.net
        first, second = self._refs()
        if not first:
            return
        for step in (1, 3, 2):
            owner = place.at(place.pair, place.turn(-step))
            for pair in (0, 1):
                net.receive(self.round[step - 1][pair], first[0].at[step - 1, pair], place.axis, owner)
        other = 1 - place.pair
        total = self.block(self._owner(other, place.ring), *self.first)[...].astype(jnp.float32)
        for step in range(3):
            total = total + first[0][step, other].astype(jnp.float32)
        first[1][0] = total.astype(first[1].dtype)
        self.over = net.send(
            first[1].at[0], first[1].at[1], place.axis, place.at(other, place.ring)
        )

    def end_first(self):
        place, net = self.place, self.net
        first, second = self._refs()
        if not first:
            return
        total = self.block(self._owner(place.pair, place.ring), *self.first)[...].astype(jnp.float32)
        for step in range(3):
            total = total + first[0][step, place.pair].astype(jnp.float32)
        other = place.at(1 - place.pair, place.ring)
        net.receive(self.over, first[1].at[1], place.axis, other)
        self.keep(self.first, total + first[1][1].astype(jnp.float32))

    def end_second(self):
        place, net = self.place, self.net
        first, second = self._refs()
        if not second:
            return
        total = (
            self.block(self._owner(place.pair, place.ring), *self.second)[...].astype(jnp.float32)
            + second[0][place.ring].astype(jnp.float32)
        )
        for step in (1, 3, 2):
            owner = place.at(place.pair, place.turn(-step))
            net.receive(self.last[step - 1], second[2].at[step - 1], place.axis, owner)
            total = total + second[2][step - 1].astype(jnp.float32)
        self.keep(self.second, total)


def comm_call(body, name, collective_id, out_shapes, in_spaces, out_spaces, copies, scratch=(), args=(), aliases=None):
    return pl.pallas_call(
        body,
        name=name,
        out_shape=out_shapes,
        in_specs=[pl.BlockSpec(memory_space=space) for space in in_spaces],
        out_specs=tuple(pl.BlockSpec(memory_space=space) for space in out_spaces),
        scratch_shapes=[
            pltpu.SemaphoreType.DMA((copies,)),
            pltpu.SemaphoreType.DMA((copies,)),
            *scratch,
        ],
        input_output_aliases=aliases or {},
        compiler_params=pltpu.CompilerParams(
            collective_id=collective_id, has_side_effects=True, vmem_limit_bytes=VMEM_BYTES
        ),
    )(*args)


def plane_slots(ref, plane):
    return lambda owner, low, count: ref.at[
        plane, pl.ds(pl.multiple_of(owner * (D // ROWS) + low, 16), count)
    ]


def plane_gather(net, row, source, ref, plane, cut):
    return Gather(net, row, source, plane_slots(ref, plane), D // ROWS, cut, True)


def front_body(hidden, grad, w1, qu, lu, ao, sg, su, sd, gate, down, *rest):
    hidden_all, grad_all, w1_all, qu_all, lu_all, ao_all, sg_all, su_all, sd_all = rest[:9]
    planes, down_chip, ss, rs, down_other = rest[9:]
    row, col = Place("row"), Place("col")
    greet(row, col)
    net = Net(ss, rs)
    partner = row.at(row.pair, row.ring, 1 - row.core)
    gathers = [
        Gather(net, col, hidden, lane_slots(hidden_all, D // COLS), 2 * TS, 2 * TS, True),
        *(
            Gather(net, row, term, row_slots(ref, term.shape[0]), term.shape[0], cut, True)
            for term, ref, cut in (
                (qu, qu_all, 96),
                (lu, lu_all, 32),
            )
        ),
        *(
            Gather(net, row, term, lane_slots(ref, term.shape[1]), term.shape[0], cut, True)
            for term, ref, cut in (
                (w1, w1_all, 192),
                (ao, ao_all, 192),
                (sg, sg_all, 352),
                (su, su_all, 256),
                (sd, sd_all, 256),
            )
        ),
        plane_gather(net, row, gate.at[0], planes, 0, 64),
        Gather(net, col, grad, lane_slots(grad_all, D // COLS), 2 * TS, 2 * TS, True),
    ]
    number = net.send(down.at[1 - row.core], down_other, "row", partner)
    run_stages(gathers, STAGES[:1])
    net.receive(number, down_other, "row", partner)
    height = down_chip.shape[0] // 2
    own = down[row.core].astype(f32)[:height]
    given = down_other[...].astype(f32)[:height]
    even = row.core == 0
    down_chip[...] = jnp.concatenate(
        [jnp.where(even, own, given), jnp.where(even, given, own)], axis=0
    ).astype(bf16)
    run_stages(gathers, STAGES[1:])
    net.finish()


def stacked(term):
    return shape_of((ROWS * term.shape[0], term.shape[1]), term.dtype)


def side_by_side(term):
    return shape_of((term.shape[0], ROWS * term.shape[1]), term.dtype)


def front(hidden, grad, w1, qu, lu, ao, sg, su, sd, gate, down, units):
    return comm_call(
        front_body,
        "gather_front",
        1,
        (
            shape_of((2 * TS, D), bf16),
            shape_of((2 * TS, D), bf16),
            side_by_side(w1),
            stacked(qu),
            stacked(lu),
            side_by_side(ao),
            side_by_side(sg),
            side_by_side(su),
            side_by_side(sd),
            shape_of((2 * EXP_DEV, D, units), bf16),
            shape_of((2 * units // ROWS, D), bf16),
        ),
        [ANY] * 10 + [VM],
        [ANY] * 10 + [VM],
        256,
        [pltpu.VMEM(down.shape[1:], bf16)],
        (hidden, grad, w1, qu, lu, ao, sg, su, sd, gate, down),
    )


def latent_body(query, latent, gate, up, _, query_all, rows_all, latent_all, planes, ss, rs):
    row, col = Place("row"), Place("col")
    greet(row, col)
    net = Net(ss, rs)
    queries = Gather(
        net, col, query, row_slots(query_all, query.shape[0]), query.shape[0], 192, True
    )
    weights = [
        plane_gather(net, row, up.at[0], planes, 1, 96),
        plane_gather(net, row, gate.at[1], planes, 2, 96),
    ]
    rows = Gather(net, row, latent, lead_slots(rows_all), latent.shape[0], 48)
    half = ROWS // 2
    base = row.core * half
    partner = row.at(row.pair, row.ring, 1 - row.core)

    def slot(owner, low, count):
        return latent_all.at[owner, pl.ds(base + low, count)]

    def other(pair, ring, low, count):
        return latent_all.at[col.at(pair, ring), pl.ds(half - base + low, count)]

    every = Gather(
        net, col, rows_all.at[pl.ds(base, half)], slot, half, LATENT_CUT, True, ("row", partner, other)
    )
    run_stages((rows, queries), STAGES[:1])
    run_stages((rows,), STAGES[1:])
    net.settle()
    run_stages((every, *weights), STAGES[:1])
    run_stages((queries, every, *weights), STAGES[1:])
    net.finish()


def latents(query, latent, gate, up, planes):
    return comm_call(
        latent_body,
        "gather_latents",
        2,
        (
            shape_of((COLS * query.shape[0], query.shape[1]), bf16),
            shape_of((ROWS, *latent.shape), bf16),
            shape_of((COLS, ROWS, *latent.shape), bf16),
            shape_of(planes.shape, bf16),
        ),
        [ANY] * 5,
        [ANY] * 4,
        192,
        args=(query, latent, gate, up, planes),
        aliases={4: 3},
    )


def expand_body(latent, weight, gain, cos, sin, start_cos, start_sin, out):
    @pl.when(pl.program_id(0) <= lax.axis_index("row") + 1)
    def _():
        features = latent.shape[0] * latent.shape[2]
        values = latent[:, 0].reshape(features, latent.shape[3]).astype(f32)
        live = features - latent.shape[2] + 8
        square = jnp.sum(values[:live] * values[:live], axis=0, keepdims=True)
        scaled = (values * lax.rsqrt(square / KL + eps) * gain[...]).astype(bf16)
        found = jnp.dot(weight[...], scaled, preferred_element_type=f32).astype(bf16)
        turn_cos = cos[...] * start_cos[0] - sin[...] * start_sin[0]
        turn_sin = sin[...] * start_cos[0] + cos[...] * start_sin[0]
        turn_cos = jnp.concatenate([turn_cos, turn_cos], axis=1)
        turn_sin = jnp.concatenate([turn_sin, turn_sin], axis=1)
        first, second = values[live : live + 32], values[live + 32 : live + 64]
        rope = jnp.concatenate(
            [first * turn_cos - second * turn_sin, second * turn_cos + first * turn_sin], axis=0
        ).astype(bf16)
        out[0, 0:128] = found[0:128]
        out[0, 128:192] = rope
        out[0, 192:256] = rope
        out[0, 256:384] = found[256:384]
        out[0, 384:512] = found[128:256]
        out[0, 512:640] = found[384:512]


def expand(latent, weight, gain, cos, sin, start_cos, start_sin):
    cols, rows, height, width = latent.shape
    return pl.pallas_call(
        expand_body,
        name="expand_keys",
        grid=(rows,),
        out_shape=shape_of((rows, 640, width), bf16),
        in_specs=[
            pl.BlockSpec((cols, 1, height, width), lambda r: (0, r, 0, 0)),
            pl.BlockSpec(weight.shape, lambda r: (0, 0)),
            pl.BlockSpec(gain.shape, lambda r: (0, 0)),
            pl.BlockSpec((32, TS), lambda r: (0, 0)),
            pl.BlockSpec((32, TS), lambda r: (0, 0)),
            pl.BlockSpec((1, 32, 1), lambda r: (r, 0, 0)),
            pl.BlockSpec((1, 32, 1), lambda r: (r, 0, 0)),
        ],
        out_specs=pl.BlockSpec((1, 640, width), lambda r: (r, 0, 0)),
        compiler_params=pltpu.CompilerParams(vmem_limit_bytes=VMEM_BYTES),
        cost_estimate=pl.CostEstimate(
            flops=6 * 10**9, bytes_accessed=22 * 10**6, transcendentals=8192
        ),
    )(latent, weight, gain, cos, sin, start_cos, start_sin)


class ColSum:
    def __init__(self, net, col, term, total, cut, scratch):
        width = D // COLS
        *scratch, mine = scratch
        count = len(Scatter.scratch_of(TS, cut, width))
        self.parts = []
        for chunk in range(2):
            first = chunk * TS

            def block(owner, low, rows, first=first):
                return lane_slots(term, width)(owner, first + low, rows)

            def slot(owner, low, rows, first=first):
                return lane_slots(total, width)(owner, first + low, rows)

            def keep(part, value, chunk=chunk):
                mine[chunk, pl.ds(*part)] = value.astype(mine.dtype)

            part_scratch = scratch[chunk * count : (chunk + 1) * count]
            self.parts.append(
                (
                    Scatter(net, col, block, TS, cut, part_scratch, keep),
                    Gather(net, col, mine.at[chunk], slot, TS, cut, True),
                )
            )

    @staticmethod
    def scratch_of(cut):
        return [
            *Scatter.scratch_of(TS, cut, D // COLS),
            *Scatter.scratch_of(TS, cut, D // COLS),
            pltpu.VMEM((2, TS, D // COLS), bf16),
        ]

    def start(self):
        for scatter, _ in self.parts:
            scatter.start()

    def summed(self, chunk):
        scatter, gather = self.parts[chunk]
        scatter.forward_second()
        scatter.forward_first()
        scatter.end_first()
        gather.start_first()
        scatter.end_second()
        gather.start_second()

    def sent(self, chunk, stages):
        run_stages((self.parts[chunk][1],), stages)


def sum_body(cut, extra_cut, term, extra, total_all, extra_all, ss, rs, *scratch):
    col = Place("col")
    greet(col)
    net = Net(ss, rs)
    total = ColSum(net, col, term, total_all, cut, scratch)
    beside = Gather(net, col, extra, lead_slots(extra_all), extra.shape[0], extra_cut, True)
    total.start()
    run_stages((beside,), STAGES[:1])
    total.summed(0)
    run_stages((beside,), STAGES[1:3])
    total.sent(0, STAGES[1:2])
    total.summed(1)
    total.sent(0, STAGES[2:4])
    total.sent(1, STAGES[1:4])
    total.sent(0, STAGES[4:])
    run_stages((beside,), STAGES[3:])
    total.sent(1, STAGES[4:])
    net.finish()


def sum_over_col(name, collective_id, term, cut, extra, extra_cut):
    return comm_call(
        functools.partial(sum_body, cut, extra_cut),
        name,
        collective_id,
        (shape_of((2 * TS, D), bf16), shape_of((COLS, *extra.shape), extra.dtype)),
        [VM, ANY],
        [ANY, ANY],
        160,
        ColSum.scratch_of(cut),
        (term, extra),
    )


def attention_sum_body(term, up, down, _, total_all, planes, down_all, ss, rs, *scratch):
    row, col = Place("row"), Place("col")
    greet(row, col)
    net = Net(ss, rs)
    width = D // COLS
    mine = scratch[-1]

    def keep(part, value):
        mine[pl.ds(*part)] = value.astype(mine.dtype)

    height = down.shape[0]

    def down_slot(owner, low, count):
        place = pl.multiple_of(lax.div(owner, 2) * height + low, 16)
        return down_all.at[lax.rem(owner, 2), pl.ds(place, count)]

    scatter = Scatter(net, col, lane_slots(term, width), 2 * TS, 2 * TS, scratch[:-1], keep)
    gather = Gather(net, col, mine, lane_slots(total_all, width), 2 * TS, 2 * TS, True)
    weights = [
        plane_gather(net, row, up.at[1], planes, 3, 96),
        Gather(net, row, down, down_slot, height, 112, True),
    ]
    scatter.start()
    run_stages(weights, STAGES[:1])
    scatter.forward_first()
    run_stages(weights, STAGES[1:2])
    scatter.end_first()
    gather.start()
    run_stages(weights, STAGES[2:3])
    run_stages((gather,), STAGES[1:3])
    run_stages(weights, STAGES[3:4])
    run_stages((gather,), STAGES[3:5])
    run_stages(weights, STAGES[4:5])
    run_stages((gather, *weights), STAGES[5:])
    net.finish()


def attention_sum_over_col(term, up, down, planes):
    return comm_call(
        attention_sum_body,
        "sum_attention",
        4,
        (
            shape_of((2 * TS, D), bf16),
            shape_of(planes.shape, bf16),
            shape_of((EXP_DEV, ROWS // 2 * down.shape[0], D), bf16),
        ),
        [VM, ANY, ANY, ANY],
        [ANY] * 3,
        128,
        [*Scatter.scratch_of(2 * TS, 2 * TS, D // COLS), pltpu.VMEM((2 * TS, D // COLS), bf16)],
        (term, up, down, planes),
        aliases={3: 1},
    )


def back_body(grad, stats, branch, grad_all, stats_all, branch_sum, ss, rs, *scratch):
    row, col = Place("row"), Place("col")
    greet(row, col)
    net = Net(ss, rs)

    def keep(part, value):
        branch_sum[pl.ds(*part)] = value

    scatter = Scatter(net, col, lane_slots(branch, D // COLS), 2 * TS, COL_CUT, scratch, keep)
    gathers = (
        Gather(net, row, grad, lead_slots(grad_all), 2 * TS, 208, True),
        Gather(net, row, stats, lead_slots(stats_all), stats.shape[0], stats.shape[0]),
    )
    run_stages(gathers, STAGES[:1])
    scatter.start()
    run_stages(gathers, STAGES[1:3])
    scatter.forward_second()
    scatter.forward_first()
    run_stages(gathers, STAGES[3:6])
    scatter.end_first()
    scatter.end_second()
    run_stages(gathers, STAGES[6:])
    net.finish()


def back(grad, stats, branch):
    return comm_call(
        back_body,
        "gather_back",
        6,
        (
            shape_of((ROWS, *grad.shape), bf16),
            shape_of((ROWS, *stats.shape), f32),
            shape_of((2 * TS, D // COLS), f32),
        ),
        [ANY, ANY, VM],
        [ANY, ANY, VM],
        96,
        Scatter.scratch_of(2 * TS, COL_CUT, D // COLS),
        (grad, stats, branch),
    )


class RowScatter:
    def __init__(self, net, place, term, cut, scratch, keep):
        self.net, self.place, self.term = net, place, term
        self.arrived, self.summed = scratch[:2]
        rows = term.shape[3]

        def block(owner, low, count):
            return self.summed.at[lax.div(owner, 2), pl.ds(low, count)]

        self.inner = Scatter(net, place, block, rows, cut, scratch[2:], keep)

    @staticmethod
    def scratch_of(rows, cut, width):
        return [
            pltpu.VMEM((2, RING, rows, width), bf16),
            pltpu.VMEM((2 * RING, rows, width), bf16),
            *Scatter.scratch_of(rows, cut, width),
        ]

    def start(self):
        place = self.place
        self.partner = place.at(place.pair, place.ring, 1 - place.core)
        self.number = self.net.send(
            self.term.at[:, :, 1 - place.core], self.arrived, place.axis, self.partner
        )

    def middle(self):
        place = self.place
        self.net.receive(self.number, self.arrived, place.axis, self.partner)
        for pair in range(2):
            for ring in range(RING):
                self.summed[pair * RING + ring] = (
                    self.term[pair, ring, place.core].astype(f32)
                    + self.arrived[pair, ring].astype(f32)
                ).astype(bf16)
        self.inner.start()


def run_scatters(scatters):
    for scatter in scatters:
        scatter.forward_second()
    for scatter in scatters:
        scatter.forward_first()
    for scatter in scatters:
        scatter.end_first()
    for scatter in scatters:
        scatter.end_second()


def keep_in(ref):
    def keep(part, value):
        ref[pl.ds(*part)] = value

    return keep


def block_slots(ref):
    return lambda owner, low, count: ref.at[owner, pl.ds(low, count)]


def rows_sum(net, place, terms, cuts, totals, scratch):
    parts = []
    for term, cut, total in zip(terms, cuts, totals):
        count = len(RowScatter.scratch_of(term.shape[3], cut, term.shape[4]))
        parts.append(RowScatter(net, place, term, cut, scratch[:count], keep_in(total)))
        scratch = scratch[count:]
    return parts


def rows_scratch(terms, cuts):
    found = []
    for term, cut in zip(terms, cuts):
        found += RowScatter.scratch_of(term.shape[3], cut, term.shape[4])
    return found


def col_and_row_body(col_cuts, row_cuts, slots, *rest):
    cols, rows = len(col_cuts), len(row_cuts)
    col_terms, rest = rest[:cols], rest[cols:]
    extra, rest = rest[0], rest[1:]
    row_terms, rest = rest[:rows], rest[rows:]
    col_totals, rest = rest[:cols], rest[cols:]
    extra_all, rest = rest[0], rest[1:]
    row_totals, rest = rest[:rows], rest[rows:]
    ss, rs, *scratch = rest
    row, col = Place("row"), Place("col")
    greet(row, col)
    net = Net(ss, rs)
    scatters = []
    for term, cut, total in zip(col_terms, col_cuts, col_totals):
        height, width = total.shape
        block = lane_slots(term, width) if slots == "lane" else block_slots(term)
        count = len(Scatter.scratch_of(height, cut, width))
        scatters.append(Scatter(net, col, block, height, cut, scratch[:count], keep_in(total)))
        scratch = scratch[count:]
    beside = Gather(net, col, extra, lead_slots(extra_all), extra.shape[0], extra.shape[0])
    parts = rows_sum(net, row, row_terms, row_cuts, row_totals, scratch)
    for part in parts:
        part.start()
    for scatter in scatters:
        scatter.start()
    beside.start()
    for part in parts:
        part.middle()
    run_stages((beside,), STAGES[1:2])
    run_scatters(scatters + [part.inner for part in parts])
    run_stages((beside,), STAGES[2:])
    net.finish()


def col_and_row(name, collective_id, slots, col_terms, col_shapes, col_cuts, extra, row_terms, row_cuts):
    scratch = []
    for shape, cut in zip(col_shapes, col_cuts):
        scratch += Scatter.scratch_of(shape[0], cut, shape[1])
    found = comm_call(
        functools.partial(col_and_row_body, tuple(col_cuts), tuple(row_cuts), slots),
        name,
        collective_id,
        (
            *(shape_of(shape, f32) for shape in col_shapes),
            shape_of((COLS, *extra.shape), f32),
            *(shape_of(term.shape[3:], f32) for term in row_terms),
        ),
        [*([VM] * len(col_terms)), ANY, *([VM] * len(row_terms))],
        [*([VM] * len(col_terms)), ANY, *([VM] * len(row_terms))],
        128,
        [*scratch, *rows_scratch(row_terms, row_cuts)],
        (*col_terms, extra, *row_terms),
    )
    count = len(col_terms)
    return found[:count], found[count], found[count + 1 :]


def first_sum_body(row_cuts, term, extra, normed, gains, *rest):
    rows = len(row_cuts)
    row_terms, rest = rest[:rows], rest[rows:]
    total, extra_all, gains_all, rest = *rest[:3], rest[3:]
    row_totals, rest = rest[:rows], rest[rows:]
    ss, rs, gains_rows, gains_mine, *scratch = rest
    row, col = Place("row"), Place("col")
    greet(row, col, everyone=True)
    net = Net(ss, rs)
    height, width = total.shape
    count = len(Scatter.scratch_of(height, FIRST_CUT, width))
    scatter = Scatter(
        net, col, lane_slots(term, width), height, FIRST_CUT, scratch[:count], keep_in(total)
    )
    beside = Direct(net, col, extra, extra_all, COLS)
    parts = rows_sum(net, row, row_terms, row_cuts, row_totals, scratch[count:])
    inner = [part.inner for part in parts]
    scatter.start()
    for part in parts:
        part.start()
    beside.start()
    for part in parts:
        part.middle()
    scatter.forward_second()
    scatter.forward_first()
    for part in inner:
        part.forward_second()
    for part in inner:
        part.forward_first()
    scatter.end_first()
    scatter.end_second()
    gain = jnp.sum(total[...] * normed[...], axis=0, keepdims=True)
    gains_mine[...] = gains[...]
    gains_mine[0:1] = gain[:, :128]
    gains_mine[1:2] = gain[:, 128:]
    every = Direct(net, row, gains_mine, gains_rows, ROWS)
    every.start()
    for part in inner:
        part.end_first()
    beside.land()
    every.land()
    net.settle()
    found = gains_rows[0]
    for index in range(1, ROWS):
        found = found + gains_rows[index]
    gains_rows[ROWS] = found
    spread = Direct(net, col, gains_rows.at[ROWS], gains_all, COLS)
    spread.start()
    for part in inner:
        part.end_second()
    spread.land()
    net.finish()


def first_sum(term, extra, normed, gains, row_terms, row_cuts):
    width = D // COLS
    found = comm_call(
        functools.partial(first_sum_body, tuple(row_cuts)),
        "sum_first",
        8,
        (
            shape_of((2 * TS, width), f32),
            shape_of((COLS, *extra.shape), f32),
            shape_of((COLS, 8, 128), f32),
            *(shape_of(term.shape[3:], f32) for term in row_terms),
        ),
        [VM] * (4 + len(row_terms)),
        [VM] * (3 + len(row_terms)),
        160,
        [
            pltpu.VMEM((ROWS + 1, 8, 128), f32),
            pltpu.VMEM((8, 128), f32),
            *Scatter.scratch_of(2 * TS, FIRST_CUT, width),
            *rows_scratch(row_terms, row_cuts),
        ],
        (term, extra, normed, gains, *row_terms),
    )
    return found[:3], found[3:]


def contract(left, right):
    return lax.dot_general(left, right, (((1,), (1,)), ((), ())), preferred_element_type=f32)


def masked_queries(pack):
    lanes = lax.broadcasted_iota(jnp.int32, (pack.shape[0], 256), 1)
    zero = jnp.zeros((), pack.dtype)
    return (
        jnp.where(lanes < 192, pack[:, :256], zero),
        jnp.where(lanes >= 64, pack[:, 128:], zero),
    )


def attend_body(lens, query, kvt, out, lse, lse_rows, scores):
    seq = pl.program_id(0)
    mine = lax.axis_index("row")
    live = lens[seq]
    steps = lax.div(jnp.minimum(mine + 1, lax.div(live + TS - 1, TS)) + 1, 2)
    places = mine * TS + lax.broadcasted_iota(jnp.int32, (TS, 1), 0)
    limit = jnp.minimum(places + 1, live)
    offsets = lax.broadcasted_iota(jnp.int32, (TS, TS), 1)
    queries = masked_queries(query[...])

    def first(step, tops):
        tops = list(tops)
        for half in range(2):
            index = 2 * step + half
            valid = offsets < limit - index * TS
            for head in range(2):
                key = kvt[index, head * 128 : head * 128 + 256]
                value = jnp.dot(queries[head], key, preferred_element_type=f32)
                value = jnp.where(valid, value, -1e30)
                scores[head, index] = value
                tops[head] = jnp.maximum(
                    tops[head], jnp.maximum(value[:, :128], value[:, 128:])
                )
        return tuple(tops)

    tops = lax.fori_loop(0, steps, first, (jnp.full((TS, 128), -1e30, f32),) * 2)
    tops = [jnp.max(top, axis=1, keepdims=True) * score_bits for top in tops]

    def second(step, carried):
        found = []
        for head in range(2):
            sums, total = carried[head]
            for half in range(2):
                index = 2 * step + half
                weight = jnp.exp2(scores[head, index] * score_bits - tops[head])
                sums = sums + (weight[:, :128] + weight[:, 128:])
                value = kvt[index, 384 + head * 128 : 512 + head * 128]
                total = total + contract(weight.astype(bf16), value)
            found.append((sums, total))
        return tuple(found)

    zero = jnp.zeros((TS, 128), f32)
    carried = lax.fori_loop(0, steps, second, ((zero, zero),) * 2)
    lse_rows[...] = jnp.zeros_like(lse_rows)
    for head in range(2):
        sums, total = carried[head]
        whole = jnp.sum(sums, axis=1, keepdims=True)
        lanes = pl.ds(head * 128, 128)
        out[:, lanes] = total / whole
        value = jnp.broadcast_to(tops[head] + jnp.log2(whole), (TS, 128))
        lse[:, lanes] = value
        lse_rows[head : head + 1] = value.T[:1]


def attend(lens, query, kvt):
    return pl.pallas_call(
        attend_body,
        name="attend",
        grid=(2,),
        out_shape=(
            shape_of((2 * TS, 256), f32),
            shape_of((2 * TS, 256), f32),
            shape_of((8, 2 * TS), f32),
        ),
        in_specs=[
            pl.BlockSpec(memory_space=pltpu.SMEM),
            pl.BlockSpec((TS, 384), lambda s: (s, 0)),
            pl.BlockSpec((ROWS, 640, TS), lambda s: (0, 0, s)),
        ],
        out_specs=(
            pl.BlockSpec((TS, 256), lambda s: (s, 0)),
            pl.BlockSpec((TS, 256), lambda s: (s, 0)),
            pl.BlockSpec((8, TS), lambda s: (0, s)),
        ),
        scratch_shapes=[pltpu.VMEM((2, ROWS, TS, TS), f32)],
        compiler_params=pltpu.CompilerParams(vmem_limit_bytes=VMEM_BYTES),
        cost_estimate=pl.CostEstimate(
            flops=6 * 10**9, bytes_accessed=12 * 10**6, transcendentals=4 * 10**6
        ),
    )(lens, query, kvt)


def attend_back_body(lens, query, kvt, grad, lse, delta, near, query_all, grad_all, stats, dq, dk, dv):
    seq = pl.program_id(0)
    mine = lax.axis_index("row")
    live = lens[seq]
    width = 2 * TS
    steps = lax.div(jnp.minimum(mine + 1, lax.div(live + TS - 1, TS)) + 1, 2)
    places = mine * TS + lax.broadcasted_iota(jnp.int32, (TS, 1), 0)
    limit = jnp.minimum(places + 1, live)
    narrow = lax.broadcasted_iota(jnp.int32, (TS, TS), 1)
    wide = lax.broadcasted_iota(jnp.int32, (TS, width), 1)
    queries = masked_queries(query[...])

    def queries_step(step, carried):
        totals = list(carried)
        for half in range(2):
            index = 2 * step + half
            valid = narrow < limit - index * TS
            for head in range(2):
                key = kvt[index, head * 128 : head * 128 + 256]
                value = kvt[index, 384 + head * 128 : 512 + head * 128]
                lanes = pl.ds(head * 128, 128)
                score = jnp.dot(queries[head], key, preferred_element_type=f32)
                score = score * score_bits - lse[:, lanes][:, :1]
                weight = jnp.exp2(jnp.where(valid, score, -1e30))
                slope = jnp.dot(grad[:, lanes], value, preferred_element_type=f32)
                low = (weight * (slope - delta[:, lanes][:, :1])).astype(bf16)
                totals[head] = totals[head] + contract(low, key)
        return tuple(totals)

    totals = lax.fori_loop(0, steps, queries_step, (jnp.zeros((TS, 256), f32),) * 2)
    edge = lax.broadcasted_iota(jnp.int32, (TS, 128), 1) < DR
    dq[:, 0:128] = totals[0][:, :128] * score_scale
    dq[:, 128:256] = jnp.where(edge, totals[0][:, 128:], totals[1][:, :128]) * score_scale
    dq[:, 256:384] = totals[1][:, 128:] * score_scale

    bar = jnp.where(places < live, places, 2 * ROWS * TS)
    keys = masked_queries(near[:, :384])

    def keys_step(step, carried):
        valid = wide >= bar - step * width
        queries = query_all[pl.ds(2 * step, 2)].reshape(width, query_all.shape[2])
        grads = grad_all[pl.ds(2 * step, 2)].reshape(width, 256)
        numbers = stats[pl.ds(2 * step, 2)]
        numbers = jnp.concatenate([numbers[0], numbers[1]], axis=1)
        found = []
        for head in range(2):
            key_total, value_total = carried[head]
            asked = queries[:, head * 128 : head * 128 + 256]
            given = grads[:, head * 128 : head * 128 + 128]
            score = contract(keys[head], asked) * score_bits - numbers[head : head + 1]
            weight = jnp.exp2(jnp.where(valid, score, -1e30))
            value_total = value_total + jnp.dot(
                weight.astype(bf16), given, preferred_element_type=f32
            )
            value = near[:, 384 + head * 128 : 512 + head * 128]
            slope = contract(value, given) - numbers[2 + head : 3 + head]
            low = (weight * slope).astype(bf16)
            key_total = key_total + jnp.dot(low, asked, preferred_element_type=f32)
            found.append((key_total, value_total))
        return tuple(found)

    zero = (jnp.zeros((TS, 256), f32), jnp.zeros((TS, 128), f32))
    last_step = jnp.where(mine * TS < live, ROWS // 2, 0)
    totals = lax.fori_loop(lax.div(mine, 2), last_step, keys_step, (zero, zero))
    dk[:, 0:128] = totals[0][0][:, :128] * score_scale
    dk[:, 128:256] = jnp.where(edge, totals[0][0][:, 128:], totals[1][0][:, :128]) * score_scale
    dk[:, 256:384] = totals[1][0][:, 128:] * score_scale
    dv[:, 0:128] = totals[0][1]
    dv[:, 128:256] = totals[1][1]


def attend_back(lens, query, kvt, grad, lse, delta, near, query_all, grad_all, stats):
    def lanes(width):
        return pl.BlockSpec((TS, width), lambda s: (s, 0))

    return pl.pallas_call(
        attend_back_body,
        name="attend_back",
        grid=(2,),
        out_shape=(
            shape_of((2 * TS, 384), f32),
            shape_of((2 * TS, 384), f32),
            shape_of((2 * TS, 256), f32),
        ),
        in_specs=[
            pl.BlockSpec(memory_space=pltpu.SMEM),
            lanes(384),
            pl.BlockSpec((ROWS, 640, TS), lambda s: (0, 0, s)),
            lanes(256),
            lanes(256),
            lanes(256),
            lanes(640),
            pl.BlockSpec((ROWS, TS, query_all.shape[2]), lambda s: (0, s, 0)),
            pl.BlockSpec((ROWS, TS, 256), lambda s: (0, s, 0)),
            pl.BlockSpec((ROWS, 8, TS), lambda s: (0, 0, s)),
        ],
        out_specs=(lanes(384), lanes(384), lanes(256)),
        compiler_params=pltpu.CompilerParams(vmem_limit_bytes=VMEM_BYTES),
        cost_estimate=pl.CostEstimate(
            flops=12 * 10**9, bytes_accessed=24 * 10**6, transcendentals=8 * 10**6
        ),
    )(lens, query, kvt, grad, lse, delta, near, query_all, grad_all, stats)


def project_back_body(
    dq, dk, dv, cos, sin, query_up, latent_up, query_in, latent_in, query_raw, latent_raw,
    query_gain, latent_gain, query_up_grad, latent_up_grad, query_grad, latent_grad, numbers,
):
    def turn_back(tile):
        return tile * cos[...] - swap_halves(tile) * sin[...]

    queries = jnp.concatenate(
        [dq[:, :128], turn_back(dq[:, 128:256]), dq[:, 256:]], axis=1
    ).astype(bf16)
    middle = dk[:, 128:256]
    middle = middle + pltpu.roll(middle, DR, 1)
    rope = turn_back(middle)
    pairs = jnp.concatenate(
        [dk[:, :128], dv[:, :128], dk[:, 256:], dv[:, 128:]], axis=1
    ).astype(bf16)
    query_up_grad[...] = jnp.dot(query_in[...], queries, preferred_element_type=f32).astype(bf16)
    latent_up_grad[...] = jnp.dot(latent_in[...], pairs, preferred_element_type=f32).astype(bf16)
    back = contract(query_up[...], queries)
    query_grad[...] = back.astype(bf16)
    numbers[...] = jnp.zeros_like(numbers)
    numbers[0:1] = jnp.sum(back * query_gain[...] * query_raw[...].astype(f32), axis=0, keepdims=True)
    back = contract(latent_up[...], pairs)
    numbers[1:2] = jnp.sum(
        back * latent_gain[...] * latent_raw[...].astype(f32), axis=0, keepdims=True
    )
    latent_grad[:KL] = back.astype(bf16)
    latent_grad[KL:] = rope.T[:DR].astype(bf16)


def project_back(*terms):
    query_up, latent_up, query_in, latent_in = terms[5:9]
    return pl.pallas_call(
        project_back_body,
        name="project_back",
        out_shape=(
            shape_of(query_up.shape, bf16),
            shape_of(latent_up.shape, bf16),
            shape_of(query_in.shape, bf16),
            shape_of((KL + DR, 2 * TS), bf16),
            shape_of((8, 2 * TS), f32),
        ),
        in_specs=[pl.BlockSpec(memory_space=VM)] * len(terms),
        out_specs=(pl.BlockSpec(memory_space=VM),) * 5,
        compiler_params=pltpu.CompilerParams(vmem_limit_bytes=VMEM_BYTES),
        cost_estimate=pl.CostEstimate(
            flops=2 * 10**9, bytes_accessed=16 * 10**6, transcendentals=0
        ),
    )(*terms)


def silu_parts(gate_value):
    sigmoid_value = 1.0 / (1.0 + jnp.exp(-gate_value))
    return (gate_value * sigmoid_value, sigmoid_value * (1.0 + gate_value * (1.0 - sigmoid_value)))


def transposed(left, right):
    return lax.dot_general(left, right, (((0,), (0,)), ((), ())), preferred_element_type=f32)


def shared_body(
    hidden, attention, gain, grad, gate, up, down, normed, branch, back_grad, weight_grad
):
    residual = hidden[...].astype(f32) + attention[...].astype(f32)
    scale = lax.rsqrt(jnp.mean(residual * residual, axis=1, keepdims=True) + eps)
    normed_value, grad_value = (residual * scale * gain[...]).astype(bf16), grad[...]
    normed[...] = normed_value
    gate_value = contract(normed_value, gate[...])
    up_value = contract(normed_value, up[...])
    silu_value, slope = silu_parts(gate_value)
    act = (silu_value * up_value).astype(bf16)
    act_grad = contract(grad_value, down[...])
    gate_low = (act_grad * up_value * slope).astype(bf16)
    up_low = (act_grad * silu_value).astype(bf16)
    branch[...] = jnp.dot(act, down[...], preferred_element_type=f32)
    back_grad[...] = jnp.dot(gate_low, gate[...], preferred_element_type=f32) + jnp.dot(
        up_low, up[...], preferred_element_type=f32
    )
    lanes = weight_grad.shape[1] // 3
    blank = jnp.zeros((gate_low.shape[0], lanes - gate_low.shape[1]), bf16)
    parts = ((normed_value, gate_low), (normed_value, up_low), (grad_value, act))
    for index, (left, right) in enumerate(parts):
        right = jnp.concatenate([right, blank], axis=1)
        weight_grad[:, index * lanes : (index + 1) * lanes] = transposed(left, right).astype(bf16)


def shared_experts(hidden, attention, gain, grad, gate, up, down):
    units = gate.shape[0]
    return pl.pallas_call(
        shared_body,
        name="shared_experts",
        out_shape=(
            shape_of((2 * TS, D), bf16),
            shape_of((2 * TS, D), f32),
            shape_of((2 * TS, D), f32),
            shape_of((D, 3 * (units + (-units) % 128)), bf16),
        ),
        in_specs=[pl.BlockSpec(memory_space=VM)] * 7,
        out_specs=(pl.BlockSpec(memory_space=VM),) * 4,
        compiler_params=pltpu.CompilerParams(vmem_limit_bytes=VMEM_BYTES),
        cost_estimate=pl.CostEstimate(
            flops=8 * 10**9, bytes_accessed=24 * 10**6, transcendentals=10**6
        ),
    )(hidden, attention, gain, grad, gate, up, down)


def experts_body(
    slots, gates, normed, grad, branch_in, back_in, w_in, w_down,
    branch, back_grad, gate_grad, sums,
    dispatch, taken, taken_turned, given, routed, result, back_sum, branch_sum, back_total,
    act_turned, staged, down_staged, sems,
):
    expert, step = pl.program_id(0), pl.program_id(1)
    steps = pl.num_programs(1)
    capacity = dispatch.shape[0]
    units = w_down.shape[1]
    height = D // ROWS
    number = expert * steps + step
    slot = lax.rem(number, 2)
    down_rows = act_turned.shape[0] // ROWS

    def in_copy(slot, expert, step):
        target = sums.at[
            :,
            pl.ds(pl.multiple_of(expert * 2 * height, 2 * height), 2 * height),
            pl.ds(pl.multiple_of(step * units, units), units),
        ]
        return pltpu.make_async_copy(staged.at[slot], target, sems.at[slot])

    def down_copy(expert):
        first = pl.multiple_of(2 * EXP_DEV * height + expert * height, height)
        return pltpu.make_async_copy(down_staged, sums.at[:, pl.ds(first, height)], sems.at[2])

    @pl.when(step == 0)
    def _():
        places = lax.broadcasted_iota(jnp.int32, dispatch.shape, 0)
        chosen = places == slots[pl.ds(expert, 1)]
        dispatch[...] = chosen.astype(bf16)
        weight = jnp.sum(jnp.where(chosen, gates[pl.ds(expert, 1)], 0.0), axis=1, keepdims=True)
        rows = jnp.dot(dispatch[...], normed[...], preferred_element_type=f32).astype(bf16)
        taken[...] = rows
        taken_turned[...] = rows.T
        grads = jnp.dot(dispatch[...], grad[...], preferred_element_type=f32)
        given[...] = grads.astype(bf16)
        routed[...] = (weight * grads).astype(bf16)
        result[...] = jnp.zeros_like(result)
        back_sum[...] = jnp.zeros_like(back_sum)

    weights = jnp.concatenate([w_in[0], w_in[1]], axis=1)
    hidden = jnp.dot(taken[...], weights, preferred_element_type=f32)
    gate_value, up_value = hidden[:, :units], hidden[:, units:]
    silu_value, slope = silu_parts(gate_value)
    act = (silu_value * up_value).astype(bf16)
    act_turned[pl.ds(pl.multiple_of(step * units, units), units)] = act.T
    act_grad = contract(routed[...], w_down[0])
    low = jnp.concatenate(
        [
            (act_grad * up_value * slope).astype(bf16),
            (act_grad * silu_value).astype(bf16),
        ],
        axis=1,
    )
    result[...] += jnp.dot(act, w_down[0], preferred_element_type=f32)
    back_sum[...] += contract(low, weights)
    in_grad = jnp.dot(taken_turned[...], low, preferred_element_type=f32).astype(bf16)

    @pl.when(number >= 2)
    def _():
        in_copy(slot, expert, step).wait()

    staged[slot, :, :height] = in_grad[:, :units].reshape(ROWS, height, units)
    staged[slot, :, height:] = in_grad[:, units:].reshape(ROWS, height, units)
    in_copy(slot, expert, step).start()

    @pl.when(step == steps - 1)
    def _():
        places = lax.broadcasted_iota(jnp.int32, dispatch.shape, 0)
        chosen = places == slots[pl.ds(expert, 1)]
        weight = jnp.sum(jnp.where(chosen, gates[pl.ds(expert, 1)], 0.0), axis=1, keepdims=True)
        number = jnp.sum(result[...] * given[...].astype(f32), axis=1, keepdims=True)
        gate_grad[pl.ds(expert, 1)] = jnp.sum(
            jnp.where(chosen, number, 0.0), axis=0, keepdims=True
        )

        @pl.when(expert > 0)
        def _():
            down_copy(expert).wait()

        def down_step(part, carried):
            columns = pl.ds(pl.multiple_of(part * 256, 256), 256)
            value = jnp.dot(act_turned[...], routed[:, columns], preferred_element_type=f32)
            for owner in range(ROWS):
                block = value[owner * down_rows : (owner + 1) * down_rows]
                bands = [
                    jnp.concatenate(
                        [
                            block[low : low + 8, half * 128 : half * 128 + 128]
                            for low in range(0, down_rows, 8)
                        ],
                        axis=1,
                    )
                    for half in range(2)
                ]
                rows = pl.ds(pl.multiple_of(part * 16, 16), 16)
                down_staged[owner, rows] = jnp.concatenate(bands, axis=0).astype(bf16)
            return carried

        lax.fori_loop(0, D // 256, down_step, 0)
        down_copy(expert).start()
        outward = transposed(dispatch[...], (weight * result[...]).astype(bf16))
        inward = transposed(dispatch[...], back_sum[...].astype(bf16))

        @pl.when(expert == 0)
        def _():
            branch_sum[...] = branch_in[...] + outward
            back_total[...] = back_in[...] + inward

        @pl.when(expert == EXP_DEV - 1)
        def _():
            branch[...] = (branch_sum[...] + outward).astype(bf16)
            back_grad[...] = (back_total[...] + inward).astype(bf16)
            in_copy(1 - slot, expert, step).wait()
            in_copy(slot, expert, step).wait()
            down_copy(expert).wait()


def experts(capacity, slots, gates, normed, grad, branch_in, back_in, planes, w_down):
    units = 128
    hidden_units = w_down.shape[1]
    steps = hidden_units // units
    height = D // ROWS
    whole = pl.BlockSpec(memory_space=VM)
    in_block = pl.BlockSpec((2, D, units), lambda e, k: (e, 0, k))
    down_block = pl.BlockSpec((1, units, D), lambda e, k: (e, k, 0))
    return pl.pallas_call(
        experts_body,
        name="experts",
        grid=(EXP_DEV, steps),
        out_shape=(
            shape_of((2 * TS, D), bf16),
            shape_of((2 * TS, D), bf16),
            shape_of((8, 2 * TS), f32),
            shape_of((ROWS, 3 * EXP_DEV * height, hidden_units), bf16),
        ),
        in_specs=[whole] * 6 + [in_block, down_block],
        out_specs=(whole, whole, whole, pl.BlockSpec(memory_space=ANY)),
        scratch_shapes=[
            pltpu.VMEM((capacity, 2 * TS), bf16),
            pltpu.VMEM((capacity, D), bf16),
            pltpu.VMEM((D, capacity), bf16),
            pltpu.VMEM((capacity, D), bf16),
            pltpu.VMEM((capacity, D), bf16),
            pltpu.VMEM((capacity, D), f32),
            pltpu.VMEM((capacity, D), f32),
            pltpu.VMEM((2 * TS, D), f32),
            pltpu.VMEM((2 * TS, D), f32),
            pltpu.VMEM((hidden_units, capacity), bf16),
            pltpu.VMEM((2, ROWS, 2 * height, units), bf16),
            pltpu.VMEM((ROWS, height, hidden_units), bf16),
            pltpu.SemaphoreType.DMA((3,)),
        ],
        compiler_params=pltpu.CompilerParams(vmem_limit_bytes=VMEM_BYTES),
        cost_estimate=pl.CostEstimate(
            flops=40 * 10**9, bytes_accessed=80 * 10**6, transcendentals=10**6
        ),
    )(slots, gates, normed, grad, branch_in, back_in, planes, w_down)


def finish_body(
    sums, down_sum, query_up_sum, gains, shared_sum, first, numbers, residual, normed, scale, gain,
    gate, up, down, query_down, latent_down, router, query_up, gain_first, gain_second, query_gain,
    latent_gain, shared_gate, shared_up, shared_down, hidden_grad,
):
    height = gate.shape[1]
    rows = down.shape[1]
    for expert in range(EXP_DEV):
        low = 2 * expert * height
        gate[expert] = sums[low : low + height].astype(f32)
        up[expert] = sums[low + height : low + 2 * height].astype(f32)
        low = (2 * EXP_DEV + expert) * height
        value = sums[low : low + height].astype(f32)
        for column in range(D // 128):
            band = value[column * 8 : column * 8 + 8]
            down[expert, :, column * 128 : column * 128 + 128] = jnp.concatenate(
                [band[:, tile * 128 : tile * 128 + 128] for tile in range(rows // 8)], axis=0
            )
    turned = down_sum[...].T
    query_rows, latent_rows = query_down.shape[0], latent_down.shape[0]
    query_down[...] = turned[:query_rows]
    latent_down[...] = turned[query_rows : query_rows + latent_rows]
    router[...] = turned[query_rows + latent_rows :]
    query_up[...] = jnp.concatenate(
        [query_up_sum[:, :192], query_up_sum[:, 256:], query_up_sum[:, 192:256]], axis=1
    )
    for col in range(COLS):
        gain_first[2 * col : 2 * col + 2] = gains[col, 0:2]
        gain_second[2 * col : 2 * col + 2] = gains[col, 2:4]
        query_gain[col : col + 1, :128] = gains[col, 4:5]
        query_gain[col : col + 1, 128:] = gains[col, 5:6, : query_rows - 128]
        latent_gain[col : col + 1] = gains[col, 6:7, :latent_rows]
    units = shared_gate.shape[0]
    lanes = shared_sum.shape[1] // 3
    for index, ref in enumerate((shared_gate, shared_up, shared_down)):
        part = shared_sum[:, index * lanes : (index + 1) * lanes].astype(f32)
        ref[...] = part.T[:units]
    total = numbers[0]
    for index in range(1, COLS):
        total = total + numbers[index]
    mean = total.T[:, :1] / D
    hidden_grad[...] = residual[...] + scale[...] * (
        first[...] * gain[...] - normed[...] * (scale[...] * mean)
    )


def finish(*terms):
    height, units = D // ROWS, terms[0].shape[1]
    query_rows = QL // COLS
    outs = (
        shape_of((EXP_DEV, height, units), f32),
        shape_of((EXP_DEV, height, units), f32),
        shape_of((EXP_DEV, units // ROWS, D), f32),
        shape_of((query_rows, height), f32),
        shape_of((KV_COLS, height), f32),
        shape_of((terms[1].shape[1] - query_rows - KV_COLS, height), f32),
        shape_of(terms[2].shape, f32),
        shape_of((2 * COLS, 128), f32),
        shape_of((2 * COLS, 128), f32),
        shape_of((COLS, query_rows), f32),
        shape_of((COLS, KV_COLS), f32),
        *((shape_of((SHARED_UNITS, height), f32),) * 3),
        shape_of(terms[5].shape, f32),
    )
    return simple_call(finish_body, "finish", outs, terms, 0, 12 * 10**6)


def second_back_body(
    normed_sum, logits, router, hidden, attention, grad, gain, out_weight, attended, lse_rows,
    attended_grad, delta, delta_rows, out_grad, residual_here, router_grad, gain_grad, whole,
):
    total = logits[0]
    for index in range(1, COLS):
        total = total + logits[index]
    logit_low = total.T.astype(bf16)
    spare = jnp.zeros((8, 2 * TS), f32)
    wide = jnp.concatenate([spare, total, spare], axis=0).astype(bf16)
    normed_grad = normed_sum[...].astype(f32) + transposed(wide, router[256:])
    residual = hidden[...].astype(f32) + attention[...].astype(f32)
    scale = lax.rsqrt(jnp.mean(residual * residual, axis=1, keepdims=True) + eps)
    normed = residual * scale
    router_grad[...] = transposed((normed * gain[...]).astype(bf16), logit_low).astype(bf16)
    gain_grad[...] = jnp.broadcast_to(
        jnp.sum(normed_grad * normed, axis=0, keepdims=True), gain_grad.shape
    )
    weighted = normed_grad * gain[...]
    inner = jnp.mean(weighted * residual, axis=1, keepdims=True)
    residual_grad = (
        grad[...].astype(f32) + scale * weighted - residual * (scale * scale * scale * inner)
    )
    whole[...] = residual_grad
    width = residual_here.shape[1]
    first = pl.multiple_of(lax.axis_index("col") * width, 128)
    residual_here[...] = whole[:, pl.ds(first, width)]
    low = residual_grad.astype(bf16)
    found = contract(low, out_weight[...]).astype(bf16)
    attended_grad[...] = found
    weights = transposed(attended[...].astype(bf16), low).astype(bf16)
    for index in range(ROWS):
        out_grad[index] = weights[:, index * 128 : (index + 1) * 128]
    numbers = found.astype(f32) * attended[...]
    delta_rows[...] = lse_rows[...]
    for head in range(2):
        lanes = slice(head * 128, head * 128 + 128)
        number = jnp.sum(numbers[:, lanes], axis=1, keepdims=True)
        number = jnp.broadcast_to(number, (2 * TS, 128))
        delta[:, lanes] = number
        delta_rows[2 + head : 3 + head] = number.T[:1]


def second_back(*terms):
    rows = 2 * TS
    outs = (
        shape_of((rows, 256), bf16),
        shape_of((rows, 256), f32),
        shape_of((8, rows), f32),
        shape_of((ROWS, 256, D // ROWS), bf16),
        shape_of((rows, D // COLS), f32),
        shape_of((D, 16), bf16),
        shape_of((8, D), f32),
    )
    return pl.pallas_call(
        second_back_body,
        name="second_back",
        out_shape=outs,
        in_specs=[pl.BlockSpec(memory_space=VM)] * len(terms),
        out_specs=(pl.BlockSpec(memory_space=VM),) * len(outs),
        scratch_shapes=[pltpu.VMEM((rows, D), f32)],
        compiler_params=pltpu.CompilerParams(vmem_limit_bytes=VMEM_BYTES),
        cost_estimate=pl.CostEstimate(
            flops=2 * 10**9, bytes_accessed=16 * 10**6, transcendentals=512
        ),
    )(*terms)


def first_project_body(hidden, gain, weight, normed, query, latent):
    values = hidden[...].astype(f32)
    scale = lax.rsqrt(jnp.mean(values * values, axis=1, keepdims=True) + eps)
    low = (values * scale * gain[...]).astype(bf16)
    normed[...] = low
    found = contract(weight[...], low)
    height = query.shape[0]
    live = KV_COLS
    query[...] = found[:height].astype(bf16)
    blank = jnp.zeros((latent.shape[0] - live, found.shape[1]), f32)
    latent[...] = jnp.concatenate([found[height : height + live], blank], axis=0).astype(bf16)


def simple_call(body, name, outs, terms, flops, moved, scratch=()):
    return pl.pallas_call(
        body,
        name=name,
        out_shape=outs,
        in_specs=[pl.BlockSpec(memory_space=VM)] * len(terms),
        out_specs=(pl.BlockSpec(memory_space=VM),) * len(outs),
        scratch_shapes=list(scratch),
        compiler_params=pltpu.CompilerParams(vmem_limit_bytes=VMEM_BYTES),
        cost_estimate=pl.CostEstimate(flops=flops, bytes_accessed=moved, transcendentals=0),
    )(*terms)


def first_project(hidden, gain, weight):
    outs = (
        shape_of((2 * TS, D), bf16),
        shape_of((QL // COLS, 2 * TS), bf16),
        shape_of((KV_COLS + (-KV_COLS) % 16, 2 * TS), bf16),
    )
    return simple_call(
        first_project_body, "first_project", outs, (hidden, gain, weight), 10**9, 6 * 10**6
    )


def swap_halves(tile):
    lane = lax.broadcasted_iota(jnp.int32, tile.shape, 1)
    lower = lax.rem(lane, DR) < DR // 2
    return jnp.where(lower, pltpu.roll(tile, 128 - DR // 2, 1), pltpu.roll(tile, DR // 2, 1))


def project_body(
    query_raw, latent_raw, query_gain, latent_gain, query_up, latent_up, cos, sin,
    query_in, latent_in, query, near,
):
    def normed(values, gain):
        scale = lax.rsqrt(jnp.mean(values * values, axis=0, keepdims=True) + eps)
        column = jnp.broadcast_to(gain[...], (8, gain.shape[1])).T[:, :1]
        return (values * scale * column).astype(bf16)

    low = normed(query_raw[...].astype(f32), query_gain)
    query_in[...] = low
    found = transposed(low, query_up[...])
    middle = found[:, 128:256]
    query[:, :128] = found[:, :128].astype(bf16)
    query[:, 128:256] = (middle * cos[...] + swap_halves(middle) * sin[...]).astype(bf16)
    query[:, 256:] = found[:, 256:].astype(bf16)
    raw = latent_raw[...].astype(f32)
    low = normed(raw[:KL], latent_gain)
    latent_in[...] = low
    found = transposed(low, latent_up[...]).astype(bf16)
    rope = jnp.concatenate([raw[KL:], raw[KL:]], axis=0).T
    near[:, :128] = found[:, :128]
    near[:, 128:256] = (rope * cos[...] + swap_halves(rope) * sin[...]).astype(bf16)
    near[:, 256:384] = found[:, 256:384]
    near[:, 384:512] = found[:, 128:256]
    near[:, 512:] = found[:, 384:]


def project(*terms):
    outs = (
        shape_of((QL, 2 * TS), bf16),
        shape_of((KL, 2 * TS), bf16),
        shape_of((2 * TS, 384), bf16),
        shape_of((2 * TS, 640), bf16),
    )
    return simple_call(project_body, "project", outs, terms, 2 * 10**9, 8 * 10**6)


def latent_back_body(
    query_sum, kv_sum, numbers, query_raw, kv_raw, query_gain, kv_gain, live, query_square, kv_square,
    normed, weight, gain, hidden, router_grad, second_gain,
    first_part, first_numbers, down_grad, gains,
):
    total = numbers[0]
    for index in range(1, COLS):
        total = total + numbers[index]
    query_scale = lax.rsqrt(query_square[:1] + eps)
    kv_scale = lax.rsqrt(kv_square[:1] + eps)
    query_raw_value = query_raw[...].astype(f32)
    kv_raw_value = kv_raw[...].astype(f32)
    query_value = query_sum[...]
    kv_value = kv_sum[: kv_raw.shape[0]]
    query_normed, kv_normed = query_raw_value * query_scale, kv_raw_value * kv_scale


    def as_row(values):
        number = jnp.sum(values, axis=1, keepdims=True)
        return jnp.broadcast_to(number, (values.shape[0], 128)).T[:1]

    row = as_row(query_value * query_normed)
    gains[...] = jnp.zeros_like(gains)
    gains[2:4] = second_gain[...]
    gains[4:5] = row[:, :128]
    gains[5:6, : row.shape[1] - 128] = row[:, 128:]
    gains[6:7, : kv_value.shape[0]] = as_row(kv_value * kv_normed)
    query_low = query_scale * (query_value * query_gain[...]) - query_normed * (
        query_scale * query_scale * (total[0:1] / QL)
    )
    kv_low = kv_scale * (kv_value * kv_gain[...]) - kv_normed * (
        kv_scale * kv_scale * (total[1:2] / KL)
    )
    kv_low = jnp.where(live[...] > 0, kv_low, kv_value)
    width = query_low.shape[0] + kv_low.shape[0]
    spare = jnp.zeros((weight.shape[0] - width, 2 * TS), f32)
    turned = jnp.concatenate([query_low, kv_low, spare], axis=0).T.astype(bf16)
    part = jnp.dot(turned, weight[...], preferred_element_type=f32)
    first_part[...] = part.astype(bf16)
    number = jnp.sum(part * gain[...] * hidden[...].astype(f32), axis=1, keepdims=True)
    first_numbers[...] = jnp.broadcast_to(number, (2 * TS, 128)).T[:8]
    grads = transposed(normed[...], turned).astype(bf16)
    down_grad[:, :width] = grads[:, :width]
    down_grad[:, width:] = router_grad[...]


def latent_back(*terms):
    width = terms[3].shape[0] + terms[4].shape[0] + terms[14].shape[1]
    outs = (
        shape_of((2 * TS, D), bf16),
        shape_of((8, 2 * TS), f32),
        shape_of((D, width), bf16),
        shape_of((8, 128), f32),
    )
    return simple_call(latent_back_body, "latent_back", outs, terms, 2 * 10**9, 10**7)


def rope_tables(positions, width):
    half_width = width // 2
    frequency = jnp.exp(
        -jnp.log(rope_base) * (2.0 * jnp.arange(half_width, dtype=jnp.float32) / width)
    )
    angles = positions.astype(jnp.float32)[:, None] * frequency[None, :]
    return (jnp.cos(angles), jnp.sin(angles))


def rms_scale(values):
    return lax.rsqrt(jnp.mean(values * values, axis=-1, keepdims=True) + eps)


def product(left, right):
    return jnp.dot(left, right, preferred_element_type=jnp.float32)


def left_product(left, right):
    return lax.dot_general(
        left, right, (((0,), (0,)), ((), ())), preferred_element_type=jnp.float32
    )


def right_product(left, right):
    return lax.dot_general(
        left, right, (((1,), (1,)), ((), ())), preferred_element_type=jnp.float32
    )


def turned_product(left, right):
    return lax.dot_general(
        left, right, (((0,), (1,)), ((), ())), preferred_element_type=jnp.float32
    )


def einsum(text, *terms):
    return jnp.einsum(text, *terms, preferred_element_type=f32)


def to_blocks(term):
    return term.reshape(2, RING, 2, term.shape[0] // ROWS, term.shape[1])


def local(
    hidden_in,
    gain_first,
    query_down,
    query_gain,
    query_up,
    latent_down,
    latent_gain,
    latent_up,
    attention_out,
    gain_second,
    router,
    expert_gate,
    expert_up,
    expert_down,
    shared_gate,
    shared_up,
    shared_down,
    seq_lens,
    routes,
    out_grad,
):
    row_index = lax.axis_index("row")
    col_index = lax.axis_index("col")
    seq_count, local_len, col_width = hidden_in.shape
    row_total = seq_count * local_len
    experts_all = EXP_DEV * COLS
    most_rows = (5 * local_len * TOPK + 4 * experts_all - 1) // (4 * experts_all)
    capacity = seq_count * most_rows
    query_cols = QL // COLS
    kv_cols = (KL + DR) // COLS

    def here(values, axis=-1):
        width = values.shape[axis] // COLS
        return lax.dynamic_slice_in_dim(values, col_index * width, width, axis)

    split = DN + DR
    (
        hidden_low,
        grad_full,
        down_all,
        query_up_pack,
        latent_up_all,
        attention_out_all,
        shared_gate_all,
        shared_up_all,
        shared_down_all,
        planes,
        down_chip,
    ) = front(
        hidden_in.reshape(row_total, col_width),
        out_grad.reshape(row_total, col_width),
        jnp.pad(
            jnp.concatenate([query_down.T, latent_down.T, router.T], axis=0), ((0, 8), (0, 0))
        ),
        jnp.concatenate(
            [query_up[:, :split], query_up[:, split + DN :], query_up[:, split : split + DN]],
            axis=1,
        ),
        latent_up,
        attention_out,
        shared_gate.T,
        shared_up.T,
        shared_down,
        expert_gate,
        jnp.pad(expert_down, ((0, 0), (0, (-expert_down.shape[1]) % 16), (0, 0))),
        expert_gate.shape[2],
    )
    expert_units = expert_gate.shape[2]
    latent_width = query_cols + kv_cols
    router_turned = down_all[latent_width : latent_width + experts_all]
    kv_pad = (-kv_cols) % 16
    normed_first, query_here, latent_here = first_project(hidden_low, gain_first[None], down_all)
    query_latent, _, latent_all, planes = latents(
        query_here,
        latent_here,
        expert_gate,
        expert_up,
        planes,
    )
    kv_latent = lax.dynamic_index_in_dim(latent_all, row_index, 1, False)
    kv_latent = kv_latent[:, :kv_cols].reshape(KL + DR, row_total)
    latent_pad = ((0, 0), (0, kv_pad), (0, 0))
    within_cos, within_sin = rope_tables(jnp.arange(local_len, dtype=jnp.int32), DR)
    start_cos, start_sin = rope_tables(jnp.arange(ROWS, dtype=jnp.int32) * local_len, DR)
    kvt_all = expand(
        latent_all,
        jnp.pad(
            jnp.pad(latent_up_all, ((0, DR), (0, 0))).reshape(COLS, kv_cols, -1), latent_pad
        ).reshape(COLS * (kv_cols + kv_pad), -1).T,
        jnp.pad(
            jnp.pad(latent_gain, (0, DR)).reshape(COLS, kv_cols, 1), latent_pad
        ).reshape(COLS * (kv_cols + kv_pad), 1),
        within_cos.T,
        within_sin.T,
        start_cos[:, :, None],
        start_sin[:, :, None],
    )
    lane = jnp.arange(2 * DR, dtype=jnp.int32)[None, :]
    position = row_index * local_len + jnp.arange(row_total, dtype=jnp.int32) % local_len
    frequency = jnp.exp(-math.log(rope_base) * (2.0 / DR) * (lane % (DR // 2)).astype(f32))
    angles = position.astype(f32)[:, None] * frequency
    tile_cos = jnp.cos(angles)
    tile_sin = jnp.where(lane % DR < DR // 2, -1.0, 1.0) * jnp.sin(angles)
    query_input, latent_input, query_pack, near = project(
        query_latent,
        kv_latent,
        query_gain[None],
        latent_gain[None],
        query_up_pack,
        latent_up_all,
        tile_cos,
        tile_sin,
    )
    attended_float, lse, lse_rows = attend(seq_lens, query_pack, kvt_all)
    attended = attended_float.astype(bf16)
    attention_part = product(attended, attention_out_all).astype(bf16)
    attention_sum, planes, expert_down_all = attention_sum_over_col(
        attention_part, expert_up, down_chip, planes
    )
    query_all = lax.all_gather(query_pack, "row", axis=0, tiled=False)

    attention_sum, query_all = lax.optimization_barrier((attention_sum, query_all))
    normed_second, shared_branch, shared_back, shared_grad = shared_experts(
        hidden_low,
        attention_sum,
        gain_second[None],
        grad_full,
        shared_gate_all,
        shared_up_all,
        shared_down_all,
    )
    logits = right_product(router_turned, normed_second)
    sigmoid_all = jax.nn.sigmoid(logits)
    routes_turned = routes.reshape(row_total, TOPK).T
    chosen = jnp.sum(
        (
            routes_turned[:, None, :] == jnp.arange(experts_all, dtype=jnp.int32)[None, :, None]
        ).astype(f32),
        axis=0,
    )
    weighted_sig = sigmoid_all * chosen
    denominator = jnp.sum(weighted_sig, axis=0, keepdims=True)
    gate_weights = route_scale * weighted_sig / denominator
    gate_here = here(gate_weights, 0)
    member = here(chosen, 0).reshape(EXP_DEV * seq_count, local_len)
    before = jnp.triu(jnp.ones((local_len, local_len), bf16), 1)
    rank = product(member.astype(bf16), before).reshape(EXP_DEV, seq_count, local_len)
    rank = rank + (jnp.arange(seq_count, dtype=f32) * most_rows)[None, :, None]
    slots = jnp.where(member.reshape(rank.shape) > 0, rank, float(capacity))
    slots = slots.astype(jnp.int32).reshape(EXP_DEV, row_total)
    branch_part, normed_part, gate_grad_here, expert_part = experts(
        capacity,
        slots,
        gate_here,
        normed_second,
        grad_full,
        shared_branch,
        shared_back,
        planes,
        expert_down_all,
    )
    shared_sum = lax.psum_scatter(shared_grad, "row", scatter_dimension=0, tiled=True)
    expert_sum = lax.psum_scatter(
        expert_part.reshape(-1, expert_units), "row", scatter_dimension=0, tiled=True
    )
    gate_grad_all = lax.dynamic_update_slice_in_dim(
        jnp.zeros((experts_all, row_total), f32), gate_grad_here[:EXP_DEV], col_index * EXP_DEV, 0
    )
    inner_sum = jnp.sum(gate_grad_all * gate_weights, axis=0, keepdims=True)
    logit_part = (
        sigmoid_all
        * (1.0 - sigmoid_all)
        * chosen
        / denominator
        * (route_scale * gate_grad_all - inner_sum)
    )
    normed_sum, logit_all = sum_over_col(
        "sum_normed", 5, normed_part, NORMED_CUT, logit_part, experts_all
    )
    (
        attended_grad,
        delta,
        stats,
        attention_out_grad,
        residual_here,
        router_grad,
        gain_second_grad,
    ) = second_back(
        normed_sum,
        logit_all,
        down_all,
        hidden_low,
        attention_sum,
        grad_full,
        gain_second[None],
        attention_out_all,
        attended_float,
        lse_rows,
    )
    attended_grad_all, stats_all, branch_here = back(attended_grad, stats, branch_part)
    hidden_here = here(hidden_low).astype(f32)
    attended_here = here(attention_sum).astype(f32)
    block_out = (
        (hidden_here + attended_here + branch_here).astype(bf16).reshape(seq_count, local_len, col_width)
    )
    dq, dk, dv = attend_back(
        seq_lens,
        query_pack,
        kvt_all,
        attended_grad,
        lse,
        delta,
        near,
        query_all,
        attended_grad_all,
        stats_all,
    )
    query_up_grad, latent_up_grad, query_in_grad, kv_part, numbers = project_back(
        dq,
        dk,
        dv,
        tile_cos,
        tile_sin,
        query_up_pack,
        latent_up_all,
        query_input,
        latent_input,
        query_latent,
        kv_latent[:KL],
        query_gain[:, None],
        latent_gain[:, None],
    )
    kv_part = jnp.pad(kv_part.reshape(COLS, kv_cols, row_total), latent_pad)
    shared_width = shared_gate.shape[1]
    (query_in_here, kv_in_here), numbers_all, summed = col_and_row(
        "sum_latents",
        7,
        "lead",
        (query_in_grad.reshape(COLS, query_cols, row_total), kv_part),
        ((query_cols, row_total), (kv_cols + kv_pad, row_total)),
        (128, 80),
        numbers,
        (attention_out_grad.reshape(2, RING, 2, col_width, D // ROWS),),
        (96,),
    )
    (attention_out_sum,) = summed
    is_latent = (col_index * kv_cols + jnp.arange(kv_cols)) < KL
    latent_gain_here = here(jnp.concatenate([latent_gain, jnp.ones((DR,), f32)]))
    query_square, kv_square = (
        jnp.broadcast_to(
            jnp.mean(jnp.square(values.astype(f32)), axis=0, keepdims=True), (8, row_total)
        )
        for values in (query_latent, kv_latent[:KL])
    )
    first_part, first_numbers, down_grads, gains = latent_back(
        query_in_here,
        kv_in_here,
        numbers_all,
        here(query_latent, 0),
        here(kv_latent, 0),
        here(query_gain)[:, None],
        latent_gain_here[:, None],
        is_latent.astype(f32)[:, None],
        query_square,
        kv_square,
        normed_first,
        down_all,
        gain_first[None],
        hidden_low,
        router_grad,
        here(gain_second_grad[0]).reshape(2, 128),
    )
    scale_first = rms_scale(hidden_low.astype(f32))
    normed_here = hidden_here * scale_first
    (first_here, first_numbers_all, gains_all), summed = first_sum(
        first_part,
        first_numbers,
        normed_here,
        gains,
        (to_blocks(down_grads), to_blocks(query_up_grad), to_blocks(latent_up_grad)),
        (0, QL // ROWS, KL // ROWS),
    )
    down_sum, query_up_sum, latent_up_sum = summed
    (
        expert_gate_grad,
        expert_up_grad,
        expert_down_grad,
        query_down_grad,
        latent_down_grad,
        router_grad,
        query_up_grad,
        gain_first_grad,
        gain_second_grad,
        query_gain_grad,
        latent_gain_grad,
        shared_gate_grad,
        shared_up_grad,
        shared_down_grad,
        hidden_grad,
    ) = finish(
        expert_sum,
        down_sum,
        query_up_sum,
        gains_all,
        shared_sum,
        first_here,
        first_numbers_all,
        residual_here,
        normed_here,
        scale_first,
        here(gain_first)[None],
    )
    return (
        block_out,
        hidden_grad.reshape(seq_count, local_len, col_width),
        gain_first_grad.reshape(D),
        query_down_grad.T,
        query_gain_grad.reshape(QL),
        query_up_grad,
        latent_down_grad.T,
        latent_gain_grad.reshape(KL + DR)[:KL],
        latent_up_sum,
        attention_out_sum,
        gain_second_grad.reshape(D),
        router_grad.T,
        expert_gate_grad,
        expert_up_grad,
        expert_down_grad,
        shared_gate_grad.T,
        shared_up_grad.T,
        shared_down_grad,
    )


def solution(mesh):
    in_specs = (
        P(None, "row", "col"),
        P(),
        P("row", "col"),
        P(),
        P("row", "col"),
        P("row", "col"),
        P(),
        P("row", "col"),
        P("col", "row"),
        P(),
        P("row", None),
        P("col", "row", None),
        P("col", "row", None),
        P("col", "row", None),
        P("row", "col"),
        P("row", "col"),
        P("col", "row"),
        P(),
        P(None, "row", None),
        P(None, "row", "col"),
    )
    out_specs = (
        P(None, "row", "col"),
        P(None, "row", "col"),
        P(),
        P("row", "col"),
        P(),
        P("row", "col"),
        P("row", "col"),
        P(),
        P("row", "col"),
        P("col", "row"),
        P(),
        P("row", None),
        P("col", "row", None),
        P("col", "row", None),
        P("col", "row", None),
        P("row", "col"),
        P("row", "col"),
        P("col", "row"),
    )
    return jax.shard_map(local, mesh=mesh, in_specs=in_specs, out_specs=out_specs, check_vma=False)
```

```python
import functools
import math

import jax
import jax.numpy as jnp
from jax import lax
from jax.experimental import pallas as pl
from jax.experimental.pallas import tpu as pltpu
from jax.sharding import PartitionSpec as P

D = 2048
H = 16
DN = 128
DR = 64
DV = 128
QL = 1536
KL = 512
EXP_DEV = 2
TOPK = 6
ROWS = 16
COLS = 8
TS = 256
CUT = 208
COL_CUT = 400
LATENT_CUT = 6
FIRST_CUT = 384
DOWN_CUT = 112
SUM_CUT = 208
NORMED_CUT = 208
KV_COLS = (KL + DR) // COLS
SHARED_UNITS = 352

eps = 1e-06
route_scale = 2.446
rope_base = 50000.0
score_scale = 1.0 / math.sqrt(DN + DR)
score_bits = score_scale * math.log2(math.e)

bf16 = jnp.bfloat16
f32 = jnp.float32
ANY = pl.ANY
VM = pltpu.VMEM


def shape_of(shape, dtype):
    return jax.ShapeDtypeStruct(shape, dtype)

MESH = pl.DeviceIdType.MESH
RING = 4
VMEM_BYTES = 56 * 2**20


class Place:
    def __init__(self, axis):
        self.axis = axis
        self.index = lax.axis_index(axis)
        self.cores = 2 if axis == "row" else 1
        self.core = lax.rem(self.index, self.cores)
        self.ring = lax.rem(lax.div(self.index, self.cores), RING)
        self.pair = lax.div(self.index, self.cores * RING)

    def at(self, pair, ring, core=None):
        core = self.core if core is None else core
        return (pair * RING + ring) * self.cores + core

    def turn(self, step):
        return lax.rem(self.ring + step + RING, RING)

    def peers(self):
        found = [self.at(self.pair, self.turn(step)) for step in (1, 2, 3)]
        found.append(self.at(1 - self.pair, self.ring))
        if self.cores == 2:
            found.append(self.at(self.pair, self.ring, 1 - self.core))
        return found


class Net:
    def __init__(self, send_sems, recv_sems):
        self.send_sems, self.recv_sems = send_sems, recv_sems
        self.count = 0
        self.sent = []
        self.own = []

    def send(self, source, target, axis, index):
        number = self.count
        self.count += 1
        copy = pltpu.make_async_remote_copy(
            source,
            target,
            self.send_sems.at[number],
            self.recv_sems.at[number],
            device_id={axis: index},
            device_id_type=MESH,
        )
        copy.start()
        self.sent.append(copy)
        return number

    def receive(self, number, target, axis, index):
        pltpu.make_async_remote_copy(
            target,
            target,
            self.send_sems.at[number],
            self.recv_sems.at[number],
            device_id={axis: index},
            device_id_type=MESH,
        ).wait_recv()

    def local(self, source, target):
        number = self.count
        self.count += 1
        copy = pltpu.make_async_copy(source, target, self.send_sems.at[number])
        copy.start()
        self.own.append(copy)

    def settle(self):
        for copy in self.own:
            copy.wait()
        self.own = []

    def finish(self):
        for copy in self.sent:
            copy.wait_send()
        self.settle()


def greet(*places, everyone=False):
    barrier = pltpu.get_barrier_semaphore()
    count = 0
    for place in places:
        members = lax.axis_size(place.axis)
        all_peers = [lax.rem(place.index + step, members) for step in range(1, members)]
        for peer in all_peers if everyone else place.peers():
            pl.semaphore_signal(
                barrier, inc=1, device_id={place.axis: peer}, device_id_type=MESH
            )
            count += 1
    pl.semaphore_wait(barrier, count)


class Gather:
    def __init__(self, net, place, source, slot, rows, cut, relay=False, cross=None):
        self.net, self.place, self.source, self.slot = net, place, source, slot
        self.rows, self.cut, self.relay = rows, cut, relay
        self.first, self.second = (0, cut), (cut, rows - cut)
        self.crossed = []
        if place.cores == 2:
            partner = place.at(place.pair, place.ring, 1 - place.core)

            def other(pair, ring, low, count):
                return slot(place.at(pair, ring, 1 - place.core), low, count)

            cross = (place.axis, partner, other)
        self.cross = cross

    def _send(self, owner, part, peer, own=False):
        piece = self.slot(owner, *part)
        start = self.source.at[pl.ds(*part)] if own else piece
        return self.net.send(start, piece, self.place.axis, peer)

    def _receive(self, number, pair, ring, part, peer):
        place = self.place
        self.net.receive(number, self.slot(place.at(pair, ring), *part), place.axis, peer)

    def _cross(self, pair, ring, part, own=False):
        if self.cross is None:
            return
        piece = self.slot(self.place.at(pair, ring), *part)
        start = self.source.at[pl.ds(*part)] if own else piece
        number = self.net.send(start, piece, self.cross[0], self.cross[1])
        self.crossed.append((number, pair, ring, part))

    def _halves(self, part):
        low, count = part
        unit = 16 if count % 16 == 0 else 1
        half = max(count // 2 // unit, 1) * unit
        return (low, half), (low + half, count - half)

    def _relays(self, part):
        return self.relay and part[1] >= (32 if part[1] % 16 == 0 else 2)

    def _round(self, pair, part, own=False):
        place = self.place
        owner = place.at(pair, place.ring)
        steps = (1, 3) if self._relays(part) else (1, 3, 2)
        return {
            step: self._send(owner, part, place.at(place.pair, place.turn(step)), own)
            for step in steps
        }

    def _pass(self, numbers, pair, part, then):
        place = self.place
        passed = {}
        for step in (1, 3):
            ring = place.turn(-step)
            self._receive(numbers[step], pair, ring, part, place.at(place.pair, ring))
            if self._relays(part):
                half = self._halves(part)[step // 2]
                passed[step] = self._send(
                    place.at(pair, ring), half, place.at(place.pair, place.turn(step))
                )
            then(pair, ring, part)
        return passed

    def _meet(self, numbers, passed, pair, part, then):
        place = self.place
        far = place.turn(2)
        if self._relays(part):
            for step in (1, 3):
                half = self._halves(part)[step // 2]
                self._receive(
                    passed[step], pair, far, half, place.at(place.pair, place.turn(-step))
                )
        else:
            self._receive(numbers[2], pair, far, part, place.at(place.pair, far))
        then(pair, far, part)

    def start_first(self):
        place = self.place
        if self.cut:
            other = place.at(1 - place.pair, place.ring)
            self.across = self._send(place.index, self.first, other, True)
            self.near = self._round(place.pair, self.first, True)

    def start_second(self):
        place = self.place
        if self.second[1]:
            self.round = self._round(place.pair, self.second, True)
            other = place.at(1 - place.pair, place.ring)
            self.over = [(place.ring, self._send(place.index, self.second, other, True))]
        self._cross(place.pair, place.ring, (0, self.rows), True)
        self.net.local(self.source, self.slot(place.index, 0, self.rows))

    def start(self):
        self.start_first()
        self.start_second()

    def forward_first(self):
        place = self.place
        if self.cut:
            other = place.at(1 - place.pair, place.ring)
            self._receive(self.across, 1 - place.pair, place.ring, self.first, other)
            self.far = self._round(1 - place.pair, self.first)
            self._cross(1 - place.pair, place.ring, self.first)

    def _over(self, pair, ring, part):
        place = self.place
        other = place.at(1 - place.pair, place.ring)
        self.over.append((ring, self._send(place.at(pair, ring), part, other)))
        self._cross(pair, ring, part)

    def near_pass(self):
        place = self.place
        if self.second[1]:
            self.round_passed = self._pass(self.round, place.pair, self.second, self._over)
        if self.cut:
            self.near_passed = self._pass(self.near, place.pair, self.first, self._cross)

    def far_pass(self):
        if self.cut:
            pair = 1 - self.place.pair
            self.far_passed = self._pass(self.far, pair, self.first, self._cross)

    def near_meet(self):
        place = self.place
        if self.second[1]:
            self._meet(self.round, self.round_passed, place.pair, self.second, self._over)
        if self.cut:
            self._meet(self.near, self.near_passed, place.pair, self.first, self._cross)

    def far_meet(self):
        place = self.place
        if self.cut:
            self._meet(self.far, self.far_passed, 1 - place.pair, self.first, self._cross)
        if self.second[1]:
            other = place.at(1 - place.pair, place.ring)
            for ring, number in self.over:
                self._receive(number, 1 - place.pair, ring, self.second, other)
                self._cross(1 - place.pair, ring, self.second)

    def end(self):
        for number, pair, ring, part in self.crossed:
            axis, partner, other = self.cross
            self.net.receive(number, other(pair, ring, *part), axis, partner)


class Direct:
    def __init__(self, net, place, source, ref, count):
        self.net, self.place, self.source, self.ref, self.count = net, place, source, ref, count

    def start(self):
        place = self.place
        self.numbers = [
            self.net.send(
                self.source,
                self.ref.at[place.index],
                place.axis,
                lax.rem(place.index + step, self.count),
            )
            for step in range(1, self.count)
        ]
        self.net.local(self.source, self.ref.at[place.index])

    def land(self):
        place = self.place
        for step, number in zip(range(1, self.count), self.numbers):
            owner = lax.rem(place.index + self.count - step, self.count)
            self.net.receive(number, self.ref.at[owner], place.axis, owner)


STAGES = ("start", "forward_first", "near_pass", "far_pass", "near_meet", "far_meet", "end")


def run_stages(gathers, stages=STAGES):
    for stage in stages:
        for gather in gathers:
            getattr(gather, stage)()


def run_gathers(*gathers):
    run_stages(gathers)


def row_slots(ref, rows):
    return lambda owner, low, count: ref.at[
        pl.ds(pl.multiple_of(owner * rows + low, 16), count)
    ]


def lead_slots(ref):
    return lambda owner, low, count: ref.at[owner, pl.ds(low, count)]


def lane_slots(ref, width):
    return lambda owner, low, count: ref.at[
        pl.ds(low, count), pl.ds(pl.multiple_of(owner * width, 128), width)
    ]


class Scatter:
    def __init__(self, net, place, block, rows, cut, scratch, keep):
        self.net, self.place, self.block, self.rows, self.cut = net, place, block, rows, cut
        self.scratch, self.keep = scratch, keep
        self.first, self.second = (0, cut), (cut, rows - cut)

    @staticmethod
    def scratch_of(rows, cut, width, dtype=jnp.bfloat16):
        shapes = []
        if cut:
            shapes += [(3, 2, cut, width), (2, cut, width)]
        if rows - cut:
            shapes += [(4, rows - cut, width), (4, rows - cut, width), (3, rows - cut, width)]
        return [pltpu.VMEM(shape, dtype) for shape in shapes]

    def _refs(self):
        refs = list(self.scratch)
        first = refs[:2] if self.cut else None
        second = refs[-3:] if self.second[1] else None
        return first, second

    def _owner(self, pair, ring):
        return self.place.at(pair, ring)

    def start(self):
        place, net = self.place, self.net
        first, second = self._refs()
        if first:
            self.round = [
                [
                    net.send(
                        self.block(self._owner(pair, place.turn(step)), *self.first),
                        first[0].at[step - 1, pair],
                        place.axis,
                        place.at(place.pair, place.turn(step)),
                    )
                    for pair in (0, 1)
                ]
                for step in (1, 2, 3)
            ]
        if second:
            self.across = [
                net.send(
                    self.block(self._owner(1 - place.pair, ring), *self.second),
                    second[0].at[ring],
                    place.axis,
                    place.at(1 - place.pair, place.ring),
                )
                for ring in range(RING)
            ]

    def forward_second(self):
        place, net = self.place, self.net
        first, second = self._refs()
        if not second:
            return
        other = place.at(1 - place.pair, place.ring)
        for ring in range(RING):
            net.receive(self.across[ring], second[0].at[ring], place.axis, other)
        for ring in range(RING):
            total = (
                self.block(self._owner(place.pair, ring), *self.second)[...].astype(jnp.float32)
                + second[0][ring].astype(jnp.float32)
            )
            second[1][ring] = total.astype(second[1].dtype)
        self.last = [
            net.send(
                second[1].at[place.turn(step)],
                second[2].at[step - 1],
                place.axis,
                place.at(place.pair, place.turn(step)),
            )
            for step in (1, 2, 3)
        ]

    def forward_first(self):
        place, net = self.place, self.net
        first, second = self._refs()
        if not first:
            return
        for step in (1, 3, 2):
            owner = place.at(place.pair, place.turn(-step))
            for pair in (0, 1):
                net.receive(self.round[step - 1][pair], first[0].at[step - 1, pair], place.axis, owner)
        other = 1 - place.pair
        total = self.block(self._owner(other, place.ring), *self.first)[...].astype(jnp.float32)
        for step in range(3):
            total = total + first[0][step, other].astype(jnp.float32)
        first[1][0] = total.astype(first[1].dtype)
        self.over = net.send(
            first[1].at[0], first[1].at[1], place.axis, place.at(other, place.ring)
        )

    def end_first(self):
        place, net = self.place, self.net
        first, second = self._refs()
        if not first:
            return
        total = self.block(self._owner(place.pair, place.ring), *self.first)[...].astype(jnp.float32)
        for step in range(3):
            total = total + first[0][step, place.pair].astype(jnp.float32)
        other = place.at(1 - place.pair, place.ring)
        net.receive(self.over, first[1].at[1], place.axis, other)
        self.keep(self.first, total + first[1][1].astype(jnp.float32))

    def end_second(self):
        place, net = self.place, self.net
        first, second = self._refs()
        if not second:
            return
        total = (
            self.block(self._owner(place.pair, place.ring), *self.second)[...].astype(jnp.float32)
            + second[0][place.ring].astype(jnp.float32)
        )
        for step in (1, 3, 2):
            owner = place.at(place.pair, place.turn(-step))
            net.receive(self.last[step - 1], second[2].at[step - 1], place.axis, owner)
            total = total + second[2][step - 1].astype(jnp.float32)
        self.keep(self.second, total)


def comm_call(body, name, collective_id, out_shapes, in_spaces, out_spaces, copies, scratch=(), args=(), aliases=None):
    return pl.pallas_call(
        body,
        name=name,
        out_shape=out_shapes,
        in_specs=[pl.BlockSpec(memory_space=space) for space in in_spaces],
        out_specs=tuple(pl.BlockSpec(memory_space=space) for space in out_spaces),
        scratch_shapes=[
            pltpu.SemaphoreType.DMA((copies,)),
            pltpu.SemaphoreType.DMA((copies,)),
            *scratch,
        ],
        input_output_aliases=aliases or {},
        compiler_params=pltpu.CompilerParams(
            collective_id=collective_id, has_side_effects=True, vmem_limit_bytes=VMEM_BYTES
        ),
    )(*args)


def plane_slots(ref, plane):
    return lambda owner, low, count: ref.at[
        plane, pl.ds(pl.multiple_of(owner * (D // ROWS) + low, 16), count)
    ]


def plane_gather(net, row, source, ref, plane, cut):
    return Gather(net, row, source, plane_slots(ref, plane), D // ROWS, cut, True)


def front_body(hidden, grad, w1, qu, lu, ao, sg, su, sd, gate, down, *rest):
    hidden_all, grad_all, w1_all, qu_all, lu_all, ao_all, sg_all, su_all, sd_all = rest[:9]
    planes, down_chip, ss, rs, down_other = rest[9:]
    row, col = Place("row"), Place("col")
    greet(row, col)
    net = Net(ss, rs)
    partner = row.at(row.pair, row.ring, 1 - row.core)
    gathers = [
        Gather(net, col, hidden, lane_slots(hidden_all, D // COLS), 2 * TS, 2 * TS, True),
        *(
            Gather(net, row, term, row_slots(ref, term.shape[0]), term.shape[0], cut, True)
            for term, ref, cut in (
                (qu, qu_all, 96),
                (lu, lu_all, 32),
            )
        ),
        *(
            Gather(net, row, term, lane_slots(ref, term.shape[1]), term.shape[0], cut, True)
            for term, ref, cut in (
                (w1, w1_all, 192),
                (ao, ao_all, 192),
                (sg, sg_all, 352),
                (su, su_all, 256),
                (sd, sd_all, 256),
            )
        ),
        plane_gather(net, row, gate.at[0], planes, 0, 64),
        Gather(net, col, grad, lane_slots(grad_all, D // COLS), 2 * TS, 2 * TS, True),
    ]
    number = net.send(down.at[1 - row.core], down_other, "row", partner)
    run_stages(gathers, STAGES[:1])
    net.receive(number, down_other, "row", partner)
    height = down_chip.shape[0] // 2
    own = down[row.core].astype(f32)[:height]
    given = down_other[...].astype(f32)[:height]
    even = row.core == 0
    down_chip[...] = jnp.concatenate(
        [jnp.where(even, own, given), jnp.where(even, given, own)], axis=0
    ).astype(bf16)
    run_stages(gathers, STAGES[1:])
    net.finish()


def stacked(term):
    return shape_of((ROWS * term.shape[0], term.shape[1]), term.dtype)


def side_by_side(term):
    return shape_of((term.shape[0], ROWS * term.shape[1]), term.dtype)


def front(hidden, grad, w1, qu, lu, ao, sg, su, sd, gate, down, units):
    return comm_call(
        front_body,
        "gather_front",
        1,
        (
            shape_of((2 * TS, D), bf16),
            shape_of((2 * TS, D), bf16),
            side_by_side(w1),
            stacked(qu),
            stacked(lu),
            side_by_side(ao),
            side_by_side(sg),
            side_by_side(su),
            side_by_side(sd),
            shape_of((2 * EXP_DEV, D, units), bf16),
            shape_of((2 * units // ROWS, D), bf16),
        ),
        [ANY] * 10 + [VM],
        [ANY] * 10 + [VM],
        256,
        [pltpu.VMEM(down.shape[1:], bf16)],
        (hidden, grad, w1, qu, lu, ao, sg, su, sd, gate, down),
    )


def latent_body(query, latent, gate, up, _, query_all, rows_all, latent_all, planes, ss, rs):
    row, col = Place("row"), Place("col")
    greet(row, col)
    net = Net(ss, rs)
    queries = Gather(
        net, col, query, row_slots(query_all, query.shape[0]), query.shape[0], 192, True
    )
    weights = [
        plane_gather(net, row, up.at[0], planes, 1, 96),
        plane_gather(net, row, gate.at[1], planes, 2, 96),
    ]
    rows = Gather(net, row, latent, lead_slots(rows_all), latent.shape[0], 48)
    half = ROWS // 2
    base = row.core * half
    partner = row.at(row.pair, row.ring, 1 - row.core)

    def slot(owner, low, count):
        return latent_all.at[owner, pl.ds(base + low, count)]

    def other(pair, ring, low, count):
        return latent_all.at[col.at(pair, ring), pl.ds(half - base + low, count)]

    every = Gather(
        net, col, rows_all.at[pl.ds(base, half)], slot, half, LATENT_CUT, True, ("row", partner, other)
    )
    run_stages((rows, queries), STAGES[:1])
    run_stages((rows,), STAGES[1:])
    net.settle()
    run_stages((every, *weights), STAGES[:1])
    run_stages((queries, every, *weights), STAGES[1:])
    net.finish()


def latents(query, latent, gate, up, planes):
    return comm_call(
        latent_body,
        "gather_latents",
        2,
        (
            shape_of((COLS * query.shape[0], query.shape[1]), bf16),
            shape_of((ROWS, *latent.shape), bf16),
            shape_of((COLS, ROWS, *latent.shape), bf16),
            shape_of(planes.shape, bf16),
        ),
        [ANY] * 5,
        [ANY] * 4,
        192,
        args=(query, latent, gate, up, planes),
        aliases={4: 3},
    )


def expand_body(latent, weight, gain, cos, sin, start_cos, start_sin, out):
    @pl.when(pl.program_id(0) <= lax.axis_index("row") + 1)
    def _():
        features = latent.shape[0] * latent.shape[2]
        values = latent[:, 0].reshape(features, latent.shape[3]).astype(f32)
        live = features - latent.shape[2] + 8
        square = jnp.sum(values[:live] * values[:live], axis=0, keepdims=True)
        scaled = (values * lax.rsqrt(square / KL + eps) * gain[...]).astype(bf16)
        found = jnp.dot(weight[...], scaled, preferred_element_type=f32).astype(bf16)
        turn_cos = cos[...] * start_cos[0] - sin[...] * start_sin[0]
        turn_sin = sin[...] * start_cos[0] + cos[...] * start_sin[0]
        turn_cos = jnp.concatenate([turn_cos, turn_cos], axis=1)
        turn_sin = jnp.concatenate([turn_sin, turn_sin], axis=1)
        first, second = values[live : live + 32], values[live + 32 : live + 64]
        rope = jnp.concatenate(
            [first * turn_cos - second * turn_sin, second * turn_cos + first * turn_sin], axis=0
        ).astype(bf16)
        out[0, 0:128] = found[0:128]
        out[0, 128:192] = rope
        out[0, 192:256] = rope
        out[0, 256:384] = found[256:384]
        out[0, 384:512] = found[128:256]
        out[0, 512:640] = found[384:512]


def expand(latent, weight, gain, cos, sin, start_cos, start_sin):
    cols, rows, height, width = latent.shape
    return pl.pallas_call(
        expand_body,
        name="expand_keys",
        grid=(rows,),
        out_shape=shape_of((rows, 640, width), bf16),
        in_specs=[
            pl.BlockSpec((cols, 1, height, width), lambda r: (0, r, 0, 0)),
            pl.BlockSpec(weight.shape, lambda r: (0, 0)),
            pl.BlockSpec(gain.shape, lambda r: (0, 0)),
            pl.BlockSpec((32, TS), lambda r: (0, 0)),
            pl.BlockSpec((32, TS), lambda r: (0, 0)),
            pl.BlockSpec((1, 32, 1), lambda r: (r, 0, 0)),
            pl.BlockSpec((1, 32, 1), lambda r: (r, 0, 0)),
        ],
        out_specs=pl.BlockSpec((1, 640, width), lambda r: (r, 0, 0)),
        compiler_params=pltpu.CompilerParams(vmem_limit_bytes=VMEM_BYTES),
        cost_estimate=pl.CostEstimate(
            flops=6 * 10**9, bytes_accessed=22 * 10**6, transcendentals=8192
        ),
    )(latent, weight, gain, cos, sin, start_cos, start_sin)


class ColSum:
    def __init__(self, net, col, term, total, cut, scratch):
        width = D // COLS
        *scratch, mine = scratch
        count = len(Scatter.scratch_of(TS, cut, width))
        self.parts = []
        for chunk in range(2):
            first = chunk * TS

            def block(owner, low, rows, first=first):
                return lane_slots(term, width)(owner, first + low, rows)

            def slot(owner, low, rows, first=first):
                return lane_slots(total, width)(owner, first + low, rows)

            def keep(part, value, chunk=chunk):
                mine[chunk, pl.ds(*part)] = value.astype(mine.dtype)

            part_scratch = scratch[chunk * count : (chunk + 1) * count]
            self.parts.append(
                (
                    Scatter(net, col, block, TS, cut, part_scratch, keep),
                    Gather(net, col, mine.at[chunk], slot, TS, cut, True),
                )
            )

    @staticmethod
    def scratch_of(cut):
        return [
            *Scatter.scratch_of(TS, cut, D // COLS),
            *Scatter.scratch_of(TS, cut, D // COLS),
            pltpu.VMEM((2, TS, D // COLS), bf16),
        ]

    def start(self):
        for scatter, _ in self.parts:
            scatter.start()

    def summed(self, chunk):
        scatter, gather = self.parts[chunk]
        scatter.forward_second()
        scatter.forward_first()
        scatter.end_first()
        gather.start_first()
        scatter.end_second()
        gather.start_second()

    def sent(self, chunk, stages):
        run_stages((self.parts[chunk][1],), stages)


def sum_body(cut, extra_cut, term, extra, total_all, extra_all, ss, rs, *scratch):
    col = Place("col")
    greet(col)
    net = Net(ss, rs)
    total = ColSum(net, col, term, total_all, cut, scratch)
    beside = Gather(net, col, extra, lead_slots(extra_all), extra.shape[0], extra_cut, True)
    total.start()
    run_stages((beside,), STAGES[:1])
    total.summed(0)
    run_stages((beside,), STAGES[1:3])
    total.sent(0, STAGES[1:2])
    total.summed(1)
    total.sent(0, STAGES[2:4])
    total.sent(1, STAGES[1:4])
    total.sent(0, STAGES[4:])
    run_stages((beside,), STAGES[3:])
    total.sent(1, STAGES[4:])
    net.finish()


def sum_over_col(name, collective_id, term, cut, extra, extra_cut):
    return comm_call(
        functools.partial(sum_body, cut, extra_cut),
        name,
        collective_id,
        (shape_of((2 * TS, D), bf16), shape_of((COLS, *extra.shape), extra.dtype)),
        [VM, ANY],
        [ANY, ANY],
        160,
        ColSum.scratch_of(cut),
        (term, extra),
    )


def attention_sum_body(term, up, down, _, total_all, planes, down_all, ss, rs, *scratch):
    row, col = Place("row"), Place("col")
    greet(row, col)
    net = Net(ss, rs)
    width = D // COLS
    mine = scratch[-1]

    def keep(part, value):
        mine[pl.ds(*part)] = value.astype(mine.dtype)

    height = down.shape[0]

    def down_slot(owner, low, count):
        place = pl.multiple_of(lax.div(owner, 2) * height + low, 16)
        return down_all.at[lax.rem(owner, 2), pl.ds(place, count)]

    scatter = Scatter(net, col, lane_slots(term, width), 2 * TS, 2 * TS, scratch[:-1], keep)
    gather = Gather(net, col, mine, lane_slots(total_all, width), 2 * TS, 2 * TS, True)
    weights = [
        plane_gather(net, row, up.at[1], planes, 3, 96),
        Gather(net, row, down, down_slot, height, 112, True),
    ]
    scatter.start()
    run_stages(weights, STAGES[:1])
    scatter.forward_first()
    run_stages(weights, STAGES[1:2])
    scatter.end_first()
    gather.start()
    run_stages(weights, STAGES[2:3])
    run_stages((gather,), STAGES[1:3])
    run_stages(weights, STAGES[3:4])
    run_stages((gather,), STAGES[3:5])
    run_stages(weights, STAGES[4:5])
    run_stages((gather, *weights), STAGES[5:])
    net.finish()


def attention_sum_over_col(term, up, down, planes):
    return comm_call(
        attention_sum_body,
        "sum_attention",
        4,
        (
            shape_of((2 * TS, D), bf16),
            shape_of(planes.shape, bf16),
            shape_of((EXP_DEV, ROWS // 2 * down.shape[0], D), bf16),
        ),
        [VM, ANY, ANY, ANY],
        [ANY] * 3,
        128,
        [*Scatter.scratch_of(2 * TS, 2 * TS, D // COLS), pltpu.VMEM((2 * TS, D // COLS), bf16)],
        (term, up, down, planes),
        aliases={3: 1},
    )


def back_body(grad, stats, branch, grad_all, stats_all, branch_sum, ss, rs, *scratch):
    row, col = Place("row"), Place("col")
    greet(row, col)
    net = Net(ss, rs)

    def keep(part, value):
        branch_sum[pl.ds(*part)] = value

    scatter = Scatter(net, col, lane_slots(branch, D // COLS), 2 * TS, COL_CUT, scratch, keep)
    gathers = (
        Gather(net, row, grad, lead_slots(grad_all), 2 * TS, 208, True),
        Gather(net, row, stats, lead_slots(stats_all), stats.shape[0], stats.shape[0]),
    )
    run_stages(gathers, STAGES[:1])
    scatter.start()
    run_stages(gathers, STAGES[1:3])
    scatter.forward_second()
    scatter.forward_first()
    run_stages(gathers, STAGES[3:6])
    scatter.end_first()
    scatter.end_second()
    run_stages(gathers, STAGES[6:])
    net.finish()


def back(grad, stats, branch):
    return comm_call(
        back_body,
        "gather_back",
        6,
        (
            shape_of((ROWS, *grad.shape), bf16),
            shape_of((ROWS, *stats.shape), f32),
            shape_of((2 * TS, D // COLS), f32),
        ),
        [ANY, ANY, VM],
        [ANY, ANY, VM],
        96,
        Scatter.scratch_of(2 * TS, COL_CUT, D // COLS),
        (grad, stats, branch),
    )


class RowScatter:
    def __init__(self, net, place, term, cut, scratch, keep):
        self.net, self.place, self.term = net, place, term
        self.arrived, self.summed = scratch[:2]
        rows = term.shape[3]

        def block(owner, low, count):
            return self.summed.at[lax.div(owner, 2), pl.ds(low, count)]

        self.inner = Scatter(net, place, block, rows, cut, scratch[2:], keep)

    @staticmethod
    def scratch_of(rows, cut, width):
        return [
            pltpu.VMEM((2, RING, rows, width), bf16),
            pltpu.VMEM((2 * RING, rows, width), bf16),
            *Scatter.scratch_of(rows, cut, width),
        ]

    def start(self):
        place = self.place
        self.partner = place.at(place.pair, place.ring, 1 - place.core)
        self.number = self.net.send(
            self.term.at[:, :, 1 - place.core], self.arrived, place.axis, self.partner
        )

    def middle(self):
        place = self.place
        self.net.receive(self.number, self.arrived, place.axis, self.partner)
        for pair in range(2):
            for ring in range(RING):
                self.summed[pair * RING + ring] = (
                    self.term[pair, ring, place.core].astype(f32)
                    + self.arrived[pair, ring].astype(f32)
                ).astype(bf16)
        self.inner.start()


def run_scatters(scatters):
    for scatter in scatters:
        scatter.forward_second()
    for scatter in scatters:
        scatter.forward_first()
    for scatter in scatters:
        scatter.end_first()
    for scatter in scatters:
        scatter.end_second()


def keep_in(ref):
    def keep(part, value):
        ref[pl.ds(*part)] = value

    return keep


def block_slots(ref):
    return lambda owner, low, count: ref.at[owner, pl.ds(low, count)]


def rows_sum(net, place, terms, cuts, totals, scratch):
    parts = []
    for term, cut, total in zip(terms, cuts, totals):
        count = len(RowScatter.scratch_of(term.shape[3], cut, term.shape[4]))
        parts.append(RowScatter(net, place, term, cut, scratch[:count], keep_in(total)))
        scratch = scratch[count:]
    return parts


def rows_scratch(terms, cuts):
    found = []
    for term, cut in zip(terms, cuts):
        found += RowScatter.scratch_of(term.shape[3], cut, term.shape[4])
    return found


def col_and_row_body(col_cuts, row_cuts, slots, *rest):
    cols, rows = len(col_cuts), len(row_cuts)
    col_terms, rest = rest[:cols], rest[cols:]
    extra, rest = rest[0], rest[1:]
    row_terms, rest = rest[:rows], rest[rows:]
    col_totals, rest = rest[:cols], rest[cols:]
    extra_all, rest = rest[0], rest[1:]
    row_totals, rest = rest[:rows], rest[rows:]
    ss, rs, *scratch = rest
    row, col = Place("row"), Place("col")
    greet(row, col)
    net = Net(ss, rs)
    scatters = []
    for term, cut, total in zip(col_terms, col_cuts, col_totals):
        height, width = total.shape
        block = lane_slots(term, width) if slots == "lane" else block_slots(term)
        count = len(Scatter.scratch_of(height, cut, width))
        scatters.append(Scatter(net, col, block, height, cut, scratch[:count], keep_in(total)))
        scratch = scratch[count:]
    beside = Gather(net, col, extra, lead_slots(extra_all), extra.shape[0], extra.shape[0])
    parts = rows_sum(net, row, row_terms, row_cuts, row_totals, scratch)
    for part in parts:
        part.start()
    for scatter in scatters:
        scatter.start()
    beside.start()
    for part in parts:
        part.middle()
    run_stages((beside,), STAGES[1:2])
    run_scatters(scatters + [part.inner for part in parts])
    run_stages((beside,), STAGES[2:])
    net.finish()


def col_and_row(name, collective_id, slots, col_terms, col_shapes, col_cuts, extra, row_terms, row_cuts):
    scratch = []
    for shape, cut in zip(col_shapes, col_cuts):
        scratch += Scatter.scratch_of(shape[0], cut, shape[1])
    found = comm_call(
        functools.partial(col_and_row_body, tuple(col_cuts), tuple(row_cuts), slots),
        name,
        collective_id,
        (
            *(shape_of(shape, f32) for shape in col_shapes),
            shape_of((COLS, *extra.shape), f32),
            *(shape_of(term.shape[3:], f32) for term in row_terms),
        ),
        [*([VM] * len(col_terms)), ANY, *([VM] * len(row_terms))],
        [*([VM] * len(col_terms)), ANY, *([VM] * len(row_terms))],
        128,
        [*scratch, *rows_scratch(row_terms, row_cuts)],
        (*col_terms, extra, *row_terms),
    )
    count = len(col_terms)
    return found[:count], found[count], found[count + 1 :]


def first_sum_body(row_cuts, term, extra, normed, gains, *rest):
    rows = len(row_cuts)
    row_terms, rest = rest[:rows], rest[rows:]
    total, extra_all, gains_all, rest = *rest[:3], rest[3:]
    row_totals, rest = rest[:rows], rest[rows:]
    ss, rs, gains_rows, gains_mine, *scratch = rest
    row, col = Place("row"), Place("col")
    greet(row, col, everyone=True)
    net = Net(ss, rs)
    height, width = total.shape
    count = len(Scatter.scratch_of(height, FIRST_CUT, width))
    scatter = Scatter(
        net, col, lane_slots(term, width), height, FIRST_CUT, scratch[:count], keep_in(total)
    )
    beside = Direct(net, col, extra, extra_all, COLS)
    parts = rows_sum(net, row, row_terms, row_cuts, row_totals, scratch[count:])
    inner = [part.inner for part in parts]
    scatter.start()
    for part in parts:
        part.start()
    beside.start()
    for part in parts:
        part.middle()
    scatter.forward_second()
    scatter.forward_first()
    for part in inner:
        part.forward_second()
    for part in inner:
        part.forward_first()
    scatter.end_first()
    scatter.end_second()
    gain = jnp.sum(total[...] * normed[...], axis=0, keepdims=True)
    gains_mine[...] = gains[...]
    gains_mine[0:1] = gain[:, :128]
    gains_mine[1:2] = gain[:, 128:]
    every = Direct(net, row, gains_mine, gains_rows, ROWS)
    every.start()
    for part in inner:
        part.end_first()
    beside.land()
    every.land()
    net.settle()
    found = gains_rows[0]
    for index in range(1, ROWS):
        found = found + gains_rows[index]
    gains_rows[ROWS] = found
    spread = Direct(net, col, gains_rows.at[ROWS], gains_all, COLS)
    spread.start()
    for part in inner:
        part.end_second()
    spread.land()
    net.finish()


def first_sum(term, extra, normed, gains, row_terms, row_cuts):
    width = D // COLS
    found = comm_call(
        functools.partial(first_sum_body, tuple(row_cuts)),
        "sum_first",
        8,
        (
            shape_of((2 * TS, width), f32),
            shape_of((COLS, *extra.shape), f32),
            shape_of((COLS, 8, 128), f32),
            *(shape_of(term.shape[3:], f32) for term in row_terms),
        ),
        [VM] * (4 + len(row_terms)),
        [VM] * (3 + len(row_terms)),
        160,
        [
            pltpu.VMEM((ROWS + 1, 8, 128), f32),
            pltpu.VMEM((8, 128), f32),
            *Scatter.scratch_of(2 * TS, FIRST_CUT, width),
            *rows_scratch(row_terms, row_cuts),
        ],
        (term, extra, normed, gains, *row_terms),
    )
    return found[:3], found[3:]


def contract(left, right):
    return lax.dot_general(left, right, (((1,), (1,)), ((), ())), preferred_element_type=f32)


def masked_queries(pack):
    lanes = lax.broadcasted_iota(jnp.int32, (pack.shape[0], 256), 1)
    zero = jnp.zeros((), pack.dtype)
    return (
        jnp.where(lanes < 192, pack[:, :256], zero),
        jnp.where(lanes >= 64, pack[:, 128:], zero),
    )


def attend_body(lens, query, kvt, out, lse, lse_rows, scores):
    seq = pl.program_id(0)
    mine = lax.axis_index("row")
    live = lens[seq]
    steps = lax.div(jnp.minimum(mine + 1, lax.div(live + TS - 1, TS)) + 1, 2)
    places = mine * TS + lax.broadcasted_iota(jnp.int32, (TS, 1), 0)
    limit = jnp.minimum(places + 1, live)
    offsets = lax.broadcasted_iota(jnp.int32, (TS, TS), 1)
    queries = masked_queries(query[...])

    def first(step, tops):
        tops = list(tops)
        for half in range(2):
            index = 2 * step + half
            valid = offsets < limit - index * TS
            for head in range(2):
                key = kvt[index, head * 128 : head * 128 + 256]
                value = jnp.dot(queries[head], key, preferred_element_type=f32)
                value = jnp.where(valid, value, -1e30)
                scores[head, index] = value
                tops[head] = jnp.maximum(
                    tops[head], jnp.maximum(value[:, :128], value[:, 128:])
                )
        return tuple(tops)

    tops = lax.fori_loop(0, steps, first, (jnp.full((TS, 128), -1e30, f32),) * 2)
    tops = [jnp.max(top, axis=1, keepdims=True) * score_bits for top in tops]

    def second(step, carried):
        found = []
        for head in range(2):
            sums, total = carried[head]
            for half in range(2):
                index = 2 * step + half
                weight = jnp.exp2(scores[head, index] * score_bits - tops[head])
                sums = sums + (weight[:, :128] + weight[:, 128:])
                value = kvt[index, 384 + head * 128 : 512 + head * 128]
                total = total + contract(weight.astype(bf16), value)
            found.append((sums, total))
        return tuple(found)

    zero = jnp.zeros((TS, 128), f32)
    carried = lax.fori_loop(0, steps, second, ((zero, zero),) * 2)
    lse_rows[...] = jnp.zeros_like(lse_rows)
    for head in range(2):
        sums, total = carried[head]
        whole = jnp.sum(sums, axis=1, keepdims=True)
        lanes = pl.ds(head * 128, 128)
        out[:, lanes] = total / whole
        value = jnp.broadcast_to(tops[head] + jnp.log2(whole), (TS, 128))
        lse[:, lanes] = value
        lse_rows[head : head + 1] = value.T[:1]


def attend(lens, query, kvt):
    return pl.pallas_call(
        attend_body,
        name="attend",
        grid=(2,),
        out_shape=(
            shape_of((2 * TS, 256), f32),
            shape_of((2 * TS, 256), f32),
            shape_of((8, 2 * TS), f32),
        ),
        in_specs=[
            pl.BlockSpec(memory_space=pltpu.SMEM),
            pl.BlockSpec((TS, 384), lambda s: (s, 0)),
            pl.BlockSpec((ROWS, 640, TS), lambda s: (0, 0, s)),
        ],
        out_specs=(
            pl.BlockSpec((TS, 256), lambda s: (s, 0)),
            pl.BlockSpec((TS, 256), lambda s: (s, 0)),
            pl.BlockSpec((8, TS), lambda s: (0, s)),
        ),
        scratch_shapes=[pltpu.VMEM((2, ROWS, TS, TS), f32)],
        compiler_params=pltpu.CompilerParams(vmem_limit_bytes=VMEM_BYTES),
        cost_estimate=pl.CostEstimate(
            flops=6 * 10**9, bytes_accessed=12 * 10**6, transcendentals=4 * 10**6
        ),
    )(lens, query, kvt)


def attend_back_body(lens, query, kvt, grad, lse, delta, near, query_all, grad_all, stats, dq, dk, dv):
    seq = pl.program_id(0)
    mine = lax.axis_index("row")
    live = lens[seq]
    width = 2 * TS
    steps = lax.div(jnp.minimum(mine + 1, lax.div(live + TS - 1, TS)) + 1, 2)
    places = mine * TS + lax.broadcasted_iota(jnp.int32, (TS, 1), 0)
    limit = jnp.minimum(places + 1, live)
    narrow = lax.broadcasted_iota(jnp.int32, (TS, TS), 1)
    wide = lax.broadcasted_iota(jnp.int32, (TS, width), 1)
    queries = masked_queries(query[...])

    def queries_step(step, carried):
        totals = list(carried)
        for half in range(2):
            index = 2 * step + half
            valid = narrow < limit - index * TS
            for head in range(2):
                key = kvt[index, head * 128 : head * 128 + 256]
                value = kvt[index, 384 + head * 128 : 512 + head * 128]
                lanes = pl.ds(head * 128, 128)
                score = jnp.dot(queries[head], key, preferred_element_type=f32)
                score = score * score_bits - lse[:, lanes][:, :1]
                weight = jnp.exp2(jnp.where(valid, score, -1e30))
                slope = jnp.dot(grad[:, lanes], value, preferred_element_type=f32)
                low = (weight * (slope - delta[:, lanes][:, :1])).astype(bf16)
                totals[head] = totals[head] + contract(low, key)
        return tuple(totals)

    totals = lax.fori_loop(0, steps, queries_step, (jnp.zeros((TS, 256), f32),) * 2)
    edge = lax.broadcasted_iota(jnp.int32, (TS, 128), 1) < DR
    dq[:, 0:128] = totals[0][:, :128] * score_scale
    dq[:, 128:256] = jnp.where(edge, totals[0][:, 128:], totals[1][:, :128]) * score_scale
    dq[:, 256:384] = totals[1][:, 128:] * score_scale

    bar = jnp.where(places < live, places, 2 * ROWS * TS)
    keys = masked_queries(near[:, :384])

    def keys_step(step, carried):
        valid = wide >= bar - step * width
        queries = query_all[pl.ds(2 * step, 2)].reshape(width, query_all.shape[2])
        grads = grad_all[pl.ds(2 * step, 2)].reshape(width, 256)
        numbers = stats[pl.ds(2 * step, 2)]
        numbers = jnp.concatenate([numbers[0], numbers[1]], axis=1)
        found = []
        for head in range(2):
            key_total, value_total = carried[head]
            asked = queries[:, head * 128 : head * 128 + 256]
            given = grads[:, head * 128 : head * 128 + 128]
            score = contract(keys[head], asked) * score_bits - numbers[head : head + 1]
            weight = jnp.exp2(jnp.where(valid, score, -1e30))
            value_total = value_total + jnp.dot(
                weight.astype(bf16), given, preferred_element_type=f32
            )
            value = near[:, 384 + head * 128 : 512 + head * 128]
            slope = contract(value, given) - numbers[2 + head : 3 + head]
            low = (weight * slope).astype(bf16)
            key_total = key_total + jnp.dot(low, asked, preferred_element_type=f32)
            found.append((key_total, value_total))
        return tuple(found)

    zero = (jnp.zeros((TS, 256), f32), jnp.zeros((TS, 128), f32))
    last_step = jnp.where(mine * TS < live, ROWS // 2, 0)
    totals = lax.fori_loop(lax.div(mine, 2), last_step, keys_step, (zero, zero))
    dk[:, 0:128] = totals[0][0][:, :128] * score_scale
    dk[:, 128:256] = jnp.where(edge, totals[0][0][:, 128:], totals[1][0][:, :128]) * score_scale
    dk[:, 256:384] = totals[1][0][:, 128:] * score_scale
    dv[:, 0:128] = totals[0][1]
    dv[:, 128:256] = totals[1][1]


def attend_back(lens, query, kvt, grad, lse, delta, near, query_all, grad_all, stats):
    def lanes(width):
        return pl.BlockSpec((TS, width), lambda s: (s, 0))

    return pl.pallas_call(
        attend_back_body,
        name="attend_back",
        grid=(2,),
        out_shape=(
            shape_of((2 * TS, 384), f32),
            shape_of((2 * TS, 384), f32),
            shape_of((2 * TS, 256), f32),
        ),
        in_specs=[
            pl.BlockSpec(memory_space=pltpu.SMEM),
            lanes(384),
            pl.BlockSpec((ROWS, 640, TS), lambda s: (0, 0, s)),
            lanes(256),
            lanes(256),
            lanes(256),
            lanes(640),
            pl.BlockSpec((ROWS, TS, query_all.shape[2]), lambda s: (0, s, 0)),
            pl.BlockSpec((ROWS, TS, 256), lambda s: (0, s, 0)),
            pl.BlockSpec((ROWS, 8, TS), lambda s: (0, 0, s)),
        ],
        out_specs=(lanes(384), lanes(384), lanes(256)),
        compiler_params=pltpu.CompilerParams(vmem_limit_bytes=VMEM_BYTES),
        cost_estimate=pl.CostEstimate(
            flops=12 * 10**9, bytes_accessed=24 * 10**6, transcendentals=8 * 10**6
        ),
    )(lens, query, kvt, grad, lse, delta, near, query_all, grad_all, stats)


def project_back_body(
    dq, dk, dv, cos, sin, query_up, latent_up, query_in, latent_in, query_raw, latent_raw,
    query_gain, latent_gain, query_up_grad, latent_up_grad, query_grad, latent_grad, numbers,
):
    def turn_back(tile):
        return tile * cos[...] - swap_halves(tile) * sin[...]

    queries = jnp.concatenate(
        [dq[:, :128], turn_back(dq[:, 128:256]), dq[:, 256:]], axis=1
    ).astype(bf16)
    middle = dk[:, 128:256]
    middle = middle + pltpu.roll(middle, DR, 1)
    rope = turn_back(middle)
    pairs = jnp.concatenate(
        [dk[:, :128], dv[:, :128], dk[:, 256:], dv[:, 128:]], axis=1
    ).astype(bf16)
    query_up_grad[...] = jnp.dot(query_in[...], queries, preferred_element_type=f32).astype(bf16)
    latent_up_grad[...] = jnp.dot(latent_in[...], pairs, preferred_element_type=f32).astype(bf16)
    back = contract(query_up[...], queries)
    query_grad[...] = back.astype(bf16)
    numbers[...] = jnp.zeros_like(numbers)
    numbers[0:1] = jnp.sum(back * query_gain[...] * query_raw[...].astype(f32), axis=0, keepdims=True)
    back = contract(latent_up[...], pairs)
    numbers[1:2] = jnp.sum(
        back * latent_gain[...] * latent_raw[...].astype(f32), axis=0, keepdims=True
    )
    latent_grad[:KL] = back.astype(bf16)
    latent_grad[KL:] = rope.T[:DR].astype(bf16)


def project_back(*terms):
    query_up, latent_up, query_in, latent_in = terms[5:9]
    return pl.pallas_call(
        project_back_body,
        name="project_back",
        out_shape=(
            shape_of(query_up.shape, bf16),
            shape_of(latent_up.shape, bf16),
            shape_of(query_in.shape, bf16),
            shape_of((KL + DR, 2 * TS), bf16),
            shape_of((8, 2 * TS), f32),
        ),
        in_specs=[pl.BlockSpec(memory_space=VM)] * len(terms),
        out_specs=(pl.BlockSpec(memory_space=VM),) * 5,
        compiler_params=pltpu.CompilerParams(vmem_limit_bytes=VMEM_BYTES),
        cost_estimate=pl.CostEstimate(
            flops=2 * 10**9, bytes_accessed=16 * 10**6, transcendentals=0
        ),
    )(*terms)


def silu_parts(gate_value):
    sigmoid_value = 1.0 / (1.0 + jnp.exp(-gate_value))
    return (gate_value * sigmoid_value, sigmoid_value * (1.0 + gate_value * (1.0 - sigmoid_value)))


def transposed(left, right):
    return lax.dot_general(left, right, (((0,), (0,)), ((), ())), preferred_element_type=f32)


def shared_body(
    hidden, attention, gain, grad, gate, up, down, normed, branch, back_grad, weight_grad
):
    residual = hidden[...].astype(f32) + attention[...].astype(f32)
    scale = lax.rsqrt(jnp.mean(residual * residual, axis=1, keepdims=True) + eps)
    normed_value, grad_value = (residual * scale * gain[...]).astype(bf16), grad[...]
    normed[...] = normed_value
    gate_value = contract(normed_value, gate[...])
    up_value = contract(normed_value, up[...])
    silu_value, slope = silu_parts(gate_value)
    act = (silu_value * up_value).astype(bf16)
    act_grad = contract(grad_value, down[...])
    gate_low = (act_grad * up_value * slope).astype(bf16)
    up_low = (act_grad * silu_value).astype(bf16)
    branch[...] = jnp.dot(act, down[...], preferred_element_type=f32)
    back_grad[...] = jnp.dot(gate_low, gate[...], preferred_element_type=f32) + jnp.dot(
        up_low, up[...], preferred_element_type=f32
    )
    lanes = weight_grad.shape[1] // 3
    blank = jnp.zeros((gate_low.shape[0], lanes - gate_low.shape[1]), bf16)
    parts = ((normed_value, gate_low), (normed_value, up_low), (grad_value, act))
    for index, (left, right) in enumerate(parts):
        right = jnp.concatenate([right, blank], axis=1)
        weight_grad[:, index * lanes : (index + 1) * lanes] = transposed(left, right).astype(bf16)


def shared_experts(hidden, attention, gain, grad, gate, up, down):
    units = gate.shape[0]
    return pl.pallas_call(
        shared_body,
        name="shared_experts",
        out_shape=(
            shape_of((2 * TS, D), bf16),
            shape_of((2 * TS, D), f32),
            shape_of((2 * TS, D), f32),
            shape_of((D, 3 * (units + (-units) % 128)), bf16),
        ),
        in_specs=[pl.BlockSpec(memory_space=VM)] * 7,
        out_specs=(pl.BlockSpec(memory_space=VM),) * 4,
        compiler_params=pltpu.CompilerParams(vmem_limit_bytes=VMEM_BYTES),
        cost_estimate=pl.CostEstimate(
            flops=8 * 10**9, bytes_accessed=24 * 10**6, transcendentals=10**6
        ),
    )(hidden, attention, gain, grad, gate, up, down)


def experts_body(
    slots, gates, normed, grad, branch_in, back_in, w_in, w_down,
    branch, back_grad, gate_grad, sums,
    dispatch, taken, taken_turned, given, routed, result, back_sum, branch_sum, back_total,
    act_turned, staged, down_staged, sems,
):
    expert, step = pl.program_id(0), pl.program_id(1)
    steps = pl.num_programs(1)
    capacity = dispatch.shape[0]
    units = w_down.shape[1]
    height = D // ROWS
    number = expert * steps + step
    slot = lax.rem(number, 2)
    down_rows = act_turned.shape[0] // ROWS

    def in_copy(slot, expert, step):
        target = sums.at[
            :,
            pl.ds(pl.multiple_of(expert * 2 * height, 2 * height), 2 * height),
            pl.ds(pl.multiple_of(step * units, units), units),
        ]
        return pltpu.make_async_copy(staged.at[slot], target, sems.at[slot])

    def down_copy(expert):
        first = pl.multiple_of(2 * EXP_DEV * height + expert * height, height)
        return pltpu.make_async_copy(down_staged, sums.at[:, pl.ds(first, height)], sems.at[2])

    @pl.when(step == 0)
    def _():
        places = lax.broadcasted_iota(jnp.int32, dispatch.shape, 0)
        chosen = places == slots[pl.ds(expert, 1)]
        dispatch[...] = chosen.astype(bf16)
        weight = jnp.sum(jnp.where(chosen, gates[pl.ds(expert, 1)], 0.0), axis=1, keepdims=True)
        rows = jnp.dot(dispatch[...], normed[...], preferred_element_type=f32).astype(bf16)
        taken[...] = rows
        taken_turned[...] = rows.T
        grads = jnp.dot(dispatch[...], grad[...], preferred_element_type=f32)
        given[...] = grads.astype(bf16)
        routed[...] = (weight * grads).astype(bf16)
        result[...] = jnp.zeros_like(result)
        back_sum[...] = jnp.zeros_like(back_sum)

    weights = jnp.concatenate([w_in[0], w_in[1]], axis=1)
    hidden = jnp.dot(taken[...], weights, preferred_element_type=f32)
    gate_value, up_value = hidden[:, :units], hidden[:, units:]
    silu_value, slope = silu_parts(gate_value)
    act = (silu_value * up_value).astype(bf16)
    act_turned[pl.ds(pl.multiple_of(step * units, units), units)] = act.T
    act_grad = contract(routed[...], w_down[0])
    low = jnp.concatenate(
        [
            (act_grad * up_value * slope).astype(bf16),
            (act_grad * silu_value).astype(bf16),
        ],
        axis=1,
    )
    result[...] += jnp.dot(act, w_down[0], preferred_element_type=f32)
    back_sum[...] += contract(low, weights)
    in_grad = jnp.dot(taken_turned[...], low, preferred_element_type=f32).astype(bf16)

    @pl.when(number >= 2)
    def _():
        in_copy(slot, expert, step).wait()

    staged[slot, :, :height] = in_grad[:, :units].reshape(ROWS, height, units)
    staged[slot, :, height:] = in_grad[:, units:].reshape(ROWS, height, units)
    in_copy(slot, expert, step).start()

    @pl.when(step == steps - 1)
    def _():
        places = lax.broadcasted_iota(jnp.int32, dispatch.shape, 0)
        chosen = places == slots[pl.ds(expert, 1)]
        weight = jnp.sum(jnp.where(chosen, gates[pl.ds(expert, 1)], 0.0), axis=1, keepdims=True)
        number = jnp.sum(result[...] * given[...].astype(f32), axis=1, keepdims=True)
        gate_grad[pl.ds(expert, 1)] = jnp.sum(
            jnp.where(chosen, number, 0.0), axis=0, keepdims=True
        )

        @pl.when(expert > 0)
        def _():
            down_copy(expert).wait()

        def down_step(part, carried):
            columns = pl.ds(pl.multiple_of(part * 256, 256), 256)
            value = jnp.dot(act_turned[...], routed[:, columns], preferred_element_type=f32)
            for owner in range(ROWS):
                block = value[owner * down_rows : (owner + 1) * down_rows]
                bands = [
                    jnp.concatenate(
                        [
                            block[low : low + 8, half * 128 : half * 128 + 128]
                            for low in range(0, down_rows, 8)
                        ],
                        axis=1,
                    )
                    for half in range(2)
                ]
                rows = pl.ds(pl.multiple_of(part * 16, 16), 16)
                down_staged[owner, rows] = jnp.concatenate(bands, axis=0).astype(bf16)
            return carried

        lax.fori_loop(0, D // 256, down_step, 0)
        down_copy(expert).start()
        outward = transposed(dispatch[...], (weight * result[...]).astype(bf16))
        inward = transposed(dispatch[...], back_sum[...].astype(bf16))

        @pl.when(expert == 0)
        def _():
            branch_sum[...] = branch_in[...] + outward
            back_total[...] = back_in[...] + inward

        @pl.when(expert == EXP_DEV - 1)
        def _():
            branch[...] = (branch_sum[...] + outward).astype(bf16)
            back_grad[...] = (back_total[...] + inward).astype(bf16)
            in_copy(1 - slot, expert, step).wait()
            in_copy(slot, expert, step).wait()
            down_copy(expert).wait()


def experts(capacity, slots, gates, normed, grad, branch_in, back_in, planes, w_down):
    units = 128
    hidden_units = w_down.shape[1]
    steps = hidden_units // units
    height = D // ROWS
    whole = pl.BlockSpec(memory_space=VM)
    in_block = pl.BlockSpec((2, D, units), lambda e, k: (e, 0, k))
    down_block = pl.BlockSpec((1, units, D), lambda e, k: (e, k, 0))
    return pl.pallas_call(
        experts_body,
        name="experts",
        grid=(EXP_DEV, steps),
        out_shape=(
            shape_of((2 * TS, D), bf16),
            shape_of((2 * TS, D), bf16),
            shape_of((8, 2 * TS), f32),
            shape_of((ROWS, 3 * EXP_DEV * height, hidden_units), bf16),
        ),
        in_specs=[whole] * 6 + [in_block, down_block],
        out_specs=(whole, whole, whole, pl.BlockSpec(memory_space=ANY)),
        scratch_shapes=[
            pltpu.VMEM((capacity, 2 * TS), bf16),
            pltpu.VMEM((capacity, D), bf16),
            pltpu.VMEM((D, capacity), bf16),
            pltpu.VMEM((capacity, D), bf16),
            pltpu.VMEM((capacity, D), bf16),
            pltpu.VMEM((capacity, D), f32),
            pltpu.VMEM((capacity, D), f32),
            pltpu.VMEM((2 * TS, D), f32),
            pltpu.VMEM((2 * TS, D), f32),
            pltpu.VMEM((hidden_units, capacity), bf16),
            pltpu.VMEM((2, ROWS, 2 * height, units), bf16),
            pltpu.VMEM((ROWS, height, hidden_units), bf16),
            pltpu.SemaphoreType.DMA((3,)),
        ],
        compiler_params=pltpu.CompilerParams(vmem_limit_bytes=VMEM_BYTES),
        cost_estimate=pl.CostEstimate(
            flops=40 * 10**9, bytes_accessed=80 * 10**6, transcendentals=10**6
        ),
    )(slots, gates, normed, grad, branch_in, back_in, planes, w_down)


def unpack_body(sums, gate, up, down):
    height = gate.shape[1]
    rows = down.shape[1]
    for expert in range(EXP_DEV):
        low = 2 * expert * height
        gate[expert] = sums[low : low + height].astype(f32)
        up[expert] = sums[low + height : low + 2 * height].astype(f32)
        low = (2 * EXP_DEV + expert) * height
        value = sums[low : low + height].astype(f32)
        for column in range(D // 128):
            band = value[column * 8 : column * 8 + 8]
            down[expert, :, column * 128 : column * 128 + 128] = jnp.concatenate(
                [band[:, tile * 128 : tile * 128 + 128] for tile in range(rows // 8)], axis=0
            )


def unpack(sums):
    height, units = D // ROWS, sums.shape[1]
    outs = (
        shape_of((EXP_DEV, height, units), f32),
        shape_of((EXP_DEV, height, units), f32),
        shape_of((EXP_DEV, units // ROWS, D), f32),
    )
    return simple_call(unpack_body, "unpack", outs, (sums,), 0, 7 * 10**6)


def finish_body(
    down_sum, query_up_sum, gains, shared_sum, first, numbers, residual, normed, scale, gain,
    query_down, latent_down, router, query_up, gain_first, gain_second, query_gain,
    latent_gain, shared_gate, shared_up, shared_down, hidden_grad,
):
    turned = down_sum[...].T
    query_rows, latent_rows = query_down.shape[0], latent_down.shape[0]
    query_down[...] = turned[:query_rows]
    latent_down[...] = turned[query_rows : query_rows + latent_rows]
    router[...] = turned[query_rows + latent_rows :]
    query_up[...] = jnp.concatenate(
        [query_up_sum[:, :192], query_up_sum[:, 256:], query_up_sum[:, 192:256]], axis=1
    )
    for col in range(COLS):
        gain_first[2 * col : 2 * col + 2] = gains[col, 0:2]
        gain_second[2 * col : 2 * col + 2] = gains[col, 2:4]
        query_gain[col : col + 1, :128] = gains[col, 4:5]
        query_gain[col : col + 1, 128:] = gains[col, 5:6, : query_rows - 128]
        latent_gain[col : col + 1] = gains[col, 6:7, :latent_rows]
    units = shared_gate.shape[0]
    lanes = shared_sum.shape[1] // 3
    for index, ref in enumerate((shared_gate, shared_up, shared_down)):
        part = shared_sum[:, index * lanes : (index + 1) * lanes].astype(f32)
        ref[...] = part.T[:units]
    total = numbers[0]
    for index in range(1, COLS):
        total = total + numbers[index]
    mean = total.T[:, :1] / D
    hidden_grad[...] = residual[...] + scale[...] * (
        first[...] * gain[...] - normed[...] * (scale[...] * mean)
    )


def finish(*terms):
    height, query_rows = D // ROWS, QL // COLS
    outs = (
        shape_of((query_rows, height), f32),
        shape_of((KV_COLS, height), f32),
        shape_of((terms[0].shape[1] - query_rows - KV_COLS, height), f32),
        shape_of(terms[1].shape, f32),
        shape_of((2 * COLS, 128), f32),
        shape_of((2 * COLS, 128), f32),
        shape_of((COLS, query_rows), f32),
        shape_of((COLS, KV_COLS), f32),
        *((shape_of((SHARED_UNITS, height), f32),) * 3),
        shape_of(terms[4].shape, f32),
    )
    return simple_call(finish_body, "finish", outs, terms, 0, 4 * 10**6)


def second_back_body(
    normed_sum, logits, router, hidden, attention, grad, gain, out_weight, attended, lse_rows,
    attended_grad, delta, delta_rows, out_grad, residual_here, router_grad, gain_grad, whole,
):
    total = logits[0]
    for index in range(1, COLS):
        total = total + logits[index]
    logit_low = total.T.astype(bf16)
    spare = jnp.zeros((8, 2 * TS), f32)
    wide = jnp.concatenate([spare, total, spare], axis=0).astype(bf16)
    normed_grad = normed_sum[...].astype(f32) + transposed(wide, router[256:])
    residual = hidden[...].astype(f32) + attention[...].astype(f32)
    scale = lax.rsqrt(jnp.mean(residual * residual, axis=1, keepdims=True) + eps)
    normed = residual * scale
    router_grad[...] = transposed((normed * gain[...]).astype(bf16), logit_low).astype(bf16)
    gain_grad[...] = jnp.broadcast_to(
        jnp.sum(normed_grad * normed, axis=0, keepdims=True), gain_grad.shape
    )
    weighted = normed_grad * gain[...]
    inner = jnp.mean(weighted * residual, axis=1, keepdims=True)
    residual_grad = (
        grad[...].astype(f32) + scale * weighted - residual * (scale * scale * scale * inner)
    )
    whole[...] = residual_grad
    width = residual_here.shape[1]
    first = pl.multiple_of(lax.axis_index("col") * width, 128)
    residual_here[...] = whole[:, pl.ds(first, width)]
    low = residual_grad.astype(bf16)
    found = contract(low, out_weight[...]).astype(bf16)
    attended_grad[...] = found
    weights = transposed(attended[...].astype(bf16), low).astype(bf16)
    for index in range(ROWS):
        out_grad[index] = weights[:, index * 128 : (index + 1) * 128]
    numbers = found.astype(f32) * attended[...]
    delta_rows[...] = lse_rows[...]
    for head in range(2):
        lanes = slice(head * 128, head * 128 + 128)
        number = jnp.sum(numbers[:, lanes], axis=1, keepdims=True)
        number = jnp.broadcast_to(number, (2 * TS, 128))
        delta[:, lanes] = number
        delta_rows[2 + head : 3 + head] = number.T[:1]


def second_back(*terms):
    rows = 2 * TS
    outs = (
        shape_of((rows, 256), bf16),
        shape_of((rows, 256), f32),
        shape_of((8, rows), f32),
        shape_of((ROWS, 256, D // ROWS), bf16),
        shape_of((rows, D // COLS), f32),
        shape_of((D, 16), bf16),
        shape_of((8, D), f32),
    )
    return pl.pallas_call(
        second_back_body,
        name="second_back",
        out_shape=outs,
        in_specs=[pl.BlockSpec(memory_space=VM)] * len(terms),
        out_specs=(pl.BlockSpec(memory_space=VM),) * len(outs),
        scratch_shapes=[pltpu.VMEM((rows, D), f32)],
        compiler_params=pltpu.CompilerParams(vmem_limit_bytes=VMEM_BYTES),
        cost_estimate=pl.CostEstimate(
            flops=2 * 10**9, bytes_accessed=16 * 10**6, transcendentals=512
        ),
    )(*terms)


def first_project_body(hidden, gain, weight, normed, query, latent):
    values = hidden[...].astype(f32)
    scale = lax.rsqrt(jnp.mean(values * values, axis=1, keepdims=True) + eps)
    low = (values * scale * gain[...]).astype(bf16)
    normed[...] = low
    found = contract(weight[...], low)
    height = query.shape[0]
    live = KV_COLS
    query[...] = found[:height].astype(bf16)
    blank = jnp.zeros((latent.shape[0] - live, found.shape[1]), f32)
    latent[...] = jnp.concatenate([found[height : height + live], blank], axis=0).astype(bf16)


def simple_call(body, name, outs, terms, flops, moved, scratch=()):
    return pl.pallas_call(
        body,
        name=name,
        out_shape=outs,
        in_specs=[pl.BlockSpec(memory_space=VM)] * len(terms),
        out_specs=(pl.BlockSpec(memory_space=VM),) * len(outs),
        scratch_shapes=list(scratch),
        compiler_params=pltpu.CompilerParams(vmem_limit_bytes=VMEM_BYTES),
        cost_estimate=pl.CostEstimate(flops=flops, bytes_accessed=moved, transcendentals=0),
    )(*terms)


def first_project(hidden, gain, weight):
    outs = (
        shape_of((2 * TS, D), bf16),
        shape_of((QL // COLS, 2 * TS), bf16),
        shape_of((KV_COLS + (-KV_COLS) % 16, 2 * TS), bf16),
    )
    return simple_call(
        first_project_body, "first_project", outs, (hidden, gain, weight), 10**9, 6 * 10**6
    )


def swap_halves(tile):
    lane = lax.broadcasted_iota(jnp.int32, tile.shape, 1)
    lower = lax.rem(lane, DR) < DR // 2
    return jnp.where(lower, pltpu.roll(tile, 128 - DR // 2, 1), pltpu.roll(tile, DR // 2, 1))


def project_body(
    query_raw, latent_raw, query_gain, latent_gain, query_up, latent_up, cos, sin,
    query_in, latent_in, query, near,
):
    def normed(values, gain):
        scale = lax.rsqrt(jnp.mean(values * values, axis=0, keepdims=True) + eps)
        column = jnp.broadcast_to(gain[...], (8, gain.shape[1])).T[:, :1]
        return (values * scale * column).astype(bf16)

    low = normed(query_raw[...].astype(f32), query_gain)
    query_in[...] = low
    found = transposed(low, query_up[...])
    middle = found[:, 128:256]
    query[:, :128] = found[:, :128].astype(bf16)
    query[:, 128:256] = (middle * cos[...] + swap_halves(middle) * sin[...]).astype(bf16)
    query[:, 256:] = found[:, 256:].astype(bf16)
    raw = latent_raw[...].astype(f32)
    low = normed(raw[:KL], latent_gain)
    latent_in[...] = low
    found = transposed(low, latent_up[...]).astype(bf16)
    rope = jnp.concatenate([raw[KL:], raw[KL:]], axis=0).T
    near[:, :128] = found[:, :128]
    near[:, 128:256] = (rope * cos[...] + swap_halves(rope) * sin[...]).astype(bf16)
    near[:, 256:384] = found[:, 256:384]
    near[:, 384:512] = found[:, 128:256]
    near[:, 512:] = found[:, 384:]


def project(*terms):
    outs = (
        shape_of((QL, 2 * TS), bf16),
        shape_of((KL, 2 * TS), bf16),
        shape_of((2 * TS, 384), bf16),
        shape_of((2 * TS, 640), bf16),
    )
    return simple_call(project_body, "project", outs, terms, 2 * 10**9, 8 * 10**6)


def latent_back_body(
    query_sum, kv_sum, numbers, query_raw, kv_raw, query_gain, kv_gain, live, query_square, kv_square,
    normed, weight, gain, hidden, router_grad, second_gain,
    first_part, first_numbers, down_grad, gains,
):
    total = numbers[0]
    for index in range(1, COLS):
        total = total + numbers[index]
    query_scale = lax.rsqrt(query_square[:1] + eps)
    kv_scale = lax.rsqrt(kv_square[:1] + eps)
    query_raw_value = query_raw[...].astype(f32)
    kv_raw_value = kv_raw[...].astype(f32)
    query_value = query_sum[...]
    kv_value = kv_sum[: kv_raw.shape[0]]
    query_normed, kv_normed = query_raw_value * query_scale, kv_raw_value * kv_scale


    def as_row(values):
        number = jnp.sum(values, axis=1, keepdims=True)
        return jnp.broadcast_to(number, (values.shape[0], 128)).T[:1]

    row = as_row(query_value * query_normed)
    gains[...] = jnp.zeros_like(gains)
    gains[2:4] = second_gain[...]
    gains[4:5] = row[:, :128]
    gains[5:6, : row.shape[1] - 128] = row[:, 128:]
    gains[6:7, : kv_value.shape[0]] = as_row(kv_value * kv_normed)
    query_low = query_scale * (query_value * query_gain[...]) - query_normed * (
        query_scale * query_scale * (total[0:1] / QL)
    )
    kv_low = kv_scale * (kv_value * kv_gain[...]) - kv_normed * (
        kv_scale * kv_scale * (total[1:2] / KL)
    )
    kv_low = jnp.where(live[...] > 0, kv_low, kv_value)
    width = query_low.shape[0] + kv_low.shape[0]
    spare = jnp.zeros((weight.shape[0] - width, 2 * TS), f32)
    turned = jnp.concatenate([query_low, kv_low, spare], axis=0).T.astype(bf16)
    part = jnp.dot(turned, weight[...], preferred_element_type=f32)
    first_part[...] = part.astype(bf16)
    number = jnp.sum(part * gain[...] * hidden[...].astype(f32), axis=1, keepdims=True)
    first_numbers[...] = jnp.broadcast_to(number, (2 * TS, 128)).T[:8]
    grads = transposed(normed[...], turned).astype(bf16)
    down_grad[:, :width] = grads[:, :width]
    down_grad[:, width:] = router_grad[...]


def latent_back(*terms):
    width = terms[3].shape[0] + terms[4].shape[0] + terms[14].shape[1]
    outs = (
        shape_of((2 * TS, D), bf16),
        shape_of((8, 2 * TS), f32),
        shape_of((D, width), bf16),
        shape_of((8, 128), f32),
    )
    return simple_call(latent_back_body, "latent_back", outs, terms, 2 * 10**9, 10**7)


def rope_tables(positions, width):
    half_width = width // 2
    frequency = jnp.exp(
        -jnp.log(rope_base) * (2.0 * jnp.arange(half_width, dtype=jnp.float32) / width)
    )
    angles = positions.astype(jnp.float32)[:, None] * frequency[None, :]
    return (jnp.cos(angles), jnp.sin(angles))


def rms_scale(values):
    return lax.rsqrt(jnp.mean(values * values, axis=-1, keepdims=True) + eps)


def product(left, right):
    return jnp.dot(left, right, preferred_element_type=jnp.float32)


def left_product(left, right):
    return lax.dot_general(
        left, right, (((0,), (0,)), ((), ())), preferred_element_type=jnp.float32
    )


def right_product(left, right):
    return lax.dot_general(
        left, right, (((1,), (1,)), ((), ())), preferred_element_type=jnp.float32
    )


def turned_product(left, right):
    return lax.dot_general(
        left, right, (((0,), (1,)), ((), ())), preferred_element_type=jnp.float32
    )


def einsum(text, *terms):
    return jnp.einsum(text, *terms, preferred_element_type=f32)


def to_blocks(term):
    return term.reshape(2, RING, 2, term.shape[0] // ROWS, term.shape[1])


def local(
    hidden_in,
    gain_first,
    query_down,
    query_gain,
    query_up,
    latent_down,
    latent_gain,
    latent_up,
    attention_out,
    gain_second,
    router,
    expert_gate,
    expert_up,
    expert_down,
    shared_gate,
    shared_up,
    shared_down,
    seq_lens,
    routes,
    out_grad,
):
    row_index = lax.axis_index("row")
    col_index = lax.axis_index("col")
    seq_count, local_len, col_width = hidden_in.shape
    row_total = seq_count * local_len
    experts_all = EXP_DEV * COLS
    most_rows = (5 * local_len * TOPK + 4 * experts_all - 1) // (4 * experts_all)
    capacity = seq_count * most_rows
    query_cols = QL // COLS
    kv_cols = (KL + DR) // COLS

    def here(values, axis=-1):
        width = values.shape[axis] // COLS
        return lax.dynamic_slice_in_dim(values, col_index * width, width, axis)

    split = DN + DR
    (
        hidden_low,
        grad_full,
        down_all,
        query_up_pack,
        latent_up_all,
        attention_out_all,
        shared_gate_all,
        shared_up_all,
        shared_down_all,
        planes,
        down_chip,
    ) = front(
        hidden_in.reshape(row_total, col_width),
        out_grad.reshape(row_total, col_width),
        jnp.pad(
            jnp.concatenate([query_down.T, latent_down.T, router.T], axis=0), ((0, 8), (0, 0))
        ),
        jnp.concatenate(
            [query_up[:, :split], query_up[:, split + DN :], query_up[:, split : split + DN]],
            axis=1,
        ),
        latent_up,
        attention_out,
        shared_gate.T,
        shared_up.T,
        shared_down,
        expert_gate,
        jnp.pad(expert_down, ((0, 0), (0, (-expert_down.shape[1]) % 16), (0, 0))),
        expert_gate.shape[2],
    )
    expert_units = expert_gate.shape[2]
    latent_width = query_cols + kv_cols
    router_turned = down_all[latent_width : latent_width + experts_all]
    kv_pad = (-kv_cols) % 16
    normed_first, query_here, latent_here = first_project(hidden_low, gain_first[None], down_all)
    query_latent, _, latent_all, planes = latents(
        query_here,
        latent_here,
        expert_gate,
        expert_up,
        planes,
    )
    kv_latent = lax.dynamic_index_in_dim(latent_all, row_index, 1, False)
    kv_latent = kv_latent[:, :kv_cols].reshape(KL + DR, row_total)
    latent_pad = ((0, 0), (0, kv_pad), (0, 0))
    within_cos, within_sin = rope_tables(jnp.arange(local_len, dtype=jnp.int32), DR)
    start_cos, start_sin = rope_tables(jnp.arange(ROWS, dtype=jnp.int32) * local_len, DR)
    kvt_all = expand(
        latent_all,
        jnp.pad(
            jnp.pad(latent_up_all, ((0, DR), (0, 0))).reshape(COLS, kv_cols, -1), latent_pad
        ).reshape(COLS * (kv_cols + kv_pad), -1).T,
        jnp.pad(
            jnp.pad(latent_gain, (0, DR)).reshape(COLS, kv_cols, 1), latent_pad
        ).reshape(COLS * (kv_cols + kv_pad), 1),
        within_cos.T,
        within_sin.T,
        start_cos[:, :, None],
        start_sin[:, :, None],
    )
    lane = jnp.arange(2 * DR, dtype=jnp.int32)[None, :]
    position = row_index * local_len + jnp.arange(row_total, dtype=jnp.int32) % local_len
    frequency = jnp.exp(-math.log(rope_base) * (2.0 / DR) * (lane % (DR // 2)).astype(f32))
    angles = position.astype(f32)[:, None] * frequency
    tile_cos = jnp.cos(angles)
    tile_sin = jnp.where(lane % DR < DR // 2, -1.0, 1.0) * jnp.sin(angles)
    query_input, latent_input, query_pack, near = project(
        query_latent,
        kv_latent,
        query_gain[None],
        latent_gain[None],
        query_up_pack,
        latent_up_all,
        tile_cos,
        tile_sin,
    )
    attended_float, lse, lse_rows = attend(seq_lens, query_pack, kvt_all)
    attended = attended_float.astype(bf16)
    attention_part = product(attended, attention_out_all).astype(bf16)
    attention_sum, planes, expert_down_all = attention_sum_over_col(
        attention_part, expert_up, down_chip, planes
    )
    query_all = lax.all_gather(query_pack, "row", axis=0, tiled=False)

    attention_sum, query_all = lax.optimization_barrier((attention_sum, query_all))
    normed_second, shared_branch, shared_back, shared_grad = shared_experts(
        hidden_low,
        attention_sum,
        gain_second[None],
        grad_full,
        shared_gate_all,
        shared_up_all,
        shared_down_all,
    )
    logits = right_product(router_turned, normed_second)
    sigmoid_all = jax.nn.sigmoid(logits)
    routes_turned = routes.reshape(row_total, TOPK).T
    chosen = jnp.sum(
        (
            routes_turned[:, None, :] == jnp.arange(experts_all, dtype=jnp.int32)[None, :, None]
        ).astype(f32),
        axis=0,
    )
    weighted_sig = sigmoid_all * chosen
    denominator = jnp.sum(weighted_sig, axis=0, keepdims=True)
    gate_weights = route_scale * weighted_sig / denominator
    gate_here = here(gate_weights, 0)
    member = here(chosen, 0).reshape(EXP_DEV * seq_count, local_len)
    before = jnp.triu(jnp.ones((local_len, local_len), bf16), 1)
    rank = product(member.astype(bf16), before).reshape(EXP_DEV, seq_count, local_len)
    rank = rank + (jnp.arange(seq_count, dtype=f32) * most_rows)[None, :, None]
    slots = jnp.where(member.reshape(rank.shape) > 0, rank, float(capacity))
    slots = slots.astype(jnp.int32).reshape(EXP_DEV, row_total)
    branch_part, normed_part, gate_grad_here, expert_part = experts(
        capacity,
        slots,
        gate_here,
        normed_second,
        grad_full,
        shared_branch,
        shared_back,
        planes,
        expert_down_all,
    )
    shared_sum = lax.psum_scatter(shared_grad, "row", scatter_dimension=0, tiled=True)
    expert_sum = lax.psum_scatter(
        expert_part.reshape(-1, expert_units), "row", scatter_dimension=0, tiled=True
    )
    gate_grad_all = lax.dynamic_update_slice_in_dim(
        jnp.zeros((experts_all, row_total), f32), gate_grad_here[:EXP_DEV], col_index * EXP_DEV, 0
    )
    inner_sum = jnp.sum(gate_grad_all * gate_weights, axis=0, keepdims=True)
    logit_part = (
        sigmoid_all
        * (1.0 - sigmoid_all)
        * chosen
        / denominator
        * (route_scale * gate_grad_all - inner_sum)
    )
    normed_sum, logit_all = sum_over_col(
        "sum_normed", 5, normed_part, NORMED_CUT, logit_part, experts_all
    )
    (
        attended_grad,
        delta,
        stats,
        attention_out_grad,
        residual_here,
        router_grad,
        gain_second_grad,
    ) = second_back(
        normed_sum,
        logit_all,
        down_all,
        hidden_low,
        attention_sum,
        grad_full,
        gain_second[None],
        attention_out_all,
        attended_float,
        lse_rows,
    )
    attended_grad_all, stats_all, branch_here = back(attended_grad, stats, branch_part)
    hidden_here = here(hidden_low).astype(f32)
    attended_here = here(attention_sum).astype(f32)
    block_out = (
        (hidden_here + attended_here + branch_here).astype(bf16).reshape(seq_count, local_len, col_width)
    )
    dq, dk, dv = attend_back(
        seq_lens,
        query_pack,
        kvt_all,
        attended_grad,
        lse,
        delta,
        near,
        query_all,
        attended_grad_all,
        stats_all,
    )
    query_up_grad, latent_up_grad, query_in_grad, kv_part, numbers = project_back(
        dq,
        dk,
        dv,
        tile_cos,
        tile_sin,
        query_up_pack,
        latent_up_all,
        query_input,
        latent_input,
        query_latent,
        kv_latent[:KL],
        query_gain[:, None],
        latent_gain[:, None],
    )
    kv_part = jnp.pad(kv_part.reshape(COLS, kv_cols, row_total), latent_pad)
    shared_width = shared_gate.shape[1]
    (query_in_here, kv_in_here), numbers_all, summed = col_and_row(
        "sum_latents",
        7,
        "lead",
        (query_in_grad.reshape(COLS, query_cols, row_total), kv_part),
        ((query_cols, row_total), (kv_cols + kv_pad, row_total)),
        (128, 80),
        numbers,
        (attention_out_grad.reshape(2, RING, 2, col_width, D // ROWS),),
        (96,),
    )
    (attention_out_sum,) = summed
    is_latent = (col_index * kv_cols + jnp.arange(kv_cols)) < KL
    latent_gain_here = here(jnp.concatenate([latent_gain, jnp.ones((DR,), f32)]))
    query_square, kv_square = (
        jnp.broadcast_to(
            jnp.mean(jnp.square(values.astype(f32)), axis=0, keepdims=True), (8, row_total)
        )
        for values in (query_latent, kv_latent[:KL])
    )
    first_part, first_numbers, down_grads, gains = latent_back(
        query_in_here,
        kv_in_here,
        numbers_all,
        here(query_latent, 0),
        here(kv_latent, 0),
        here(query_gain)[:, None],
        latent_gain_here[:, None],
        is_latent.astype(f32)[:, None],
        query_square,
        kv_square,
        normed_first,
        down_all,
        gain_first[None],
        hidden_low,
        router_grad,
        here(gain_second_grad[0]).reshape(2, 128),
    )
    scale_first = rms_scale(hidden_low.astype(f32))
    normed_here = hidden_here * scale_first
    (first_here, first_numbers_all, gains_all), summed = first_sum(
        first_part,
        first_numbers,
        normed_here,
        gains,
        (to_blocks(down_grads), to_blocks(query_up_grad), to_blocks(latent_up_grad)),
        (0, QL // ROWS, KL // ROWS),
    )
    down_sum, query_up_sum, latent_up_sum = summed
    expert_gate_grad, expert_up_grad, expert_down_grad = unpack(expert_sum)
    (
        query_down_grad,
        latent_down_grad,
        router_grad,
        query_up_grad,
        gain_first_grad,
        gain_second_grad,
        query_gain_grad,
        latent_gain_grad,
        shared_gate_grad,
        shared_up_grad,
        shared_down_grad,
        hidden_grad,
    ) = finish(
        down_sum,
        query_up_sum,
        gains_all,
        shared_sum,
        first_here,
        first_numbers_all,
        residual_here,
        normed_here,
        scale_first,
        here(gain_first)[None],
    )
    return (
        block_out,
        hidden_grad.reshape(seq_count, local_len, col_width),
        gain_first_grad.reshape(D),
        query_down_grad.T,
        query_gain_grad.reshape(QL),
        query_up_grad,
        latent_down_grad.T,
        latent_gain_grad.reshape(KL + DR)[:KL],
        latent_up_sum,
        attention_out_sum,
        gain_second_grad.reshape(D),
        router_grad.T,
        expert_gate_grad,
        expert_up_grad,
        expert_down_grad,
        shared_gate_grad.T,
        shared_up_grad.T,
        shared_down_grad,
    )


def solution(mesh):
    in_specs = (
        P(None, "row", "col"),
        P(),
        P("row", "col"),
        P(),
        P("row", "col"),
        P("row", "col"),
        P(),
        P("row", "col"),
        P("col", "row"),
        P(),
        P("row", None),
        P("col", "row", None),
        P("col", "row", None),
        P("col", "row", None),
        P("row", "col"),
        P("row", "col"),
        P("col", "row"),
        P(),
        P(None, "row", None),
        P(None, "row", "col"),
    )
    out_specs = (
        P(None, "row", "col"),
        P(None, "row", "col"),
        P(),
        P("row", "col"),
        P(),
        P("row", "col"),
        P("row", "col"),
        P(),
        P("row", "col"),
        P("col", "row"),
        P(),
        P("row", None),
        P("col", "row", None),
        P("col", "row", None),
        P("col", "row", None),
        P("row", "col"),
        P("row", "col"),
        P("col", "row"),
    )
    return jax.shard_map(local, mesh=mesh, in_specs=in_specs, out_specs=out_specs, check_vma=False)
```
